32 devices in a mesh: gx: 4 (over z), gy: 4 (over x, core), gz: 2 (over y).
Axes of the slice: x: 2, y: 2, z: 4, core: 2. Of those that a mesh axis runs over, the one named last changes fastest.
Arguments:
- adjoint_efield: float32 [3, 48, 32, 2048], P(None, 'gz', 'gx', 'gy'), may hold values from -6 to 6
- adjoint_hfield: float32 [3, 48, 32, 2048], P(None, 'gz', 'gx', 'gy'), may hold values from -6 to 6
- forward_efield: float32 [3, 48, 32, 2048], P(None, 'gz', 'gx', 'gy'), may hold values from -6 to 6
- material: int32 [48, 32, 2048], P('gz', 'gx', 'gy'), may hold values from 0 to 3
- permittivity: float32 [4], replicated, may hold values from 1 to 12
- design_mask: int32 [4, 256], P('gx', 'gy'), may hold values 0 or 1
- grad_sum: float32 [32, 32, 2048], P('gz', 'gx', 'gy'), may hold values from -6 to 6
Outputs:
- efield_next: float32 [3, 48, 32, 2048], P(None, 'gz', 'gx', 'gy')
- hfield_next: float32 [3, 48, 32, 2048], P(None, 'gz', 'gx', 'gy')
- grad_total: float32 [32, 32, 2048], P('gz', 'gx', 'gy')
- grad_filtered: float32 [32, 32, 2048], P('gz', 'gx', 'gy')
The draws below stay inside these ranges and needn't reach their ends.
Inputs may be any that keep to these rules, and one draw needn't show every extreme that they name: material indices name rows of permittivity.
All inputs are finite; a program needn't handle non-finite values. No bound on the sum of `design_mask` on one device may be relied on, other than what follows from the above.
Results may differ from the reference program's by a relative error of at most 0.0003.
Values sent between devices are 32-bit elements; how exact they have to be, the bound alone decides.
No kernel may reach another device: no remote copies, remote signals or barrier semaphores. Data moves between devices by JAX's collectives and lax.ppermute only.
A program may use at most 128 MiB of HBM per device.

```python
import math
import jax
import jax.numpy as jnp
from jax import lax

CZ = 24
LAY_DEV = 16
RADIUS = 6
BLOCK = 8
MATS = 4
NX = 32
NY = 2048
NZ = 48
LAYERS = 32


def touch_ends(entries, key, smallest, high):
    index_at = [jax.random.randint(jax.random.fold_in(key, axis), (), 0, length) for axis, length in enumerate(entries.shape)]
    widest = entries.shape.index(max(entries.shape))
    neighbour = index_at[:widest] + [(index_at[widest] + 1) % entries.shape[widest]] + index_at[widest + 1:]
    return entries.at[tuple(index_at)].set(smallest).at[tuple(neighbour)].set(high)


def block_scale(rng, shape, cuts, low, high):
    loudness = 1.0
    for axis_at, blocks in cuts:
        heights = jax.random.uniform(jax.random.fold_in(jax.random.fold_in(rng, 6), axis_at), (blocks,), jnp.float32, low / len(cuts), high / len(cuts))
        loudness = loudness * jnp.repeat(jnp.exp(heights), shape[axis_at] // blocks).reshape((-1,) + (1,) * (len(shape) - 1 - axis_at))
    return loudness


def scatter_about(rng, dims, scale, limit, shards=(), kind=jnp.bfloat16):
    result = scale * jax.random.normal(rng, dims, jnp.float32)
    if shards:
        result = result * block_scale(rng, dims, shards, -0.22, 0.18)
    return jnp.clip(result, -limit, limit).astype(kind)


def setup_inputs(seed: int = 0) -> dict:
    streams_of = jax.random.split(jax.random.key(seed), 8)
    adjoint_efield = scatter_about(streams_of[0], (3, NZ, NX, NY), 1.0, 6.0, ((1, 2), (2, 4), (3, 4)), jnp.float32)
    adjoint_hfield = scatter_about(streams_of[1], (3, NZ, NX, NY), 1.0, 6.0, ((1, 2), (2, 4), (3, 4)), jnp.float32)
    forward_efield = scatter_about(streams_of[2], (3, NZ, NX, NY), 1.0, 6.0, ((1, 2), (2, 4), (3, 4)), jnp.float32)
    material = touch_ends(jax.random.randint(streams_of[3], (NZ, NX, NY), 0, MATS), jax.random.fold_in(streams_of[3], 1), 0, MATS - 1).astype(jnp.int32)
    permittivity = jnp.clip(jnp.exp(jax.random.uniform(streams_of[4], (MATS,), jnp.float32, math.log(1.0), math.log(12.0))), 1.0, 12.0)
    design_mask = touch_ends((jax.random.randint(streams_of[5], (NX // BLOCK, NY // BLOCK), 0, 2) < 1).astype(jnp.int32), jax.random.fold_in(streams_of[5], 1), 0, 1)
    grad_sum = scatter_about(streams_of[6], (LAYERS, NX, NY), 1.0, 6.0, ((0, 2), (1, 4), (2, 4)), jnp.float32)
    return dict(adjoint_efield=adjoint_efield, adjoint_hfield=adjoint_hfield, forward_efield=forward_efield, material=material, permittivity=permittivity, design_mask=design_mask, grad_sum=grad_sum)


COURANT = 0.5

def curl(parts, differ):
    return (differ(parts[2], 2) - differ(parts[1], 0), differ(parts[0], 0) - differ(parts[2], 1), differ(parts[1], 1) - differ(parts[0], 2))

def advance(extended, inv_permit):
    inner_shape = (extended.shape[1] - 2, extended.shape[2] - 2, extended.shape[3] - 2)
    outer_shape = tuple((count + 1 for count in inner_shape))

    def forward(field, direction):
        unit_step = tuple((1 if which == direction else 0 for which in range(3)))
        upper_part = lax.slice(field, unit_step, tuple((a + b for a, b in zip(unit_step, outer_shape))))
        return upper_part - lax.slice(field, (0, 0, 0), outer_shape)

    def backward(field, direction):
        lower_start = tuple((0 if which == direction else 1 for which in range(3)))
        centre_part = lax.slice(field, (1, 1, 1), tuple((1 + count for count in inner_shape)))
        return centre_part - lax.slice(field, lower_start, tuple((a + b for a, b in zip(lower_start, inner_shape))))
    efield_old = [extended[component] for component in range(3)]
    curl_e = curl(efield_old, forward)
    h_new = [lax.slice(extended[3 + component], (0, 0, 0), outer_shape) - COURANT * curl_e[component] for component in range(3)]
    curl_h = curl(h_new, backward)
    inner_end = tuple((1 + count for count in inner_shape))
    e_next = [lax.slice(efield_old[component], (1, 1, 1), inner_end) + COURANT * inv_permit * curl_h[component] for component in range(3)]
    h_next = [lax.slice(h_new[component], (1, 1, 1), inner_end) for component in range(3)]
    return (jnp.stack(e_next), jnp.stack(h_next))

def inverse_permittivity(material, permittivity):
    permit = jnp.zeros(material.shape, jnp.float32)
    for which in range(permittivity.shape[0]):
        permit = permit + jnp.where(material == which, permittivity[which], jnp.float32(0.0))
    return 1.0 / permit

def expand_mask(design_mask):
    return jnp.repeat(jnp.repeat(design_mask, BLOCK, 0), BLOCK, 1).astype(jnp.float32)

def cone_weight(offset_x, offset_y, radius):
    distance = jnp.sqrt(offset_x * offset_x + offset_y * offset_y)
    return jnp.maximum(jnp.float32(radius) - distance, jnp.float32(0.0))

def cone_total(radius):
    span_values = jnp.arange(2 * radius + 1, dtype=jnp.float32) - radius
    return jnp.sum(cone_weight(span_values[:, None], span_values[None, :], radius))

def reference(adjoint_efield, adjoint_hfield, forward_efield, material, permittivity, design_mask, grad_sum):
    stacked = jnp.concatenate([adjoint_efield, adjoint_hfield], axis=0)
    extended = jnp.pad(stacked, ((0, 0), (1, 1), (1, 1), (1, 1)))
    efield_next, hfield_next = advance(extended, inverse_permittivity(material, permittivity))
    slab_first = CZ - LAY_DEV
    design_e = efield_next[:, slab_first:slab_first + LAYERS]
    design_f = forward_efield[:, slab_first:slab_first + LAYERS]
    grad_total = grad_sum + expand_mask(design_mask)[None] * lax.optimization_barrier(jnp.sum(design_f * design_e, axis=0))
    symmetric = grad_total + jnp.flip(grad_total, 1)
    padded = jnp.pad(symmetric, ((0, 0), (RADIUS, RADIUS), (RADIUS, RADIUS)))
    weight_sum = cone_total(RADIUS)
    filtered = jnp.zeros(symmetric.shape, jnp.float32)
    for shift_x in range(2 * RADIUS + 1):
        for shift_y in range(2 * RADIUS + 1):
            weight = cone_weight(jnp.float32(shift_x - RADIUS), jnp.float32(shift_y - RADIUS), RADIUS) / weight_sum
            filtered = filtered + weight * padded[:, shift_x:shift_x + NX, shift_y:shift_y + NY]
    return (efield_next, hfield_next, grad_total, filtered)
```

```python
import functools
import math

import jax
import jax.numpy as jnp
import numpy as np
from jax import lax
from jax.experimental import pallas as pl
from jax.experimental.pallas import tpu as pltpu
from jax.sharding import PartitionSpec as P

RADIUS = 6
BLOCK = 8
HALF = 0.5

ROWS = 8
LANES = 128
STRIP = 8
SLOTS = LANES // STRIP
VMEM_LIMIT = 24 * 1024 * 1024

VMEM = pl.BlockSpec(memory_space=pltpu.VMEM)
SMEM = pl.BlockSpec(memory_space=pltpu.SMEM)


def params():
    return pltpu.CompilerParams(vmem_limit_bytes=VMEM_LIMIT)


def f32(*shape):
    return jax.ShapeDtypeStruct(shape, jnp.float32)


def exchange(to_lower, to_upper, axis):
    count = lax.axis_size(axis)
    zero = jnp.zeros_like(to_lower)
    if count == 1:
        return zero, zero
    odd = lax.axis_index(axis) % 2 == 1
    even_pairs = [(i, i + 1) for i in range(0, count - 1, 2)]
    odd_pairs = [(i, i + 1) for i in range(1, count - 1, 2)]

    def swap(value, pairs):
        return lax.ppermute(value, axis, pairs + [(b, a) for a, b in pairs])

    first = swap(jnp.where(odd, to_lower, to_upper), even_pairs)
    second = swap(jnp.where(odd, to_upper, to_lower), odd_pairs) if odd_pairs else zero
    return jnp.where(odd, first, second), jnp.where(odd, second, first)


def z_faces_kernel(e_low, e_high, h_high, low_ref, high_ref):
    low_ref[0] = e_low[0, 0]
    low_ref[1] = e_low[1, 0]
    low_ref[2] = jnp.zeros_like(e_low[0, 0])
    ez = e_high[2, 0]
    high_ref[0] = h_high[0, 0] + HALF * ez - HALF * e_high[1, 0]
    high_ref[1] = h_high[1, 0] + HALF * e_high[0, 0] - HALF * ez
    high_ref[2] = ez


def z_faces(efield, hfield):
    _, cells_z, cells_x, cells_y = efield.shape
    block = (3, 1, cells_x, cells_y)
    face = f32(3, cells_x, cells_y)
    whole = pl.BlockSpec((3, cells_x, cells_y), lambda i: (0, 0, 0))
    return pl.pallas_call(
        z_faces_kernel,
        grid=(1,),
        in_specs=[
            pl.BlockSpec(block, lambda i: (0, 0, 0, 0)),
            pl.BlockSpec(block, lambda i: (0, cells_z - 1, 0, 0)),
            pl.BlockSpec(block, lambda i: (0, cells_z - 1, 0, 0)),
        ],
        out_specs=[whole, whole],
        out_shape=[face, face],
        compiler_params=params(),
    )(efield, efield, hfield)


def x_faces_kernel(e_ref, h_ref, below_ref, above_ref, low_ref, high_ref, rows_ref):
    cells_z = e_ref.shape[1]
    last = ROWS - 1
    low_ref[...] = jnp.zeros_like(low_ref)
    for z in range(cells_z):
        low_ref[z : z + 1, :] = e_ref[1, z, 0:1, :]
        low_ref[cells_z + z : cells_z + z + 1, :] = e_ref[2, z, 0:1, :]
        for c in range(3):
            rows_ref[c, z : z + 1, :] = e_ref[c, z, last : last + 1, :]
        for c in range(2):
            rows_ref[3 + c, z : z + 1, :] = h_ref[1 + c, z, last : last + 1, :]
        if z > 0:
            rows_ref[5, z - 1 : z, :] = e_ref[0, z, last : last + 1, :]
    rows_ref[5, cells_z - 1 : cells_z, :] = above_ref[0, last : last + 1, :]
    low_ref[2 * cells_z : 2 * cells_z + 1, :] = below_ref[2, 0:1, :]
    ex = rows_ref[0]
    high_ref[0:cells_z, :] = rows_ref[3] - HALF * (rows_ref[5] - ex + rows_ref[2])
    high_ref[cells_z : 2 * cells_z, :] = rows_ref[4] + HALF * rows_ref[1] - HALF * ex
    high_ref[2 * cells_z : 3 * cells_z, :] = ex


def x_faces(efield, hfield, below, above):
    cells_z, cells_y = efield.shape[1], efield.shape[3]
    face = f32(3 * cells_z, cells_y)
    return pl.pallas_call(
        x_faces_kernel,
        in_specs=[VMEM] * 4,
        out_specs=[VMEM] * 2,
        out_shape=[face, face],
        scratch_shapes=[pltpu.VMEM((6, cells_z, cells_y), jnp.float32)],
        compiler_params=params(),
    )(efield, hfield, below, above)


def lane_group():
    return lax.broadcasted_iota(jnp.int32, (ROWS, LANES), 1) // STRIP


def pack_strips(tiles, low_ref, high_ref, first):
    group = lane_group()
    width = tiles[0][1]
    for start in range(0, len(tiles), SLOTS):
        low = jnp.zeros((ROWS, LANES), jnp.float32)
        high = jnp.zeros((ROWS, LANES), jnp.float32)
        for k, (load, _) in enumerate(tiles[start : start + SLOTS]):
            if load is None:
                continue
            here = group == k
            shift = (STRIP * k) % LANES
            left = load(slice(0, LANES))
            right = load(slice(width - LANES, width))
            low = jnp.where(here, pltpu.roll(left, shift, 1) if shift else left, low)
            shift = (STRIP * k + STRIP) % LANES
            high = jnp.where(here, pltpu.roll(right, shift, 1) if shift else right, high)
        low_ref[first + start // SLOTS] = low
        high_ref[first + start // SLOTS] = high


def y_own_kernel(e_ref, h_ref, f_ref, mat_ref, grad_ref, mask_ref, place_ref, low_ref, high_ref, wide_ref):
    cells_z, width = e_ref.shape[1], e_ref.shape[3]
    layers = grad_ref.shape[0]
    blocks = mask_ref.shape[1]
    spread = (
        lax.broadcasted_iota(jnp.int32, (blocks, width), 0)
        == lax.broadcasted_iota(jnp.int32, (blocks, width), 1) // BLOCK
    ).astype(jnp.float32)
    mask = jnp.broadcast_to(mask_ref[...].astype(jnp.float32), (ROWS, blocks))
    wide_ref[...] = jnp.dot(mask, spread, preferred_element_type=jnp.float32)
    first = place_ref[1]
    tiles = []
    for z in range(cells_z):
        for ref in (e_ref, h_ref):
            for c in range(3):
                tiles.append((lambda s, r=ref, c=c, z=z: r[c, z, :, s], width))
    for layer in range(layers):
        for c in range(3):
            tiles.append((lambda s, c=c, l=layer: f_ref[c, first + l, :, s], width))
        tiles.append((lambda s, l=layer: mat_ref[first + l, :, s].astype(jnp.float32), width))
        tiles.append((lambda s, l=layer: grad_ref[l, :, s], width))
        tiles.append((lambda s: wide_ref[:, s], width) if layer % ROWS == 0 else (None, width))
    pack_strips(tiles, low_ref, high_ref, 0)


def y_halo_kernel(own_low, own_high, below_ref, above_ref, left_ref, right_ref, low_ref, high_ref):
    count = own_low.shape[0]
    width = below_ref.shape[2]
    low_ref[0:count] = own_low[...]
    high_ref[0:count] = own_high[...]
    pack_strips(halo_tiles(below_ref, above_ref, left_ref, right_ref, width), low_ref, high_ref, count)


def halo_tiles(below_ref, above_ref, left_ref, right_ref, width):
    tiles = []
    for c in range(3):
        tiles.append((lambda s, c=c: below_ref[c, :, s], width))
    for c in range(2):
        tiles.append((lambda s, c=c: above_ref[c, :, s], width))
    for ref in (left_ref, right_ref):
        for start in range(0, ref.shape[0], ROWS):
            tiles.append((lambda s, r=ref, t=start: r[t : t + ROWS, s], width))
    return tiles


def y_own(efield, hfield, forward, material, grad_sum, mask, place):
    cells_z, width = efield.shape[1], efield.shape[3]
    count = (cells_z * 6 + grad_sum.shape[0] * 6) // SLOTS
    packed = f32(count, ROWS, LANES)
    return pl.pallas_call(
        y_own_kernel,
        in_specs=[VMEM] * 6 + [SMEM],
        out_specs=[VMEM] * 3,
        out_shape=[packed, packed, f32(ROWS, width)],
        compiler_params=params(),
    )(efield, hfield, forward, material, grad_sum, mask, place)


def y_halo(own_low, own_high, below, above, left, right):
    extra = 5 + (left.shape[0] + right.shape[0]) // ROWS
    packed = f32(own_low.shape[0] + math.ceil(extra / SLOTS), ROWS, LANES)
    return pl.pallas_call(
        y_halo_kernel,
        in_specs=[VMEM] * 6,
        out_specs=[VMEM] * 2,
        out_shape=[packed, packed],
        compiler_params=params(),
    )(own_low, own_high, below, above, left, right)


def step_kernel(
    per_device,
    e_ref,
    h_ref,
    f_ref,
    mat_ref,
    grad_ref,
    mask_ref,
    below_ref,
    above_ref,
    left_ref,
    right_ref,
    ylow_ref,
    yhigh_ref,
    permit_ref,
    place_ref,
    e_out,
    h_out,
    grad_out,
    send_ref,
    left_wide,
    right_wide,
    grad_halo,
):
    _, cells_z, _, width = e_ref.shape
    layers = grad_ref.shape[0]
    mats = permit_ref.shape[0]
    wide = width + LANES
    lane = lax.broadcasted_iota(jnp.int32, (ROWS, LANES), 1)
    row = lax.broadcasted_iota(jnp.int32, (ROWS, wide), 0)
    per_group = 6 * ROWS // SLOTS
    groups = cells_z // ROWS
    grad_base = per_group * groups
    halo_base = grad_base + per_group * (layers // ROWS)
    me = place_ref[0]
    first_group = place_ref[1] // ROWS

    def halo(tile, k):
        right = yhigh_ref[tile]
        left = ylow_ref[tile]
        back = (LANES - STRIP * k) % LANES
        over = (LANES - STRIP - STRIP * k) % LANES
        return jnp.where(
            lane < STRIP,
            pltpu.roll(right, back, 1) if back else right,
            pltpu.roll(left, over, 1) if over else left,
        )

    def with_halo(own, tile, k):
        return jnp.concatenate([own, halo(tile, k)], axis=1)

    def static_slot(index):
        return halo_base + index // SLOTS, index % SLOTS

    def y_up(v):
        return pltpu.roll(v, wide - 1, 1)

    def y_down(v):
        return pltpu.roll(v, 1, 1)

    def x_up(v, line):
        return jnp.where(row == ROWS - 1, line, pltpu.roll(v, ROWS - 1, 0))

    def x_down(v, line):
        return jnp.where(row == 0, line, pltpu.roll(v, 1, 0))

    below = [with_halo(below_ref[c], *static_slot(c)) for c in range(3)]
    above = [with_halo(above_ref[c], *static_slot(3 + c)) for c in range(2)]
    slot = 5
    for source, target in ((left_ref, left_wide), (right_ref, right_wide)):
        for start in range(0, source.shape[0], ROWS):
            target[start : start + ROWS, :] = with_halo(source[start : start + ROWS, :], *static_slot(slot))
            slot += 1
    left_wide[cells_z : 2 * cells_z, :] += HALF * y_up(left_wide[2 * cells_z : 3 * cells_z, :])

    def field(ref, which, c, a, b):
        slot = 6 * b + 3 * which + c
        return with_halo(ref[c, ROWS * a + b], per_group * a + slot // SLOTS, slot % SLOTS)

    inverse = [1.0 / permit_ref[m] for m in range(mats)]

    ex0 = field(e_ref, 0, 0, 0, 0)
    ey0 = field(e_ref, 0, 1, 0, 0)
    low_line = jnp.broadcast_to(right_wide[2 * cells_z : 2 * cells_z + 1, :], (ROWS, wide))
    hx_z = below[0] - HALF * y_up(below[2]) + HALF * ey0
    hy_z = below[1] - HALF * ex0 + HALF * x_up(below[2], low_line)

    def group(a, carry):
        ex, ey, hx_z, hy_z = carry
        layer_group = a - first_group
        design = jnp.logical_and(layer_group >= 0, layer_group < layers // ROWS)
        safe_group = jnp.clip(layer_group, 0, layers // ROWS - 1)
        for b in range(ROWS):
            z = ROWS * a + b

            def line(ref, base):
                return jnp.broadcast_to(ref[pl.ds(base + z, 1), :], (ROWS, wide))

            ez = field(e_ref, 0, 2, a, b)
            if b < ROWS - 1:
                ex_next = field(e_ref, 0, 0, a, b + 1)
                ey_next = field(e_ref, 0, 1, a, b + 1)
            else:
                end = a == groups - 1
                after = jnp.minimum(a + 1, groups - 1)
                ex_next = jnp.where(end, above[0], field(e_ref, 0, 0, after, 0))
                ey_next = jnp.where(end, above[1], field(e_ref, 0, 1, after, 0))
            hx = field(h_ref, 1, 0, a, b) - HALF * (y_up(ez) - ez - ey_next + ey)
            hy = field(h_ref, 1, 1, a, b) - HALF * (
                ex_next - ex - x_up(ez, line(right_wide, cells_z)) + ez
            )
            hz = field(h_ref, 1, 2, a, b) - HALF * (x_up(ey, line(right_wide, 0)) - ey - y_up(ex) + ex)
            hy_x = x_down(hy, line(left_wide, 0) + HALF * ez)
            hz_x = x_down(hz, line(left_wide, cells_z) - HALF * ey)
            curl_x = (hz - y_down(hz)) - (hy - hy_z)
            curl_y = (hx - hx_z) - (hz - hz_x)
            curl_z = (hy - hy_x) - (hx - y_down(hx))

            grad_tile = grad_base + per_group * safe_group
            mat_halo = halo(grad_tile + (6 * b + 3) // SLOTS, (6 * b + 3) % SLOTS)
            mat = jnp.concatenate([mat_ref[z], mat_halo.astype(jnp.int32)], axis=1)
            inv = jnp.full((ROWS, wide), inverse[0])
            for m in range(1, mats):
                inv = jnp.where(mat == m, inverse[m], inv)
            half_inv = HALF * inv
            e_new = [
                ex + half_inv * curl_x,
                ey + half_inv * curl_y,
                ez + half_inv * curl_z,
            ]
            for c, (new_e, new_h) in enumerate(zip(e_new, (hx, hy, hz))):
                e_out[c, z] = new_e[:, :width]
                h_out[c, z] = new_h[:, :width]

            @pl.when(design)
            def _():
                layer = ROWS * safe_group + b
                total = None
                for c in range(3):
                    slot = 6 * b + c
                    fwd = with_halo(f_ref[c, z], grad_tile + slot // SLOTS, slot % SLOTS)
                    total = fwd * e_new[c] if total is None else total + fwd * e_new[c]
                slot = 6 * b + 4
                grad = with_halo(grad_ref[layer], grad_tile + slot // SLOTS, slot % SLOTS)
                mask = with_halo(mask_ref[...], grad_base, 5)
                grad = grad + mask * total
                grad_out[layer] = grad[:, :width]
                grad_halo[layer] = grad[:, width:]

            ex, ey, hx_z, hy_z = ex_next, ey_next, hx, hy
        return ex, ey, hx_z, hy_z

    lax.fori_loop(0, groups, group, (ex0, ey0, hx_z, hy_z))

    def pack(k, carry):
        chunk = lax.bitwise_xor(me, k)
        edge = jnp.zeros((ROWS, LANES), jnp.float32)
        for i in range(per_device):
            layer = chunk * per_device + i
            send_ref[k, :, i * width : (i + 1) * width] = grad_out[layer]
            side = grad_halo[layer]
            at = 2 * STRIP * i
            upper = pltpu.roll(side, at, 1) if at else side
            lower = pltpu.roll(side, (at + 2 * STRIP) % LANES, 1)
            edge = jnp.where(lane // STRIP == 2 * i, upper, edge)
            edge = jnp.where(lane // STRIP == 2 * i + 1, lower, edge)
        send_ref[k, :, per_device * width :] = edge
        return carry

    lax.fori_loop(0, send_ref.shape[0], pack, 0)


def step(efield, hfield, forward, material, grad_sum, mask, below, above, left, right, ylow, yhigh, permit, place, count):
    _, cells_z, _, width = efield.shape
    layers = grad_sum.shape[0]
    per_device = layers // count
    wide = width + LANES
    return pl.pallas_call(
        functools.partial(step_kernel, per_device),
        in_specs=[VMEM] * 12 + [SMEM] * 2,
        out_specs=[VMEM] * 4,
        out_shape=[
            f32(*efield.shape),
            f32(*efield.shape),
            f32(*grad_sum.shape),
            f32(count, ROWS, per_device * width + LANES),
        ],
        scratch_shapes=[
            pltpu.VMEM((left.shape[0], wide), jnp.float32),
            pltpu.VMEM((right.shape[0], wide), jnp.float32),
            pltpu.VMEM((layers, ROWS, LANES), jnp.float32),
        ],
        compiler_params=params(),
    )(efield, hfield, forward, material, grad_sum, mask, below, above, left, right, ylow, yhigh, permit, place)


def cone_matrix(rows):
    span = np.arange(-RADIUS, RADIUS + 1, dtype=np.float64)
    cone = np.maximum(RADIUS - np.sqrt(span[:, None] ** 2 + span[None, :] ** 2), 0.0)
    weight = cone / cone.sum()
    x = np.arange(rows)
    out = np.zeros((RADIUS + 1, rows, rows))
    for b in range(RADIUS + 1):
        for apart in (x[:, None] - x[None, :], 2 * rows - 1 - x[:, None] - x[None, :]):
            near = np.abs(apart) <= RADIUS
            out[b] += np.where(near, weight[np.clip(apart, -RADIUS, RADIUS) + RADIUS, RADIUS + b], 0.0)
    out = out.reshape((RADIUS + 1) * rows, rows).astype(np.float32)
    high = out.astype(jnp.bfloat16)
    low = (out - high.astype(np.float32)).astype(jnp.bfloat16)
    return np.concatenate([high, low, high], axis=1)


def flip_rows(v):
    row = lax.broadcasted_iota(jnp.int32, v.shape, 0)
    v = pltpu.roll(v, 4, 0)
    v = jnp.where(row % 4 < 2, pltpu.roll(v, ROWS - 2, 0), pltpu.roll(v, 2, 0))
    return jnp.where(row % 2 < 1, pltpu.roll(v, ROWS - 1, 0), pltpu.roll(v, 1, 0))


def filter_kernel(count, per_device, width, *refs):
    taps_ref, place_ref = refs[0], refs[1]
    got = refs[2 : 2 + count]
    outs = refs[2 + count : 2 + 2 * count]
    slabs, parts, done = refs[2 + 2 * count :]
    me = place_ref[0]
    wide = width + LANES
    half = count // 2
    rows = half * ROWS
    lane = lax.broadcasted_iota(jnp.int32, (ROWS, LANES), 1)
    for k in range(count):
        slabs[lax.bitwise_xor(me, k)] = got[k][...]

    def layer_of(slab, i):
        edge = slabs[slab, :, per_device * width :]
        at = 2 * STRIP * i
        upper = pltpu.roll(edge, (LANES - at) % LANES, 1) if at else edge
        lower = pltpu.roll(edge, (LANES - 2 * STRIP - at) % LANES, 1)
        side = jnp.where(lane < STRIP, upper, lower)
        return jnp.concatenate([slabs[slab, :, i * width : (i + 1) * width], side], axis=1)

    for i in range(per_device):
        halves = [layer_of(s, i) + flip_rows(layer_of(count - 1 - s, i)) for s in range(half)]
        symmetric = jnp.concatenate(halves, axis=0)
        high = symmetric.astype(jnp.bfloat16)
        low = (symmetric - high.astype(jnp.float32)).astype(jnp.bfloat16)
        parts[0:rows, :] = high
        parts[rows : 2 * rows, :] = high
        parts[2 * rows : 3 * rows, :] = low
        mixed = jnp.dot(taps_ref[...], parts[...], preferred_element_type=jnp.float32)
        total = mixed[0:rows]
        for b in range(1, RADIUS + 1):
            part = mixed[b * rows : (b + 1) * rows]
            total = total + (pltpu.roll(part, b, 1) + pltpu.roll(part, wide - b, 1))
        for s in range(half):
            own = total[s * ROWS : (s + 1) * ROWS, :width]
            done[s, i] = own
            done[count - 1 - s, i] = flip_rows(own)
    for k in range(count):
        outs[k][...] = done[lax.bitwise_xor(me, k)]


def cone_filter(got, place, per_device, width):
    count = len(got)
    rows = count // 2 * ROWS
    taps = jnp.asarray(cone_matrix(rows))
    return pl.pallas_call(
        functools.partial(filter_kernel, count, per_device, width),
        in_specs=[VMEM, SMEM] + [VMEM] * count,
        out_specs=[VMEM] * count,
        out_shape=[f32(per_device, ROWS, width)] * count,
        scratch_shapes=[
            pltpu.VMEM((count, ROWS, per_device * width + LANES), jnp.float32),
            pltpu.VMEM((3 * rows, width + LANES), jnp.bfloat16),
            pltpu.VMEM((count, per_device, ROWS, width), jnp.float32),
        ],
        compiler_params=params(),
    )(taps, place, *got)


def place_kernel(count, per_device, place_ref, *refs):
    out = refs[count]
    me = place_ref[0]
    for k in range(count):
        out[pl.ds(lax.bitwise_xor(me, k) * per_device, per_device)] = refs[k][...]


def place_layers(parts, place):
    count = len(parts)
    per_device, rows, width = parts[0].shape
    return pl.pallas_call(
        functools.partial(place_kernel, count, per_device),
        in_specs=[SMEM] + [VMEM] * count,
        out_specs=VMEM,
        out_shape=f32(count * per_device, rows, width),
        compiler_params=params(),
    )(place, *parts)


def spread(parts):
    count = len(parts)
    return [parts[0]] + [
        lax.ppermute(parts[k], "gx", [(i, i ^ k) for i in range(count)]) for k in range(1, count)
    ]


def on_device(efield, hfield, forward, material, permittivity, design_mask, grad_sum):
    count = lax.axis_size("gx")
    cells_z, width = efield.shape[1], efield.shape[3]
    layers = grad_sum.shape[0]
    per_device = layers // count
    first = (cells_z - layers) * (1 - lax.axis_index("gz"))
    place = jnp.stack([lax.axis_index("gx"), first]).astype(jnp.int32)

    below, above = exchange(*z_faces(efield, hfield), "gz")
    left, right = exchange(*x_faces(efield, hfield, below, above), "gx")
    own_low, own_high, mask = y_own(efield, hfield, forward, material, grad_sum, design_mask, place)
    strips = y_halo(own_low, own_high, below, above, left, right)
    ylow, yhigh = exchange(*strips, "gy")
    e_next, h_next, grad_total, send = step(
        efield, hfield, forward, material, grad_sum, mask, below, above, left, right, ylow, yhigh, permittivity, place, count
    )
    got = spread([send[k] for k in range(count)])
    filtered = spread(cone_filter(got, place, per_device, width))
    return e_next, h_next, grad_total, place_layers(filtered, place)


def solution(mesh):
    field = P(None, "gz", "gx", "gy")
    cells = P("gz", "gx", "gy")
    return jax.shard_map(
        on_device,
        mesh=mesh,
        in_specs=(field, field, field, cells, P(), P("gx", "gy"), cells),
        out_specs=(field, field, cells, cells),
        check_vma=False,
    )
```

```python
import functools
import math

import jax
import jax.numpy as jnp
import numpy as np
from jax import lax
from jax.experimental import pallas as pl
from jax.experimental.pallas import tpu as pltpu
from jax.sharding import PartitionSpec as P

RADIUS = 6
BLOCK = 8
HALF = 0.5

ROWS = 8
LANES = 128
STRIP = 8
SLOTS = LANES // STRIP
VMEM_LIMIT = 24 * 1024 * 1024

VMEM = pl.BlockSpec(memory_space=pltpu.VMEM)
SMEM = pl.BlockSpec(memory_space=pltpu.SMEM)
HBM = pl.BlockSpec(memory_space=pltpu.HBM)
ANY = pl.BlockSpec(memory_space=pl.ANY)


def params():
    return pltpu.CompilerParams(vmem_limit_bytes=VMEM_LIMIT)


def f32(*shape):
    return jax.ShapeDtypeStruct(shape, jnp.float32)


GX, GY, GZ, FIRST = range(4)


def swap_pairs(value, axis, pairs):
    return lax.ppermute(value, axis, pairs + [(b, a) for a, b in pairs])


def exchange(first, second, axis, wrap=False):
    count = lax.axis_size(axis)
    if count == 1:
        return first, second
    got_first = swap_pairs(first, axis, [(i, i + 1) for i in range(0, count - 1, 2)])
    odd_pairs = [(i, i + 1) for i in range(1, count - 1, 2)]
    if not odd_pairs:
        return got_first, got_first
    if wrap and count % 2 == 0:
        odd_pairs.append((0, count - 1))
    return got_first, swap_pairs(second, axis, odd_pairs)


class Side:
    def __init__(self, index, count):
        self.odd = index % 2 == 1
        self.bottom = index == 0
        self.top = index == count - 1

    def sends(self, low, high):
        return jnp.where(self.odd, low, high), jnp.where(self.odd, high, low)

    def lower(self, first, second):
        return jnp.where(self.bottom, 0.0, jnp.where(self.odd, first, second))

    def upper(self, first, second):
        return jnp.where(self.top, 0.0, jnp.where(self.odd, second, first))


def z_faces_kernel(count, place_ref, e_ref, h_ref, first_ref, second_ref, e_low, e_high, h_high, sems):
    last = e_ref.shape[1] - 1
    copies = [
        pltpu.make_async_copy(e_ref.at[:, 0], e_low, sems.at[0]),
        pltpu.make_async_copy(e_ref.at[:, last], e_high, sems.at[1]),
        pltpu.make_async_copy(h_ref.at[:, last], h_high, sems.at[2]),
    ]
    for copy in copies:
        copy.start()
    for copy in copies:
        copy.wait()
    side = Side(place_ref[GZ], count)
    ez = e_high[2]
    lows = (e_low[0], e_low[1], jnp.zeros_like(ez))
    highs = (
        h_high[0] + HALF * ez - HALF * e_high[1],
        h_high[1] + HALF * e_high[0] - HALF * ez,
        ez,
    )
    for c in range(3):
        first_ref[c], second_ref[c] = side.sends(lows[c], highs[c])


def z_faces(efield, hfield, place):
    _, _, cells_x, cells_y = efield.shape
    face = f32(3, cells_x, cells_y)
    scratch = pltpu.VMEM(face.shape, jnp.float32)
    return pl.pallas_call(
        functools.partial(z_faces_kernel, lax.axis_size("gz")),
        in_specs=[SMEM, HBM, HBM],
        out_specs=[VMEM] * 2,
        out_shape=[face, face],
        scratch_shapes=[scratch] * 3 + [pltpu.SemaphoreType.DMA((3,))],
        compiler_params=params(),
    )(place, efield, hfield)


def x_faces_kernel(counts, place_ref, e_ref, h_ref, zfirst_ref, zsecond_ref, first_ref, second_ref, low_ref, rows_ref):
    cells_z = e_ref.shape[1]
    last = ROWS - 1
    z_side = Side(place_ref[GZ], counts[1])
    low_ref[...] = jnp.zeros_like(low_ref)
    for z in range(cells_z):
        low_ref[z : z + 1, :] = e_ref[1, z, 0:1, :]
        low_ref[cells_z + z : cells_z + z + 1, :] = e_ref[2, z, 0:1, :]
        for c in range(3):
            rows_ref[c, z : z + 1, :] = e_ref[c, z, last : last + 1, :]
        for c in range(2):
            rows_ref[3 + c, z : z + 1, :] = h_ref[1 + c, z, last : last + 1, :]
        if z > 0:
            rows_ref[5, z - 1 : z, :] = e_ref[0, z, last : last + 1, :]
    rows_ref[5, cells_z - 1 : cells_z, :] = z_side.upper(
        zfirst_ref[0, last : last + 1, :], zsecond_ref[0, last : last + 1, :]
    )
    low_ref[2 * cells_z : 2 * cells_z + 1, :] = z_side.lower(zfirst_ref[2, 0:1, :], zsecond_ref[2, 0:1, :])
    ex = rows_ref[0]
    high = (
        rows_ref[3] - HALF * (rows_ref[5] - ex + rows_ref[2]),
        rows_ref[4] + HALF * rows_ref[1] - HALF * ex,
        ex,
    )
    side = Side(place_ref[GX], counts[0])
    for c in range(3):
        here = slice(c * cells_z, (c + 1) * cells_z)
        first_ref[here, :], second_ref[here, :] = side.sends(low_ref[here, :], high[c])


def x_faces(efield, hfield, zfaces, place):
    cells_z, cells_y = efield.shape[1], efield.shape[3]
    face = f32(3 * cells_z, cells_y)
    return pl.pallas_call(
        functools.partial(x_faces_kernel, (lax.axis_size("gx"), lax.axis_size("gz"))),
        in_specs=[SMEM] + [VMEM] * 4,
        out_specs=[VMEM] * 2,
        out_shape=[face, face],
        scratch_shapes=[
            pltpu.VMEM(face.shape, jnp.float32),
            pltpu.VMEM((6, cells_z, cells_y), jnp.float32),
        ],
        compiler_params=params(),
    )(place, efield, hfield, *zfaces)


def lane_group():
    return lax.broadcasted_iota(jnp.int32, (ROWS, LANES), 1) // STRIP


def pack_strips(tiles, low_ref, high_ref, first):
    group = lane_group()
    width = tiles[0][1]
    for start in range(0, len(tiles), SLOTS):
        low = jnp.zeros((ROWS, LANES), jnp.float32)
        high = jnp.zeros((ROWS, LANES), jnp.float32)
        for k, (load, _) in enumerate(tiles[start : start + SLOTS]):
            if load is None:
                continue
            here = group == k
            shift = (STRIP * k) % LANES
            left = load(slice(0, LANES))
            right = load(slice(width - LANES, width))
            low = jnp.where(here, pltpu.roll(left, shift, 1) if shift else left, low)
            shift = (STRIP * k + STRIP) % LANES
            high = jnp.where(here, pltpu.roll(right, shift, 1) if shift else right, high)
        low_ref[first + start // SLOTS] = low
        high_ref[first + start // SLOTS] = high


def y_own_kernel(place_ref, e_ref, h_ref, f_ref, mat_ref, grad_ref, mask_ref, low_ref, high_ref, wide_ref):
    cells_z, width = e_ref.shape[1], e_ref.shape[3]
    layers = grad_ref.shape[0]
    blocks = mask_ref.shape[1]
    spread = (
        lax.broadcasted_iota(jnp.int32, (blocks, width), 0)
        == lax.broadcasted_iota(jnp.int32, (blocks, width), 1) // BLOCK
    ).astype(jnp.float32)
    mask = jnp.broadcast_to(mask_ref[...].astype(jnp.float32), (ROWS, blocks))
    wide_ref[...] = jnp.dot(mask, spread, preferred_element_type=jnp.float32)
    first = place_ref[FIRST]
    tiles = []
    for z in range(cells_z):
        for ref in (e_ref, h_ref):
            for c in range(3):
                tiles.append((lambda s, r=ref, c=c, z=z: r[c, z, :, s], width))
    for layer in range(layers):
        for c in range(3):
            tiles.append((lambda s, c=c, l=layer: f_ref[c, first + l, :, s], width))
        tiles.append((lambda s, l=layer: mat_ref[first + l, :, s].astype(jnp.float32), width))
        tiles.append((lambda s, l=layer: grad_ref[l, :, s], width))
        tiles.append((lambda s: wide_ref[:, s], width) if layer % ROWS == 0 else (None, width))
    pack_strips(tiles, low_ref, high_ref, 0)


def y_own(efield, hfield, forward, material, grad_sum, mask, place):
    cells_z, width = efield.shape[1], efield.shape[3]
    count = (cells_z * 6 + grad_sum.shape[0] * 6) // SLOTS
    packed = f32(count, ROWS, LANES)
    return pl.pallas_call(
        y_own_kernel,
        in_specs=[SMEM] + [VMEM] * 6,
        out_specs=[VMEM] * 3,
        out_shape=[packed, packed, f32(ROWS, width)],
        compiler_params=params(),
    )(place, efield, hfield, forward, material, grad_sum, mask)


def face_tiles(place_ref, counts, zfirst, zsecond, xfirst, xsecond):
    width = xfirst.shape[1]
    z_side = Side(place_ref[GZ], counts[2])
    x_side = Side(place_ref[GX], counts[0])
    tiles = []
    for c in range(3):
        tiles.append((lambda s, c=c: z_side.lower(zfirst[c, :, s], zsecond[c, :, s]), width))
    for c in range(2):
        tiles.append((lambda s, c=c: z_side.upper(zfirst[c, :, s], zsecond[c, :, s]), width))
    for pick in (x_side.lower, x_side.upper):
        for t in range(0, xfirst.shape[0], ROWS):
            tiles.append((lambda s, p=pick, t=t: p(xfirst[t : t + ROWS, s], xsecond[t : t + ROWS, s]), width))
    return tiles


def face_count(xface):
    return 5 + 2 * (xface.shape[0] // ROWS)


def y_faces_kernel(
    counts, place_ref, own_low, own_high, zfirst, zsecond, xfirst, xsecond, first_ref, second_ref, low_ref, high_ref
):
    count = own_low.shape[0]
    pack_strips(face_tiles(place_ref, counts, zfirst, zsecond, xfirst, xsecond), low_ref, high_ref, 0)
    side = Side(place_ref[GY], counts[1])
    first_ref[0:count], second_ref[0:count] = side.sends(own_low[...], own_high[...])
    first_ref[count:], second_ref[count:] = side.sends(low_ref[...], high_ref[...])


def y_faces(own_low, own_high, zfaces, xfaces, place):
    extra = math.ceil(face_count(xfaces[0]) / SLOTS)
    packed = f32(own_low.shape[0] + extra, ROWS, LANES)
    return pl.pallas_call(
        functools.partial(y_faces_kernel, axis_sizes()),
        in_specs=[SMEM] + [VMEM] * 6,
        out_specs=[VMEM] * 2,
        out_shape=[packed, packed],
        scratch_shapes=[pltpu.VMEM((extra, ROWS, LANES), jnp.float32)] * 2,
        compiler_params=params(),
    )(place, own_low, own_high, *zfaces, *xfaces)


def axis_sizes():
    return lax.axis_size("gx"), lax.axis_size("gy"), lax.axis_size("gz")


class Fields:
    def __init__(self, counts, layers, place_ref, e_ref, h_ref, faces, ybuf, left_wide, right_wide):
        self.e_ref, self.h_ref = e_ref, h_ref
        self.cells_z, self.width = e_ref.shape[1], e_ref.shape[3]
        self.wide = self.width + LANES
        self.lane = lax.broadcasted_iota(jnp.int32, (ROWS, LANES), 1)
        self.row = lax.broadcasted_iota(jnp.int32, (ROWS, self.wide), 0)
        self.per_group = 6 * ROWS // SLOTS
        self.groups = self.cells_z // ROWS
        self.grad_base = self.per_group * self.groups
        halo_base = self.grad_base + self.per_group * (layers // ROWS)
        zfirst, zsecond, xfirst, xsecond, yfirst, ysecond = faces
        y_side = Side(place_ref[GY], counts[1])
        ybuf[0] = y_side.lower(yfirst[...], ysecond[...])
        ybuf[1] = y_side.upper(yfirst[...], ysecond[...])
        self.ybuf = ybuf
        self.left_wide, self.right_wide = left_wide, right_wide

        tiles = face_tiles(place_ref, counts, zfirst, zsecond, xfirst, xsecond)
        whole = slice(0, self.width)
        full = [
            self.with_halo(load(whole), halo_base + t // SLOTS, t % SLOTS)
            for t, (load, _) in enumerate(tiles)
        ]
        self.below, self.above = full[:3], full[3:5]
        per_face = xfirst.shape[0] // ROWS
        for t in range(per_face):
            left_wide[t * ROWS : (t + 1) * ROWS, :] = full[5 + t]
            right_wide[t * ROWS : (t + 1) * ROWS, :] = full[5 + per_face + t]
        cells_z = self.cells_z
        left_wide[cells_z : 2 * cells_z, :] += HALF * self.y_up(left_wide[2 * cells_z : 3 * cells_z, :])

    def halo(self, tile, k):
        right = self.ybuf[1, tile]
        left = self.ybuf[0, tile]
        back = (LANES - STRIP * k) % LANES
        over = (LANES - STRIP - STRIP * k) % LANES
        return jnp.where(
            self.lane < STRIP,
            pltpu.roll(right, back, 1) if back else right,
            pltpu.roll(left, over, 1) if over else left,
        )

    def with_halo(self, own, tile, k):
        return jnp.concatenate([own, self.halo(tile, k)], axis=1)

    def y_up(self, v):
        return pltpu.roll(v, self.wide - 1, 1)

    def y_down(self, v):
        return pltpu.roll(v, 1, 1)

    def x_up(self, v, line):
        return jnp.where(self.row == ROWS - 1, line, pltpu.roll(v, ROWS - 1, 0))

    def x_down(self, v, line):
        return jnp.where(self.row == 0, line, pltpu.roll(v, 1, 0))

    def line(self, ref, at):
        return jnp.broadcast_to(ref[pl.ds(at, 1), :], (ROWS, self.wide))

    def field(self, which, c, a, b):
        slot = 6 * b + 3 * which + c
        ref = self.h_ref if which else self.e_ref
        return self.with_halo(ref[c, ROWS * a + b], self.per_group * a + slot // SLOTS, slot % SLOTS)

    def hx(self, a, b, ey, ez, ey_next):
        return self.field(1, 0, a, b) - HALF * (self.y_up(ez) - ez - ey_next + ey)

    def hy(self, a, b, ex, ez, ex_next):
        up = self.x_up(ez, self.line(self.right_wide, self.cells_z + ROWS * a + b))
        return self.field(1, 1, a, b) - HALF * (ex_next - ex - up + ez)

    def hz(self, a, b, ex, ey):
        up = self.x_up(ey, self.line(self.right_wide, ROWS * a + b))
        return self.field(1, 2, a, b) - HALF * (up - ey - self.y_up(ex) + ex)

    def start(self, a):
        ex, ey = self.field(0, 0, a, 0), self.field(0, 1, a, 0)
        below = self.below
        at_bottom = (
            below[0] - HALF * self.y_up(below[2]) + HALF * ey,
            below[1] - HALF * ex + HALF * self.x_up(below[2], self.line(self.right_wide, 2 * self.cells_z)),
        )
        before, b = jnp.maximum(a - 1, 0), ROWS - 1
        ex_before, ey_before, ez_before = (self.field(0, c, before, b) for c in range(3))
        inside = (
            self.hx(before, b, ey_before, ez_before, ey),
            self.hy(before, b, ex_before, ez_before, ex),
        )
        bottom = a == 0
        return (ex, ey) + tuple(jnp.where(bottom, one, two) for one, two in zip(at_bottom, inside))

    def group(self, a, carry, emit):
        ex, ey, hx_z, hy_z = carry
        for b in range(ROWS):
            z = ROWS * a + b
            ez = self.field(0, 2, a, b)
            if b < ROWS - 1:
                ex_next, ey_next = (self.field(0, c, a, b + 1) for c in range(2))
            else:
                end = a == self.groups - 1
                after = jnp.minimum(a + 1, self.groups - 1)
                ex_next, ey_next = (
                    jnp.where(end, self.above[c], self.field(0, c, after, 0)) for c in range(2)
                )
            hx = self.hx(a, b, ey, ez, ey_next)
            hy = self.hy(a, b, ex, ez, ex_next)
            hz = self.hz(a, b, ex, ey)
            hy_x = self.x_down(hy, self.line(self.left_wide, z) + HALF * ez)
            hz_x = self.x_down(hz, self.line(self.left_wide, self.cells_z + z) - HALF * ey)
            curl = (
                (hz - self.y_down(hz)) - (hy - hy_z),
                (hx - hx_z) - (hz - hz_x),
                (hy - hy_x) - (hx - self.y_down(hx)),
            )
            emit(a, b, (ex, ey, ez), (hx, hy, hz), curl)
            ex, ey, hx_z, hy_z = ex_next, ey_next, hx, hy
        return ex, ey, hx_z, hy_z


def half_inverse(permit_ref, mat):
    inverse = [HALF * (1.0 / permit_ref[m]) for m in range(permit_ref.shape[0])]
    out = jnp.full(mat.shape, inverse[0])
    for m in range(1, len(inverse)):
        out = jnp.where(mat == m, inverse[m], out)
    return out


def gradient_kernel(counts, per_device, *refs):
    place_ref, permit_ref, e_ref, h_ref, f_ref, mat_ref, grad_ref, mask_ref = refs[:8]
    faces, (grad_out, send_ref), (ybuf, left_wide, right_wide, grad_halo) = refs[8:14], refs[14:16], refs[16:]
    layers, _, width = grad_ref.shape
    lane = lax.broadcasted_iota(jnp.int32, (ROWS, LANES), 1)
    me = place_ref[GX]
    first_group = place_ref[FIRST] // ROWS
    fields = Fields(counts, layers, place_ref, e_ref, h_ref, faces, ybuf, left_wide, right_wide)
    mask = fields.with_halo(mask_ref[...], fields.grad_base, 5)

    def emit(a, b, efield, hfield, curl):
        z = ROWS * a + b
        layer = z - place_ref[FIRST]
        tile = fields.grad_base + fields.per_group * (a - first_group)

        def spot(which):
            return tile + (6 * b + which) // SLOTS, (6 * b + which) % SLOTS

        mat_halo = fields.halo(*spot(3)).astype(jnp.int32)
        half_inv = half_inverse(permit_ref, jnp.concatenate([mat_ref[z], mat_halo], axis=1))
        total = None
        for c in range(3):
            term = fields.with_halo(f_ref[c, z], *spot(c)) * (efield[c] + half_inv * curl[c])
            total = term if total is None else total + term
        grad = fields.with_halo(grad_ref[layer], *spot(4)) + mask * total
        grad_out[layer] = grad[:, :width]
        grad_halo[layer] = grad[:, width:]

    carry = fields.start(first_group)
    lax.fori_loop(0, layers // ROWS, lambda i, c: fields.group(first_group + i, c, emit), carry)

    def pack(k, carry):
        chunk = lax.bitwise_xor(me, k)
        edge = jnp.zeros((ROWS, LANES), jnp.float32)
        for i in range(per_device):
            layer = chunk * per_device + i
            send_ref[k, :, i * width : (i + 1) * width] = grad_out[layer]
            side = grad_halo[layer]
            at = 2 * STRIP * i
            upper = pltpu.roll(side, at, 1) if at else side
            lower = pltpu.roll(side, (at + 2 * STRIP) % LANES, 1)
            edge = jnp.where(lane // STRIP == 2 * i, upper, edge)
            edge = jnp.where(lane // STRIP == 2 * i + 1, lower, edge)
        send_ref[k, :, per_device * width :] = edge
        return carry

    lax.fori_loop(0, send_ref.shape[0], pack, 0)


def wide_scratch(xface, yface, width):
    rows = xface.shape[0]
    return [
        pltpu.VMEM((2,) + yface.shape, jnp.float32),
        pltpu.VMEM((rows, width + LANES), jnp.float32),
        pltpu.VMEM((rows, width + LANES), jnp.float32),
    ]


def gradient(place, permit, efield, hfield, forward, material, grad_sum, mask, faces):
    layers, _, width = grad_sum.shape
    count = lax.axis_size("gx")
    per_device = layers // count
    return pl.pallas_call(
        functools.partial(gradient_kernel, axis_sizes(), per_device),
        in_specs=[SMEM] * 2 + [VMEM] * 12,
        out_specs=[VMEM] * 2,
        out_shape=[f32(*grad_sum.shape), f32(count, ROWS, per_device * width + LANES)],
        scratch_shapes=wide_scratch(faces[2], faces[4], width)
        + [pltpu.VMEM((layers, ROWS, LANES), jnp.float32)],
        compiler_params=params(),
    )(place, permit, efield, hfield, forward, material, grad_sum, mask, *faces)


def step_kernel(counts, layers, *refs):
    place_ref, permit_ref, e_ref, h_ref, mat_ref = refs[:5]
    faces, (e_out, h_out), (ybuf, left_wide, right_wide, carry_ref) = refs[5:11], refs[11:13], refs[13:]
    width = e_ref.shape[3]
    fields = Fields(counts, layers, place_ref, e_ref, h_ref, faces, ybuf, left_wide, right_wide)
    a = pl.program_id(0)

    def emit(a, b, efield, hfield, curl):
        half_inv = half_inverse(permit_ref, mat_ref[ROWS * a + b])
        for c in range(3):
            e_out[c, b] = efield[c][:, :width] + half_inv * curl[c][:, :width]
            h_out[c, b] = hfield[c][:, :width]

    @pl.when(a == 0)
    def _():
        for i, v in enumerate(fields.start(0)):
            carry_ref[i] = v

    carry = tuple(carry_ref[i] for i in range(4))
    for i, v in enumerate(fields.group(a, carry, emit)):
        carry_ref[i] = v


def step(place, permit, efield, hfield, material, faces, layers):
    _, cells_z, _, width = efield.shape
    block = pl.BlockSpec((3, ROWS, ROWS, width), lambda a: (0, a, 0, 0))
    return pl.pallas_call(
        functools.partial(step_kernel, axis_sizes(), layers),
        grid=(cells_z // ROWS,),
        in_specs=[SMEM] * 2 + [VMEM] * 9,
        out_specs=[block] * 2,
        out_shape=[f32(*efield.shape)] * 2,
        scratch_shapes=wide_scratch(faces[2], faces[4], width)
        + [pltpu.VMEM((4, ROWS, width + LANES), jnp.float32)],
        compiler_params=params(),
    )(place, permit, efield, hfield, material, *faces)


def cone_matrix(rows):
    span = np.arange(-RADIUS, RADIUS + 1, dtype=np.float64)
    cone = np.maximum(RADIUS - np.sqrt(span[:, None] ** 2 + span[None, :] ** 2), 0.0)
    weight = cone / cone.sum()
    x = np.arange(rows)
    out = np.zeros((RADIUS + 1, rows, rows))
    for b in range(RADIUS + 1):
        for apart in (x[:, None] - x[None, :], 2 * rows - 1 - x[:, None] - x[None, :]):
            near = np.abs(apart) <= RADIUS
            out[b] += np.where(near, weight[np.clip(apart, -RADIUS, RADIUS) + RADIUS, RADIUS + b], 0.0)
    out = out.reshape((RADIUS + 1) * rows, rows).astype(np.float32)
    high = out.astype(jnp.bfloat16)
    low = (out - high.astype(np.float32)).astype(jnp.bfloat16)
    return np.concatenate([high, low, high], axis=1)


def flip_rows(v):
    row = lax.broadcasted_iota(jnp.int32, v.shape, 0)
    v = pltpu.roll(v, 4, 0)
    v = jnp.where(row % 4 < 2, pltpu.roll(v, ROWS - 2, 0), pltpu.roll(v, 2, 0))
    return jnp.where(row % 2 < 1, pltpu.roll(v, ROWS - 1, 0), pltpu.roll(v, 1, 0))


def filter_kernel(count, per_device, width, *refs):
    taps_ref, place_ref = refs[0], refs[1]
    got = refs[2 : 2 + count]
    outs = refs[2 + count : 2 + 2 * count]
    slabs, parts, done = refs[2 + 2 * count :]
    me = place_ref[GX]
    wide = width + LANES
    half = count // 2
    rows = half * ROWS
    lane = lax.broadcasted_iota(jnp.int32, (ROWS, LANES), 1)
    for k in range(count):
        slabs[lax.bitwise_xor(me, k)] = got[k][...]

    def layer_of(slab, i):
        edge = slabs[slab, :, per_device * width :]
        at = 2 * STRIP * i
        upper = pltpu.roll(edge, (LANES - at) % LANES, 1) if at else edge
        lower = pltpu.roll(edge, (LANES - 2 * STRIP - at) % LANES, 1)
        side = jnp.where(lane < STRIP, upper, lower)
        return jnp.concatenate([slabs[slab, :, i * width : (i + 1) * width], side], axis=1)

    for i in range(per_device):
        halves = [layer_of(s, i) + flip_rows(layer_of(count - 1 - s, i)) for s in range(half)]
        symmetric = jnp.concatenate(halves, axis=0)
        high = symmetric.astype(jnp.bfloat16)
        low = (symmetric - high.astype(jnp.float32)).astype(jnp.bfloat16)
        parts[0:rows, :] = high
        parts[rows : 2 * rows, :] = high
        parts[2 * rows : 3 * rows, :] = low
        mixed = jnp.dot(taps_ref[...], parts[...], preferred_element_type=jnp.float32)
        total = mixed[0:rows]
        for b in range(1, RADIUS + 1):
            part = mixed[b * rows : (b + 1) * rows]
            total = total + (pltpu.roll(part, b, 1) + pltpu.roll(part, wide - b, 1))
        for s in range(half):
            own = total[s * ROWS : (s + 1) * ROWS, :width]
            done[s, i] = own
            done[count - 1 - s, i] = flip_rows(own)
    for k in range(count):
        outs[k][...] = done[lax.bitwise_xor(me, k)]


def cone_filter(got, place, per_device, width):
    count = len(got)
    rows = count // 2 * ROWS
    taps = jnp.asarray(cone_matrix(rows))
    return pl.pallas_call(
        functools.partial(filter_kernel, count, per_device, width),
        in_specs=[VMEM, SMEM] + [VMEM] * count,
        out_specs=[VMEM] * count,
        out_shape=[f32(per_device, ROWS, width)] * count,
        scratch_shapes=[
            pltpu.VMEM((count, ROWS, per_device * width + LANES), jnp.float32),
            pltpu.VMEM((3 * rows, width + LANES), jnp.bfloat16),
            pltpu.VMEM((count, per_device, ROWS, width), jnp.float32),
        ],
        compiler_params=params(),
    )(taps, place, *got)


def place_kernel(count, per_device, place_ref, *refs):
    out, sems = refs[count], refs[count + 1]
    copies = []
    for k in range(count):
        at = lax.bitwise_xor(place_ref[GX], k) * per_device
        copies.append(pltpu.make_async_copy(refs[k], out.at[pl.ds(at, per_device)], sems.at[k]))
    for copy in copies:
        copy.start()
    for copy in copies:
        copy.wait()


def place_layers(parts, place):
    count = len(parts)
    per_device, rows, width = parts[0].shape
    return pl.pallas_call(
        functools.partial(place_kernel, count, per_device),
        in_specs=[SMEM] + [ANY] * count,
        out_specs=ANY,
        out_shape=f32(count * per_device, rows, width),
        scratch_shapes=[pltpu.SemaphoreType.DMA((count,))],
        compiler_params=params(),
    )(place, *parts)


def spread(parts):
    count = len(parts)
    return [parts[0]] + [
        lax.ppermute(parts[k], "gx", [(i, i ^ k) for i in range(count)]) for k in range(1, count)
    ]


def on_device(efield, hfield, forward, material, permit, design_mask, grad_sum):
    cells_z, width = efield.shape[1], efield.shape[3]
    layers = grad_sum.shape[0]
    first = (cells_z - layers) * (1 - lax.axis_index("gz"))
    indices = [lax.axis_index(axis) for axis in ("gx", "gy", "gz")]
    place = jnp.stack(indices + [first]).astype(jnp.int32)

    zfaces = exchange(*z_faces(efield, hfield, place), "gz")
    xfaces = exchange(*x_faces(efield, hfield, zfaces, place), "gx")
    own_low, own_high, mask = y_own(efield, hfield, forward, material, grad_sum, design_mask, place)
    yfaces = exchange(*y_faces(own_low, own_high, zfaces, xfaces, place), "gy", wrap=True)
    faces = zfaces + xfaces + yfaces
    grad_total, send = gradient(place, permit, efield, hfield, forward, material, grad_sum, mask, faces)
    got = spread([send[k] for k in range(send.shape[0])])
    e_next, h_next = step(place, permit, efield, hfield, material, faces, layers)
    filtered = spread(cone_filter(got, place, layers // len(got), width))
    return e_next, h_next, grad_total, place_layers(filtered, place)


def solution(mesh):
    field = P(None, "gz", "gx", "gy")
    cells = P("gz", "gx", "gy")
    return jax.shard_map(
        on_device,
        mesh=mesh,
        in_specs=(field, field, field, cells, P(), P("gx", "gy"), cells),
        out_specs=(field, field, cells, cells),
        check_vma=False,
    )
```

```python
import functools
import math

import jax
import jax.numpy as jnp
import numpy as np
from jax import lax
from jax.experimental import pallas as pl
from jax.experimental.pallas import tpu as pltpu
from jax.sharding import PartitionSpec as P

RADIUS = 6
BLOCK = 8
HALF = 0.5

ROWS = 8
LANES = 128
STRIP = 8
SLOTS = LANES // STRIP
VMEM_LIMIT = 24 * 1024 * 1024

VMEM = pl.BlockSpec(memory_space=pltpu.VMEM)
SMEM = pl.BlockSpec(memory_space=pltpu.SMEM)
ANY = pl.BlockSpec(memory_space=pl.ANY)


def params():
    return pltpu.CompilerParams(vmem_limit_bytes=VMEM_LIMIT)


def f32(*shape):
    return jax.ShapeDtypeStruct(shape, jnp.float32)


def swap_pairs(value, axis, pairs):
    return lax.ppermute(value, axis, pairs + [(b, a) for a, b in pairs])


def rounds(axis):
    return 2 if lax.axis_size(axis) > 2 else 1


def exchange(sends, axis, wrap=False):
    count = lax.axis_size(axis)
    if count == 1:
        return sends
    got = [swap_pairs(sends[0], axis, [(i, i + 1) for i in range(0, count - 1, 2)])]
    if len(sends) > 1:
        odd_pairs = [(i, i + 1) for i in range(1, count - 1, 2)]
        if wrap and count % 2 == 0:
            odd_pairs.append((0, count - 1))
        got.append(swap_pairs(sends[1], axis, odd_pairs))
    return got


class Side:
    def __init__(self, axis):
        index = lax.axis_index(axis)
        self.rounds = rounds(axis)
        self.odd = index % 2 == 1
        self.bottom = index == 0
        self.top = index == lax.axis_size(axis) - 1

    def sends(self, low, high):
        both = [jnp.where(self.odd, low, high)]
        if self.rounds > 1:
            both.append(jnp.where(self.odd, high, low))
        return both

    def lower(self, got):
        return jnp.where(self.bottom, 0.0, jnp.where(self.odd, got[0], got[-1]))

    def upper(self, got):
        return jnp.where(self.top, 0.0, jnp.where(self.odd, got[-1], got[0]))


def first_layer(cells_z, layers):
    return (cells_z - layers) * (1 - lax.axis_index("gz"))


def z_faces(efield, hfield):
    top = efield.shape[1] - 1
    ex, ey, ez = (efield[c, top] for c in range(3))
    high = jnp.stack(
        [
            hfield[0, top] + HALF * ez - HALF * ey,
            hfield[1, top] + HALF * ex - HALF * ez,
            ez,
        ]
    )
    return Side("gz").sends(efield[:, 0], high)


def x_faces_kernel(z_rounds, *refs):
    e_ref, h_ref = refs[:2]
    zfaces = refs[2 : 2 + z_rounds]
    sends, (low_ref, rows_ref) = refs[2 + z_rounds : -2], refs[-2:]
    cells_z = e_ref.shape[1]
    last = ROWS - 1
    z_side = Side("gz")
    low_ref[...] = jnp.zeros_like(low_ref)
    for z in range(cells_z):
        low_ref[z : z + 1, :] = e_ref[1, z, 0:1, :]
        low_ref[cells_z + z : cells_z + z + 1, :] = e_ref[2, z, 0:1, :]
        for c in range(3):
            rows_ref[c, z : z + 1, :] = e_ref[c, z, last : last + 1, :]
        for c in range(2):
            rows_ref[3 + c, z : z + 1, :] = h_ref[1 + c, z, last : last + 1, :]
        if z > 0:
            rows_ref[5, z - 1 : z, :] = e_ref[0, z, last : last + 1, :]
    rows_ref[5, cells_z - 1 : cells_z, :] = z_side.upper([f[0, last : last + 1, :] for f in zfaces])
    low_ref[2 * cells_z : 2 * cells_z + 1, :] = z_side.lower([f[2, 0:1, :] for f in zfaces])
    ex = rows_ref[0]
    high = (
        rows_ref[3] - HALF * (rows_ref[5] - ex + rows_ref[2]),
        rows_ref[4] + HALF * rows_ref[1] - HALF * ex,
        ex,
    )
    side = Side("gx")
    for c in range(3):
        here = slice(c * cells_z, (c + 1) * cells_z)
        for ref, value in zip(sends, side.sends(low_ref[here, :], high[c])):
            ref[here, :] = value


def x_faces(efield, hfield, zfaces):
    cells_z, cells_y = efield.shape[1], efield.shape[3]
    face = f32(3 * cells_z, cells_y)
    return pl.pallas_call(
        functools.partial(x_faces_kernel, len(zfaces)),
        in_specs=[VMEM] * (2 + len(zfaces)),
        out_specs=[VMEM] * rounds("gx"),
        out_shape=[face] * rounds("gx"),
        scratch_shapes=[
            pltpu.VMEM(face.shape, jnp.float32),
            pltpu.VMEM((6, cells_z, cells_y), jnp.float32),
        ],
        compiler_params=params(),
    )(efield, hfield, *zfaces)


def lane_group():
    return lax.broadcasted_iota(jnp.int32, (ROWS, LANES), 1) // STRIP


def pack_strips(tiles, low_ref, high_ref, first):
    group = lane_group()
    width = tiles[0][1]
    for start in range(0, len(tiles), SLOTS):
        low = jnp.zeros((ROWS, LANES), jnp.float32)
        high = jnp.zeros((ROWS, LANES), jnp.float32)
        for k, (load, _) in enumerate(tiles[start : start + SLOTS]):
            if load is None:
                continue
            here = group == k
            shift = (STRIP * k) % LANES
            left = load(slice(0, LANES))
            right = load(slice(width - LANES, width))
            low = jnp.where(here, pltpu.roll(left, shift, 1) if shift else left, low)
            shift = (STRIP * k + STRIP) % LANES
            high = jnp.where(here, pltpu.roll(right, shift, 1) if shift else right, high)
        low_ref[first + start // SLOTS] = low
        high_ref[first + start // SLOTS] = high


def y_own_kernel(
    permit_ref, e_ref, h_ref, f_ref, mat_ref, grad_ref, mask_ref, low_ref, high_ref, wide_ref, inv_ref
):
    cells_z, width = e_ref.shape[1], e_ref.shape[3]
    layers = grad_ref.shape[0]
    blocks = mask_ref.shape[1]
    inverse = [HALF * (1.0 / permit_ref[m]) for m in range(permit_ref.shape[0])]
    for z in range(cells_z):
        inv = jnp.full((ROWS, width), inverse[0])
        for m in range(1, len(inverse)):
            inv = jnp.where(mat_ref[z] == m, inverse[m], inv)
        inv_ref[z] = inv
    spread = (
        lax.broadcasted_iota(jnp.int32, (blocks, width), 0)
        == lax.broadcasted_iota(jnp.int32, (blocks, width), 1) // BLOCK
    ).astype(jnp.float32)
    mask = jnp.broadcast_to(mask_ref[...].astype(jnp.float32), (ROWS, blocks))
    wide_ref[...] = jnp.dot(mask, spread, preferred_element_type=jnp.float32)
    first = first_layer(cells_z, layers)
    tiles = []
    for z in range(cells_z):
        for ref in (e_ref, h_ref):
            for c in range(3):
                tiles.append((lambda s, r=ref, c=c, z=z: r[c, z, :, s], width))
    for layer in range(layers):
        for c in range(3):
            tiles.append((lambda s, c=c, l=layer: f_ref[c, first + l, :, s], width))
        tiles.append((lambda s, l=layer: inv_ref[first + l, :, s], width))
        tiles.append((lambda s, l=layer: grad_ref[l, :, s], width))
        tiles.append((lambda s: wide_ref[:, s], width) if layer % ROWS == 0 else (None, width))
    pack_strips(tiles, low_ref, high_ref, 0)


def y_own(permit, efield, hfield, forward, material, grad_sum, mask):
    cells_z, width = efield.shape[1], efield.shape[3]
    count = (cells_z * 6 + grad_sum.shape[0] * 6) // SLOTS
    packed = f32(count, ROWS, LANES)
    return pl.pallas_call(
        y_own_kernel,
        in_specs=[SMEM] + [VMEM] * 6,
        out_specs=[VMEM] * 4,
        out_shape=[packed, packed, f32(ROWS, width), f32(*material.shape)],
        compiler_params=params(),
    )(permit, efield, hfield, forward, material, grad_sum, mask)


def face_tiles(zfaces, xfaces):
    width = xfaces[0].shape[1]
    z_side, x_side = Side("gz"), Side("gx")
    tiles = []
    for c in range(3):
        tiles.append((lambda s, c=c: z_side.lower([f[c, :, s] for f in zfaces]), width))
    for c in range(2):
        tiles.append((lambda s, c=c: z_side.upper([f[c, :, s] for f in zfaces]), width))
    for pick in (x_side.lower, x_side.upper):
        for t in range(0, xfaces[0].shape[0], ROWS):
            tiles.append((lambda s, p=pick, t=t: p([f[t : t + ROWS, s] for f in xfaces]), width))
    return tiles


def face_count(xface):
    return 5 + 2 * (xface.shape[0] // ROWS)


def y_faces_kernel(counts, *refs):
    own_low, own_high = refs[:2]
    zfaces, xfaces = refs[2 : 2 + counts[0]], refs[2 + counts[0] : 2 + sum(counts)]
    sends, (low_ref, high_ref) = refs[2 + sum(counts) : -2], refs[-2:]
    own = own_low.shape[0]
    pack_strips(face_tiles(zfaces, xfaces), low_ref, high_ref, 0)
    side = Side("gy")
    for ref, value in zip(sends, side.sends(own_low[...], own_high[...])):
        ref[0:own] = value
    for ref, value in zip(sends, side.sends(low_ref[...], high_ref[...])):
        ref[own:] = value


def y_faces(own_low, own_high, zfaces, xfaces):
    extra = math.ceil(face_count(xfaces[0]) / SLOTS)
    packed = f32(own_low.shape[0] + extra, ROWS, LANES)
    return pl.pallas_call(
        functools.partial(y_faces_kernel, (len(zfaces), len(xfaces))),
        in_specs=[VMEM] * (2 + len(zfaces) + len(xfaces)),
        out_specs=[VMEM] * rounds("gy"),
        out_shape=[packed] * rounds("gy"),
        scratch_shapes=[pltpu.VMEM((extra, ROWS, LANES), jnp.float32)] * 2,
        compiler_params=params(),
    )(own_low, own_high, *zfaces, *xfaces)


OWN, CIRCLE, EDGE = range(3)


def faces_wide(mode, width):
    return {OWN: width, CIRCLE: width + LANES, EDGE: LANES}[mode]


class Fields:
    def __init__(self, mode, layers, e_ref, h_ref, zfaces, xfaces, yfaces, scratch):
        self.mode = mode
        self.e_ref, self.h_ref = e_ref, h_ref
        self.cells_z, self.width = e_ref.shape[1], e_ref.shape[3]
        self.wide = faces_wide(mode, self.width)
        self.lane = lax.broadcasted_iota(jnp.int32, (ROWS, LANES), 1)
        self.row = lax.broadcasted_iota(jnp.int32, (ROWS, self.wide), 0)
        self.per_group = 6 * ROWS // SLOTS
        self.groups = self.cells_z // ROWS
        self.grad_base = self.per_group * self.groups
        halo_base = self.grad_base + self.per_group * (layers // ROWS)
        self.left_wide, self.right_wide = left_wide, right_wide = scratch[:2]
        if mode != OWN:
            self.ybuf = scratch[2]
            y_side = Side("gy")
            self.ybuf[0] = y_side.lower([f[...] for f in yfaces])
            self.ybuf[1] = y_side.upper([f[...] for f in yfaces])

        full = [
            self.wider(load, halo_base + t // SLOTS, t % SLOTS)
            for t, (load, _) in enumerate(face_tiles(zfaces, xfaces))
        ]
        self.below, self.above = full[:3], full[3:5]
        per_face = xfaces[0].shape[0] // ROWS
        for t in range(per_face):
            left_wide[t * ROWS : (t + 1) * ROWS, :] = full[5 + t]
            right_wide[t * ROWS : (t + 1) * ROWS, :] = full[5 + per_face + t]
        cells_z = self.cells_z
        left_wide[cells_z : 2 * cells_z, :] += HALF * self.y_up(left_wide[2 * cells_z : 3 * cells_z, :])

    def wider(self, load, tile, k):
        if self.mode == OWN:
            return load(slice(0, self.width))

        def moved(v, to):
            shift = (to - STRIP * k) % LANES
            return pltpu.roll(v, shift, 1) if shift else v

        lower, upper = self.ybuf[0, tile], self.ybuf[1, tile]
        if self.mode == CIRCLE:
            halo = jnp.where(self.lane < STRIP, moved(upper, 0), moved(lower, LANES - STRIP))
            return jnp.concatenate([load(slice(0, self.width)), halo], axis=1)
        head = pltpu.roll(load(slice(0, LANES)), STRIP, 1)
        tail = pltpu.roll(load(slice(self.width - LANES, self.width)), LANES - STRIP, 1)
        own = jnp.where(self.lane < LANES // 2, head, tail)
        own = jnp.where(self.lane < STRIP, moved(lower, 0), own)
        return jnp.where(self.lane >= LANES - STRIP, moved(upper, LANES - STRIP), own)

    def y_up(self, v):
        return pltpu.roll(v, self.wide - 1, 1)

    def y_down(self, v):
        return pltpu.roll(v, 1, 1)

    def x_up(self, v, line):
        return jnp.where(self.row == ROWS - 1, line, pltpu.roll(v, ROWS - 1, 0))

    def x_down(self, v, line):
        return jnp.where(self.row == 0, line, pltpu.roll(v, 1, 0))

    def line(self, ref, at):
        return jnp.broadcast_to(ref[pl.ds(at, 1), :], (ROWS, self.wide))

    def field(self, which, c, a, b):
        slot = 6 * b + 3 * which + c
        ref = self.h_ref if which else self.e_ref
        tile = self.per_group * a + slot // SLOTS
        return self.wider(lambda s: ref[c, ROWS * a + b, :, s], tile, slot % SLOTS)

    def hx(self, a, b, ey, ez, ey_next):
        return self.field(1, 0, a, b) - HALF * (self.y_up(ez) - ez - ey_next + ey)

    def hy(self, a, b, ex, ez, ex_next):
        up = self.x_up(ez, self.line(self.right_wide, self.cells_z + ROWS * a + b))
        return self.field(1, 1, a, b) - HALF * (ex_next - ex - up + ez)

    def hz(self, a, b, ex, ey):
        up = self.x_up(ey, self.line(self.right_wide, ROWS * a + b))
        return self.field(1, 2, a, b) - HALF * (up - ey - self.y_up(ex) + ex)

    def start(self, a):
        ex, ey = self.field(0, 0, a, 0), self.field(0, 1, a, 0)
        below = self.below
        at_bottom = (
            below[0] - HALF * self.y_up(below[2]) + HALF * ey,
            below[1] - HALF * ex + HALF * self.x_up(below[2], self.line(self.right_wide, 2 * self.cells_z)),
        )
        before, b = jnp.maximum(a - 1, 0), ROWS - 1
        ex_before, ey_before, ez_before = (self.field(0, c, before, b) for c in range(3))
        inside = (
            self.hx(before, b, ey_before, ez_before, ey),
            self.hy(before, b, ex_before, ez_before, ex),
        )
        bottom = a == 0
        return (ex, ey) + tuple(jnp.where(bottom, one, two) for one, two in zip(at_bottom, inside))

    def group(self, a, carry, emit):
        ex, ey, hx_z, hy_z = carry
        for b in range(ROWS):
            z = ROWS * a + b
            ez = self.field(0, 2, a, b)
            if b < ROWS - 1:
                ex_next, ey_next = (self.field(0, c, a, b + 1) for c in range(2))
            else:
                end = a == self.groups - 1
                after = jnp.minimum(a + 1, self.groups - 1)
                ex_next, ey_next = (
                    jnp.where(end, self.above[c], self.field(0, c, after, 0)) for c in range(2)
                )
            hx = self.hx(a, b, ey, ez, ey_next)
            hy = self.hy(a, b, ex, ez, ex_next)
            hz = self.hz(a, b, ex, ey)
            hy_x = self.x_down(hy, self.line(self.left_wide, z) + HALF * ez)
            hz_x = self.x_down(hz, self.line(self.left_wide, self.cells_z + z) - HALF * ey)
            curl = (
                (hz - self.y_down(hz)) - (hy - hy_z),
                (hx - hx_z) - (hz - hz_x),
                (hy - hy_x) - (hx - self.y_down(hx)),
            )
            emit(a, b, (ex, ey, ez), (hx, hy, hz), curl)
            ex, ey, hx_z, hy_z = ex_next, ey_next, hx, hy
        return ex, ey, hx_z, hy_z

    def gradient(self, f_ref, inv_ref, grad_ref, mask_ref, store):
        layers = grad_ref.shape[0]
        first = first_layer(self.cells_z, layers)
        first_group = first // ROWS
        mask = self.wider(lambda s: mask_ref[:, s], self.grad_base, 5)

        def emit(a, b, efield, hfield, curl):
            z = ROWS * a + b
            tile = self.grad_base + self.per_group * (a - first_group)

            def wider(load, which):
                slot = 6 * b + which
                return self.wider(load, tile + slot // SLOTS, slot % SLOTS)

            half_inv = wider(lambda s: inv_ref[z, :, s], 3)
            total = None
            for c in range(3):
                term = wider(lambda s: f_ref[c, z, :, s], c) * (efield[c] + half_inv * curl[c])
                total = term if total is None else total + term
            store(z - first, wider(lambda s: grad_ref[z - first, :, s], 4) + mask * total)

        def body(i, carry):
            return self.group(first_group + i, carry, emit)

        lax.fori_loop(0, layers // ROWS, body, self.start(first_group))


def fields_scratch(mode, xface, yface, width):
    rows, wide = xface.shape[0], faces_wide(mode, width)
    out = [pltpu.VMEM((rows, wide), jnp.float32)] * 2
    if mode != OWN:
        out.append(pltpu.VMEM((2,) + yface.shape, jnp.float32))
    return out


def own_gradient_kernel(counts, *refs):
    e_ref, h_ref, f_ref, inv_ref, grad_ref, mask_ref = refs[:6]
    zfaces, xfaces = refs[6 : 6 + counts[0]], refs[6 + counts[0] : 6 + sum(counts)]
    grad_out, scratch = refs[6 + sum(counts)], refs[7 + sum(counts) :]
    fields = Fields(OWN, grad_ref.shape[0], e_ref, h_ref, zfaces, xfaces, None, scratch)

    def store(layer, value):
        grad_out[layer] = value

    fields.gradient(f_ref, inv_ref, grad_ref, mask_ref, store)


def own_gradient(arrays, zfaces, xfaces):
    grad_sum = arrays[4]
    return pl.pallas_call(
        functools.partial(own_gradient_kernel, (len(zfaces), len(xfaces))),
        in_specs=[VMEM] * (6 + len(zfaces) + len(xfaces)),
        out_specs=VMEM,
        out_shape=f32(*grad_sum.shape),
        scratch_shapes=fields_scratch(OWN, xfaces[0], None, grad_sum.shape[2]),
        compiler_params=params(),
    )(*arrays, *zfaces, *xfaces)


def edge_gradient_kernel(counts, per_device, *refs):
    own_ref, e_ref, h_ref, f_ref, inv_ref, grad_ref, mask_ref = refs[:7]
    ends = np.cumsum((7,) + counts)
    zfaces, xfaces, yfaces = (refs[i:j] for i, j in zip(ends[:-1], ends[1:]))
    sends, scratch, edge_ref = refs[ends[-1] : -4], refs[-4:-1], refs[-1]
    layers, _, width = grad_ref.shape
    lane = lax.broadcasted_iota(jnp.int32, (ROWS, LANES), 1)
    me = lax.axis_index("gx")
    fields = Fields(EDGE, layers, e_ref, h_ref, zfaces, xfaces, yfaces, scratch)

    def store(layer, value):
        edge_ref[layer] = value

    fields.gradient(f_ref, inv_ref, grad_ref, mask_ref, store)

    for k, send_ref in enumerate(sends):
        chunk = lax.bitwise_xor(me, k)
        packed = jnp.zeros((ROWS, LANES), jnp.float32)
        for i in range(per_device):
            layer = chunk * per_device + i
            edge = edge_ref[layer]
            at = i * width
            head, tail = own_ref[layer, :, 0:LANES], own_ref[layer, :, width - LANES :]
            send_ref[:, at : at + LANES] = jnp.where(lane == 0, pltpu.roll(edge, LANES - STRIP, 1), head)
            send_ref[:, at + LANES : at + width - LANES] = own_ref[layer, :, LANES : width - LANES]
            send_ref[:, at + width - LANES : at + width] = jnp.where(
                lane == LANES - 1, pltpu.roll(edge, STRIP, 1), tail
            )
            side = pltpu.roll(edge, (2 * STRIP * i + STRIP) % LANES, 1)
            packed = jnp.where(lane // (2 * STRIP) == i, side, packed)
        send_ref[:, per_device * width :] = packed


def edge_gradient(own, arrays, zfaces, xfaces, yfaces):
    layers, _, width = own.shape
    count = lax.axis_size("gx")
    per_device = layers // count
    faces = (*zfaces, *xfaces, *yfaces)
    return pl.pallas_call(
        functools.partial(edge_gradient_kernel, (len(zfaces), len(xfaces), len(yfaces)), per_device),
        in_specs=[VMEM] * (7 + len(faces)),
        out_specs=[VMEM] * count,
        out_shape=[f32(ROWS, per_device * width + LANES)] * count,
        scratch_shapes=fields_scratch(EDGE, xfaces[0], yfaces[0], width)
        + [pltpu.VMEM((layers, ROWS, LANES), jnp.float32)],
        compiler_params=params(),
    )(own, *arrays, *faces)


def step_kernel(counts, layers, *refs):
    e_ref, h_ref, inv_ref = refs[:3]
    ends = np.cumsum((3,) + counts)
    zfaces, xfaces, yfaces, shares = (refs[i:j] for i, j in zip(ends[:-1], ends[1:]))
    (e_out, h_out, grad_out), scratch, carry_ref = refs[ends[-1] : -4], refs[-4:-1], refs[-1]
    width = e_ref.shape[3]
    fields = Fields(CIRCLE, layers, e_ref, h_ref, zfaces, xfaces, yfaces, scratch)
    a = pl.program_id(0)

    def emit(a, b, efield, hfield, curl):
        half_inv = inv_ref[ROWS * a + b]
        for c in range(3):
            e_out[c, b] = efield[c][:, :width] + half_inv * curl[c][:, :width]
            h_out[c, b] = hfield[c][:, :width]

    @pl.when(a == 0)
    def _():
        for i, v in enumerate(fields.start(0)):
            carry_ref[i] = v
        per_device = layers // len(shares)
        me = lax.axis_index("gx")
        for k, share in enumerate(shares):
            chunk = lax.bitwise_xor(me, k)
            for i in range(per_device):
                grad_out[chunk * per_device + i] = share[:, i * width : (i + 1) * width]

    carry = tuple(carry_ref[i] for i in range(4))
    for i, v in enumerate(fields.group(a, carry, emit)):
        carry_ref[i] = v


def step(efield, hfield, inv, zfaces, xfaces, yfaces, shares, layers):
    _, cells_z, _, width = efield.shape
    block = pl.BlockSpec((3, ROWS, ROWS, width), lambda a: (0, a, 0, 0))
    groups = (zfaces, xfaces, yfaces, shares)
    counts = tuple(len(group) for group in groups)
    return pl.pallas_call(
        functools.partial(step_kernel, counts, layers),
        grid=(cells_z // ROWS,),
        in_specs=[VMEM] * (3 + sum(counts)),
        out_specs=[block, block, VMEM],
        out_shape=[f32(*efield.shape)] * 2 + [f32(layers, ROWS, width)],
        scratch_shapes=fields_scratch(CIRCLE, xfaces[0], yfaces[0], width)
        + [pltpu.VMEM((4, ROWS, width + LANES), jnp.float32)],
        compiler_params=params(),
    )(efield, hfield, inv, *(one for group in groups for one in group))


def cone_matrix(rows):
    span = np.arange(-RADIUS, RADIUS + 1, dtype=np.float64)
    cone = np.maximum(RADIUS - np.sqrt(span[:, None] ** 2 + span[None, :] ** 2), 0.0)
    weight = cone / cone.sum()
    x = np.arange(rows)
    out = np.zeros((RADIUS + 1, rows, rows))
    for b in range(RADIUS + 1):
        for apart in (x[:, None] - x[None, :], 2 * rows - 1 - x[:, None] - x[None, :]):
            near = np.abs(apart) <= RADIUS
            out[b] += np.where(near, weight[np.clip(apart, -RADIUS, RADIUS) + RADIUS, RADIUS + b], 0.0)
    out = out.reshape((RADIUS + 1) * rows, rows).astype(np.float32)
    high = out.astype(jnp.bfloat16)
    low = (out - high.astype(np.float32)).astype(jnp.bfloat16)
    return np.concatenate([high, low, high], axis=1)


def flip_rows(v):
    row = lax.broadcasted_iota(jnp.int32, v.shape, 0)
    v = pltpu.roll(v, 4, 0)
    v = jnp.where(row % 4 < 2, pltpu.roll(v, ROWS - 2, 0), pltpu.roll(v, 2, 0))
    return jnp.where(row % 2 < 1, pltpu.roll(v, ROWS - 1, 0), pltpu.roll(v, 1, 0))


def filter_kernel(count, per_device, width, *refs):
    taps_ref = refs[0]
    got = refs[1 : 1 + count]
    outs = refs[1 + count : 1 + 2 * count]
    slabs, parts, done = refs[1 + 2 * count :]
    me = lax.axis_index("gx")
    wide = width + LANES
    half = count // 2
    rows = half * ROWS
    lane = lax.broadcasted_iota(jnp.int32, (ROWS, LANES), 1)
    for k in range(count):
        slabs[lax.bitwise_xor(me, k)] = got[k][...]

    def layer_of(slab, i):
        edge = slabs[slab, :, per_device * width :]
        at = 2 * STRIP * i
        upper = pltpu.roll(edge, (LANES - at) % LANES, 1) if at else edge
        lower = pltpu.roll(edge, (LANES - 2 * STRIP - at) % LANES, 1)
        side = jnp.where(lane < STRIP, upper, lower)
        return jnp.concatenate([slabs[slab, :, i * width : (i + 1) * width], side], axis=1)

    for i in range(per_device):
        halves = [layer_of(s, i) + flip_rows(layer_of(count - 1 - s, i)) for s in range(half)]
        symmetric = jnp.concatenate(halves, axis=0)
        high = symmetric.astype(jnp.bfloat16)
        low = (symmetric - high.astype(jnp.float32)).astype(jnp.bfloat16)
        parts[0:rows, :] = high
        parts[rows : 2 * rows, :] = high
        parts[2 * rows : 3 * rows, :] = low
        mixed = jnp.dot(taps_ref[...], parts[...], preferred_element_type=jnp.float32)
        total = mixed[0:rows]
        for b in range(1, RADIUS + 1):
            part = mixed[b * rows : (b + 1) * rows]
            total = total + (pltpu.roll(part, b, 1) + pltpu.roll(part, wide - b, 1))
        for s in range(half):
            own = total[s * ROWS : (s + 1) * ROWS, :width]
            done[s, i] = own
            done[count - 1 - s, i] = flip_rows(own)
    for k in range(count):
        outs[k][...] = done[lax.bitwise_xor(me, k)]


def cone_filter(got, per_device, width):
    count = len(got)
    rows = count // 2 * ROWS
    taps = jnp.asarray(cone_matrix(rows))
    return pl.pallas_call(
        functools.partial(filter_kernel, count, per_device, width),
        in_specs=[VMEM] * (1 + count),
        out_specs=[VMEM] * count,
        out_shape=[f32(per_device, ROWS, width)] * count,
        scratch_shapes=[
            pltpu.VMEM((count, ROWS, per_device * width + LANES), jnp.float32),
            pltpu.VMEM((3 * rows, width + LANES), jnp.bfloat16),
            pltpu.VMEM((count, per_device, ROWS, width), jnp.float32),
        ],
        compiler_params=params(),
    )(taps, *got)


def place_kernel(count, per_device, *refs):
    out, sems = refs[count], refs[count + 1]
    copies = []
    for k in range(count):
        at = lax.bitwise_xor(lax.axis_index("gx"), k) * per_device
        copies.append(pltpu.make_async_copy(refs[k], out.at[pl.ds(at, per_device)], sems.at[k]))
    for copy in copies:
        copy.start()
    for copy in copies:
        copy.wait()


def place_layers(parts):
    count = len(parts)
    per_device, rows, width = parts[0].shape
    return pl.pallas_call(
        functools.partial(place_kernel, count, per_device),
        in_specs=[ANY] * count,
        out_specs=ANY,
        out_shape=f32(count * per_device, rows, width),
        scratch_shapes=[pltpu.SemaphoreType.DMA((count,))],
        compiler_params=params(),
    )(*parts)


def spread(parts):
    count = len(parts)
    return [parts[0]] + [
        lax.ppermute(parts[k], "gx", [(i, i ^ k) for i in range(count)]) for k in range(1, count)
    ]


def on_device(efield, hfield, forward, material, permit, design_mask, grad_sum):
    layers, _, width = grad_sum.shape
    zfaces = exchange(z_faces(efield, hfield), "gz")
    xfaces = exchange(x_faces(efield, hfield, zfaces), "gx")
    own_low, own_high, mask, inv = y_own(permit, efield, hfield, forward, material, grad_sum, design_mask)
    arrays = (efield, hfield, forward, inv, grad_sum, mask)
    yfaces = exchange(y_faces(own_low, own_high, zfaces, xfaces), "gy", wrap=True)
    own = own_gradient(arrays, zfaces, xfaces)
    shares = edge_gradient(own, arrays, zfaces, xfaces, yfaces)
    got = spread(shares)
    e_next, h_next, grad_total = step(efield, hfield, inv, zfaces, xfaces, yfaces, shares, layers)
    filtered = spread(cone_filter(got, layers // len(got), width))
    return e_next, h_next, grad_total, place_layers(filtered)


def solution(mesh):
    field = P(None, "gz", "gx", "gy")
    cells = P("gz", "gx", "gy")
    return jax.shard_map(
        on_device,
        mesh=mesh,
        in_specs=(field, field, field, cells, P(), P("gx", "gy"), cells),
        out_specs=(field, field, cells, cells),
        check_vma=False,
    )
```

```python
import functools
import math

import jax
import jax.numpy as jnp
import numpy as np
from jax import lax
from jax.experimental import pallas as pl
from jax.experimental.pallas import tpu as pltpu
from jax.sharding import PartitionSpec as P

RADIUS = 6
BLOCK = 8
HALF = 0.5

ROWS = 8
LANES = 128
STRIP = 8
SLOTS = LANES // STRIP
MIB = 1024 * 1024

VMEM = pl.BlockSpec(memory_space=pltpu.VMEM)
SMEM = pl.BlockSpec(memory_space=pltpu.SMEM)
ANY = pl.BlockSpec(memory_space=pl.ANY)


def params(mib=24):
    return pltpu.CompilerParams(vmem_limit_bytes=mib * MIB)


def f32(*shape):
    return jax.ShapeDtypeStruct(shape, jnp.float32)


def swap_pairs(value, axis, pairs):
    return lax.ppermute(value, axis, pairs + [(b, a) for a, b in pairs])


def rounds(axis):
    return 2 if lax.axis_size(axis) > 2 else 1


def exchange(sends, axis, wrap=False):
    count = lax.axis_size(axis)
    if count == 1:
        return sends
    got = [swap_pairs(sends[0], axis, [(i, i + 1) for i in range(0, count - 1, 2)])]
    if len(sends) > 1:
        odd_pairs = [(i, i + 1) for i in range(1, count - 1, 2)]
        if wrap and count % 2 == 0:
            odd_pairs.append((0, count - 1))
        got.append(swap_pairs(sends[1], axis, odd_pairs))
    return got


class Side:
    def __init__(self, axis):
        index = lax.axis_index(axis)
        self.rounds = rounds(axis)
        self.odd = index % 2 == 1
        self.bottom = index == 0
        self.top = index == lax.axis_size(axis) - 1

    def sends(self, low, high):
        both = [jnp.where(self.odd, low, high)]
        if self.rounds > 1:
            both.append(jnp.where(self.odd, high, low))
        return both

    def lower(self, got):
        return jnp.where(self.bottom, 0.0, jnp.where(self.odd, got[0], got[-1]))

    def upper(self, got):
        return jnp.where(self.top, 0.0, jnp.where(self.odd, got[-1], got[0]))


def first_layer(cells_z, layers):
    return (cells_z - layers) * (1 - lax.axis_index("gz"))


def z_faces_kernel(*refs):
    e_ref, h_ref = refs[:2]
    sends, (e_low, e_high, h_high, sems) = refs[2:-4], refs[-4:]
    top = e_ref.shape[1] - 1
    copies = [
        pltpu.make_async_copy(e_ref.at[:, 0], e_low, sems.at[0]),
        pltpu.make_async_copy(e_ref.at[:, top], e_high, sems.at[1]),
        pltpu.make_async_copy(h_ref.at[:, top], h_high, sems.at[2]),
    ]
    for copy in copies:
        copy.start()
    for copy in copies:
        copy.wait()
    side = Side("gz")
    ex, ey, ez = (e_high[c] for c in range(3))
    high = (h_high[0] + HALF * ez - HALF * ey, h_high[1] + HALF * ex - HALF * ez, ez)
    for c in range(3):
        for ref, value in zip(sends, side.sends(e_low[c], high[c])):
            ref[c] = value


def z_faces(efield, hfield):
    face = f32(*efield.shape[:1], *efield.shape[2:])
    return pl.pallas_call(
        z_faces_kernel,
        in_specs=[ANY] * 2,
        out_specs=[VMEM] * rounds("gz"),
        out_shape=[face] * rounds("gz"),
        scratch_shapes=[pltpu.VMEM(face.shape, jnp.float32)] * 3 + [pltpu.SemaphoreType.DMA((3,))],
        compiler_params=params(60),
    )(efield, hfield)


def x_faces_kernel(z_rounds, *refs):
    e_ref, h_ref = refs[:2]
    zfaces = refs[2 : 2 + z_rounds]
    sends, (low_ref, rows_ref) = refs[2 + z_rounds : -2], refs[-2:]
    cells_z = e_ref.shape[1]
    last = ROWS - 1
    z_side = Side("gz")
    low_ref[...] = jnp.zeros_like(low_ref)
    for z in range(cells_z):
        low_ref[z : z + 1, :] = e_ref[1, z, 0:1, :]
        low_ref[cells_z + z : cells_z + z + 1, :] = e_ref[2, z, 0:1, :]
        for c in range(3):
            rows_ref[c, z : z + 1, :] = e_ref[c, z, last : last + 1, :]
        for c in range(2):
            rows_ref[3 + c, z : z + 1, :] = h_ref[1 + c, z, last : last + 1, :]
        if z > 0:
            rows_ref[5, z - 1 : z, :] = e_ref[0, z, last : last + 1, :]
    rows_ref[5, cells_z - 1 : cells_z, :] = z_side.upper([f[0, last : last + 1, :] for f in zfaces])
    low_ref[2 * cells_z : 2 * cells_z + 1, :] = z_side.lower([f[2, 0:1, :] for f in zfaces])
    ex = rows_ref[0]
    high = (
        rows_ref[3] - HALF * (rows_ref[5] - ex + rows_ref[2]),
        rows_ref[4] + HALF * rows_ref[1] - HALF * ex,
        ex,
    )
    side = Side("gx")
    for c in range(3):
        here = slice(c * cells_z, (c + 1) * cells_z)
        for ref, value in zip(sends, side.sends(low_ref[here, :], high[c])):
            ref[here, :] = value


def x_faces(efield, hfield, zfaces):
    cells_z, cells_y = efield.shape[1], efield.shape[3]
    face = f32(3 * cells_z, cells_y)
    return pl.pallas_call(
        functools.partial(x_faces_kernel, len(zfaces)),
        in_specs=[VMEM] * (2 + len(zfaces)),
        out_specs=[VMEM] * rounds("gx"),
        out_shape=[face] * rounds("gx"),
        scratch_shapes=[
            pltpu.VMEM(face.shape, jnp.float32),
            pltpu.VMEM((6, cells_z, cells_y), jnp.float32),
        ],
        compiler_params=params(),
    )(efield, hfield, *zfaces)


def lane_group():
    return lax.broadcasted_iota(jnp.int32, (ROWS, LANES), 1) // STRIP


def pack_strips(tiles, low_ref, high_ref, first):
    group = lane_group()
    width = tiles[0][1]
    for start in range(0, len(tiles), SLOTS):
        low = jnp.zeros((ROWS, LANES), jnp.float32)
        high = jnp.zeros((ROWS, LANES), jnp.float32)
        for k, (load, _) in enumerate(tiles[start : start + SLOTS]):
            if load is None:
                continue
            here = group == k
            shift = (STRIP * k) % LANES
            left = load(slice(0, LANES))
            right = load(slice(width - LANES, width))
            low = jnp.where(here, pltpu.roll(left, shift, 1) if shift else left, low)
            shift = (STRIP * k + STRIP) % LANES
            high = jnp.where(here, pltpu.roll(right, shift, 1) if shift else right, high)
        low_ref[first + start // SLOTS] = low
        high_ref[first + start // SLOTS] = high


def load_kernel(
    permit_ref, e_in, h_in, f_in, mat_in, grad_in, mask_ref,
    e_ref, h_ref, f_ref, grad_ref, low_ref, high_ref, wide_ref, inv_ref, mat_ref, sems,
):
    cells_z, width = e_ref.shape[1], e_ref.shape[3]
    layers = grad_ref.shape[0]
    blocks = mask_ref.shape[1]
    pairs = [(e_in, e_ref), (h_in, h_ref), (f_in, f_ref)]
    copies = [[pltpu.make_async_copy(mat_in, mat_ref, sems.at[0])]]
    copies.append([pltpu.make_async_copy(grad_in, grad_ref, sems.at[1])])
    for n, (source, target) in enumerate(pairs):
        copies.append(
            [pltpu.make_async_copy(source.at[c], target.at[c], sems.at[2 + 3 * n + c]) for c in range(3)]
        )
    for group in copies:
        for copy in group:
            copy.start()

    spread = (
        lax.broadcasted_iota(jnp.int32, (blocks, width), 0)
        == lax.broadcasted_iota(jnp.int32, (blocks, width), 1) // BLOCK
    ).astype(jnp.float32)
    mask = jnp.broadcast_to(mask_ref[...].astype(jnp.float32), (ROWS, blocks))
    wide_ref[...] = jnp.dot(mask, spread, preferred_element_type=jnp.float32)

    def arrived(*groups):
        for n in groups:
            for copy in copies[n]:
                copy.wait()

    arrived(0)
    inverse = [HALF * (1.0 / permit_ref[m]) for m in range(permit_ref.shape[0])]
    for z in range(cells_z):
        inv = jnp.full((ROWS, width), inverse[0])
        for m in range(1, len(inverse)):
            inv = jnp.where(mat_ref[z] == m, inverse[m], inv)
        inv_ref[z] = inv
    arrived(1, 2, 3)
    first = first_layer(cells_z, layers)
    tiles = []
    for z in range(cells_z):
        for ref in (e_ref, h_ref):
            for c in range(3):
                tiles.append((lambda s, r=ref, c=c, z=z: r[c, z, :, s], width))
    pack_strips(tiles, low_ref, high_ref, 0)
    arrived(4)
    done = len(tiles) // SLOTS
    tiles = []
    for layer in range(layers):
        for c in range(3):
            tiles.append((lambda s, c=c, l=layer: f_ref[c, first + l, :, s], width))
        tiles.append((lambda s, l=layer: inv_ref[first + l, :, s], width))
        tiles.append((lambda s, l=layer: grad_ref[l, :, s], width))
        tiles.append((lambda s: wide_ref[:, s], width) if layer % ROWS == 0 else (None, width))
    pack_strips(tiles, low_ref, high_ref, done)


def load(permit, efield, hfield, forward, material, grad_sum, mask):
    cells_z, width = efield.shape[1], efield.shape[3]
    count = (cells_z * 6 + grad_sum.shape[0] * 6) // SLOTS
    packed = (count, ROWS, LANES)
    return pl.pallas_call(
        load_kernel,
        in_specs=[SMEM] + [ANY] * 5 + [VMEM],
        out_specs=[VMEM] * 8,
        out_shape=[
            pltpu.VMEM(shape, jnp.float32)
            for shape in (
                efield.shape,
                hfield.shape,
                forward.shape,
                grad_sum.shape,
                packed,
                packed,
                (ROWS, width),
                material.shape,
            )
        ],
        scratch_shapes=[pltpu.VMEM(material.shape, jnp.int32), pltpu.SemaphoreType.DMA((11,))],
        compiler_params=params(56),
    )(permit, efield, hfield, forward, material, grad_sum, mask)


def edge_tile(load, width):
    lane = lax.broadcasted_iota(jnp.int32, (ROWS, LANES), 1)
    head = pltpu.roll(load(slice(0, LANES)), STRIP, 1)
    tail = pltpu.roll(load(slice(width - LANES, width)), LANES - STRIP, 1)
    return jnp.where(lane < LANES // 2, head, tail)


def edges_kernel(e_ref, h_ref, f_ref, inv_ref, grad_ref, mask_ref, eh_out, grad_out, mask_out):
    cells_z, width = e_ref.shape[1], e_ref.shape[3]
    layers = grad_ref.shape[0]
    first = first_layer(cells_z, layers)
    for z in range(cells_z):
        for c in range(3):
            eh_out[z, c] = edge_tile(lambda s: e_ref[c, z, :, s], width)
            eh_out[z, 3 + c] = edge_tile(lambda s: h_ref[c, z, :, s], width)
    for layer in range(layers):
        for c in range(3):
            grad_out[layer, c] = edge_tile(lambda s: f_ref[c, first + layer, :, s], width)
        grad_out[layer, 3] = edge_tile(lambda s: inv_ref[first + layer, :, s], width)
        grad_out[layer, 4] = edge_tile(lambda s: grad_ref[layer, :, s], width)
    mask_out[...] = edge_tile(lambda s: mask_ref[:, s], width)


def own_edges(arrays):
    cells_z, layers = arrays[0].shape[1], arrays[4].shape[0]
    return pl.pallas_call(
        edges_kernel,
        in_specs=[VMEM] * 6,
        out_specs=[VMEM] * 3,
        out_shape=[f32(cells_z, 6, ROWS, LANES), f32(layers, 5, ROWS, LANES), f32(ROWS, LANES)],
        compiler_params=params(),
    )(*arrays)


def face_tiles(zfaces, xfaces):
    width = xfaces[0].shape[1]
    z_side, x_side = Side("gz"), Side("gx")
    tiles = []
    for c in range(3):
        tiles.append((lambda s, c=c: z_side.lower([f[c, :, s] for f in zfaces]), width))
    for c in range(2):
        tiles.append((lambda s, c=c: z_side.upper([f[c, :, s] for f in zfaces]), width))
    for pick in (x_side.lower, x_side.upper):
        for t in range(0, xfaces[0].shape[0], ROWS):
            tiles.append((lambda s, p=pick, t=t: p([f[t : t + ROWS, s] for f in xfaces]), width))
    return tiles


def face_count(xface):
    return 5 + 2 * (xface.shape[0] // ROWS)


def y_faces_kernel(counts, *refs):
    own_low, own_high = refs[:2]
    zfaces, xfaces = refs[2 : 2 + counts[0]], refs[2 + counts[0] : 2 + sum(counts)]
    sends, (low_ref, high_ref) = refs[2 + sum(counts) : -2], refs[-2:]
    own = own_low.shape[0]
    pack_strips(face_tiles(zfaces, xfaces), low_ref, high_ref, 0)
    side = Side("gy")
    for ref, value in zip(sends, side.sends(own_low[...], own_high[...])):
        ref[0:own] = value
    for ref, value in zip(sends, side.sends(low_ref[...], high_ref[...])):
        ref[own:] = value


def y_faces(own_low, own_high, zfaces, xfaces):
    extra = math.ceil(face_count(xfaces[0]) / SLOTS)
    packed = f32(own_low.shape[0] + extra, ROWS, LANES)
    return pl.pallas_call(
        functools.partial(y_faces_kernel, (len(zfaces), len(xfaces))),
        in_specs=[VMEM] * (2 + len(zfaces) + len(xfaces)),
        out_specs=[VMEM] * rounds("gy"),
        out_shape=[packed] * rounds("gy"),
        scratch_shapes=[pltpu.VMEM((extra, ROWS, LANES), jnp.float32)] * 2,
        compiler_params=params(),
    )(own_low, own_high, *zfaces, *xfaces)


OWN, CIRCLE, EDGE = range(3)


def faces_wide(mode, width):
    return {OWN: width, CIRCLE: width + LANES, EDGE: LANES}[mode]


class Fields:
    def __init__(self, mode, layers, fields, zfaces, xfaces, yfaces, scratch):
        self.mode = mode
        self.fields = fields
        if mode == EDGE:
            self.cells_z, self.width = fields.shape[0], xfaces[0].shape[1]
        else:
            self.cells_z, self.width = fields[0].shape[1], fields[0].shape[3]
        self.wide = faces_wide(mode, self.width)
        self.lane = lax.broadcasted_iota(jnp.int32, (ROWS, LANES), 1)
        self.row = lax.broadcasted_iota(jnp.int32, (ROWS, self.wide), 0)
        self.per_group = 6 * ROWS // SLOTS
        self.groups = self.cells_z // ROWS
        self.grad_base = self.per_group * self.groups
        halo_base = self.grad_base + self.per_group * (layers // ROWS)
        self.left_wide, self.right_wide = left_wide, right_wide = scratch[:2]
        if mode != OWN:
            self.ybuf = scratch[2]
            y_side = Side("gy")
            for t in range(yfaces[0].shape[0]):
                lower = y_side.lower([f[t] for f in yfaces])
                upper = y_side.upper([f[t] for f in yfaces])
                if mode == EDGE:
                    even = self.lane // STRIP % 2 == 0
                    lower, upper = (
                        jnp.where(even, upper, pltpu.roll(lower, STRIP, 1)),
                        jnp.where(even, pltpu.roll(upper, LANES - STRIP, 1), lower),
                    )
                self.ybuf[0, t] = lower
                self.ybuf[1, t] = upper

        def face(load, slot):
            if mode == EDGE:
                own = edge_tile(load, self.width)
                return self.edge(own, halo_base + slot // SLOTS, slot % SLOTS)
            return self.wider(load, halo_base + slot // SLOTS, slot % SLOTS)

        full = [face(load, slot) for slot, (load, _) in enumerate(face_tiles(zfaces, xfaces))]
        self.below, self.above = full[:3], full[3:5]
        per_face = xfaces[0].shape[0] // ROWS
        for t in range(per_face):
            left_wide[t * ROWS : (t + 1) * ROWS, :] = full[5 + t]
            right_wide[t * ROWS : (t + 1) * ROWS, :] = full[5 + per_face + t]
        cells_z = self.cells_z
        left_wide[cells_z : 2 * cells_z, :] += HALF * self.y_up(left_wide[2 * cells_z : 3 * cells_z, :])

    def wider(self, load, tile, k):
        if self.mode == OWN:
            return load(slice(0, self.width))

        def moved(v, to):
            shift = (to - STRIP * k) % LANES
            return pltpu.roll(v, shift, 1) if shift else v

        lower, upper = self.ybuf[0, tile], self.ybuf[1, tile]
        halo = jnp.where(self.lane < STRIP, moved(upper, 0), moved(lower, LANES - STRIP))
        return jnp.concatenate([load(slice(0, self.width)), halo], axis=1)

    def edge(self, own, tile, k):
        shift = (LANES - STRIP - 2 * STRIP * (k // 2)) % LANES
        both = pltpu.roll(self.ybuf[k % 2, tile], shift, 1)
        inside = jnp.logical_and(self.lane >= STRIP, self.lane < LANES - STRIP)
        return jnp.where(inside, own, both)

    def y_up(self, v):
        return pltpu.roll(v, self.wide - 1, 1)

    def y_down(self, v):
        return pltpu.roll(v, 1, 1)

    def x_up(self, v, line):
        return jnp.where(self.row == ROWS - 1, line, pltpu.roll(v, ROWS - 1, 0))

    def x_down(self, v, line):
        return jnp.where(self.row == 0, line, pltpu.roll(v, 1, 0))

    def line(self, ref, at):
        return jnp.broadcast_to(ref[pl.ds(at, 1), :], (ROWS, self.wide))

    def field(self, which, c, a, b):
        slot = 6 * b + 3 * which + c
        tile = self.per_group * a + slot // SLOTS
        if self.mode == EDGE:
            return self.edge(self.fields[ROWS * a + b, 3 * which + c], tile, slot % SLOTS)
        ref = self.fields[which]
        return self.wider(lambda s: ref[c, ROWS * a + b, :, s], tile, slot % SLOTS)

    def hx(self, a, b, ey, ez, ey_next):
        return self.field(1, 0, a, b) - HALF * (self.y_up(ez) - ez - ey_next + ey)

    def hy(self, a, b, ex, ez, ex_next):
        up = self.x_up(ez, self.line(self.right_wide, self.cells_z + ROWS * a + b))
        return self.field(1, 1, a, b) - HALF * (ex_next - ex - up + ez)

    def hz(self, a, b, ex, ey):
        up = self.x_up(ey, self.line(self.right_wide, ROWS * a + b))
        return self.field(1, 2, a, b) - HALF * (up - ey - self.y_up(ex) + ex)

    def start(self, a):
        ex, ey = self.field(0, 0, a, 0), self.field(0, 1, a, 0)
        below = self.below
        at_bottom = (
            below[0] - HALF * self.y_up(below[2]) + HALF * ey,
            below[1] - HALF * ex + HALF * self.x_up(below[2], self.line(self.right_wide, 2 * self.cells_z)),
        )
        before, b = jnp.maximum(a - 1, 0), ROWS - 1
        ex_before, ey_before, ez_before = (self.field(0, c, before, b) for c in range(3))
        inside = (
            self.hx(before, b, ey_before, ez_before, ey),
            self.hy(before, b, ex_before, ez_before, ex),
        )
        bottom = a == 0
        return (ex, ey) + tuple(jnp.where(bottom, one, two) for one, two in zip(at_bottom, inside))

    def group(self, a, carry, emit):
        ex, ey, hx_z, hy_z = carry
        for b in range(ROWS):
            z = ROWS * a + b
            ez = self.field(0, 2, a, b)
            if b < ROWS - 1:
                ex_next, ey_next = (self.field(0, c, a, b + 1) for c in range(2))
            else:
                end = a == self.groups - 1
                after = jnp.minimum(a + 1, self.groups - 1)
                ex_next, ey_next = (
                    jnp.where(end, self.above[c], self.field(0, c, after, 0)) for c in range(2)
                )
            hx = self.hx(a, b, ey, ez, ey_next)
            hy = self.hy(a, b, ex, ez, ex_next)
            hz = self.hz(a, b, ex, ey)
            hy_x = self.x_down(hy, self.line(self.left_wide, z) + HALF * ez)
            hz_x = self.x_down(hz, self.line(self.left_wide, self.cells_z + z) - HALF * ey)
            curl = (
                (hz - self.y_down(hz)) - (hy - hy_z),
                (hx - hx_z) - (hz - hz_x),
                (hy - hy_x) - (hx - self.y_down(hx)),
            )
            emit(a, b, (ex, ey, ez), (hx, hy, hz), curl)
            ex, ey, hx_z, hy_z = ex_next, ey_next, hx, hy
        return ex, ey, hx_z, hy_z

    def gradient(self, layers, arrays, store):
        first = first_layer(self.cells_z, layers)
        first_group = first // ROWS
        if self.mode == EDGE:
            grad_edges, mask_ref = arrays
            mask = self.edge(mask_ref[...], self.grad_base, 5)
        else:
            f_ref, inv_ref, grad_ref, mask_ref = arrays
            mask = mask_ref[...]

        def emit(a, b, efield, hfield, curl):
            z = ROWS * a + b
            layer = z - first
            if self.mode == EDGE:
                tile = self.grad_base + self.per_group * (a - first_group)
                slots = [6 * b + n for n in range(5)]
                values = [
                    self.edge(grad_edges[layer, n], tile + slot // SLOTS, slot % SLOTS)
                    for n, slot in enumerate(slots)
                ]
            else:
                values = [f_ref[c, z] for c in range(3)] + [inv_ref[z], grad_ref[layer]]
            total = None
            for c in range(3):
                term = values[c] * (efield[c] + values[3] * curl[c])
                total = term if total is None else total + term
            store(layer, values[4] + mask * total)

        def body(i, carry):
            return self.group(first_group + i, carry, emit)

        lax.fori_loop(0, layers // ROWS, body, self.start(first_group))


def fields_scratch(mode, xface, yface, width):
    rows, wide = xface.shape[0], faces_wide(mode, width)
    out = [pltpu.VMEM((rows, wide), jnp.float32)] * 2
    if mode != OWN:
        out.append(pltpu.VMEM((2,) + yface.shape, jnp.float32))
    return out


def own_gradient_kernel(counts, *refs):
    e_ref, h_ref, f_ref, inv_ref, grad_ref, mask_ref = refs[:6]
    zfaces, xfaces = refs[6 : 6 + counts[0]], refs[6 + counts[0] : 6 + sum(counts)]
    grad_out, scratch = refs[6 + sum(counts)], refs[7 + sum(counts) :]
    layers = grad_ref.shape[0]
    fields = Fields(OWN, layers, (e_ref, h_ref), zfaces, xfaces, None, scratch)

    def store(layer, value):
        grad_out[layer] = value

    fields.gradient(layers, (f_ref, inv_ref, grad_ref, mask_ref), store)


def own_gradient(arrays, zfaces, xfaces):
    grad_sum = arrays[4]
    return pl.pallas_call(
        functools.partial(own_gradient_kernel, (len(zfaces), len(xfaces))),
        in_specs=[VMEM] * (6 + len(zfaces) + len(xfaces)),
        out_specs=VMEM,
        out_shape=f32(*grad_sum.shape),
        scratch_shapes=fields_scratch(OWN, xfaces[0], None, grad_sum.shape[2]),
        compiler_params=params(),
    )(*arrays, *zfaces, *xfaces)


def edge_gradient_kernel(counts, per_device, *refs):
    own_ref, eh_ref, grad_ref, mask_ref = refs[:4]
    ends = np.cumsum((4,) + counts)
    zfaces, xfaces, yfaces = (refs[i:j] for i, j in zip(ends[:-1], ends[1:]))
    sends, scratch, edge_ref = refs[ends[-1] : -4], refs[-4:-1], refs[-1]
    layers, _, width = own_ref.shape
    lane = lax.broadcasted_iota(jnp.int32, (ROWS, LANES), 1)
    me = lax.axis_index("gx")
    fields = Fields(EDGE, layers, eh_ref, zfaces, xfaces, yfaces, scratch)

    def store(layer, value):
        edge_ref[layer] = value

    fields.gradient(layers, (grad_ref, mask_ref), store)

    for k, send_ref in enumerate(sends):
        chunk = lax.bitwise_xor(me, k)
        packed = jnp.zeros((ROWS, LANES), jnp.float32)
        for i in range(per_device):
            layer = chunk * per_device + i
            edge = edge_ref[layer]
            at = i * width
            head, tail = own_ref[layer, :, 0:LANES], own_ref[layer, :, width - LANES :]
            send_ref[:, at : at + LANES] = jnp.where(lane == 0, pltpu.roll(edge, LANES - STRIP, 1), head)
            send_ref[:, at + LANES : at + width - LANES] = own_ref[layer, :, LANES : width - LANES]
            send_ref[:, at + width - LANES : at + width] = jnp.where(
                lane == LANES - 1, pltpu.roll(edge, STRIP, 1), tail
            )
            side = pltpu.roll(edge, (2 * STRIP * i + STRIP) % LANES, 1)
            packed = jnp.where(lane // (2 * STRIP) == i, side, packed)
        send_ref[:, per_device * width :] = packed


def edge_gradient(own, edges, zfaces, xfaces, yfaces):
    layers, _, width = own.shape
    count = lax.axis_size("gx")
    per_device = layers // count
    faces = (*zfaces, *xfaces, *yfaces)
    return pl.pallas_call(
        functools.partial(edge_gradient_kernel, (len(zfaces), len(xfaces), len(yfaces)), per_device),
        in_specs=[VMEM] * (4 + len(faces)),
        out_specs=[VMEM] * count,
        out_shape=[f32(ROWS, per_device * width + LANES)] * count,
        scratch_shapes=fields_scratch(EDGE, xfaces[0], yfaces[0], width)
        + [pltpu.VMEM((layers, ROWS, LANES), jnp.float32)],
        compiler_params=params(),
    )(own, *edges, *faces)


def step_kernel(counts, layers, *refs):
    e_ref, h_ref, inv_ref = refs[:3]
    ends = np.cumsum((3,) + counts)
    zfaces, xfaces, yfaces, shares = (refs[i:j] for i, j in zip(ends[:-1], ends[1:]))
    (e_out, h_out, grad_out), scratch, carry_ref = refs[ends[-1] : -4], refs[-4:-1], refs[-1]
    width = e_ref.shape[3]
    fields = Fields(CIRCLE, layers, (e_ref, h_ref), zfaces, xfaces, yfaces, scratch)
    a = pl.program_id(0)

    def emit(a, b, efield, hfield, curl):
        half_inv = inv_ref[ROWS * a + b]
        for c in range(3):
            e_out[c, b] = efield[c][:, :width] + half_inv * curl[c][:, :width]
            h_out[c, b] = hfield[c][:, :width]

    @pl.when(a == 0)
    def _():
        for i, v in enumerate(fields.start(0)):
            carry_ref[i] = v
        per_device = layers // len(shares)
        me = lax.axis_index("gx")
        for k, share in enumerate(shares):
            chunk = lax.bitwise_xor(me, k)
            for i in range(per_device):
                grad_out[chunk * per_device + i] = share[:, i * width : (i + 1) * width]

    carry = tuple(carry_ref[i] for i in range(4))
    for i, v in enumerate(fields.group(a, carry, emit)):
        carry_ref[i] = v


def step(efield, hfield, inv, zfaces, xfaces, yfaces, shares, layers):
    _, cells_z, _, width = efield.shape
    block = pl.BlockSpec((3, ROWS, ROWS, width), lambda a: (0, a, 0, 0))
    groups = (zfaces, xfaces, yfaces, shares)
    counts = tuple(len(group) for group in groups)
    return pl.pallas_call(
        functools.partial(step_kernel, counts, layers),
        grid=(cells_z // ROWS,),
        in_specs=[VMEM] * (3 + sum(counts)),
        out_specs=[block, block, VMEM],
        out_shape=[f32(*efield.shape)] * 2 + [f32(layers, ROWS, width)],
        scratch_shapes=fields_scratch(CIRCLE, xfaces[0], yfaces[0], width)
        + [pltpu.VMEM((4, ROWS, width + LANES), jnp.float32)],
        compiler_params=params(),
    )(efield, hfield, inv, *(one for group in groups for one in group))


def cone_matrix(rows):
    span = np.arange(-RADIUS, RADIUS + 1, dtype=np.float64)
    cone = np.maximum(RADIUS - np.sqrt(span[:, None] ** 2 + span[None, :] ** 2), 0.0)
    weight = cone / cone.sum()
    x = np.arange(rows)
    out = np.zeros((RADIUS + 1, rows, rows))
    for b in range(RADIUS + 1):
        for apart in (x[:, None] - x[None, :], 2 * rows - 1 - x[:, None] - x[None, :]):
            near = np.abs(apart) <= RADIUS
            out[b] += np.where(near, weight[np.clip(apart, -RADIUS, RADIUS) + RADIUS, RADIUS + b], 0.0)
    out = out.reshape((RADIUS + 1) * rows, rows).astype(np.float32)
    high = out.astype(jnp.bfloat16)
    low = (out - high.astype(np.float32)).astype(jnp.bfloat16)
    return np.concatenate([high, low, high], axis=1)


def flip_rows(v):
    row = lax.broadcasted_iota(jnp.int32, v.shape, 0)
    v = pltpu.roll(v, 4, 0)
    v = jnp.where(row % 4 < 2, pltpu.roll(v, ROWS - 2, 0), pltpu.roll(v, 2, 0))
    return jnp.where(row % 2 < 1, pltpu.roll(v, ROWS - 1, 0), pltpu.roll(v, 1, 0))


def filter_kernel(count, per_device, width, *refs):
    taps_ref = refs[0]
    got = refs[1 : 1 + count]
    outs = refs[1 + count : 1 + 2 * count]
    slabs, parts, done = refs[1 + 2 * count :]
    me = lax.axis_index("gx")
    wide = width + LANES
    half = count // 2
    rows = half * ROWS
    lane = lax.broadcasted_iota(jnp.int32, (ROWS, LANES), 1)
    for k in range(count):
        slabs[lax.bitwise_xor(me, k)] = got[k][...]

    def layer_of(slab, i):
        edge = slabs[slab, :, per_device * width :]
        at = 2 * STRIP * i
        upper = pltpu.roll(edge, (LANES - at) % LANES, 1) if at else edge
        lower = pltpu.roll(edge, (LANES - 2 * STRIP - at) % LANES, 1)
        side = jnp.where(lane < STRIP, upper, lower)
        return jnp.concatenate([slabs[slab, :, i * width : (i + 1) * width], side], axis=1)

    for i in range(per_device):
        halves = [layer_of(s, i) + flip_rows(layer_of(count - 1 - s, i)) for s in range(half)]
        symmetric = jnp.concatenate(halves, axis=0)
        high = symmetric.astype(jnp.bfloat16)
        low = (symmetric - high.astype(jnp.float32)).astype(jnp.bfloat16)
        parts[0:rows, :] = high
        parts[rows : 2 * rows, :] = high
        parts[2 * rows : 3 * rows, :] = low
        mixed = jnp.dot(taps_ref[...], parts[...], preferred_element_type=jnp.float32)
        total = mixed[0:rows]
        for b in range(1, RADIUS + 1):
            part = mixed[b * rows : (b + 1) * rows]
            total = total + (pltpu.roll(part, b, 1) + pltpu.roll(part, wide - b, 1))
        for s in range(half):
            own = total[s * ROWS : (s + 1) * ROWS, :width]
            done[s, i] = own
            done[count - 1 - s, i] = flip_rows(own)
    for k in range(count):
        outs[k][...] = done[lax.bitwise_xor(me, k)]


def cone_filter(got, per_device, width):
    count = len(got)
    rows = count // 2 * ROWS
    taps = jnp.asarray(cone_matrix(rows))
    return pl.pallas_call(
        functools.partial(filter_kernel, count, per_device, width),
        in_specs=[VMEM] * (1 + count),
        out_specs=[VMEM] * count,
        out_shape=[f32(per_device, ROWS, width)] * count,
        scratch_shapes=[
            pltpu.VMEM((count, ROWS, per_device * width + LANES), jnp.float32),
            pltpu.VMEM((3 * rows, width + LANES), jnp.bfloat16),
            pltpu.VMEM((count, per_device, ROWS, width), jnp.float32),
        ],
        compiler_params=params(),
    )(taps, *got)


def place_kernel(count, per_device, *refs):
    out, sems = refs[count], refs[count + 1]
    copies = []
    for k in range(count):
        at = lax.bitwise_xor(lax.axis_index("gx"), k) * per_device
        copies.append(pltpu.make_async_copy(refs[k], out.at[pl.ds(at, per_device)], sems.at[k]))
    for copy in copies:
        copy.start()
    for copy in copies:
        copy.wait()


def place_layers(parts):
    count = len(parts)
    per_device, rows, width = parts[0].shape
    return pl.pallas_call(
        functools.partial(place_kernel, count, per_device),
        in_specs=[ANY] * count,
        out_specs=ANY,
        out_shape=f32(count * per_device, rows, width),
        scratch_shapes=[pltpu.SemaphoreType.DMA((count,))],
        compiler_params=params(),
    )(*parts)


def spread(parts):
    count = len(parts)
    got = list(parts)
    for k in range(count - 1, 0, -1):
        got[k] = lax.ppermute(parts[k], "gx", [(i, i ^ k) for i in range(count)])
    return got


def on_device(efield, hfield, forward, material, permit, design_mask, grad_sum):
    layers, _, width = grad_sum.shape
    zfaces = exchange(z_faces(efield, hfield), "gz")
    efield, hfield, forward, grad_sum, own_low, own_high, mask, inv = load(
        permit, efield, hfield, forward, material, grad_sum, design_mask
    )
    arrays = (efield, hfield, forward, inv, grad_sum, mask)
    xfaces = exchange(x_faces(efield, hfield, zfaces), "gx")
    edges = own_edges(arrays)
    yfaces = exchange(y_faces(own_low, own_high, zfaces, xfaces), "gy", wrap=True)
    own = own_gradient(arrays, zfaces, xfaces)
    shares = edge_gradient(own, edges, zfaces, xfaces, yfaces)
    got = spread(shares)
    e_next, h_next, grad_total = step(efield, hfield, inv, zfaces, xfaces, yfaces, shares, layers)
    filtered = spread(cone_filter(got, layers // len(got), width))
    return e_next, h_next, grad_total, place_layers(filtered)


def solution(mesh):
    field = P(None, "gz", "gx", "gy")
    cells = P("gz", "gx", "gy")
    return jax.shard_map(
        on_device,
        mesh=mesh,
        in_specs=(field, field, field, cells, P(), P("gx", "gy"), cells),
        out_specs=(field, field, cells, cells),
        check_vma=False,
    )
```

```python
import functools
import math

import jax
import jax.numpy as jnp
import numpy as np
from jax import lax
from jax.experimental import pallas as pl
from jax.experimental.pallas import tpu as pltpu
from jax.sharding import PartitionSpec as P

RADIUS = 6
BLOCK = 8
HALF = 0.5

ROWS = 8
LANES = 128
STRIP = 8
SLOTS = LANES // STRIP
MIB = 1024 * 1024

VMEM = pl.BlockSpec(memory_space=pltpu.VMEM)
SMEM = pl.BlockSpec(memory_space=pltpu.SMEM)
ANY = pl.BlockSpec(memory_space=pl.ANY)


def params(mib=24):
    return pltpu.CompilerParams(vmem_limit_bytes=mib * MIB)


def f32(*shape):
    return jax.ShapeDtypeStruct(shape, jnp.float32)


def swap_pairs(value, axis, pairs):
    return lax.ppermute(value, axis, pairs + [(b, a) for a, b in pairs])


def rounds(axis):
    return 2 if lax.axis_size(axis) > 2 else 1


def exchange(sends, axis, wrap=False):
    count = lax.axis_size(axis)
    if count == 1:
        return sends
    got = [swap_pairs(sends[0], axis, [(i, i + 1) for i in range(0, count - 1, 2)])]
    if len(sends) > 1:
        odd_pairs = [(i, i + 1) for i in range(1, count - 1, 2)]
        if wrap and count % 2 == 0:
            odd_pairs.append((0, count - 1))
        got.append(swap_pairs(sends[1], axis, odd_pairs))
    return got


class Side:
    def __init__(self, axis):
        index = lax.axis_index(axis)
        self.rounds = rounds(axis)
        self.odd = index % 2 == 1
        self.bottom = index == 0
        self.top = index == lax.axis_size(axis) - 1

    def sends(self, low, high):
        both = [jnp.where(self.odd, low, high)]
        if self.rounds > 1:
            both.append(jnp.where(self.odd, high, low))
        return both

    def lower(self, got):
        return jnp.where(self.bottom, 0.0, jnp.where(self.odd, got[0], got[-1]))

    def upper(self, got):
        return jnp.where(self.top, 0.0, jnp.where(self.odd, got[-1], got[0]))


def first_layer(cells_z, layers):
    return (cells_z - layers) * (1 - lax.axis_index("gz"))


def z_faces_kernel(*refs):
    e_ref, h_ref = refs[:2]
    sends, (e_low, e_high, h_high, sems) = refs[2:-4], refs[-4:]
    top = e_ref.shape[1] - 1
    copies = [
        pltpu.make_async_copy(e_ref.at[:, 0], e_low, sems.at[0]),
        pltpu.make_async_copy(e_ref.at[:, top], e_high, sems.at[1]),
        pltpu.make_async_copy(h_ref.at[:, top], h_high, sems.at[2]),
    ]
    for copy in copies:
        copy.start()
    for copy in copies:
        copy.wait()
    side = Side("gz")
    ex, ey, ez = (e_high[c] for c in range(3))
    high = (h_high[0] + HALF * ez - HALF * ey, h_high[1] + HALF * ex - HALF * ez, ez)
    for c in range(3):
        for ref, value in zip(sends, side.sends(e_low[c], high[c])):
            ref[c] = value


def z_faces(efield, hfield):
    face = f32(*efield.shape[:1], *efield.shape[2:])
    return pl.pallas_call(
        z_faces_kernel,
        in_specs=[ANY] * 2,
        out_specs=[VMEM] * rounds("gz"),
        out_shape=[face] * rounds("gz"),
        scratch_shapes=[pltpu.VMEM(face.shape, jnp.float32)] * 3 + [pltpu.SemaphoreType.DMA((3,))],
        compiler_params=params(60),
    )(efield, hfield)


def x_faces_kernel(z_rounds, *refs):
    e_ref, h_ref = refs[:2]
    zfaces = refs[2 : 2 + z_rounds]
    sends, (low_ref, rows_ref) = refs[2 + z_rounds : -2], refs[-2:]
    cells_z = e_ref.shape[1]
    last = ROWS - 1
    z_side = Side("gz")
    low_ref[...] = jnp.zeros_like(low_ref)
    for z in range(cells_z):
        low_ref[z : z + 1, :] = e_ref[1, z, 0:1, :]
        low_ref[cells_z + z : cells_z + z + 1, :] = e_ref[2, z, 0:1, :]
        for c in range(3):
            rows_ref[c, z : z + 1, :] = e_ref[c, z, last : last + 1, :]
        for c in range(2):
            rows_ref[3 + c, z : z + 1, :] = h_ref[1 + c, z, last : last + 1, :]
        if z > 0:
            rows_ref[5, z - 1 : z, :] = e_ref[0, z, last : last + 1, :]
    rows_ref[5, cells_z - 1 : cells_z, :] = z_side.upper([f[0, last : last + 1, :] for f in zfaces])
    low_ref[2 * cells_z : 2 * cells_z + 1, :] = z_side.lower([f[2, 0:1, :] for f in zfaces])
    ex = rows_ref[0]
    high = (
        rows_ref[3] - HALF * (rows_ref[5] - ex + rows_ref[2]),
        rows_ref[4] + HALF * rows_ref[1] - HALF * ex,
        ex,
    )
    side = Side("gx")
    for c in range(3):
        here = slice(c * cells_z, (c + 1) * cells_z)
        for ref, value in zip(sends, side.sends(low_ref[here, :], high[c])):
            ref[here, :] = value


def x_faces(efield, hfield, zfaces):
    cells_z, cells_y = efield.shape[1], efield.shape[3]
    face = f32(3 * cells_z, cells_y)
    return pl.pallas_call(
        functools.partial(x_faces_kernel, len(zfaces)),
        in_specs=[VMEM] * (2 + len(zfaces)),
        out_specs=[VMEM] * rounds("gx"),
        out_shape=[face] * rounds("gx"),
        scratch_shapes=[
            pltpu.VMEM(face.shape, jnp.float32),
            pltpu.VMEM((6, cells_z, cells_y), jnp.float32),
        ],
        compiler_params=params(),
    )(efield, hfield, *zfaces)


def lane_group():
    return lax.broadcasted_iota(jnp.int32, (ROWS, LANES), 1) // STRIP


def pack_strips(tiles, low_ref, high_ref, first):
    group = lane_group()
    width = tiles[0][1]
    for start in range(0, len(tiles), SLOTS):
        low = jnp.zeros((ROWS, LANES), jnp.float32)
        high = jnp.zeros((ROWS, LANES), jnp.float32)
        for k, (load, _) in enumerate(tiles[start : start + SLOTS]):
            if load is None:
                continue
            here = group == k
            shift = (STRIP * k) % LANES
            left = load(slice(0, LANES))
            right = load(slice(width - LANES, width))
            low = jnp.where(here, pltpu.roll(left, shift, 1) if shift else left, low)
            shift = (STRIP * k + STRIP) % LANES
            high = jnp.where(here, pltpu.roll(right, shift, 1) if shift else right, high)
        low_ref[first + start // SLOTS] = low
        high_ref[first + start // SLOTS] = high


def load_kernel(
    permit_ref, e_in, h_in, f_in, mat_in, grad_in, mask_ref,
    e_ref, h_ref, f_ref, grad_ref, low_ref, high_ref, wide_ref, inv_ref, mat_ref, sems,
):
    cells_z, width = e_ref.shape[1], e_ref.shape[3]
    layers = grad_ref.shape[0]
    blocks = mask_ref.shape[1]
    pairs = [(e_in, e_ref), (h_in, h_ref), (f_in, f_ref)]
    copies = [[pltpu.make_async_copy(mat_in, mat_ref, sems.at[0])]]
    copies.append([pltpu.make_async_copy(grad_in, grad_ref, sems.at[1])])
    for n, (source, target) in enumerate(pairs):
        copies.append(
            [pltpu.make_async_copy(source.at[c], target.at[c], sems.at[2 + 3 * n + c]) for c in range(3)]
        )
    for group in copies:
        for copy in group:
            copy.start()

    spread = (
        lax.broadcasted_iota(jnp.int32, (blocks, width), 0)
        == lax.broadcasted_iota(jnp.int32, (blocks, width), 1) // BLOCK
    ).astype(jnp.float32)
    mask = jnp.broadcast_to(mask_ref[...].astype(jnp.float32), (ROWS, blocks))
    wide_ref[...] = jnp.dot(mask, spread, preferred_element_type=jnp.float32)

    def arrived(*groups):
        for n in groups:
            for copy in copies[n]:
                copy.wait()

    arrived(0)
    inverse = [HALF * (1.0 / permit_ref[m]) for m in range(permit_ref.shape[0])]
    for z in range(cells_z):
        inv = jnp.full((ROWS, width), inverse[0])
        for m in range(1, len(inverse)):
            inv = jnp.where(mat_ref[z] == m, inverse[m], inv)
        inv_ref[z] = inv
    arrived(1, 2, 3)
    first = first_layer(cells_z, layers)
    tiles = []
    for z in range(cells_z):
        for ref in (e_ref, h_ref):
            for c in range(3):
                tiles.append((lambda s, r=ref, c=c, z=z: r[c, z, :, s], width))
    pack_strips(tiles, low_ref, high_ref, 0)
    arrived(4)
    done = len(tiles) // SLOTS
    tiles = []
    for layer in range(layers):
        for c in range(3):
            tiles.append((lambda s, c=c, l=layer: f_ref[c, first + l, :, s], width))
        tiles.append((lambda s, l=layer: inv_ref[first + l, :, s], width))
        tiles.append((lambda s, l=layer: grad_ref[l, :, s], width))
        tiles.append((lambda s: wide_ref[:, s], width) if layer % ROWS == 0 else (None, width))
    pack_strips(tiles, low_ref, high_ref, done)


def load(permit, efield, hfield, forward, material, grad_sum, mask):
    cells_z, width = efield.shape[1], efield.shape[3]
    count = (cells_z * 6 + grad_sum.shape[0] * 6) // SLOTS
    packed = (count, ROWS, LANES)
    return pl.pallas_call(
        load_kernel,
        in_specs=[SMEM] + [ANY] * 5 + [VMEM],
        out_specs=[VMEM] * 8,
        out_shape=[
            pltpu.VMEM(shape, jnp.float32)
            for shape in (
                efield.shape,
                hfield.shape,
                forward.shape,
                grad_sum.shape,
                packed,
                packed,
                (ROWS, width),
                material.shape,
            )
        ],
        scratch_shapes=[pltpu.VMEM(material.shape, jnp.int32), pltpu.SemaphoreType.DMA((11,))],
        compiler_params=params(56),
    )(permit, efield, hfield, forward, material, grad_sum, mask)


def edge_tile(load, width):
    lane = lax.broadcasted_iota(jnp.int32, (ROWS, LANES), 1)
    head = pltpu.roll(load(slice(0, LANES)), STRIP, 1)
    tail = pltpu.roll(load(slice(width - LANES, width)), LANES - STRIP, 1)
    return jnp.where(lane < LANES // 2, head, tail)


def edges_kernel(e_ref, h_ref, f_ref, inv_ref, grad_ref, mask_ref, eh_out, grad_out, mask_out):
    cells_z, width = e_ref.shape[1], e_ref.shape[3]
    layers = grad_ref.shape[0]
    first = first_layer(cells_z, layers)
    for z in range(cells_z):
        for c in range(3):
            eh_out[z, c] = edge_tile(lambda s: e_ref[c, z, :, s], width)
            eh_out[z, 3 + c] = edge_tile(lambda s: h_ref[c, z, :, s], width)
    for layer in range(layers):
        for c in range(3):
            grad_out[layer, c] = edge_tile(lambda s: f_ref[c, first + layer, :, s], width)
        grad_out[layer, 3] = edge_tile(lambda s: inv_ref[first + layer, :, s], width)
        grad_out[layer, 4] = edge_tile(lambda s: grad_ref[layer, :, s], width)
    mask_out[...] = edge_tile(lambda s: mask_ref[:, s], width)


def own_edges(arrays):
    cells_z, layers = arrays[0].shape[1], arrays[4].shape[0]
    return pl.pallas_call(
        edges_kernel,
        in_specs=[VMEM] * 6,
        out_specs=[VMEM] * 3,
        out_shape=[f32(cells_z, 6, ROWS, LANES), f32(layers, 5, ROWS, LANES), f32(ROWS, LANES)],
        compiler_params=params(),
    )(*arrays)


def face_tiles(zfaces, xfaces):
    width = xfaces[0].shape[1]
    z_side, x_side = Side("gz"), Side("gx")
    tiles = []
    for c in range(3):
        tiles.append((lambda s, c=c: z_side.lower([f[c, :, s] for f in zfaces]), width))
    for c in range(2):
        tiles.append((lambda s, c=c: z_side.upper([f[c, :, s] for f in zfaces]), width))
    for pick in (x_side.lower, x_side.upper):
        for t in range(0, xfaces[0].shape[0], ROWS):
            tiles.append((lambda s, p=pick, t=t: p([f[t : t + ROWS, s] for f in xfaces]), width))
    return tiles


def face_count(xface):
    return 5 + 2 * (xface.shape[0] // ROWS)


def y_faces_kernel(counts, *refs):
    own_low, own_high = refs[:2]
    zfaces, xfaces = refs[2 : 2 + counts[0]], refs[2 + counts[0] : 2 + sum(counts)]
    sends, (low_ref, high_ref) = refs[2 + sum(counts) : -2], refs[-2:]
    own = own_low.shape[0]
    pack_strips(face_tiles(zfaces, xfaces), low_ref, high_ref, 0)
    side = Side("gy")
    for ref, value in zip(sends, side.sends(own_low[...], own_high[...])):
        ref[0:own] = value
    for ref, value in zip(sends, side.sends(low_ref[...], high_ref[...])):
        ref[own:] = value


def y_faces(own_low, own_high, zfaces, xfaces):
    extra = math.ceil(face_count(xfaces[0]) / SLOTS)
    packed = f32(own_low.shape[0] + extra, ROWS, LANES)
    return pl.pallas_call(
        functools.partial(y_faces_kernel, (len(zfaces), len(xfaces))),
        in_specs=[VMEM] * (2 + len(zfaces) + len(xfaces)),
        out_specs=[VMEM] * rounds("gy"),
        out_shape=[packed] * rounds("gy"),
        scratch_shapes=[pltpu.VMEM((extra, ROWS, LANES), jnp.float32)] * 2,
        compiler_params=params(),
    )(own_low, own_high, *zfaces, *xfaces)


OWN, CIRCLE, EDGE = range(3)


def faces_wide(mode, width):
    return {OWN: width, CIRCLE: width + LANES, EDGE: LANES}[mode]


class Fields:
    def __init__(self, mode, layers, fields, zfaces, xfaces, yfaces, scratch):
        self.mode = mode
        self.fields = fields
        if mode == EDGE:
            self.cells_z, self.width = fields.shape[0], xfaces[0].shape[1]
        else:
            self.cells_z, self.width = fields[0].shape[1], fields[0].shape[3]
        self.wide = faces_wide(mode, self.width)
        self.lane = lax.broadcasted_iota(jnp.int32, (ROWS, LANES), 1)
        self.row = lax.broadcasted_iota(jnp.int32, (ROWS, self.wide), 0)
        self.per_group = 6 * ROWS // SLOTS
        self.groups = self.cells_z // ROWS
        self.grad_base = self.per_group * self.groups
        halo_base = self.grad_base + self.per_group * (layers // ROWS)
        self.left_wide, self.right_wide = left_wide, right_wide = scratch[:2]
        if mode != OWN:
            self.ybuf = scratch[2]
            y_side = Side("gy")
            for t in range(yfaces[0].shape[0]):
                lower = y_side.lower([f[t] for f in yfaces])
                upper = y_side.upper([f[t] for f in yfaces])
                if mode == EDGE:
                    even = self.lane // STRIP % 2 == 0
                    lower, upper = (
                        jnp.where(even, upper, pltpu.roll(lower, STRIP, 1)),
                        jnp.where(even, pltpu.roll(upper, LANES - STRIP, 1), lower),
                    )
                self.ybuf[0, t] = lower
                self.ybuf[1, t] = upper

        def face(load, slot):
            if mode == EDGE:
                own = edge_tile(load, self.width)
                return self.edge(own, halo_base + slot // SLOTS, slot % SLOTS)
            return self.wider(load, halo_base + slot // SLOTS, slot % SLOTS)

        full = [face(load, slot) for slot, (load, _) in enumerate(face_tiles(zfaces, xfaces))]
        self.below, self.above = full[:3], full[3:5]
        per_face = xfaces[0].shape[0] // ROWS
        for t in range(per_face):
            left_wide[t * ROWS : (t + 1) * ROWS, :] = full[5 + t]
            right_wide[t * ROWS : (t + 1) * ROWS, :] = full[5 + per_face + t]
        cells_z = self.cells_z
        left_wide[cells_z : 2 * cells_z, :] += HALF * self.y_up(left_wide[2 * cells_z : 3 * cells_z, :])

    def wider(self, load, tile, k):
        if self.mode == OWN:
            return load(slice(0, self.width))

        def moved(v, to):
            shift = (to - STRIP * k) % LANES
            return pltpu.roll(v, shift, 1) if shift else v

        lower, upper = self.ybuf[0, tile], self.ybuf[1, tile]
        halo = jnp.where(self.lane < STRIP, moved(upper, 0), moved(lower, LANES - STRIP))
        return jnp.concatenate([load(slice(0, self.width)), halo], axis=1)

    def edge(self, own, tile, k):
        shift = (LANES - STRIP - 2 * STRIP * (k // 2)) % LANES
        both = pltpu.roll(self.ybuf[k % 2, tile], shift, 1)
        inside = jnp.logical_and(self.lane >= STRIP, self.lane < LANES - STRIP)
        return jnp.where(inside, own, both)

    def y_up(self, v):
        return pltpu.roll(v, self.wide - 1, 1)

    def y_down(self, v):
        return pltpu.roll(v, 1, 1)

    def x_up(self, v, line):
        return jnp.where(self.row == ROWS - 1, line, pltpu.roll(v, ROWS - 1, 0))

    def x_down(self, v, line):
        return jnp.where(self.row == 0, line, pltpu.roll(v, 1, 0))

    def line(self, ref, at):
        return jnp.broadcast_to(ref[pl.ds(at, 1), :], (ROWS, self.wide))

    def field(self, which, c, a, b):
        slot = 6 * b + 3 * which + c
        tile = self.per_group * a + slot // SLOTS
        if self.mode == EDGE:
            return self.edge(self.fields[ROWS * a + b, 3 * which + c], tile, slot % SLOTS)
        ref = self.fields[which]
        return self.wider(lambda s: ref[c, ROWS * a + b, :, s], tile, slot % SLOTS)

    def hx(self, a, b, ey, ez, ey_next):
        return self.field(1, 0, a, b) - HALF * (self.y_up(ez) - ez - ey_next + ey)

    def hy(self, a, b, ex, ez, ex_next):
        up = self.x_up(ez, self.line(self.right_wide, self.cells_z + ROWS * a + b))
        return self.field(1, 1, a, b) - HALF * (ex_next - ex - up + ez)

    def hz(self, a, b, ex, ey):
        up = self.x_up(ey, self.line(self.right_wide, ROWS * a + b))
        return self.field(1, 2, a, b) - HALF * (up - ey - self.y_up(ex) + ex)

    def start(self, a):
        ex, ey = self.field(0, 0, a, 0), self.field(0, 1, a, 0)
        below = self.below
        at_bottom = (
            below[0] - HALF * self.y_up(below[2]) + HALF * ey,
            below[1] - HALF * ex + HALF * self.x_up(below[2], self.line(self.right_wide, 2 * self.cells_z)),
        )
        before, b = jnp.maximum(a - 1, 0), ROWS - 1
        ex_before, ey_before, ez_before = (self.field(0, c, before, b) for c in range(3))
        inside = (
            self.hx(before, b, ey_before, ez_before, ey),
            self.hy(before, b, ex_before, ez_before, ex),
        )
        bottom = a == 0
        return (ex, ey) + tuple(jnp.where(bottom, one, two) for one, two in zip(at_bottom, inside))

    def group(self, a, carry, emit):
        ex, ey, hx_z, hy_z = carry
        for b in range(ROWS):
            z = ROWS * a + b
            ez = self.field(0, 2, a, b)
            if b < ROWS - 1:
                ex_next, ey_next = (self.field(0, c, a, b + 1) for c in range(2))
            else:
                end = a == self.groups - 1
                after = jnp.minimum(a + 1, self.groups - 1)
                ex_next, ey_next = (
                    jnp.where(end, self.above[c], self.field(0, c, after, 0)) for c in range(2)
                )
            hx = self.hx(a, b, ey, ez, ey_next)
            hy = self.hy(a, b, ex, ez, ex_next)
            hz = self.hz(a, b, ex, ey)
            hy_x = self.x_down(hy, self.line(self.left_wide, z) + HALF * ez)
            hz_x = self.x_down(hz, self.line(self.left_wide, self.cells_z + z) - HALF * ey)
            curl = (
                (hz - self.y_down(hz)) - (hy - hy_z),
                (hx - hx_z) - (hz - hz_x),
                (hy - hy_x) - (hx - self.y_down(hx)),
            )
            emit(a, b, (ex, ey, ez), (hx, hy, hz), curl)
            ex, ey, hx_z, hy_z = ex_next, ey_next, hx, hy
        return ex, ey, hx_z, hy_z

    def gradient(self, layers, arrays, store):
        first = first_layer(self.cells_z, layers)
        first_group = first // ROWS
        if self.mode == EDGE:
            grad_edges, mask_ref = arrays
            mask = self.edge(mask_ref[...], self.grad_base, 5)
        else:
            f_ref, inv_ref, grad_ref, mask_ref = arrays
            mask = mask_ref[...]

        def emit(a, b, efield, hfield, curl):
            z = ROWS * a + b
            layer = z - first
            if self.mode == EDGE:
                tile = self.grad_base + self.per_group * (a - first_group)
                slots = [6 * b + n for n in range(5)]
                values = [
                    self.edge(grad_edges[layer, n], tile + slot // SLOTS, slot % SLOTS)
                    for n, slot in enumerate(slots)
                ]
            else:
                values = [f_ref[c, z] for c in range(3)] + [inv_ref[z], grad_ref[layer]]
            total = None
            for c in range(3):
                term = values[c] * (efield[c] + values[3] * curl[c])
                total = term if total is None else total + term
            store(layer, values[4] + mask * total)

        def body(i, carry):
            return self.group(first_group + i, carry, emit)

        lax.fori_loop(0, layers // ROWS, body, self.start(first_group))


def fields_scratch(mode, xface, yface, width):
    rows, wide = xface.shape[0], faces_wide(mode, width)
    out = [pltpu.VMEM((rows, wide), jnp.float32)] * 2
    if mode != OWN:
        out.append(pltpu.VMEM((2,) + yface.shape, jnp.float32))
    return out


def own_gradient_kernel(counts, *refs):
    e_ref, h_ref, f_ref, inv_ref, grad_ref, mask_ref = refs[:6]
    zfaces, xfaces = refs[6 : 6 + counts[0]], refs[6 + counts[0] : 6 + sum(counts)]
    grad_out, scratch = refs[6 + sum(counts)], refs[7 + sum(counts) :]
    layers = grad_ref.shape[0]
    fields = Fields(OWN, layers, (e_ref, h_ref), zfaces, xfaces, None, scratch)

    def store(layer, value):
        grad_out[layer] = value

    fields.gradient(layers, (f_ref, inv_ref, grad_ref, mask_ref), store)


def own_gradient(arrays, zfaces, xfaces):
    grad_sum = arrays[4]
    return pl.pallas_call(
        functools.partial(own_gradient_kernel, (len(zfaces), len(xfaces))),
        in_specs=[VMEM] * (6 + len(zfaces) + len(xfaces)),
        out_specs=VMEM,
        out_shape=f32(*grad_sum.shape),
        scratch_shapes=fields_scratch(OWN, xfaces[0], None, grad_sum.shape[2]),
        compiler_params=params(),
    )(*arrays, *zfaces, *xfaces)


def edge_gradient_kernel(counts, per_device, *refs):
    own_ref, eh_ref, grad_ref, mask_ref = refs[:4]
    ends = np.cumsum((4,) + counts)
    zfaces, xfaces, yfaces = (refs[i:j] for i, j in zip(ends[:-1], ends[1:]))
    sends, scratch, edge_ref = refs[ends[-1] : -4], refs[-4:-1], refs[-1]
    layers, _, width = own_ref.shape
    lane = lax.broadcasted_iota(jnp.int32, (ROWS, LANES), 1)
    me = lax.axis_index("gx")
    fields = Fields(EDGE, layers, eh_ref, zfaces, xfaces, yfaces, scratch)

    def store(layer, value):
        edge_ref[layer] = value

    fields.gradient(layers, (grad_ref, mask_ref), store)

    for k, send_ref in enumerate(sends[::-1]):
        chunk = lax.bitwise_xor(me, k)
        packed = jnp.zeros((ROWS, LANES), jnp.float32)
        for i in range(per_device):
            layer = chunk * per_device + i
            edge = edge_ref[layer]
            at = i * width
            head, tail = own_ref[layer, :, 0:LANES], own_ref[layer, :, width - LANES :]
            send_ref[:, at : at + LANES] = jnp.where(lane == 0, pltpu.roll(edge, LANES - STRIP, 1), head)
            send_ref[:, at + LANES : at + width - LANES] = own_ref[layer, :, LANES : width - LANES]
            send_ref[:, at + width - LANES : at + width] = jnp.where(
                lane == LANES - 1, pltpu.roll(edge, STRIP, 1), tail
            )
            side = pltpu.roll(edge, (2 * STRIP * i + STRIP) % LANES, 1)
            packed = jnp.where(lane // (2 * STRIP) == i, side, packed)
        send_ref[:, per_device * width :] = packed


def edge_gradient(own, edges, zfaces, xfaces, yfaces):
    layers, _, width = own.shape
    count = lax.axis_size("gx")
    per_device = layers // count
    faces = (*zfaces, *xfaces, *yfaces)
    shares = pl.pallas_call(
        functools.partial(edge_gradient_kernel, (len(zfaces), len(xfaces), len(yfaces)), per_device),
        in_specs=[VMEM] * (4 + len(faces)),
        out_specs=[VMEM] * count,
        out_shape=[f32(ROWS, per_device * width + LANES)] * count,
        scratch_shapes=fields_scratch(EDGE, xfaces[0], yfaces[0], width)
        + [pltpu.VMEM((layers, ROWS, LANES), jnp.float32)],
        compiler_params=params(),
    )(own, *edges, *faces)
    return shares[::-1]


def step_kernel(counts, layers, *refs):
    e_ref, h_ref, inv_ref = refs[:3]
    ends = np.cumsum((3,) + counts)
    zfaces, xfaces, yfaces, shares = (refs[i:j] for i, j in zip(ends[:-1], ends[1:]))
    shares = shares[::-1]
    (e_out, h_out, grad_out), scratch, carry_ref = refs[ends[-1] : -4], refs[-4:-1], refs[-1]
    width = e_ref.shape[3]
    fields = Fields(CIRCLE, layers, (e_ref, h_ref), zfaces, xfaces, yfaces, scratch)
    a = pl.program_id(0)

    def emit(a, b, efield, hfield, curl):
        half_inv = inv_ref[ROWS * a + b]
        for c in range(3):
            e_out[c, b] = efield[c][:, :width] + half_inv * curl[c][:, :width]
            h_out[c, b] = hfield[c][:, :width]

    @pl.when(a == 0)
    def _():
        for i, v in enumerate(fields.start(0)):
            carry_ref[i] = v
        per_device = layers // len(shares)
        me = lax.axis_index("gx")
        for k, share in enumerate(shares):
            chunk = lax.bitwise_xor(me, k)
            for i in range(per_device):
                grad_out[chunk * per_device + i] = share[:, i * width : (i + 1) * width]

    carry = tuple(carry_ref[i] for i in range(4))
    for i, v in enumerate(fields.group(a, carry, emit)):
        carry_ref[i] = v


def step(efield, hfield, inv, zfaces, xfaces, yfaces, shares, layers):
    _, cells_z, _, width = efield.shape
    block = pl.BlockSpec((3, ROWS, ROWS, width), lambda a: (0, a, 0, 0))
    groups = (zfaces, xfaces, yfaces, shares[::-1])
    counts = tuple(len(group) for group in groups)
    return pl.pallas_call(
        functools.partial(step_kernel, counts, layers),
        grid=(cells_z // ROWS,),
        in_specs=[VMEM] * (3 + sum(counts)),
        out_specs=[block, block, VMEM],
        out_shape=[f32(*efield.shape)] * 2 + [f32(layers, ROWS, width)],
        scratch_shapes=fields_scratch(CIRCLE, xfaces[0], yfaces[0], width)
        + [pltpu.VMEM((4, ROWS, width + LANES), jnp.float32)],
        compiler_params=params(),
    )(efield, hfield, inv, *(one for group in groups for one in group))


def cone_matrix(rows):
    span = np.arange(-RADIUS, RADIUS + 1, dtype=np.float64)
    cone = np.maximum(RADIUS - np.sqrt(span[:, None] ** 2 + span[None, :] ** 2), 0.0)
    weight = cone / cone.sum()
    x = np.arange(rows)
    out = np.zeros((RADIUS + 1, rows, rows))
    for b in range(RADIUS + 1):
        for apart in (x[:, None] - x[None, :], 2 * rows - 1 - x[:, None] - x[None, :]):
            near = np.abs(apart) <= RADIUS
            out[b] += np.where(near, weight[np.clip(apart, -RADIUS, RADIUS) + RADIUS, RADIUS + b], 0.0)
    out = out.reshape((RADIUS + 1) * rows, rows).astype(np.float32)
    high = out.astype(jnp.bfloat16)
    low = (out - high.astype(np.float32)).astype(jnp.bfloat16)
    return np.concatenate([high, low, high], axis=1)


def flip_rows(v):
    row = lax.broadcasted_iota(jnp.int32, v.shape, 0)
    v = pltpu.roll(v, 4, 0)
    v = jnp.where(row % 4 < 2, pltpu.roll(v, ROWS - 2, 0), pltpu.roll(v, 2, 0))
    return jnp.where(row % 2 < 1, pltpu.roll(v, ROWS - 1, 0), pltpu.roll(v, 1, 0))


def filter_kernel(count, per_device, width, *refs):
    taps_ref = refs[0]
    got = refs[count:0:-1]
    outs = refs[1 + count : 1 + 2 * count]
    slabs, parts, done = refs[1 + 2 * count :]
    me = lax.axis_index("gx")
    wide = width + LANES
    half = count // 2
    rows = half * ROWS
    lane = lax.broadcasted_iota(jnp.int32, (ROWS, LANES), 1)
    for k in range(count):
        slabs[lax.bitwise_xor(me, k)] = got[k][...]

    def layer_of(slab, i):
        edge = slabs[slab, :, per_device * width :]
        at = 2 * STRIP * i
        upper = pltpu.roll(edge, (LANES - at) % LANES, 1) if at else edge
        lower = pltpu.roll(edge, (LANES - 2 * STRIP - at) % LANES, 1)
        side = jnp.where(lane < STRIP, upper, lower)
        return jnp.concatenate([slabs[slab, :, i * width : (i + 1) * width], side], axis=1)

    for i in range(per_device):
        halves = [layer_of(s, i) + flip_rows(layer_of(count - 1 - s, i)) for s in range(half)]
        symmetric = jnp.concatenate(halves, axis=0)
        high = symmetric.astype(jnp.bfloat16)
        low = (symmetric - high.astype(jnp.float32)).astype(jnp.bfloat16)
        parts[0:rows, :] = high
        parts[rows : 2 * rows, :] = high
        parts[2 * rows : 3 * rows, :] = low
        mixed = jnp.dot(taps_ref[...], parts[...], preferred_element_type=jnp.float32)
        total = mixed[0:rows]
        for b in range(1, RADIUS + 1):
            part = mixed[b * rows : (b + 1) * rows]
            total = total + (pltpu.roll(part, b, 1) + pltpu.roll(part, wide - b, 1))
        for s in range(half):
            own = total[s * ROWS : (s + 1) * ROWS, :width]
            done[s, i] = own
            done[count - 1 - s, i] = flip_rows(own)
    for k in range(count):
        outs[k][...] = done[lax.bitwise_xor(me, k)]


def cone_filter(got, per_device, width):
    count = len(got)
    rows = count // 2 * ROWS
    taps = jnp.asarray(cone_matrix(rows))
    return pl.pallas_call(
        functools.partial(filter_kernel, count, per_device, width),
        in_specs=[VMEM] * (1 + count),
        out_specs=[VMEM] * count,
        out_shape=[f32(per_device, ROWS, width)] * count,
        scratch_shapes=[
            pltpu.VMEM((count, ROWS, per_device * width + LANES), jnp.float32),
            pltpu.VMEM((3 * rows, width + LANES), jnp.bfloat16),
            pltpu.VMEM((count, per_device, ROWS, width), jnp.float32),
        ],
        compiler_params=params(),
    )(taps, *got[::-1])


def place_kernel(count, per_device, *refs):
    out, sems = refs[count], refs[count + 1]
    parts = refs[count - 1 :: -1]
    copies = []
    for k in range(count):
        at = lax.bitwise_xor(lax.axis_index("gx"), k) * per_device
        copies.append(pltpu.make_async_copy(parts[k], out.at[pl.ds(at, per_device)], sems.at[k]))
    for copy in copies:
        copy.start()
    for copy in copies:
        copy.wait()


def place_layers(parts):
    count = len(parts)
    per_device, rows, width = parts[0].shape
    return pl.pallas_call(
        functools.partial(place_kernel, count, per_device),
        in_specs=[ANY] * count,
        out_specs=ANY,
        out_shape=f32(count * per_device, rows, width),
        scratch_shapes=[pltpu.SemaphoreType.DMA((count,))],
        compiler_params=params(),
    )(*parts[::-1])


def spread(parts):
    count = len(parts)
    got = list(parts)
    for k in range(count - 1, 0, -1):
        got[k] = lax.ppermute(parts[k], "gx", [(i, i ^ k) for i in range(count)])
    return got


def on_device(efield, hfield, forward, material, permit, design_mask, grad_sum):
    layers, _, width = grad_sum.shape
    zfaces = exchange(z_faces(efield, hfield), "gz")
    efield, hfield, forward, grad_sum, own_low, own_high, mask, inv = load(
        permit, efield, hfield, forward, material, grad_sum, design_mask
    )
    arrays = (efield, hfield, forward, inv, grad_sum, mask)
    xfaces = exchange(x_faces(efield, hfield, zfaces), "gx")
    edges = own_edges(arrays)
    yfaces = exchange(y_faces(own_low, own_high, zfaces, xfaces), "gy", wrap=True)
    own = own_gradient(arrays, zfaces, xfaces)
    shares = edge_gradient(own, edges, zfaces, xfaces, yfaces)
    got = spread(shares)
    e_next, h_next, grad_total = step(efield, hfield, inv, zfaces, xfaces, yfaces, shares, layers)
    filtered = spread(cone_filter(got, layers // len(got), width))
    return e_next, h_next, grad_total, place_layers(filtered)


def solution(mesh):
    field = P(None, "gz", "gx", "gy")
    cells = P("gz", "gx", "gy")
    return jax.shard_map(
        on_device,
        mesh=mesh,
        in_specs=(field, field, field, cells, P(), P("gx", "gy"), cells),
        out_specs=(field, field, cells, cells),
        check_vma=False,
    )
```

```python
import functools
import math

import jax
import jax.numpy as jnp
import numpy as np
from jax import lax
from jax.experimental import pallas as pl
from jax.experimental.pallas import tpu as pltpu
from jax.sharding import PartitionSpec as P

RADIUS = 6
BLOCK = 8
HALF = 0.5

ROWS = 8
LANES = 128
STRIP = 8
SLOTS = LANES // STRIP
MIB = 1024 * 1024

VMEM = pl.BlockSpec(memory_space=pltpu.VMEM)
SMEM = pl.BlockSpec(memory_space=pltpu.SMEM)
ANY = pl.BlockSpec(memory_space=pl.ANY)


def params(mib=24):
    return pltpu.CompilerParams(vmem_limit_bytes=mib * MIB)


def f32(*shape):
    return jax.ShapeDtypeStruct(shape, jnp.float32)


def fast(*shape):
    return pltpu.VMEM(shape, jnp.float32)


def rounds(axis):
    return 2 if lax.axis_size(axis) > 2 else 1


def exchange(sends, axis, mate):
    count = lax.axis_size(axis)
    beside = lax.axis_size(mate)
    if count == 1:
        return sends
    got = []
    for start, value in enumerate(sends):
        partner = list(range(count))
        for low in range(start, count - 1, 2):
            partner[low], partner[low + 1] = low + 1, low
        axes = sorted((axis, mate))
        steps = (beside, 1) if axes[0] == axis else (1, count)
        pairs = []
        for i in range(count):
            for m in range(beside):
                if partner[i] != i:
                    to = (partner[i], m)
                elif beside % 2 == 0:
                    to = (i, m ^ 1)
                else:
                    continue
                pairs.append((i * steps[0] + m * steps[1], to[0] * steps[0] + to[1] * steps[1]))
        got.append(lax.ppermute(value, tuple(axes), pairs))
    return got


class Side:
    def __init__(self, axis):
        index = lax.axis_index(axis)
        self.rounds = rounds(axis)
        self.odd = index % 2 == 1
        self.bottom = index == 0
        self.top = index == lax.axis_size(axis) - 1

    def sends(self, low, high):
        both = [jnp.where(self.odd, low, high)]
        if self.rounds > 1:
            both.append(jnp.where(self.odd, high, low))
        return both

    def lower(self, got):
        return jnp.where(self.bottom, 0.0, jnp.where(self.odd, got[0], got[-1]))

    def upper(self, got):
        return jnp.where(self.top, 0.0, jnp.where(self.odd, got[-1], got[0]))


def first_layer(cells_z, layers):
    return (cells_z - layers) * (1 - lax.axis_index("gz"))


def z_faces_kernel(*refs):
    e_ref, h_ref = refs[:2]
    sends, (e_low, e_high, h_high, sems) = refs[2:-4], refs[-4:]
    top = e_ref.shape[1] - 1
    planes = [(e_ref.at[c, 0], e_low.at[c]) for c in range(2)]
    planes += [(e_ref.at[c, top], e_high.at[c]) for c in range(3)]
    planes += [(h_ref.at[c, top], h_high.at[c]) for c in range(2)]
    copies = [pltpu.make_async_copy(*plane, sems.at[n]) for n, plane in enumerate(planes)]
    for copy in copies:
        copy.start()
    for copy in copies:
        copy.wait()
    side = Side("gz")
    ex, ey, ez = (e_high[c] for c in range(3))
    low = (e_low[0], e_low[1], jnp.zeros_like(ez))
    high = (h_high[0] + HALF * ez - HALF * ey, h_high[1] + HALF * ex - HALF * ez, ez)
    for c in range(3):
        for ref, value in zip(sends, side.sends(low[c], high[c])):
            ref[c] = value


def z_faces(efield, hfield):
    face = fast(*efield.shape[:1], *efield.shape[2:])
    return pl.pallas_call(
        z_faces_kernel,
        in_specs=[ANY] * 2,
        out_specs=[VMEM] * rounds("gz"),
        out_shape=[face] * rounds("gz"),
        scratch_shapes=[pltpu.VMEM(face.shape, jnp.float32)] * 3 + [pltpu.SemaphoreType.DMA((7,))],
        compiler_params=params(60),
    )(efield, hfield)


def x_faces_kernel(z_rounds, *refs):
    e_ref, h_ref = refs[:2]
    zfaces = refs[2 : 2 + z_rounds]
    sends, (low_ref, rows_ref) = refs[2 + z_rounds : -2], refs[-2:]
    cells_z = e_ref.shape[1]
    last = ROWS - 1
    z_side = Side("gz")
    low_ref[...] = jnp.zeros_like(low_ref)
    for z in range(cells_z):
        low_ref[z : z + 1, :] = e_ref[1, z, 0:1, :]
        low_ref[cells_z + z : cells_z + z + 1, :] = e_ref[2, z, 0:1, :]
        for c in range(3):
            rows_ref[c, z : z + 1, :] = e_ref[c, z, last : last + 1, :]
        for c in range(2):
            rows_ref[3 + c, z : z + 1, :] = h_ref[1 + c, z, last : last + 1, :]
        if z > 0:
            rows_ref[5, z - 1 : z, :] = e_ref[0, z, last : last + 1, :]
    rows_ref[5, cells_z - 1 : cells_z, :] = z_side.upper([f[0, last : last + 1, :] for f in zfaces])
    low_ref[2 * cells_z : 2 * cells_z + 1, :] = z_side.lower([f[2, 0:1, :] for f in zfaces])
    ex = rows_ref[0]
    high = (
        rows_ref[3] - HALF * (rows_ref[5] - ex + rows_ref[2]),
        rows_ref[4] + HALF * rows_ref[1] - HALF * ex,
        ex,
    )
    side = Side("gx")
    for c in range(3):
        here = slice(c * cells_z, (c + 1) * cells_z)
        for ref, value in zip(sends, side.sends(low_ref[here, :], high[c])):
            ref[here, :] = value


def x_faces(efield, hfield, zfaces):
    cells_z, cells_y = efield.shape[1], efield.shape[3]
    face = fast(3 * cells_z, cells_y)
    return pl.pallas_call(
        functools.partial(x_faces_kernel, len(zfaces)),
        in_specs=[VMEM] * (2 + len(zfaces)),
        out_specs=[VMEM] * rounds("gx"),
        out_shape=[face] * rounds("gx"),
        scratch_shapes=[
            pltpu.VMEM(face.shape, jnp.float32),
            pltpu.VMEM((6, cells_z, cells_y), jnp.float32),
        ],
        compiler_params=params(),
    )(efield, hfield, *zfaces)


def lane_group():
    return lax.broadcasted_iota(jnp.int32, (ROWS, LANES), 1) // STRIP


def pack_strips(tiles, low_ref, high_ref, first):
    group = lane_group()
    width = tiles[0][1]
    for start in range(0, len(tiles), SLOTS):
        low = jnp.zeros((ROWS, LANES), jnp.float32)
        high = jnp.zeros((ROWS, LANES), jnp.float32)
        for k, (load, _) in enumerate(tiles[start : start + SLOTS]):
            if load is None:
                continue
            here = group == k
            shift = (STRIP * k) % LANES
            left = load(slice(0, LANES))
            right = load(slice(width - LANES, width))
            low = jnp.where(here, pltpu.roll(left, shift, 1) if shift else left, low)
            shift = (STRIP * k + STRIP) % LANES
            high = jnp.where(here, pltpu.roll(right, shift, 1) if shift else right, high)
        low_ref[first + start // SLOTS] = low
        high_ref[first + start // SLOTS] = high


def load_kernel(e_in, h_in, mat_in, grad_in, e_ref, h_ref, mat_ref, grad_ref, sems):
    parts = [(source.at[c], target.at[c]) for source, target in ((e_in, e_ref), (h_in, h_ref)) for c in range(3)]
    parts += [(mat_in, mat_ref), (grad_in, grad_ref)]
    copies = [pltpu.make_async_copy(*part, sems.at[n]) for n, part in enumerate(parts)]
    for copy in copies:
        copy.start()
    for copy in copies:
        copy.wait()


def load(*arrays):
    return pl.pallas_call(
        load_kernel,
        in_specs=[ANY] * 4,
        out_specs=[VMEM] * 4,
        out_shape=[pltpu.VMEM(one.shape, one.dtype) for one in arrays],
        scratch_shapes=[pltpu.SemaphoreType.DMA((8,))],
        compiler_params=params(56),
    )(*arrays)


def strips_kernel(
    permit_ref, e_ref, h_ref, f_in, mat_ref, grad_ref, mask_ref, f_ref, low_ref, high_ref, wide_ref, inv_ref, sems
):
    cells_z, width = e_ref.shape[1], e_ref.shape[3]
    layers = grad_ref.shape[0]
    blocks = mask_ref.shape[1]
    copies = [pltpu.make_async_copy(f_in.at[c], f_ref.at[c], sems.at[c]) for c in range(3)]
    for copy in copies:
        copy.start()

    inverse = [
        jnp.broadcast_to(HALF * (1.0 / permit_ref[0:1, m : m + 1]), (ROWS, width))
        for m in range(permit_ref.shape[1])
    ]
    for z in range(cells_z):
        inv = inverse[0]
        for m in range(1, len(inverse)):
            inv = jnp.where(mat_ref[z] == m, inverse[m], inv)
        inv_ref[z] = inv
    spread = (
        lax.broadcasted_iota(jnp.int32, (blocks, width), 0)
        == lax.broadcasted_iota(jnp.int32, (blocks, width), 1) // BLOCK
    ).astype(jnp.float32)
    mask = jnp.broadcast_to(mask_ref[...].astype(jnp.float32), (ROWS, blocks))
    wide_ref[...] = jnp.dot(mask, spread, preferred_element_type=jnp.float32)
    first = first_layer(cells_z, layers)
    tiles = []
    for z in range(cells_z):
        for ref in (e_ref, h_ref):
            for c in range(3):
                tiles.append((lambda s, r=ref, c=c, z=z: r[c, z, :, s], width))
    pack_strips(tiles, low_ref, high_ref, 0)

    for copy in copies:
        copy.wait()
    done = len(tiles) // SLOTS
    tiles = []
    for layer in range(layers):
        for c in range(3):
            tiles.append((lambda s, c=c, l=layer: f_ref[c, first + l, :, s], width))
        tiles.append((lambda s, l=layer: inv_ref[first + l, :, s], width))
        tiles.append((lambda s, l=layer: grad_ref[l, :, s], width))
        tiles.append((lambda s: wide_ref[:, s], width) if layer % ROWS == 0 else (None, width))
    pack_strips(tiles, low_ref, high_ref, done)


def strips(permit, efield, hfield, forward, material, grad_sum, mask):
    cells_z, width = efield.shape[1], efield.shape[3]
    count = (cells_z * 6 + grad_sum.shape[0] * 6) // SLOTS
    packed = (count, ROWS, LANES)
    shapes = (forward.shape, packed, packed, (ROWS, width), material.shape)
    return pl.pallas_call(
        strips_kernel,
        in_specs=[VMEM] * 3 + [ANY] + [VMEM] * 3,
        out_specs=[VMEM] * 5,
        out_shape=[fast(*shape) for shape in shapes],
        scratch_shapes=[pltpu.SemaphoreType.DMA((3,))],
        compiler_params=params(40),
    )(permit.reshape(1, -1), efield, hfield, forward, material, grad_sum, mask)


def edge_tile(load, width):
    lane = lax.broadcasted_iota(jnp.int32, (ROWS, LANES), 1)
    head = pltpu.roll(load(slice(0, LANES)), STRIP, 1)
    tail = pltpu.roll(load(slice(width - LANES, width)), LANES - STRIP, 1)
    return jnp.where(lane < LANES // 2, head, tail)


def edges_kernel(e_ref, h_ref, f_ref, inv_ref, grad_ref, mask_ref, eh_out, grad_out, mask_out):
    cells_z, width = e_ref.shape[1], e_ref.shape[3]
    layers = grad_ref.shape[0]
    first = first_layer(cells_z, layers)
    for z in range(cells_z):
        for c in range(3):
            eh_out[z, c] = edge_tile(lambda s: e_ref[c, z, :, s], width)
            eh_out[z, 3 + c] = edge_tile(lambda s: h_ref[c, z, :, s], width)
    for layer in range(layers):
        for c in range(3):
            grad_out[layer, c] = edge_tile(lambda s: f_ref[c, first + layer, :, s], width)
        grad_out[layer, 3] = edge_tile(lambda s: inv_ref[first + layer, :, s], width)
        grad_out[layer, 4] = edge_tile(lambda s: grad_ref[layer, :, s], width)
    mask_out[...] = edge_tile(lambda s: mask_ref[:, s], width)


def own_edges(arrays):
    cells_z, layers = arrays[0].shape[1], arrays[4].shape[0]
    return pl.pallas_call(
        edges_kernel,
        in_specs=[VMEM] * 6,
        out_specs=[VMEM] * 3,
        out_shape=[fast(cells_z, 6, ROWS, LANES), fast(layers, 5, ROWS, LANES), fast(ROWS, LANES)],
        compiler_params=params(),
    )(*arrays)


def face_tiles(zfaces, xfaces):
    width = xfaces[0].shape[1]
    z_side, x_side = Side("gz"), Side("gx")
    tiles = []
    for c in range(3):
        tiles.append((lambda s, c=c: z_side.lower([f[c, :, s] for f in zfaces]), width))
    for c in range(2):
        tiles.append((lambda s, c=c: z_side.upper([f[c, :, s] for f in zfaces]), width))
    for pick in (x_side.lower, x_side.upper):
        for t in range(0, xfaces[0].shape[0], ROWS):
            tiles.append((lambda s, p=pick, t=t: p([f[t : t + ROWS, s] for f in xfaces]), width))
    return tiles


def face_count(xface):
    return 5 + 2 * (xface.shape[0] // ROWS)


def y_faces_kernel(counts, *refs):
    own_low, own_high = refs[:2]
    zfaces, xfaces = refs[2 : 2 + counts[0]], refs[2 + counts[0] : 2 + sum(counts)]
    sends, (low_ref, high_ref) = refs[2 + sum(counts) : -2], refs[-2:]
    own = own_low.shape[0]
    pack_strips(face_tiles(zfaces, xfaces), low_ref, high_ref, 0)
    side = Side("gy")
    for ref, value in zip(sends, side.sends(own_low[...], own_high[...])):
        ref[0:own] = value
    for ref, value in zip(sends, side.sends(low_ref[...], high_ref[...])):
        ref[own:] = value


def y_faces(own_low, own_high, zfaces, xfaces):
    extra = math.ceil(face_count(xfaces[0]) / SLOTS)
    packed = fast(own_low.shape[0] + extra, ROWS, LANES)
    return pl.pallas_call(
        functools.partial(y_faces_kernel, (len(zfaces), len(xfaces))),
        in_specs=[VMEM] * (2 + len(zfaces) + len(xfaces)),
        out_specs=[VMEM] * rounds("gy"),
        out_shape=[packed] * rounds("gy"),
        scratch_shapes=[pltpu.VMEM((extra, ROWS, LANES), jnp.float32)] * 2,
        compiler_params=params(),
    )(own_low, own_high, *zfaces, *xfaces)


OWN, CIRCLE, EDGE = range(3)


def faces_wide(mode, width):
    return {OWN: width, CIRCLE: width + LANES, EDGE: LANES}[mode]


class Fields:
    def __init__(self, mode, layers, fields, zfaces, xfaces, yfaces, scratch):
        self.mode = mode
        self.fields = fields
        if mode == EDGE:
            self.cells_z, self.width = fields.shape[0], xfaces[0].shape[1]
        else:
            self.cells_z, self.width = fields[0].shape[1], fields[0].shape[3]
        self.wide = faces_wide(mode, self.width)
        self.lane = lax.broadcasted_iota(jnp.int32, (ROWS, LANES), 1)
        self.row = lax.broadcasted_iota(jnp.int32, (ROWS, self.wide), 0)
        self.per_group = 6 * ROWS // SLOTS
        self.groups = self.cells_z // ROWS
        self.grad_base = self.per_group * self.groups
        halo_base = self.grad_base + self.per_group * (layers // ROWS)
        self.left_wide, self.right_wide = left_wide, right_wide = scratch[:2]
        if mode != OWN:
            self.ybuf = scratch[2]
            y_side = Side("gy")
            for t in range(yfaces[0].shape[0]):
                lower = y_side.lower([f[t] for f in yfaces])
                upper = y_side.upper([f[t] for f in yfaces])
                if mode == EDGE:
                    even = self.lane // STRIP % 2 == 0
                    lower, upper = (
                        jnp.where(even, upper, pltpu.roll(lower, STRIP, 1)),
                        jnp.where(even, pltpu.roll(upper, LANES - STRIP, 1), lower),
                    )
                self.ybuf[0, t] = lower
                self.ybuf[1, t] = upper

        def face(load, slot):
            if mode == EDGE:
                own = edge_tile(load, self.width)
                return self.edge(own, halo_base + slot // SLOTS, slot % SLOTS)
            return self.wider(load, halo_base + slot // SLOTS, slot % SLOTS)

        full = [face(load, slot) for slot, (load, _) in enumerate(face_tiles(zfaces, xfaces))]
        self.below, self.above = full[:3], full[3:5]
        per_face = xfaces[0].shape[0] // ROWS
        for t in range(per_face):
            left_wide[t * ROWS : (t + 1) * ROWS, :] = full[5 + t]
            right_wide[t * ROWS : (t + 1) * ROWS, :] = full[5 + per_face + t]
        cells_z = self.cells_z
        left_wide[cells_z : 2 * cells_z, :] += HALF * self.y_up(left_wide[2 * cells_z : 3 * cells_z, :])

    def wider(self, load, tile, k):
        if self.mode == OWN:
            return load(slice(0, self.width))

        def moved(v, to):
            shift = (to - STRIP * k) % LANES
            return pltpu.roll(v, shift, 1) if shift else v

        lower, upper = self.ybuf[0, tile], self.ybuf[1, tile]
        halo = jnp.where(self.lane < STRIP, moved(upper, 0), moved(lower, LANES - STRIP))
        return jnp.concatenate([load(slice(0, self.width)), halo], axis=1)

    def edge(self, own, tile, k):
        shift = (LANES - STRIP - 2 * STRIP * (k // 2)) % LANES
        both = pltpu.roll(self.ybuf[k % 2, tile], shift, 1)
        inside = jnp.logical_and(self.lane >= STRIP, self.lane < LANES - STRIP)
        return jnp.where(inside, own, both)

    def y_up(self, v):
        return pltpu.roll(v, self.wide - 1, 1)

    def y_down(self, v):
        return pltpu.roll(v, 1, 1)

    def x_up(self, v, line):
        return jnp.where(self.row == ROWS - 1, line, pltpu.roll(v, ROWS - 1, 0))

    def x_down(self, v, line):
        return jnp.where(self.row == 0, line, pltpu.roll(v, 1, 0))

    def line(self, ref, at):
        return jnp.broadcast_to(ref[pl.ds(at, 1), :], (ROWS, self.wide))

    def field(self, which, c, a, b):
        slot = 6 * b + 3 * which + c
        tile = self.per_group * a + slot // SLOTS
        if self.mode == EDGE:
            return self.edge(self.fields[ROWS * a + b, 3 * which + c], tile, slot % SLOTS)
        ref = self.fields[which]
        return self.wider(lambda s: ref[c, ROWS * a + b, :, s], tile, slot % SLOTS)

    def hx(self, a, b, ey, ez, ey_next):
        return self.field(1, 0, a, b) - HALF * (self.y_up(ez) - ez - ey_next + ey)

    def hy(self, a, b, ex, ez, ex_next):
        up = self.x_up(ez, self.line(self.right_wide, self.cells_z + ROWS * a + b))
        return self.field(1, 1, a, b) - HALF * (ex_next - ex - up + ez)

    def hz(self, a, b, ex, ey):
        up = self.x_up(ey, self.line(self.right_wide, ROWS * a + b))
        return self.field(1, 2, a, b) - HALF * (up - ey - self.y_up(ex) + ex)

    def start(self, a):
        ex, ey = self.field(0, 0, a, 0), self.field(0, 1, a, 0)
        below = self.below
        at_bottom = (
            below[0] - HALF * self.y_up(below[2]) + HALF * ey,
            below[1] - HALF * ex + HALF * self.x_up(below[2], self.line(self.right_wide, 2 * self.cells_z)),
        )
        before, b = jnp.maximum(a - 1, 0), ROWS - 1
        ex_before, ey_before, ez_before = (self.field(0, c, before, b) for c in range(3))
        inside = (
            self.hx(before, b, ey_before, ez_before, ey),
            self.hy(before, b, ex_before, ez_before, ex),
        )
        bottom = a == 0
        return (ex, ey) + tuple(jnp.where(bottom, one, two) for one, two in zip(at_bottom, inside))

    def group(self, a, carry, emit):
        ex, ey, hx_z, hy_z = carry
        for b in range(ROWS):
            z = ROWS * a + b
            ez = self.field(0, 2, a, b)
            if b < ROWS - 1:
                ex_next, ey_next = (self.field(0, c, a, b + 1) for c in range(2))
            else:
                end = a == self.groups - 1
                after = jnp.minimum(a + 1, self.groups - 1)
                ex_next, ey_next = (
                    jnp.where(end, self.above[c], self.field(0, c, after, 0)) for c in range(2)
                )
            hx = self.hx(a, b, ey, ez, ey_next)
            hy = self.hy(a, b, ex, ez, ex_next)
            hz = self.hz(a, b, ex, ey)
            hy_x = self.x_down(hy, self.line(self.left_wide, z) + HALF * ez)
            hz_x = self.x_down(hz, self.line(self.left_wide, self.cells_z + z) - HALF * ey)
            curl = (
                (hz - self.y_down(hz)) - (hy - hy_z),
                (hx - hx_z) - (hz - hz_x),
                (hy - hy_x) - (hx - self.y_down(hx)),
            )
            emit(a, b, (ex, ey, ez), (hx, hy, hz), curl)
            ex, ey, hx_z, hy_z = ex_next, ey_next, hx, hy
        return ex, ey, hx_z, hy_z

    def gradient(self, layers, arrays, store):
        first = first_layer(self.cells_z, layers)
        first_group = first // ROWS
        if self.mode == EDGE:
            grad_edges, mask_ref = arrays
            mask = self.edge(mask_ref[...], self.grad_base, 5)
        else:
            f_ref, inv_ref, grad_ref, mask_ref = arrays
            mask = mask_ref[...]

        def emit(a, b, efield, hfield, curl):
            z = ROWS * a + b
            layer = z - first
            if self.mode == EDGE:
                tile = self.grad_base + self.per_group * (a - first_group)
                slots = [6 * b + n for n in range(5)]
                values = [
                    self.edge(grad_edges[layer, n], tile + slot // SLOTS, slot % SLOTS)
                    for n, slot in enumerate(slots)
                ]
            else:
                values = [f_ref[c, z] for c in range(3)] + [inv_ref[z], grad_ref[layer]]
            total = None
            for c in range(3):
                term = values[c] * (efield[c] + values[3] * curl[c])
                total = term if total is None else total + term
            store(layer, values[4] + mask * total)

        def body(i, carry):
            return self.group(first_group + i, carry, emit)

        lax.fori_loop(0, layers // ROWS, body, self.start(first_group))


def fields_scratch(mode, xface, yface, width):
    rows, wide = xface.shape[0], faces_wide(mode, width)
    out = [pltpu.VMEM((rows, wide), jnp.float32)] * 2
    if mode != OWN:
        out.append(pltpu.VMEM((2,) + yface.shape, jnp.float32))
    return out


def own_gradient_kernel(counts, *refs):
    e_ref, h_ref, f_ref, inv_ref, grad_ref, mask_ref = refs[:6]
    zfaces, xfaces = refs[6 : 6 + counts[0]], refs[6 + counts[0] : 6 + sum(counts)]
    grad_out, scratch = refs[6 + sum(counts)], refs[7 + sum(counts) :]
    layers = grad_ref.shape[0]
    fields = Fields(OWN, layers, (e_ref, h_ref), zfaces, xfaces, None, scratch)

    def store(layer, value):
        grad_out[layer] = value

    fields.gradient(layers, (f_ref, inv_ref, grad_ref, mask_ref), store)


def own_gradient(arrays, zfaces, xfaces):
    grad_sum = arrays[4]
    return pl.pallas_call(
        functools.partial(own_gradient_kernel, (len(zfaces), len(xfaces))),
        in_specs=[VMEM] * (6 + len(zfaces) + len(xfaces)),
        out_specs=VMEM,
        out_shape=fast(*grad_sum.shape),
        scratch_shapes=fields_scratch(OWN, xfaces[0], None, grad_sum.shape[2]),
        compiler_params=params(),
    )(*arrays, *zfaces, *xfaces)


def edge_gradient_kernel(counts, per_device, *refs):
    own_ref, eh_ref, grad_ref, mask_ref = refs[:4]
    ends = np.cumsum((4,) + counts)
    zfaces, xfaces, yfaces = (refs[i:j] for i, j in zip(ends[:-1], ends[1:]))
    sends, scratch, edge_ref = refs[ends[-1] : -4], refs[-4:-1], refs[-1]
    layers, _, width = own_ref.shape
    lane = lax.broadcasted_iota(jnp.int32, (ROWS, LANES), 1)
    me = lax.axis_index("gx")
    fields = Fields(EDGE, layers, eh_ref, zfaces, xfaces, yfaces, scratch)

    def store(layer, value):
        edge_ref[layer] = value

    fields.gradient(layers, (grad_ref, mask_ref), store)

    for k, send_ref in enumerate(sends[::-1]):
        chunk = lax.bitwise_xor(me, k)
        packed = jnp.zeros((ROWS, LANES), jnp.float32)
        for i in range(per_device):
            layer = chunk * per_device + i
            edge = edge_ref[layer]
            at = i * width
            head, tail = own_ref[layer, :, 0:LANES], own_ref[layer, :, width - LANES :]
            send_ref[:, at : at + LANES] = jnp.where(lane == 0, pltpu.roll(edge, LANES - STRIP, 1), head)
            send_ref[:, at + LANES : at + width - LANES] = own_ref[layer, :, LANES : width - LANES]
            send_ref[:, at + width - LANES : at + width] = jnp.where(
                lane == LANES - 1, pltpu.roll(edge, STRIP, 1), tail
            )
            side = pltpu.roll(edge, (2 * STRIP * i + STRIP) % LANES, 1)
            packed = jnp.where(lane // (2 * STRIP) == i, side, packed)
        send_ref[:, per_device * width :] = packed


def edge_gradient(own, edges, zfaces, xfaces, yfaces):
    layers, _, width = own.shape
    count = lax.axis_size("gx")
    per_device = layers // count
    faces = (*zfaces, *xfaces, *yfaces)
    shares = pl.pallas_call(
        functools.partial(edge_gradient_kernel, (len(zfaces), len(xfaces), len(yfaces)), per_device),
        in_specs=[VMEM] * (4 + len(faces)),
        out_specs=[VMEM] * count,
        out_shape=[fast(ROWS, per_device * width + LANES)] * count,
        scratch_shapes=fields_scratch(EDGE, xfaces[0], yfaces[0], width)
        + [pltpu.VMEM((layers, ROWS, LANES), jnp.float32)],
        compiler_params=params(),
    )(own, *edges, *faces)
    return shares[::-1]


def step_kernel(counts, layers, *refs):
    e_ref, h_ref, inv_ref = refs[:3]
    ends = np.cumsum((3,) + counts)
    zfaces, xfaces, yfaces, shares = (refs[i:j] for i, j in zip(ends[:-1], ends[1:]))
    shares = shares[::-1]
    (e_out, h_out, grad_out), scratch, carry_ref = refs[ends[-1] : -4], refs[-4:-1], refs[-1]
    width = e_ref.shape[3]
    fields = Fields(CIRCLE, layers, (e_ref, h_ref), zfaces, xfaces, yfaces, scratch)
    a = pl.program_id(0)

    def emit(a, b, efield, hfield, curl):
        half_inv = inv_ref[ROWS * a + b]
        for c in range(3):
            e_out[c, b] = efield[c][:, :width] + half_inv * curl[c][:, :width]
            h_out[c, b] = hfield[c][:, :width]

    @pl.when(a == 0)
    def _():
        for i, v in enumerate(fields.start(0)):
            carry_ref[i] = v
        per_device = layers // len(shares)
        me = lax.axis_index("gx")
        for k, share in enumerate(shares):
            chunk = lax.bitwise_xor(me, k)
            for i in range(per_device):
                grad_out[chunk * per_device + i] = share[:, i * width : (i + 1) * width]

    carry = tuple(carry_ref[i] for i in range(4))
    for i, v in enumerate(fields.group(a, carry, emit)):
        carry_ref[i] = v


def step(efield, hfield, inv, zfaces, xfaces, yfaces, shares, layers):
    _, cells_z, _, width = efield.shape
    block = pl.BlockSpec((3, ROWS, ROWS, width), lambda a: (0, a, 0, 0))
    groups = (zfaces, xfaces, yfaces, shares[::-1])
    counts = tuple(len(group) for group in groups)
    return pl.pallas_call(
        functools.partial(step_kernel, counts, layers),
        grid=(cells_z // ROWS,),
        in_specs=[VMEM] * (3 + sum(counts)),
        out_specs=[block, block, VMEM],
        out_shape=[f32(*efield.shape)] * 2 + [f32(layers, ROWS, width)],
        scratch_shapes=fields_scratch(CIRCLE, xfaces[0], yfaces[0], width)
        + [pltpu.VMEM((4, ROWS, width + LANES), jnp.float32)],
        compiler_params=params(),
    )(efield, hfield, inv, *(one for group in groups for one in group))


def cone_matrix(rows):
    span = np.arange(-RADIUS, RADIUS + 1, dtype=np.float64)
    cone = np.maximum(RADIUS - np.sqrt(span[:, None] ** 2 + span[None, :] ** 2), 0.0)
    weight = cone / cone.sum()
    x = np.arange(rows)
    out = np.zeros((RADIUS + 1, rows, rows))
    for b in range(RADIUS + 1):
        for apart in (x[:, None] - x[None, :], 2 * rows - 1 - x[:, None] - x[None, :]):
            near = np.abs(apart) <= RADIUS
            out[b] += np.where(near, weight[np.clip(apart, -RADIUS, RADIUS) + RADIUS, RADIUS + b], 0.0)
    out = out.reshape((RADIUS + 1) * rows, rows).astype(np.float32)
    high = out.astype(jnp.bfloat16)
    low = (out - high.astype(np.float32)).astype(jnp.bfloat16)
    return np.concatenate([high, low, high], axis=1)


def flip_rows(v):
    row = lax.broadcasted_iota(jnp.int32, v.shape, 0)
    v = pltpu.roll(v, 4, 0)
    v = jnp.where(row % 4 < 2, pltpu.roll(v, ROWS - 2, 0), pltpu.roll(v, 2, 0))
    return jnp.where(row % 2 < 1, pltpu.roll(v, ROWS - 1, 0), pltpu.roll(v, 1, 0))


def filter_kernel(count, per_device, width, *refs):
    taps_ref = refs[0]
    got = refs[count:0:-1]
    outs = refs[1 + count : 1 + 2 * count]
    slabs, parts, done = refs[1 + 2 * count :]
    me = lax.axis_index("gx")
    wide = width + LANES
    half = count // 2
    rows = half * ROWS
    lane = lax.broadcasted_iota(jnp.int32, (ROWS, LANES), 1)
    for k in range(count):
        slabs[lax.bitwise_xor(me, k)] = got[k][...]

    def layer_of(slab, i):
        edge = slabs[slab, :, per_device * width :]
        at = 2 * STRIP * i
        upper = pltpu.roll(edge, (LANES - at) % LANES, 1) if at else edge
        lower = pltpu.roll(edge, (LANES - 2 * STRIP - at) % LANES, 1)
        side = jnp.where(lane < STRIP, upper, lower)
        return jnp.concatenate([slabs[slab, :, i * width : (i + 1) * width], side], axis=1)

    for i in range(per_device):
        halves = [layer_of(s, i) + flip_rows(layer_of(count - 1 - s, i)) for s in range(half)]
        symmetric = jnp.concatenate(halves, axis=0)
        high = symmetric.astype(jnp.bfloat16)
        low = (symmetric - high.astype(jnp.float32)).astype(jnp.bfloat16)
        parts[0:rows, :] = high
        parts[rows : 2 * rows, :] = high
        parts[2 * rows : 3 * rows, :] = low
        mixed = jnp.dot(taps_ref[...], parts[...], preferred_element_type=jnp.float32)
        total = mixed[0:rows]
        for b in range(1, RADIUS + 1):
            part = mixed[b * rows : (b + 1) * rows]
            total = total + (pltpu.roll(part, b, 1) + pltpu.roll(part, wide - b, 1))
        for s in range(half):
            own = total[s * ROWS : (s + 1) * ROWS, :width]
            done[s, i] = own
            done[count - 1 - s, i] = flip_rows(own)
    for k in range(count):
        outs[k][...] = done[lax.bitwise_xor(me, k)]


def cone_filter(got, per_device, width):
    count = len(got)
    rows = count // 2 * ROWS
    taps = jnp.asarray(cone_matrix(rows))
    return pl.pallas_call(
        functools.partial(filter_kernel, count, per_device, width),
        in_specs=[VMEM] * (1 + count),
        out_specs=[VMEM] * count,
        out_shape=[fast(per_device, ROWS, width)] * count,
        scratch_shapes=[
            pltpu.VMEM((count, ROWS, per_device * width + LANES), jnp.float32),
            pltpu.VMEM((3 * rows, width + LANES), jnp.bfloat16),
            pltpu.VMEM((count, per_device, ROWS, width), jnp.float32),
        ],
        compiler_params=params(),
    )(taps, *got[::-1])


def place_kernel(count, per_device, *refs):
    out, sems = refs[count], refs[count + 1]
    parts = refs[count - 1 :: -1]
    copies = []
    for k in range(count):
        at = lax.bitwise_xor(lax.axis_index("gx"), k) * per_device
        copies.append(pltpu.make_async_copy(parts[k], out.at[pl.ds(at, per_device)], sems.at[k]))
    for copy in copies:
        copy.start()
    for copy in copies:
        copy.wait()


def place_layers(parts):
    count = len(parts)
    per_device, rows, width = parts[0].shape
    return pl.pallas_call(
        functools.partial(place_kernel, count, per_device),
        in_specs=[ANY] * count,
        out_specs=ANY,
        out_shape=f32(count * per_device, rows, width),
        scratch_shapes=[pltpu.SemaphoreType.DMA((count,))],
        compiler_params=params(),
    )(*parts[::-1])


def spread(parts):
    count = len(parts)
    got = list(parts)
    for k in range(count - 1, 0, -1):
        got[k] = lax.ppermute(parts[k], "gx", [(i, i ^ k) for i in range(count)])
    return got


def on_device(efield, hfield, forward, material, permit, design_mask, grad_sum):
    layers, _, width = grad_sum.shape
    zfaces = exchange(z_faces(efield, hfield), "gz", "gy")
    efield, hfield, material, grad_sum = load(efield, hfield, material, grad_sum)
    xfaces = exchange(x_faces(efield, hfield, zfaces), "gx", "gy")
    forward, own_low, own_high, mask, inv = strips(
        permit, efield, hfield, forward, material, grad_sum, design_mask
    )
    arrays = (efield, hfield, forward, inv, grad_sum, mask)
    edges = own_edges(arrays)
    yfaces = exchange(y_faces(own_low, own_high, zfaces, xfaces), "gy", "gz")
    own = own_gradient(arrays, zfaces, xfaces)
    shares = edge_gradient(own, edges, zfaces, xfaces, yfaces)
    got = spread(shares)
    e_next, h_next, grad_total = step(efield, hfield, inv, zfaces, xfaces, yfaces, shares, layers)
    filtered = spread(cone_filter(got, layers // len(got), width))
    return e_next, h_next, grad_total, place_layers(filtered)


def solution(mesh):
    field = P(None, "gz", "gx", "gy")
    cells = P("gz", "gx", "gy")
    return jax.shard_map(
        on_device,
        mesh=mesh,
        in_specs=(field, field, field, cells, P(), P("gx", "gy"), cells),
        out_specs=(field, field, cells, cells),
        check_vma=False,
    )
```

```python
import functools
import math

import jax
import jax.numpy as jnp
import numpy as np
from jax import lax
from jax.experimental import pallas as pl
from jax.experimental.pallas import tpu as pltpu
from jax.sharding import PartitionSpec as P

RADIUS = 6
BLOCK = 8
HALF = 0.5

ROWS = 8
LANES = 128
STRIP = 8
SLOTS = LANES // STRIP
MIB = 1024 * 1024

VMEM = pl.BlockSpec(memory_space=pltpu.VMEM)
SMEM = pl.BlockSpec(memory_space=pltpu.SMEM)
ANY = pl.BlockSpec(memory_space=pl.ANY)


def params(mib=24):
    return pltpu.CompilerParams(vmem_limit_bytes=mib * MIB)


def f32(*shape):
    return jax.ShapeDtypeStruct(shape, jnp.float32)


def fast(*shape):
    return pltpu.VMEM(shape, jnp.float32)


def rounds(axis):
    return 2 if lax.axis_size(axis) > 2 else 1


def exchange(sends, axis, mate):
    count = lax.axis_size(axis)
    beside = lax.axis_size(mate)
    if count == 1:
        return sends
    got = []
    for start, value in enumerate(sends):
        partner = list(range(count))
        for low in range(start, count - 1, 2):
            partner[low], partner[low + 1] = low + 1, low
        axes = sorted((axis, mate))
        steps = (beside, 1) if axes[0] == axis else (1, count)
        pairs = []
        for i in range(count):
            for m in range(beside):
                if partner[i] != i:
                    to = (partner[i], m)
                elif beside % 2 == 0:
                    to = (i, m ^ 1)
                else:
                    continue
                pairs.append((i * steps[0] + m * steps[1], to[0] * steps[0] + to[1] * steps[1]))
        got.append(lax.ppermute(value, tuple(axes), pairs))
    return got


class Side:
    def __init__(self, axis):
        index = lax.axis_index(axis)
        self.rounds = rounds(axis)
        self.odd = index % 2 == 1
        self.bottom = index == 0
        self.top = index == lax.axis_size(axis) - 1

    def sends(self, low, high):
        both = [jnp.where(self.odd, low, high)]
        if self.rounds > 1:
            both.append(jnp.where(self.odd, high, low))
        return both

    def lower(self, got):
        return jnp.where(self.bottom, 0.0, jnp.where(self.odd, got[0], got[-1]))

    def upper(self, got):
        return jnp.where(self.top, 0.0, jnp.where(self.odd, got[-1], got[0]))


def first_layer(cells_z, layers):
    return (cells_z - layers) * (1 - lax.axis_index("gz"))


def z_faces_kernel(*refs):
    e_ref, h_ref = refs[:2]
    sends, (e_low, e_high, h_high, sems) = refs[2:-4], refs[-4:]
    top = e_ref.shape[1] - 1
    planes = [(e_ref.at[c, 0], e_low.at[c]) for c in range(2)]
    planes += [(e_ref.at[c, top], e_high.at[c]) for c in range(3)]
    planes += [(h_ref.at[c, top], h_high.at[c]) for c in range(2)]
    copies = [pltpu.make_async_copy(*plane, sems.at[n]) for n, plane in enumerate(planes)]
    for copy in copies:
        copy.start()
    for copy in copies:
        copy.wait()
    side = Side("gz")
    ex, ey, ez = (e_high[c] for c in range(3))
    low = (e_low[0], e_low[1], jnp.zeros_like(ez))
    high = (h_high[0] + HALF * ez - HALF * ey, h_high[1] + HALF * ex - HALF * ez, ez)
    for c in range(3):
        for ref, value in zip(sends, side.sends(low[c], high[c])):
            ref[c] = value


def z_faces(efield, hfield):
    face = fast(*efield.shape[:1], *efield.shape[2:])
    return pl.pallas_call(
        z_faces_kernel,
        in_specs=[ANY] * 2,
        out_specs=[VMEM] * rounds("gz"),
        out_shape=[face] * rounds("gz"),
        scratch_shapes=[pltpu.VMEM(face.shape, jnp.float32)] * 3 + [pltpu.SemaphoreType.DMA((7,))],
        compiler_params=params(60),
    )(efield, hfield)


def x_faces_kernel(z_rounds, *refs):
    e_ref, h_ref = refs[:2]
    zfaces = refs[2 : 2 + z_rounds]
    sends, (low_ref, rows_ref) = refs[2 + z_rounds : -2], refs[-2:]
    cells_z = e_ref.shape[1]
    last = ROWS - 1
    z_side = Side("gz")
    low_ref[...] = jnp.zeros_like(low_ref)
    for z in range(cells_z):
        low_ref[z : z + 1, :] = e_ref[1, z, 0:1, :]
        low_ref[cells_z + z : cells_z + z + 1, :] = e_ref[2, z, 0:1, :]
        for c in range(3):
            rows_ref[c, z : z + 1, :] = e_ref[c, z, last : last + 1, :]
        for c in range(2):
            rows_ref[3 + c, z : z + 1, :] = h_ref[1 + c, z, last : last + 1, :]
        if z > 0:
            rows_ref[5, z - 1 : z, :] = e_ref[0, z, last : last + 1, :]
    rows_ref[5, cells_z - 1 : cells_z, :] = z_side.upper([f[0, last : last + 1, :] for f in zfaces])
    low_ref[2 * cells_z : 2 * cells_z + 1, :] = z_side.lower([f[2, 0:1, :] for f in zfaces])
    ex = rows_ref[0]
    high = (
        rows_ref[3] - HALF * (rows_ref[5] - ex + rows_ref[2]),
        rows_ref[4] + HALF * rows_ref[1] - HALF * ex,
        ex,
    )
    side = Side("gx")
    for c in range(3):
        here = slice(c * cells_z, (c + 1) * cells_z)
        for ref, value in zip(sends, side.sends(low_ref[here, :], high[c])):
            ref[here, :] = value


def x_faces(efield, hfield, zfaces):
    cells_z, cells_y = efield.shape[1], efield.shape[3]
    face = fast(3 * cells_z, cells_y)
    return pl.pallas_call(
        functools.partial(x_faces_kernel, len(zfaces)),
        in_specs=[VMEM] * (2 + len(zfaces)),
        out_specs=[VMEM] * rounds("gx"),
        out_shape=[face] * rounds("gx"),
        scratch_shapes=[
            pltpu.VMEM(face.shape, jnp.float32),
            pltpu.VMEM((6, cells_z, cells_y), jnp.float32),
        ],
        compiler_params=params(),
    )(efield, hfield, *zfaces)


def lane_group():
    return lax.broadcasted_iota(jnp.int32, (ROWS, LANES), 1) // STRIP


def pack_strips(tiles, low_ref, high_ref, first):
    group = lane_group()
    width = tiles[0][1]
    for start in range(0, len(tiles), SLOTS):
        low = jnp.zeros((ROWS, LANES), jnp.float32)
        high = jnp.zeros((ROWS, LANES), jnp.float32)
        for k, (load, _) in enumerate(tiles[start : start + SLOTS]):
            if load is None:
                continue
            here = group == k
            shift = (STRIP * k) % LANES
            left = load(slice(0, LANES))
            right = load(slice(width - LANES, width))
            low = jnp.where(here, pltpu.roll(left, shift, 1) if shift else left, low)
            shift = (STRIP * k + STRIP) % LANES
            high = jnp.where(here, pltpu.roll(right, shift, 1) if shift else right, high)
        low_ref[first + start // SLOTS] = low
        high_ref[first + start // SLOTS] = high


def load_kernel(e_in, h_in, mat_in, grad_in, e_ref, h_ref, mat_ref, grad_ref, sems):
    parts = [(source.at[c], target.at[c]) for source, target in ((e_in, e_ref), (h_in, h_ref)) for c in range(3)]
    parts += [(mat_in, mat_ref), (grad_in, grad_ref)]
    copies = [pltpu.make_async_copy(*part, sems.at[n]) for n, part in enumerate(parts)]
    for copy in copies:
        copy.start()
    for copy in copies:
        copy.wait()


def load(*arrays):
    return pl.pallas_call(
        load_kernel,
        in_specs=[ANY] * 4,
        out_specs=[VMEM] * 4,
        out_shape=[pltpu.VMEM(one.shape, one.dtype) for one in arrays],
        scratch_shapes=[pltpu.SemaphoreType.DMA((8,))],
        compiler_params=params(56),
    )(*arrays)


def strips_kernel(
    permit_ref, e_ref, h_ref, f_in, mat_ref, grad_ref, mask_ref, f_ref, low_ref, high_ref, wide_ref, inv_ref, sems
):
    cells_z, width = e_ref.shape[1], e_ref.shape[3]
    layers = grad_ref.shape[0]
    blocks = mask_ref.shape[1]
    copies = [pltpu.make_async_copy(f_in.at[c], f_ref.at[c], sems.at[c]) for c in range(3)]
    for copy in copies:
        copy.start()

    inverse = [
        jnp.broadcast_to(HALF * (1.0 / permit_ref[0:1, m : m + 1]), (ROWS, width))
        for m in range(permit_ref.shape[1])
    ]
    for z in range(cells_z):
        inv = inverse[0]
        for m in range(1, len(inverse)):
            inv = jnp.where(mat_ref[z] == m, inverse[m], inv)
        inv_ref[z] = inv
    spread = (
        lax.broadcasted_iota(jnp.int32, (blocks, width), 0)
        == lax.broadcasted_iota(jnp.int32, (blocks, width), 1) // BLOCK
    ).astype(jnp.float32)
    mask = jnp.broadcast_to(mask_ref[...].astype(jnp.float32), (ROWS, blocks))
    wide_ref[...] = jnp.dot(mask, spread, preferred_element_type=jnp.float32)
    first = first_layer(cells_z, layers)
    tiles = []
    for z in range(cells_z):
        for ref in (e_ref, h_ref):
            for c in range(3):
                tiles.append((lambda s, r=ref, c=c, z=z: r[c, z, :, s], width))
    pack_strips(tiles, low_ref, high_ref, 0)

    for copy in copies:
        copy.wait()
    done = len(tiles) // SLOTS
    tiles = []
    for layer in range(layers):
        for c in range(3):
            tiles.append((lambda s, c=c, l=layer: f_ref[c, first + l, :, s], width))
        tiles.append((lambda s, l=layer: inv_ref[first + l, :, s], width))
        tiles.append((lambda s, l=layer: grad_ref[l, :, s], width))
        tiles.append((lambda s: wide_ref[:, s], width) if layer % ROWS == 0 else (None, width))
    pack_strips(tiles, low_ref, high_ref, done)


def strips(permit, efield, hfield, forward, material, grad_sum, mask):
    cells_z, width = efield.shape[1], efield.shape[3]
    count = (cells_z * 6 + grad_sum.shape[0] * 6) // SLOTS
    packed = (count, ROWS, LANES)
    shapes = (forward.shape, packed, packed, (ROWS, width), material.shape)
    return pl.pallas_call(
        strips_kernel,
        in_specs=[VMEM] * 3 + [ANY] + [VMEM] * 3,
        out_specs=[VMEM] * 5,
        out_shape=[fast(*shape) for shape in shapes],
        scratch_shapes=[pltpu.SemaphoreType.DMA((3,))],
        compiler_params=params(40),
    )(permit.reshape(1, -1), efield, hfield, forward, material, grad_sum, mask)


def edge_tile(load, width):
    lane = lax.broadcasted_iota(jnp.int32, (ROWS, LANES), 1)
    head = pltpu.roll(load(slice(0, LANES)), STRIP, 1)
    tail = pltpu.roll(load(slice(width - LANES, width)), LANES - STRIP, 1)
    return jnp.where(lane < LANES // 2, head, tail)


def edges_kernel(e_ref, h_ref, f_ref, inv_ref, grad_ref, mask_ref, eh_out, grad_out, mask_out):
    cells_z, width = e_ref.shape[1], e_ref.shape[3]
    layers = grad_ref.shape[0]
    first = first_layer(cells_z, layers)
    for z in range(cells_z):
        for c in range(3):
            eh_out[z, c] = edge_tile(lambda s: e_ref[c, z, :, s], width)
            eh_out[z, 3 + c] = edge_tile(lambda s: h_ref[c, z, :, s], width)
    for layer in range(layers):
        for c in range(3):
            grad_out[layer, c] = edge_tile(lambda s: f_ref[c, first + layer, :, s], width)
        grad_out[layer, 3] = edge_tile(lambda s: inv_ref[first + layer, :, s], width)
        grad_out[layer, 4] = edge_tile(lambda s: grad_ref[layer, :, s], width)
    mask_out[...] = edge_tile(lambda s: mask_ref[:, s], width)


def own_edges(arrays):
    cells_z, layers = arrays[0].shape[1], arrays[4].shape[0]
    return pl.pallas_call(
        edges_kernel,
        in_specs=[VMEM] * 6,
        out_specs=[VMEM] * 3,
        out_shape=[fast(cells_z, 6, ROWS, LANES), fast(layers, 5, ROWS, LANES), fast(ROWS, LANES)],
        compiler_params=params(),
    )(*arrays)


def face_tiles(zfaces, xfaces):
    width = xfaces[0].shape[1]
    z_side, x_side = Side("gz"), Side("gx")
    tiles = []
    for c in range(3):
        tiles.append((lambda s, c=c: z_side.lower([f[c, :, s] for f in zfaces]), width))
    for c in range(2):
        tiles.append((lambda s, c=c: z_side.upper([f[c, :, s] for f in zfaces]), width))
    for pick in (x_side.lower, x_side.upper):
        for t in range(0, xfaces[0].shape[0], ROWS):
            tiles.append((lambda s, p=pick, t=t: p([f[t : t + ROWS, s] for f in xfaces]), width))
    return tiles


def face_count(xface):
    return 5 + 2 * (xface.shape[0] // ROWS)


def y_faces_kernel(counts, *refs):
    own_low, own_high = refs[:2]
    zfaces, xfaces = refs[2 : 2 + counts[0]], refs[2 + counts[0] : 2 + sum(counts)]
    sends, (low_ref, high_ref) = refs[3 + sum(counts) : -2], refs[-2:]
    own = own_low.shape[0]
    pack_strips(face_tiles(zfaces, xfaces), low_ref, high_ref, 0)
    side = Side("gy")
    for ref, value in zip(sends, side.sends(own_low[...], own_high[...])):
        ref[0:own] = value
    for ref, value in zip(sends, side.sends(low_ref[...], high_ref[...])):
        ref[own:] = value


def y_faces(own_low, own_high, zfaces, xfaces, after):
    extra = math.ceil(face_count(xfaces[0]) / SLOTS)
    packed = fast(own_low.shape[0] + extra, ROWS, LANES)
    return pl.pallas_call(
        functools.partial(y_faces_kernel, (len(zfaces), len(xfaces))),
        in_specs=[VMEM] * (2 + len(zfaces) + len(xfaces)) + [ANY],
        out_specs=[VMEM] * rounds("gy"),
        out_shape=[packed] * rounds("gy"),
        scratch_shapes=[pltpu.VMEM((extra, ROWS, LANES), jnp.float32)] * 2,
        compiler_params=params(),
    )(own_low, own_high, *zfaces, *xfaces, after)


OWN, CIRCLE, EDGE = range(3)


def faces_wide(mode, width):
    return {OWN: width, CIRCLE: width + LANES, EDGE: LANES}[mode]


class Fields:
    def __init__(self, mode, layers, fields, zfaces, xfaces, yfaces, scratch):
        self.mode = mode
        self.fields = fields
        if mode == EDGE:
            self.cells_z, self.width = fields.shape[0], xfaces[0].shape[1]
        else:
            self.cells_z, self.width = fields[0].shape[1], fields[0].shape[3]
        self.wide = faces_wide(mode, self.width)
        self.lane = lax.broadcasted_iota(jnp.int32, (ROWS, LANES), 1)
        self.row = lax.broadcasted_iota(jnp.int32, (ROWS, self.wide), 0)
        self.per_group = 6 * ROWS // SLOTS
        self.groups = self.cells_z // ROWS
        self.grad_base = self.per_group * self.groups
        halo_base = self.grad_base + self.per_group * (layers // ROWS)
        self.left_wide, self.right_wide = left_wide, right_wide = scratch[:2]
        if mode != OWN:
            self.ybuf = scratch[2]
            y_side = Side("gy")
            for t in range(yfaces[0].shape[0]):
                lower = y_side.lower([f[t] for f in yfaces])
                upper = y_side.upper([f[t] for f in yfaces])
                if mode == EDGE:
                    even = self.lane // STRIP % 2 == 0
                    lower, upper = (
                        jnp.where(even, upper, pltpu.roll(lower, STRIP, 1)),
                        jnp.where(even, pltpu.roll(upper, LANES - STRIP, 1), lower),
                    )
                self.ybuf[0, t] = lower
                self.ybuf[1, t] = upper

        def face(load, slot):
            if mode == EDGE:
                own = edge_tile(load, self.width)
                return self.edge(own, halo_base + slot // SLOTS, slot % SLOTS)
            return self.wider(load, halo_base + slot // SLOTS, slot % SLOTS)

        full = [face(load, slot) for slot, (load, _) in enumerate(face_tiles(zfaces, xfaces))]
        self.below, self.above = full[:3], full[3:5]
        per_face = xfaces[0].shape[0] // ROWS
        for t in range(per_face):
            left_wide[t * ROWS : (t + 1) * ROWS, :] = full[5 + t]
            right_wide[t * ROWS : (t + 1) * ROWS, :] = full[5 + per_face + t]
        cells_z = self.cells_z
        left_wide[cells_z : 2 * cells_z, :] += HALF * self.y_up(left_wide[2 * cells_z : 3 * cells_z, :])

    def wider(self, load, tile, k):
        if self.mode == OWN:
            return load(slice(0, self.width))

        def moved(v, to):
            shift = (to - STRIP * k) % LANES
            return pltpu.roll(v, shift, 1) if shift else v

        lower, upper = self.ybuf[0, tile], self.ybuf[1, tile]
        halo = jnp.where(self.lane < STRIP, moved(upper, 0), moved(lower, LANES - STRIP))
        return jnp.concatenate([load(slice(0, self.width)), halo], axis=1)

    def edge(self, own, tile, k):
        shift = (LANES - STRIP - 2 * STRIP * (k // 2)) % LANES
        both = pltpu.roll(self.ybuf[k % 2, tile], shift, 1)
        inside = jnp.logical_and(self.lane >= STRIP, self.lane < LANES - STRIP)
        return jnp.where(inside, own, both)

    def y_up(self, v):
        return pltpu.roll(v, self.wide - 1, 1)

    def y_down(self, v):
        return pltpu.roll(v, 1, 1)

    def x_up(self, v, line):
        return jnp.where(self.row == ROWS - 1, line, pltpu.roll(v, ROWS - 1, 0))

    def x_down(self, v, line):
        return jnp.where(self.row == 0, line, pltpu.roll(v, 1, 0))

    def line(self, ref, at):
        return jnp.broadcast_to(ref[pl.ds(at, 1), :], (ROWS, self.wide))

    def field(self, which, c, a, b):
        slot = 6 * b + 3 * which + c
        tile = self.per_group * a + slot // SLOTS
        if self.mode == EDGE:
            return self.edge(self.fields[ROWS * a + b, 3 * which + c], tile, slot % SLOTS)
        ref = self.fields[which]
        return self.wider(lambda s: ref[c, ROWS * a + b, :, s], tile, slot % SLOTS)

    def hx(self, a, b, ey, ez, ey_next):
        return self.field(1, 0, a, b) - HALF * (self.y_up(ez) - ez - ey_next + ey)

    def hy(self, a, b, ex, ez, ex_next):
        up = self.x_up(ez, self.line(self.right_wide, self.cells_z + ROWS * a + b))
        return self.field(1, 1, a, b) - HALF * (ex_next - ex - up + ez)

    def hz(self, a, b, ex, ey):
        up = self.x_up(ey, self.line(self.right_wide, ROWS * a + b))
        return self.field(1, 2, a, b) - HALF * (up - ey - self.y_up(ex) + ex)

    def start(self, a):
        ex, ey = self.field(0, 0, a, 0), self.field(0, 1, a, 0)
        below = self.below
        at_bottom = (
            below[0] - HALF * self.y_up(below[2]) + HALF * ey,
            below[1] - HALF * ex + HALF * self.x_up(below[2], self.line(self.right_wide, 2 * self.cells_z)),
        )
        before, b = jnp.maximum(a - 1, 0), ROWS - 1
        ex_before, ey_before, ez_before = (self.field(0, c, before, b) for c in range(3))
        inside = (
            self.hx(before, b, ey_before, ez_before, ey),
            self.hy(before, b, ex_before, ez_before, ex),
        )
        bottom = a == 0
        return (ex, ey) + tuple(jnp.where(bottom, one, two) for one, two in zip(at_bottom, inside))

    def group(self, a, carry, emit):
        ex, ey, hx_z, hy_z = carry
        for b in range(ROWS):
            z = ROWS * a + b
            ez = self.field(0, 2, a, b)
            if b < ROWS - 1:
                ex_next, ey_next = (self.field(0, c, a, b + 1) for c in range(2))
            else:
                end = a == self.groups - 1
                after = jnp.minimum(a + 1, self.groups - 1)
                ex_next, ey_next = (
                    jnp.where(end, self.above[c], self.field(0, c, after, 0)) for c in range(2)
                )
            hx = self.hx(a, b, ey, ez, ey_next)
            hy = self.hy(a, b, ex, ez, ex_next)
            hz = self.hz(a, b, ex, ey)
            hy_x = self.x_down(hy, self.line(self.left_wide, z) + HALF * ez)
            hz_x = self.x_down(hz, self.line(self.left_wide, self.cells_z + z) - HALF * ey)
            curl = (
                (hz - self.y_down(hz)) - (hy - hy_z),
                (hx - hx_z) - (hz - hz_x),
                (hy - hy_x) - (hx - self.y_down(hx)),
            )
            emit(a, b, (ex, ey, ez), (hx, hy, hz), curl)
            ex, ey, hx_z, hy_z = ex_next, ey_next, hx, hy
        return ex, ey, hx_z, hy_z

    def gradient(self, layers, arrays, store):
        first = first_layer(self.cells_z, layers)
        first_group = first // ROWS
        if self.mode == EDGE:
            grad_edges, mask_ref = arrays
            mask = self.edge(mask_ref[...], self.grad_base, 5)
        else:
            f_ref, inv_ref, grad_ref, mask_ref = arrays
            mask = mask_ref[...]

        def emit(a, b, efield, hfield, curl):
            z = ROWS * a + b
            layer = z - first
            if self.mode == EDGE:
                tile = self.grad_base + self.per_group * (a - first_group)
                slots = [6 * b + n for n in range(5)]
                values = [
                    self.edge(grad_edges[layer, n], tile + slot // SLOTS, slot % SLOTS)
                    for n, slot in enumerate(slots)
                ]
            else:
                values = [f_ref[c, z] for c in range(3)] + [inv_ref[z], grad_ref[layer]]
            total = None
            for c in range(3):
                term = values[c] * (efield[c] + values[3] * curl[c])
                total = term if total is None else total + term
            store(layer, values[4] + mask * total)

        def body(i, carry):
            return self.group(first_group + i, carry, emit)

        lax.fori_loop(0, layers // ROWS, body, self.start(first_group))


def fields_scratch(mode, xface, yface, width):
    rows, wide = xface.shape[0], faces_wide(mode, width)
    out = [pltpu.VMEM((rows, wide), jnp.float32)] * 2
    if mode != OWN:
        out.append(pltpu.VMEM((2,) + yface.shape, jnp.float32))
    return out


def own_gradient_kernel(counts, per_device, *refs):
    e_ref, h_ref, f_ref, inv_ref, grad_ref, mask_ref = refs[:6]
    zfaces, xfaces = refs[6 : 6 + counts[0]], refs[6 + counts[0] : 6 + sum(counts)]
    shares, (own_ref, *scratch) = refs[6 + sum(counts) : -3][::-1], refs[-3:]
    layers, _, width = grad_ref.shape
    fields = Fields(OWN, layers, (e_ref, h_ref), zfaces, xfaces, None, scratch)

    def store(layer, value):
        own_ref[layer] = value

    fields.gradient(layers, (f_ref, inv_ref, grad_ref, mask_ref), store)

    me = lax.axis_index("gx")
    for k, share in enumerate(shares):
        chunk = lax.bitwise_xor(me, k)
        for i in range(per_device):
            share[:, i * width : (i + 1) * width] = own_ref[chunk * per_device + i]


def own_gradient(arrays, zfaces, xfaces):
    layers, _, width = arrays[4].shape
    count = lax.axis_size("gx")
    per_device = layers // count
    *shares, own = pl.pallas_call(
        functools.partial(own_gradient_kernel, (len(zfaces), len(xfaces)), per_device),
        in_specs=[VMEM] * (6 + len(zfaces) + len(xfaces)),
        out_specs=[VMEM] * (count + 1),
        out_shape=[fast(ROWS, per_device * width)] * count + [fast(layers, ROWS, width)],
        scratch_shapes=fields_scratch(OWN, xfaces[0], None, width),
        compiler_params=params(),
    )(*arrays, *zfaces, *xfaces)
    return shares[::-1], own


PART = 2 * STRIP


def edge_gradient_kernel(counts, *refs):
    own_ref, eh_ref, grad_ref, mask_ref = refs[:4]
    ends = np.cumsum((4,) + counts)
    zfaces, xfaces, yfaces = (refs[i:j] for i, j in zip(ends[:-1], ends[1:]))
    (message, edge_ref), scratch = refs[ends[-1] : -3], refs[-3:]
    layers, _, width = own_ref.shape
    lane = lax.broadcasted_iota(jnp.int32, (ROWS, LANES), 1)
    first, last = STRIP, LANES - STRIP - 1
    fields = Fields(EDGE, layers, eh_ref, zfaces, xfaces, yfaces, scratch)

    def store(layer, value):
        edge_ref[layer] = value

    fields.gradient(layers, (grad_ref, mask_ref), store)

    per_tile = LANES // PART
    for start in range(0, layers, per_tile):
        packed = jnp.zeros((ROWS, LANES), jnp.float32)
        for j in range(min(per_tile, layers - start)):
            layer = start + j
            edge = edge_ref[layer]
            own = edge_tile(lambda s: own_ref[layer, :, s], width)
            more = jnp.where(jnp.logical_or(lane == first, lane == last), edge - own, edge)
            left = pltpu.roll(more, (PART * j - 1) % LANES, 1)
            right = pltpu.roll(more, (PART * j + STRIP - last) % LANES, 1)
            packed = jnp.where(lane // STRIP == 2 * j, left, packed)
            packed = jnp.where(lane // STRIP == 2 * j + 1, right, packed)
        message[:, start // per_tile * LANES : (start // per_tile + 1) * LANES] = packed


def edge_gradient(own, edges, zfaces, xfaces, yfaces):
    layers, _, width = own.shape
    faces = (*zfaces, *xfaces, *yfaces)
    tiles = math.ceil(layers * PART / LANES)
    return pl.pallas_call(
        functools.partial(edge_gradient_kernel, (len(zfaces), len(xfaces), len(yfaces))),
        in_specs=[VMEM] * (4 + len(faces)),
        out_specs=[VMEM] * 2,
        out_shape=[fast(ROWS, tiles * LANES), fast(layers, ROWS, LANES)],
        scratch_shapes=fields_scratch(EDGE, xfaces[0], yfaces[0], width),
        compiler_params=params(),
    )(own, *edges, *faces)


def step_kernel(counts, *refs):
    e_ref, h_ref, inv_ref, own_ref, edge_ref = refs[:5]
    ends = np.cumsum((5,) + counts)
    zfaces, xfaces, yfaces = (refs[i:j] for i, j in zip(ends[:-1], ends[1:]))
    e_out, h_out, grad_out = refs[ends[-1] + 1 : ends[-1] + 4]
    left_wide, right_wide, ybuf, e_new, h_new, grad_new, sems = refs[ends[-1] + 4 :]
    layers, _, width = own_ref.shape
    lane = lax.broadcasted_iota(jnp.int32, (ROWS, LANES), 1)

    for layer in range(layers):
        edge = edge_ref[layer]
        head, tail = own_ref[layer, :, 0:LANES], own_ref[layer, :, width - LANES :]
        grad_new[layer] = own_ref[layer]
        grad_new[layer, :, 0:LANES] = jnp.where(lane == 0, pltpu.roll(edge, LANES - STRIP, 1), head)
        grad_new[layer, :, width - LANES :] = jnp.where(lane == LANES - 1, pltpu.roll(edge, STRIP, 1), tail)
    grad_copy = pltpu.make_async_copy(grad_new, grad_out, sems.at[0, 0])
    grad_copy.start()

    fields = Fields(CIRCLE, layers, (e_ref, h_ref), zfaces, xfaces, yfaces, (left_wide, right_wide, ybuf))

    def emit(a, b, efield, hfield, curl):
        z = ROWS * a + b
        half_inv = inv_ref[z]
        for c in range(3):
            e_new[c, z] = efield[c][:, :width] + half_inv * curl[c][:, :width]
            h_new[c, z] = hfield[c][:, :width]

    def copies(a):
        here = pl.ds(a * ROWS, ROWS)
        return [
            pltpu.make_async_copy(new.at[c, here], out.at[c, here], sems.at[1 + a, 3 * n + c])
            for n, (new, out) in enumerate(((e_new, e_out), (h_new, h_out)))
            for c in range(3)
        ]

    def body(a, carry):
        carry = fields.group(a, carry, emit)
        for copy in copies(a):
            copy.start()
        return carry

    lax.fori_loop(0, fields.groups, body, fields.start(0))
    for a in range(fields.groups):
        for copy in copies(a):
            copy.wait()
    grad_copy.wait()


def step(efield, hfield, inv, own, edge, zfaces, xfaces, yfaces, after):
    _, cells_z, _, width = efield.shape
    groups = (zfaces, xfaces, yfaces)
    counts = tuple(len(group) for group in groups)
    shapes = (efield.shape, hfield.shape, own.shape)
    return pl.pallas_call(
        functools.partial(step_kernel, counts),
        in_specs=[VMEM] * (5 + sum(counts)) + [ANY],
        out_specs=[ANY] * 3,
        out_shape=[f32(*shape) for shape in shapes],
        scratch_shapes=fields_scratch(CIRCLE, xfaces[0], yfaces[0], width)
        + [pltpu.VMEM(shape, jnp.float32) for shape in shapes]
        + [pltpu.SemaphoreType.DMA((1 + cells_z // ROWS, 6))],
        compiler_params=params(),
    )(efield, hfield, inv, own, edge, *(one for group in groups for one in group), after)


def cone_matrix(rows):
    span = np.arange(-RADIUS, RADIUS + 1, dtype=np.float64)
    cone = np.maximum(RADIUS - np.sqrt(span[:, None] ** 2 + span[None, :] ** 2), 0.0)
    weight = cone / cone.sum()
    x = np.arange(rows)
    out = np.zeros((RADIUS + 1, rows, rows))
    for b in range(RADIUS + 1):
        for apart in (x[:, None] - x[None, :], 2 * rows - 1 - x[:, None] - x[None, :]):
            near = np.abs(apart) <= RADIUS
            out[b] += np.where(near, weight[np.clip(apart, -RADIUS, RADIUS) + RADIUS, RADIUS + b], 0.0)
    out = out.reshape((RADIUS + 1) * rows, rows).astype(np.float32)
    high = out.astype(jnp.bfloat16)
    low = (out - high.astype(np.float32)).astype(jnp.bfloat16)
    return np.concatenate([high, low, high], axis=1)


def flip_rows(v):
    row = lax.broadcasted_iota(jnp.int32, v.shape, 0)
    v = pltpu.roll(v, 4, 0)
    v = jnp.where(row % 4 < 2, pltpu.roll(v, ROWS - 2, 0), pltpu.roll(v, 2, 0))
    return jnp.where(row % 2 < 1, pltpu.roll(v, ROWS - 1, 0), pltpu.roll(v, 1, 0))


def split_rows(symmetric, parts):
    rows = symmetric.shape[0]
    high = symmetric.astype(jnp.bfloat16)
    low = (symmetric - high.astype(jnp.float32)).astype(jnp.bfloat16)
    parts[0:rows, :] = high
    parts[rows : 2 * rows, :] = high
    parts[2 * rows : 3 * rows, :] = low


def cone(taps_ref, parts, rows):
    wide = parts.shape[1]
    mixed = jnp.dot(taps_ref[...], parts[...], preferred_element_type=jnp.float32)
    total = mixed[0:rows]
    for b in range(1, RADIUS + 1):
        part = mixed[b * rows : (b + 1) * rows]
        total = total + (pltpu.roll(part, b, 1) + pltpu.roll(part, wide - b, 1))
    return total


def filter_kernel(count, per_device, width, *refs):
    taps_ref, edges_ref = refs[:2]
    got = refs[count + 1 : 1 : -1]
    outs = refs[2 + count : 2 + 2 * count]
    slabs, parts, done = refs[2 + 2 * count :]
    me = lax.axis_index("gx")
    half = count // 2
    rows = half * ROWS
    for k in range(count):
        slabs[lax.bitwise_xor(me, k)] = got[k][...]

    side = jnp.zeros((rows, LANES), jnp.float32)
    for i in range(per_device):
        here = slice(i * width, (i + 1) * width)
        halves = [slabs[s, :, here] + flip_rows(slabs[count - 1 - s, :, here]) for s in range(half)]
        split_rows(jnp.concatenate([jnp.concatenate(halves, axis=0), side], axis=1), parts)
        total = cone(taps_ref, parts, rows)
        for s in range(half):
            own = total[s * ROWS : (s + 1) * ROWS, :width]
            done[s, :, here] = own
            done[count - 1 - s, :, here] = flip_rows(own)
    for k in range(count):
        outs[k][:, : per_device * width] = done[lax.bitwise_xor(me, k)]
        outs[k][:, per_device * width :] = edges_ref[...]


def cone_filter(taps, edges, got, per_device, width):
    count = len(got)
    rows = count // 2 * ROWS
    return pl.pallas_call(
        functools.partial(filter_kernel, count, per_device, width),
        in_specs=[VMEM] * (2 + count),
        out_specs=[VMEM] * count,
        out_shape=[fast(ROWS, per_device * width + edges.shape[1])] * count,
        scratch_shapes=[
            pltpu.VMEM((count, ROWS, per_device * width), jnp.float32),
            pltpu.VMEM((3 * rows, width + LANES), jnp.bfloat16),
            pltpu.VMEM((count, ROWS, per_device * width), jnp.float32),
        ],
        compiler_params=params(),
    )(taps, edges, *got[::-1])


SPAN = 2 * PART


def finish_kernel(count, per_device, width, *refs):
    taps_ref = refs[0]
    got = refs[count:0:-1]
    out, (slabs, parts, mine, left, right, done, sems) = refs[count + 1], refs[count + 2 :]
    me = lax.axis_index("gx")
    layers = count * per_device
    half = count // 2
    rows = half * ROWS
    lane = lax.broadcasted_iota(jnp.int32, (rows, LANES), 1)
    lane_out = lax.broadcasted_iota(jnp.int32, (ROWS, LANES), 1)
    for k in range(count):
        slabs[lax.bitwise_xor(me, k)] = got[k][:, per_device * width :]
    symmetric = jnp.concatenate([slabs[s] + flip_rows(slabs[count - 1 - s]) for s in range(half)], axis=0)
    per_tile = LANES // SPAN
    tiles = []
    for start in range(0, layers, per_tile):
        tile = jnp.zeros((rows, LANES), jnp.float32)
        for j in range(min(per_tile, layers - start)):
            at = PART * (start + j)
            source = symmetric[:, at // LANES * LANES : (at // LANES + 1) * LANES]
            low, high = SPAN * j + 1, SPAN * j + PART + STRIP - 1
            here = jnp.logical_and(lane >= low, lane < low + STRIP)
            tile = jnp.where(here, pltpu.roll(source, (low - at) % LANES, 1), tile)
            here = jnp.logical_and(lane >= high, lane < high + STRIP)
            tile = jnp.where(here, pltpu.roll(source, (high - at - STRIP) % LANES, 1), tile)
        tiles.append(tile)
    split_rows(jnp.concatenate(tiles, axis=1), parts)
    total = cone(taps_ref, parts, rows)
    for s in range(half):
        own = total[s * ROWS : (s + 1) * ROWS]
        mine[s] = own
        mine[count - 1 - s] = flip_rows(own)
    mine_now = mine[me]
    for layer in range(layers):
        tile = mine_now[:, layer // per_tile * LANES : (layer // per_tile + 1) * LANES]
        at = SPAN * (layer % per_tile)
        head = pltpu.roll(tile, (-at - STRIP) % LANES, 1)
        left[layer] = jnp.where(lane_out < STRIP - 1, head, 0.0)
        tail = pltpu.roll(tile, (LANES - STRIP - at - PART) % LANES, 1)
        right[layer] = jnp.where(lane_out > LANES - STRIP, tail, 0.0)

    copies = []
    for k in range(count):
        first = lax.bitwise_xor(me, k) * per_device
        for i in range(per_device):
            at = i * width
            done[k, i] = got[k][:, at : at + width]
            done[k, i, :, :LANES] += left[first + i]
            done[k, i, :, width - LANES :] += right[first + i]
        copies.append(pltpu.make_async_copy(done.at[k], out.at[pl.ds(first, per_device)], sems.at[k]))
        copies[-1].start()
    for copy in copies:
        copy.wait()


def finish(taps, parts, layers, width):
    count = len(parts)
    per_device = layers // count
    rows = count // 2 * ROWS
    edges = parts[0].shape[1] - per_device * width
    spread = math.ceil(layers * SPAN / LANES) * LANES
    return pl.pallas_call(
        functools.partial(finish_kernel, count, per_device, width),
        in_specs=[VMEM] * (1 + count),
        out_specs=ANY,
        out_shape=f32(layers, ROWS, width),
        scratch_shapes=[
            pltpu.VMEM((count, ROWS, edges), jnp.float32),
            pltpu.VMEM((3 * rows, spread), jnp.bfloat16),
            pltpu.VMEM((count, ROWS, spread), jnp.float32),
            pltpu.VMEM((layers, ROWS, LANES), jnp.float32),
            pltpu.VMEM((layers, ROWS, LANES), jnp.float32),
            pltpu.VMEM((count, per_device, ROWS, width), jnp.float32),
            pltpu.SemaphoreType.DMA((count,)),
        ],
        compiler_params=params(),
    )(taps, *parts[::-1])


def spread(parts):
    count = len(parts)
    got = list(parts)
    for k in range(count - 1, 0, -1):
        got[k] = lax.ppermute(parts[k], "gx", [(i, i ^ k) for i in range(count)])
    return got


def on_device(efield, hfield, forward, material, permit, design_mask, grad_sum):
    layers, _, width = grad_sum.shape
    zfaces = exchange(z_faces(efield, hfield), "gz", "gy")
    efield, hfield, material, grad_sum = load(efield, hfield, material, grad_sum)
    xfaces = exchange(x_faces(efield, hfield, zfaces), "gx", "gy")
    forward, own_low, own_high, mask, inv = strips(
        permit, efield, hfield, forward, material, grad_sum, design_mask
    )
    arrays = (efield, hfield, forward, inv, grad_sum, mask)
    edges = own_edges(arrays)
    shares, own = own_gradient(arrays, zfaces, xfaces)
    got = spread(shares)
    yfaces = exchange(y_faces(own_low, own_high, zfaces, xfaces, own), "gy", "gz")
    message, edge = edge_gradient(own, edges, zfaces, xfaces, yfaces)
    taps = jnp.asarray(cone_matrix(len(got) // 2 * ROWS))
    parts = cone_filter(taps, message, got, layers // len(got), width)
    e_next, h_next, grad_total = step(efield, hfield, inv, own, edge, zfaces, xfaces, yfaces, parts[0])
    return e_next, h_next, grad_total, finish(taps, spread(parts), layers, width)


def solution(mesh):
    field = P(None, "gz", "gx", "gy")
    cells = P("gz", "gx", "gy")
    return jax.shard_map(
        on_device,
        mesh=mesh,
        in_specs=(field, field, field, cells, P(), P("gx", "gy"), cells),
        out_specs=(field, field, cells, cells),
        check_vma=False,
    )
```

```python
import functools
import math

import jax
import jax.numpy as jnp
import numpy as np
from jax import lax
from jax.experimental import pallas as pl
from jax.experimental.pallas import tpu as pltpu
from jax.sharding import PartitionSpec as P

RADIUS = 6
BLOCK = 8
HALF = 0.5

ROWS = 8
LANES = 128
STRIP = 8
SLOTS = LANES // STRIP
MIB = 1024 * 1024

VMEM = pl.BlockSpec(memory_space=pltpu.VMEM)
SMEM = pl.BlockSpec(memory_space=pltpu.SMEM)
ANY = pl.BlockSpec(memory_space=pl.ANY)


def params(mib=24):
    return pltpu.CompilerParams(vmem_limit_bytes=mib * MIB)


def f32(*shape):
    return jax.ShapeDtypeStruct(shape, jnp.float32)


def fast(*shape):
    return pltpu.VMEM(shape, jnp.float32)


def rounds(axis):
    return 2 if lax.axis_size(axis) > 2 else 1


def exchange(sends, axis, mate):
    count = lax.axis_size(axis)
    beside = lax.axis_size(mate)
    if count == 1:
        return sends
    got = []
    for start, value in enumerate(sends):
        partner = list(range(count))
        for low in range(start, count - 1, 2):
            partner[low], partner[low + 1] = low + 1, low
        axes = sorted((axis, mate))
        steps = (beside, 1) if axes[0] == axis else (1, count)
        pairs = []
        for i in range(count):
            for m in range(beside):
                if partner[i] != i:
                    to = (partner[i], m)
                elif beside % 2 == 0:
                    to = (i, m ^ 1)
                else:
                    continue
                pairs.append((i * steps[0] + m * steps[1], to[0] * steps[0] + to[1] * steps[1]))
        got.append(lax.ppermute(value, tuple(axes), pairs))
    return got


def exchange_diagonal(sends):
    along_x, along_y, along_z = (lax.axis_size(axis) for axis in AXES)

    def flat(x, y, z):
        return (x * along_y + y) * along_z + z

    got = []
    for start, value in enumerate(sends):
        partner = {}
        for low in range(start, along_z - 1, 2):
            for x in range(1, along_x):
                partner[x, low] = (x - 1, low + 1)
                partner[x - 1, low + 1] = (x, low)
        pairs = []
        for x in range(along_x):
            for z in range(along_z):
                for y in range(along_y):
                    if (x, z) in partner:
                        to = partner[x, z]
                        pairs.append((flat(x, y, z), flat(to[0], y, to[1])))
                    elif along_y % 2 == 0:
                        pairs.append((flat(x, y, z), flat(x, y ^ 1, z)))
        got.append(lax.ppermute(value, AXES, pairs))
    return got


AXES = ("gx", "gy", "gz")


class Side:
    def __init__(self, axis):
        index = lax.axis_index(axis)
        self.rounds = rounds(axis)
        self.odd = index % 2 == 1
        self.bottom = index == 0
        self.top = index == lax.axis_size(axis) - 1

    def sends(self, low, high):
        both = [jnp.where(self.odd, low, high)]
        if self.rounds > 1:
            both.append(jnp.where(self.odd, high, low))
        return both

    def lower(self, got):
        return jnp.where(self.bottom, 0.0, jnp.where(self.odd, got[0], got[-1]))

    def upper(self, got):
        return jnp.where(self.top, 0.0, jnp.where(self.odd, got[-1], got[0]))


def first_layer(cells_z, layers):
    return (cells_z - layers) * (1 - lax.axis_index("gz"))


def faces_kernel(x_rounds, e_ref, h_ref, *refs):
    x_sends, (low_ref, rows_ref) = refs[:x_rounds], refs[-2:]
    others = refs[x_rounds:-2]
    z_sends, d_sends = others[: len(others) // 2], others[len(others) // 2 :]
    cells_z = e_ref.shape[1]
    last, top = ROWS - 1, cells_z - 1

    low_ref[2 * cells_z :, :] = jnp.zeros_like(low_ref[2 * cells_z :, :])
    rows_ref[5, top : top + 1, :] = jnp.zeros_like(rows_ref[5, top : top + 1, :])
    for z in range(cells_z):
        low_ref[z : z + 1, :] = e_ref[1, z, 0:1, :]
        low_ref[cells_z + z : cells_z + z + 1, :] = e_ref[2, z, 0:1, :]
        for c in range(3):
            rows_ref[c, z : z + 1, :] = e_ref[c, z, last : last + 1, :]
        for c in range(2):
            rows_ref[3 + c, z : z + 1, :] = h_ref[1 + c, z, last : last + 1, :]
        if z > 0:
            rows_ref[5, z - 1 : z, :] = e_ref[0, z, last : last + 1, :]
    ex = rows_ref[0]
    high = (
        rows_ref[3] - HALF * (rows_ref[5] - ex + rows_ref[2]),
        rows_ref[4] + HALF * rows_ref[1] - HALF * ex,
        ex,
    )
    side = Side("gx")
    for c in range(3):
        here = slice(c * cells_z, (c + 1) * cells_z)
        for ref, value in zip(x_sends, side.sends(low_ref[here, :], high[c])):
            ref[here, :] = value

    side = Side("gz")
    ex, ey, ez = (e_ref[c, top] for c in range(3))
    low = (e_ref[0, 0], e_ref[1, 0], jnp.zeros_like(ez))
    high = (h_ref[0, top] + HALF * ez - HALF * ey, h_ref[1, top] + HALF * ex - HALF * ez, ez)
    for c in range(3):
        for ref, value in zip(z_sends, side.sends(low[c], high[c])):
            ref[c] = value

    down, up = (
        jnp.broadcast_to(line, (ROWS, line.shape[1]))
        for line in (e_ref[0, 0, last : last + 1, :], e_ref[2, top, 0:1, :])
    )
    for ref, value in zip(d_sends, side.sends(down, up)):
        ref[...] = value


def halos(efield, hfield):
    _, cells_z, cells_x, cells_y = efield.shape
    x_rounds, z_rounds = rounds("gx"), rounds("gz")
    x_face, z_face, line = fast(3 * cells_z, cells_y), fast(3, cells_x, cells_y), fast(ROWS, cells_y)
    sends = pl.pallas_call(
        functools.partial(faces_kernel, x_rounds),
        in_specs=[VMEM] * 2,
        out_specs=[VMEM] * (x_rounds + 2 * z_rounds),
        out_shape=[x_face] * x_rounds + [z_face] * z_rounds + [line] * z_rounds,
        scratch_shapes=[
            pltpu.VMEM(x_face.shape, jnp.float32),
            pltpu.VMEM((6, cells_z, cells_y), jnp.float32),
        ],
        compiler_params=params(),
    )(efield, hfield)
    xfaces = exchange(sends[:x_rounds], "gx", "gy")
    zfaces = exchange(sends[x_rounds : x_rounds + z_rounds], "gz", "gy")
    return zfaces + exchange_diagonal(sends[x_rounds + z_rounds :]), xfaces


def lane_group():
    return lax.broadcasted_iota(jnp.int32, (ROWS, LANES), 1) // STRIP


def pack_strips(tiles, low_ref, high_ref, first):
    group = lane_group()
    width = tiles[0][1]
    for start in range(0, len(tiles), SLOTS):
        low = jnp.zeros((ROWS, LANES), jnp.float32)
        high = jnp.zeros((ROWS, LANES), jnp.float32)
        for k, (load, _) in enumerate(tiles[start : start + SLOTS]):
            if load is None:
                continue
            here = group == k
            shift = (STRIP * k) % LANES
            left = load(slice(0, LANES))
            right = load(slice(width - LANES, width))
            low = jnp.where(here, pltpu.roll(left, shift, 1) if shift else left, low)
            shift = (STRIP * k + STRIP) % LANES
            high = jnp.where(here, pltpu.roll(right, shift, 1) if shift else right, high)
        low_ref[first + start // SLOTS] = low
        high_ref[first + start // SLOTS] = high


def load_kernel(e_in, h_in, e_ref, h_ref, sems):
    parts = [(source.at[c], target.at[c]) for source, target in ((e_in, e_ref), (h_in, h_ref)) for c in range(3)]
    copies = [pltpu.make_async_copy(*part, sems.at[n]) for n, part in enumerate(parts)]
    for copy in copies:
        copy.start()
    for copy in copies:
        copy.wait()


def load(*fields):
    return pl.pallas_call(
        load_kernel,
        in_specs=[ANY] * 2,
        out_specs=[VMEM] * 2,
        out_shape=[fast(*one.shape) for one in fields],
        scratch_shapes=[pltpu.SemaphoreType.DMA((6,))],
        compiler_params=params(56),
    )(*fields)


def strips_kernel(
    permit_ref, e_ref, h_ref, f_in, mat_ref, grad_ref, mask_ref, f_ref, low_ref, high_ref, wide_ref, inv_ref, sems
):
    cells_z, width = e_ref.shape[1], e_ref.shape[3]
    layers = grad_ref.shape[0]
    blocks = mask_ref.shape[1]
    copies = [pltpu.make_async_copy(f_in.at[c], f_ref.at[c], sems.at[c]) for c in range(3)]
    for copy in copies:
        copy.start()

    inverse = [
        jnp.broadcast_to(HALF * (1.0 / permit_ref[0:1, m : m + 1]), (ROWS, width))
        for m in range(permit_ref.shape[1])
    ]
    for z in range(cells_z):
        inv = inverse[0]
        for m in range(1, len(inverse)):
            inv = jnp.where(mat_ref[z] == m, inverse[m], inv)
        inv_ref[z] = inv
    spread = (
        lax.broadcasted_iota(jnp.int32, (blocks, width), 0)
        == lax.broadcasted_iota(jnp.int32, (blocks, width), 1) // BLOCK
    ).astype(jnp.float32)
    mask = jnp.broadcast_to(mask_ref[...].astype(jnp.float32), (ROWS, blocks))
    wide_ref[...] = jnp.dot(mask, spread, preferred_element_type=jnp.float32)
    first = first_layer(cells_z, layers)
    tiles = []
    for z in range(cells_z):
        for ref in (e_ref, h_ref):
            for c in range(3):
                tiles.append((lambda s, r=ref, c=c, z=z: r[c, z, :, s], width))
    pack_strips(tiles, low_ref, high_ref, 0)

    for copy in copies:
        copy.wait()
    done = len(tiles) // SLOTS
    tiles = []
    for layer in range(layers):
        for c in range(3):
            tiles.append((lambda s, c=c, l=layer: f_ref[c, first + l, :, s], width))
        tiles.append((lambda s, l=layer: inv_ref[first + l, :, s], width))
        tiles.append((lambda s, l=layer: grad_ref[l, :, s], width))
        tiles.append((lambda s: wide_ref[:, s], width) if layer % ROWS == 0 else (None, width))
    pack_strips(tiles, low_ref, high_ref, done)


def strips(permit, efield, hfield, forward, material, grad_sum, mask):
    cells_z, width = efield.shape[1], efield.shape[3]
    count = (cells_z * 6 + grad_sum.shape[0] * 6) // SLOTS
    packed = (count, ROWS, LANES)
    shapes = (forward.shape, packed, packed, (ROWS, width), material.shape)
    return pl.pallas_call(
        strips_kernel,
        in_specs=[VMEM] * 3 + [ANY] + [VMEM] * 3,
        out_specs=[VMEM] * 5,
        out_shape=[fast(*shape) for shape in shapes],
        scratch_shapes=[pltpu.SemaphoreType.DMA((3,))],
        compiler_params=params(40),
    )(permit.reshape(1, -1), efield, hfield, forward, material, grad_sum, mask)


def edge_tile(load, width):
    lane = lax.broadcasted_iota(jnp.int32, (ROWS, LANES), 1)
    head = pltpu.roll(load(slice(0, LANES)), STRIP, 1)
    tail = pltpu.roll(load(slice(width - LANES, width)), LANES - STRIP, 1)
    return jnp.where(lane < LANES // 2, head, tail)


def edges_kernel(e_ref, h_ref, f_ref, inv_ref, grad_ref, mask_ref, eh_out, grad_out, mask_out):
    cells_z, width = e_ref.shape[1], e_ref.shape[3]
    layers = grad_ref.shape[0]
    first = first_layer(cells_z, layers)
    for z in range(cells_z):
        for c in range(3):
            eh_out[z, c] = edge_tile(lambda s: e_ref[c, z, :, s], width)
            eh_out[z, 3 + c] = edge_tile(lambda s: h_ref[c, z, :, s], width)
    for layer in range(layers):
        for c in range(3):
            grad_out[layer, c] = edge_tile(lambda s: f_ref[c, first + layer, :, s], width)
        grad_out[layer, 3] = edge_tile(lambda s: inv_ref[first + layer, :, s], width)
        grad_out[layer, 4] = edge_tile(lambda s: grad_ref[layer, :, s], width)
    mask_out[...] = edge_tile(lambda s: mask_ref[:, s], width)


def own_edges(arrays):
    cells_z, layers = arrays[0].shape[1], arrays[4].shape[0]
    return pl.pallas_call(
        edges_kernel,
        in_specs=[VMEM] * 6,
        out_specs=[VMEM] * 3,
        out_shape=[fast(cells_z, 6, ROWS, LANES), fast(layers, 5, ROWS, LANES), fast(ROWS, LANES)],
        compiler_params=params(),
    )(*arrays)


def face_tiles(zfaces, xfaces):
    width = xfaces[0].shape[1]
    rows = xfaces[0].shape[0]
    cells_z = rows // 3
    z_side, x_side = Side("gz"), Side("gx")
    zfaces, lines = zfaces[: len(zfaces) // 2], zfaces[len(zfaces) // 2 :]

    def corner(s):
        row = lax.broadcasted_iota(jnp.int32, (ROWS, s.stop - s.start), 0)
        line = jnp.where(x_side.bottom, 0.0, z_side.upper([f[:, s] for f in lines]))
        return jnp.where(row == ROWS - 1, -HALF * line, 0.0)

    def beyond(s):
        return jnp.where(x_side.top, 0.0, z_side.lower([f[:, s] for f in lines]))

    def x_tile(pick, t, s):
        value = pick([f[t : t + ROWS, s] for f in xfaces])
        return value + corner(s) if t == cells_z - ROWS and pick == x_side.lower else value

    tiles = []
    for c in range(3):
        tiles.append((lambda s, c=c: z_side.lower([f[c, :, s] for f in zfaces]), width))
    for c in range(2):
        tiles.append((lambda s, c=c: z_side.upper([f[c, :, s] for f in zfaces]), width))
    for t in range(0, rows, ROWS):
        tiles.append((lambda s, t=t: x_tile(x_side.lower, t, s), width))
    for t in range(0, rows, ROWS):
        if t == 2 * cells_z:
            tiles.append((beyond, width))
        else:
            tiles.append((lambda s, t=t: x_tile(x_side.upper, t, s), width))
    return tiles


def face_count(xface):
    return 5 + 2 * (xface.shape[0] // ROWS)


def y_faces_kernel(counts, *refs):
    own_low, own_high = refs[:2]
    zfaces, xfaces = refs[2 : 2 + counts[0]], refs[2 + counts[0] : 2 + sum(counts)]
    sends, (low_ref, high_ref) = refs[3 + sum(counts) : -2], refs[-2:]
    own = own_low.shape[0]
    pack_strips(face_tiles(zfaces, xfaces), low_ref, high_ref, 0)
    side = Side("gy")
    for ref, value in zip(sends, side.sends(own_low[...], own_high[...])):
        ref[0:own] = value
    for ref, value in zip(sends, side.sends(low_ref[...], high_ref[...])):
        ref[own:] = value


def y_faces(own_low, own_high, zfaces, xfaces, after):
    extra = math.ceil(face_count(xfaces[0]) / SLOTS)
    packed = fast(own_low.shape[0] + extra, ROWS, LANES)
    return pl.pallas_call(
        functools.partial(y_faces_kernel, (len(zfaces), len(xfaces))),
        in_specs=[VMEM] * (2 + len(zfaces) + len(xfaces)) + [ANY],
        out_specs=[VMEM] * rounds("gy"),
        out_shape=[packed] * rounds("gy"),
        scratch_shapes=[pltpu.VMEM((extra, ROWS, LANES), jnp.float32)] * 2,
        compiler_params=params(),
    )(own_low, own_high, *zfaces, *xfaces, after)


OWN, CIRCLE, EDGE = range(3)


def faces_wide(mode, width):
    return {OWN: width, CIRCLE: width + LANES, EDGE: LANES}[mode]


class Fields:
    def __init__(self, mode, layers, fields, zfaces, xfaces, yfaces, scratch):
        self.mode = mode
        self.fields = fields
        if mode == EDGE:
            self.cells_z, self.width = fields.shape[0], xfaces[0].shape[1]
        else:
            self.cells_z, self.width = fields[0].shape[1], fields[0].shape[3]
        self.wide = faces_wide(mode, self.width)
        self.lane = lax.broadcasted_iota(jnp.int32, (ROWS, LANES), 1)
        self.row = lax.broadcasted_iota(jnp.int32, (ROWS, self.wide), 0)
        self.per_group = 6 * ROWS // SLOTS
        self.groups = self.cells_z // ROWS
        self.grad_base = self.per_group * self.groups
        halo_base = self.grad_base + self.per_group * (layers // ROWS)
        self.left_wide, self.right_wide = left_wide, right_wide = scratch[:2]
        if mode != OWN:
            self.ybuf = scratch[2]
            y_side = Side("gy")
            for t in range(yfaces[0].shape[0]):
                lower = y_side.lower([f[t] for f in yfaces])
                upper = y_side.upper([f[t] for f in yfaces])
                if mode == EDGE:
                    even = self.lane // STRIP % 2 == 0
                    lower, upper = (
                        jnp.where(even, upper, pltpu.roll(lower, STRIP, 1)),
                        jnp.where(even, pltpu.roll(upper, LANES - STRIP, 1), lower),
                    )
                self.ybuf[0, t] = lower
                self.ybuf[1, t] = upper

        def face(load, slot):
            if mode == EDGE:
                own = edge_tile(load, self.width)
                return self.edge(own, halo_base + slot // SLOTS, slot % SLOTS)
            return self.wider(load, halo_base + slot // SLOTS, slot % SLOTS)

        full = [face(load, slot) for slot, (load, _) in enumerate(face_tiles(zfaces, xfaces))]
        self.below, self.above = full[:3], full[3:5]
        per_face = xfaces[0].shape[0] // ROWS
        for t in range(per_face):
            left_wide[t * ROWS : (t + 1) * ROWS, :] = full[5 + t]
            right_wide[t * ROWS : (t + 1) * ROWS, :] = full[5 + per_face + t]
        cells_z = self.cells_z
        left_wide[cells_z : 2 * cells_z, :] += HALF * self.y_up(left_wide[2 * cells_z : 3 * cells_z, :])

    def wider(self, load, tile, k):
        if self.mode == OWN:
            return load(slice(0, self.width))

        def moved(v, to):
            shift = (to - STRIP * k) % LANES
            return pltpu.roll(v, shift, 1) if shift else v

        lower, upper = self.ybuf[0, tile], self.ybuf[1, tile]
        halo = jnp.where(self.lane < STRIP, moved(upper, 0), moved(lower, LANES - STRIP))
        return jnp.concatenate([load(slice(0, self.width)), halo], axis=1)

    def edge(self, own, tile, k):
        shift = (LANES - STRIP - 2 * STRIP * (k // 2)) % LANES
        both = pltpu.roll(self.ybuf[k % 2, tile], shift, 1)
        inside = jnp.logical_and(self.lane >= STRIP, self.lane < LANES - STRIP)
        return jnp.where(inside, own, both)

    def y_up(self, v):
        return pltpu.roll(v, self.wide - 1, 1)

    def y_down(self, v):
        return pltpu.roll(v, 1, 1)

    def x_up(self, v, line):
        return jnp.where(self.row == ROWS - 1, line, pltpu.roll(v, ROWS - 1, 0))

    def x_down(self, v, line):
        return jnp.where(self.row == 0, line, pltpu.roll(v, 1, 0))

    def line(self, ref, at):
        return jnp.broadcast_to(ref[pl.ds(at, 1), :], (ROWS, self.wide))

    def field(self, which, c, a, b):
        slot = 6 * b + 3 * which + c
        tile = self.per_group * a + slot // SLOTS
        if self.mode == EDGE:
            return self.edge(self.fields[ROWS * a + b, 3 * which + c], tile, slot % SLOTS)
        ref = self.fields[which]
        return self.wider(lambda s: ref[c, ROWS * a + b, :, s], tile, slot % SLOTS)

    def hx(self, a, b, ey, ez, ey_next):
        return self.field(1, 0, a, b) - HALF * (self.y_up(ez) - ez - ey_next + ey)

    def hy(self, a, b, ex, ez, ex_next):
        up = self.x_up(ez, self.line(self.right_wide, self.cells_z + ROWS * a + b))
        return self.field(1, 1, a, b) - HALF * (ex_next - ex - up + ez)

    def hz(self, a, b, ex, ey):
        up = self.x_up(ey, self.line(self.right_wide, ROWS * a + b))
        return self.field(1, 2, a, b) - HALF * (up - ey - self.y_up(ex) + ex)

    def start(self, a):
        ex, ey = self.field(0, 0, a, 0), self.field(0, 1, a, 0)
        below = self.below
        at_bottom = (
            below[0] - HALF * self.y_up(below[2]) + HALF * ey,
            below[1] - HALF * ex + HALF * self.x_up(below[2], self.line(self.right_wide, 2 * self.cells_z)),
        )
        before, b = jnp.maximum(a - 1, 0), ROWS - 1
        ex_before, ey_before, ez_before = (self.field(0, c, before, b) for c in range(3))
        inside = (
            self.hx(before, b, ey_before, ez_before, ey),
            self.hy(before, b, ex_before, ez_before, ex),
        )
        bottom = a == 0
        return (ex, ey) + tuple(jnp.where(bottom, one, two) for one, two in zip(at_bottom, inside))

    def group(self, a, carry, emit):
        ex, ey, hx_z, hy_z = carry
        for b in range(ROWS):
            z = ROWS * a + b
            ez = self.field(0, 2, a, b)
            if b < ROWS - 1:
                ex_next, ey_next = (self.field(0, c, a, b + 1) for c in range(2))
            else:
                end = a == self.groups - 1
                after = jnp.minimum(a + 1, self.groups - 1)
                ex_next, ey_next = (
                    jnp.where(end, self.above[c], self.field(0, c, after, 0)) for c in range(2)
                )
            hx = self.hx(a, b, ey, ez, ey_next)
            hy = self.hy(a, b, ex, ez, ex_next)
            hz = self.hz(a, b, ex, ey)
            hy_x = self.x_down(hy, self.line(self.left_wide, z) + HALF * ez)
            hz_x = self.x_down(hz, self.line(self.left_wide, self.cells_z + z) - HALF * ey)
            curl = (
                (hz - self.y_down(hz)) - (hy - hy_z),
                (hx - hx_z) - (hz - hz_x),
                (hy - hy_x) - (hx - self.y_down(hx)),
            )
            emit(a, b, (ex, ey, ez), (hx, hy, hz), curl)
            ex, ey, hx_z, hy_z = ex_next, ey_next, hx, hy
        return ex, ey, hx_z, hy_z

    def gradient(self, layers, arrays, store):
        first = first_layer(self.cells_z, layers)
        first_group = first // ROWS
        if self.mode == EDGE:
            grad_edges, mask_ref = arrays
            mask = self.edge(mask_ref[...], self.grad_base, 5)
        else:
            f_ref, inv_ref, grad_ref, mask_ref = arrays
            mask = mask_ref[...]

        def emit(a, b, efield, hfield, curl):
            z = ROWS * a + b
            layer = z - first
            if self.mode == EDGE:
                tile = self.grad_base + self.per_group * (a - first_group)
                slots = [6 * b + n for n in range(5)]
                values = [
                    self.edge(grad_edges[layer, n], tile + slot // SLOTS, slot % SLOTS)
                    for n, slot in enumerate(slots)
                ]
            else:
                values = [f_ref[c, z] for c in range(3)] + [inv_ref[z], grad_ref[layer]]
            total = None
            for c in range(3):
                term = values[c] * (efield[c] + values[3] * curl[c])
                total = term if total is None else total + term
            store(layer, values[4] + mask * total)

        def body(i, carry):
            return self.group(first_group + i, carry, emit)

        lax.fori_loop(0, layers // ROWS, body, self.start(first_group))


def fields_scratch(mode, xface, yface, width):
    rows, wide = xface.shape[0], faces_wide(mode, width)
    out = [pltpu.VMEM((rows, wide), jnp.float32)] * 2
    if mode != OWN:
        out.append(pltpu.VMEM((2,) + yface.shape, jnp.float32))
    return out


def own_gradient_kernel(counts, per_device, *refs):
    e_ref, h_ref, f_ref, inv_ref, grad_ref, mask_ref = refs[:6]
    zfaces, xfaces = refs[6 : 6 + counts[0]], refs[6 + counts[0] : 6 + sum(counts)]
    shares, (own_ref, *scratch) = refs[6 + sum(counts) : -3][::-1], refs[-3:]
    layers, _, width = grad_ref.shape
    fields = Fields(OWN, layers, (e_ref, h_ref), zfaces, xfaces, None, scratch)

    def store(layer, value):
        own_ref[layer] = value

    fields.gradient(layers, (f_ref, inv_ref, grad_ref, mask_ref), store)

    me = lax.axis_index("gx")
    for k, share in enumerate(shares):
        chunk = lax.bitwise_xor(me, k)
        for i in range(per_device):
            share[:, i * width : (i + 1) * width] = own_ref[chunk * per_device + i]


def own_gradient(arrays, zfaces, xfaces):
    layers, _, width = arrays[4].shape
    count = lax.axis_size("gx")
    per_device = layers // count
    *shares, own = pl.pallas_call(
        functools.partial(own_gradient_kernel, (len(zfaces), len(xfaces)), per_device),
        in_specs=[VMEM] * (6 + len(zfaces) + len(xfaces)),
        out_specs=[VMEM] * (count + 1),
        out_shape=[fast(ROWS, per_device * width)] * count + [fast(layers, ROWS, width)],
        scratch_shapes=fields_scratch(OWN, xfaces[0], None, width),
        compiler_params=params(),
    )(*arrays, *zfaces, *xfaces)
    return shares[::-1], own


PART = 2 * STRIP


def edge_gradient_kernel(counts, *refs):
    own_ref, eh_ref, grad_ref, mask_ref = refs[:4]
    ends = np.cumsum((4,) + counts)
    zfaces, xfaces, yfaces = (refs[i:j] for i, j in zip(ends[:-1], ends[1:]))
    (message, edge_ref), scratch = refs[ends[-1] : -3], refs[-3:]
    layers, _, width = own_ref.shape
    lane = lax.broadcasted_iota(jnp.int32, (ROWS, LANES), 1)
    first, last = STRIP, LANES - STRIP - 1
    fields = Fields(EDGE, layers, eh_ref, zfaces, xfaces, yfaces, scratch)

    def store(layer, value):
        edge_ref[layer] = value

    fields.gradient(layers, (grad_ref, mask_ref), store)

    per_tile = LANES // PART
    for start in range(0, layers, per_tile):
        packed = jnp.zeros((ROWS, LANES), jnp.float32)
        for j in range(min(per_tile, layers - start)):
            layer = start + j
            edge = edge_ref[layer]
            own = edge_tile(lambda s: own_ref[layer, :, s], width)
            more = jnp.where(jnp.logical_or(lane == first, lane == last), edge - own, edge)
            left = pltpu.roll(more, (PART * j - 1) % LANES, 1)
            right = pltpu.roll(more, (PART * j + STRIP - last) % LANES, 1)
            packed = jnp.where(lane // STRIP == 2 * j, left, packed)
            packed = jnp.where(lane // STRIP == 2 * j + 1, right, packed)
        message[:, start // per_tile * LANES : (start // per_tile + 1) * LANES] = packed


def edge_gradient(own, edges, zfaces, xfaces, yfaces):
    layers, _, width = own.shape
    faces = (*zfaces, *xfaces, *yfaces)
    tiles = math.ceil(layers * PART / LANES)
    return pl.pallas_call(
        functools.partial(edge_gradient_kernel, (len(zfaces), len(xfaces), len(yfaces))),
        in_specs=[VMEM] * (4 + len(faces)),
        out_specs=[VMEM] * 2,
        out_shape=[fast(ROWS, tiles * LANES), fast(layers, ROWS, LANES)],
        scratch_shapes=fields_scratch(EDGE, xfaces[0], yfaces[0], width),
        compiler_params=params(),
    )(own, *edges, *faces)


def step_kernel(counts, *refs):
    e_ref, h_ref, inv_ref, own_ref, edge_ref = refs[:5]
    ends = np.cumsum((5,) + counts)
    zfaces, xfaces, yfaces = (refs[i:j] for i, j in zip(ends[:-1], ends[1:]))
    e_out, h_out, grad_out = refs[ends[-1] + 1 : ends[-1] + 4]
    left_wide, right_wide, ybuf, e_new, h_new, grad_new, sems = refs[ends[-1] + 4 :]
    layers, _, width = own_ref.shape
    lane = lax.broadcasted_iota(jnp.int32, (ROWS, LANES), 1)

    for layer in range(layers):
        edge = edge_ref[layer]
        head, tail = own_ref[layer, :, 0:LANES], own_ref[layer, :, width - LANES :]
        grad_new[layer] = own_ref[layer]
        grad_new[layer, :, 0:LANES] = jnp.where(lane == 0, pltpu.roll(edge, LANES - STRIP, 1), head)
        grad_new[layer, :, width - LANES :] = jnp.where(lane == LANES - 1, pltpu.roll(edge, STRIP, 1), tail)
    grad_copy = pltpu.make_async_copy(grad_new, grad_out, sems.at[0, 0])
    grad_copy.start()

    fields = Fields(CIRCLE, layers, (e_ref, h_ref), zfaces, xfaces, yfaces, (left_wide, right_wide, ybuf))

    def emit(a, b, efield, hfield, curl):
        z = ROWS * a + b
        half_inv = inv_ref[z]
        for c in range(3):
            e_new[c, z] = efield[c][:, :width] + half_inv * curl[c][:, :width]
            h_new[c, z] = hfield[c][:, :width]

    def copies(a):
        here = pl.ds(a * ROWS, ROWS)
        return [
            pltpu.make_async_copy(new.at[c, here], out.at[c, here], sems.at[1 + a, 3 * n + c])
            for n, (new, out) in enumerate(((e_new, e_out), (h_new, h_out)))
            for c in range(3)
        ]

    def body(a, carry):
        carry = fields.group(a, carry, emit)
        for copy in copies(a):
            copy.start()
        return carry

    lax.fori_loop(0, fields.groups, body, fields.start(0))
    for a in range(fields.groups):
        for copy in copies(a):
            copy.wait()
    grad_copy.wait()


def step(efield, hfield, inv, own, edge, zfaces, xfaces, yfaces, after):
    _, cells_z, _, width = efield.shape
    groups = (zfaces, xfaces, yfaces)
    counts = tuple(len(group) for group in groups)
    shapes = (efield.shape, hfield.shape, own.shape)
    return pl.pallas_call(
        functools.partial(step_kernel, counts),
        in_specs=[VMEM] * (5 + sum(counts)) + [ANY],
        out_specs=[ANY] * 3,
        out_shape=[f32(*shape) for shape in shapes],
        scratch_shapes=fields_scratch(CIRCLE, xfaces[0], yfaces[0], width)
        + [pltpu.VMEM(shape, jnp.float32) for shape in shapes]
        + [pltpu.SemaphoreType.DMA((1 + cells_z // ROWS, 6))],
        compiler_params=params(),
    )(efield, hfield, inv, own, edge, *(one for group in groups for one in group), after)


def cone_matrix(rows):
    span = np.arange(-RADIUS, RADIUS + 1, dtype=np.float64)
    cone = np.maximum(RADIUS - np.sqrt(span[:, None] ** 2 + span[None, :] ** 2), 0.0)
    weight = cone / cone.sum()
    x = np.arange(rows)
    out = np.zeros((RADIUS + 1, rows, rows))
    for b in range(RADIUS + 1):
        for apart in (x[:, None] - x[None, :], 2 * rows - 1 - x[:, None] - x[None, :]):
            near = np.abs(apart) <= RADIUS
            out[b] += np.where(near, weight[np.clip(apart, -RADIUS, RADIUS) + RADIUS, RADIUS + b], 0.0)
    out = out.reshape((RADIUS + 1) * rows, rows).astype(np.float32)
    high = out.astype(jnp.bfloat16)
    low = (out - high.astype(np.float32)).astype(jnp.bfloat16)
    return np.concatenate([high, low, high], axis=1)


def flip_rows(v):
    row = lax.broadcasted_iota(jnp.int32, v.shape, 0)
    v = pltpu.roll(v, 4, 0)
    v = jnp.where(row % 4 < 2, pltpu.roll(v, ROWS - 2, 0), pltpu.roll(v, 2, 0))
    return jnp.where(row % 2 < 1, pltpu.roll(v, ROWS - 1, 0), pltpu.roll(v, 1, 0))


def split_rows(symmetric, parts):
    rows = symmetric.shape[0]
    high = symmetric.astype(jnp.bfloat16)
    low = (symmetric - high.astype(jnp.float32)).astype(jnp.bfloat16)
    parts[0:rows, :] = high
    parts[rows : 2 * rows, :] = high
    parts[2 * rows : 3 * rows, :] = low


def cone(taps_ref, parts, rows):
    wide = parts.shape[1]
    mixed = jnp.dot(taps_ref[...], parts[...], preferred_element_type=jnp.float32)
    total = mixed[0:rows]
    for b in range(1, RADIUS + 1):
        part = mixed[b * rows : (b + 1) * rows]
        total = total + (pltpu.roll(part, b, 1) + pltpu.roll(part, wide - b, 1))
    return total


def filter_kernel(count, per_device, width, *refs):
    taps_ref, edges_ref = refs[:2]
    got = refs[count + 1 : 1 : -1]
    outs = refs[2 + count : 2 + 2 * count]
    slabs, parts, done = refs[2 + 2 * count :]
    me = lax.axis_index("gx")
    half = count // 2
    rows = half * ROWS
    for k in range(count):
        slabs[lax.bitwise_xor(me, k)] = got[k][...]

    side = jnp.zeros((rows, LANES), jnp.float32)
    for i in range(per_device):
        here = slice(i * width, (i + 1) * width)
        halves = [slabs[s, :, here] + flip_rows(slabs[count - 1 - s, :, here]) for s in range(half)]
        split_rows(jnp.concatenate([jnp.concatenate(halves, axis=0), side], axis=1), parts)
        total = cone(taps_ref, parts, rows)
        for s in range(half):
            own = total[s * ROWS : (s + 1) * ROWS, :width]
            done[s, :, here] = own
            done[count - 1 - s, :, here] = flip_rows(own)
    for k in range(count):
        outs[k][:, : per_device * width] = done[lax.bitwise_xor(me, k)]
        outs[k][:, per_device * width :] = edges_ref[...]


def cone_filter(taps, edges, got, per_device, width):
    count = len(got)
    rows = count // 2 * ROWS
    return pl.pallas_call(
        functools.partial(filter_kernel, count, per_device, width),
        in_specs=[VMEM] * (2 + count),
        out_specs=[VMEM] * count,
        out_shape=[fast(ROWS, per_device * width + edges.shape[1])] * count,
        scratch_shapes=[
            pltpu.VMEM((count, ROWS, per_device * width), jnp.float32),
            pltpu.VMEM((3 * rows, width + LANES), jnp.bfloat16),
            pltpu.VMEM((count, ROWS, per_device * width), jnp.float32),
        ],
        compiler_params=params(),
    )(taps, edges, *got[::-1])


SPAN = 2 * PART


def finish_kernel(count, per_device, width, *refs):
    taps_ref = refs[0]
    got = refs[count:0:-1]
    out, (slabs, parts, mine, left, right, done, sems) = refs[count + 1], refs[count + 2 :]
    me = lax.axis_index("gx")
    layers = count * per_device
    half = count // 2
    rows = half * ROWS
    lane = lax.broadcasted_iota(jnp.int32, (rows, LANES), 1)
    lane_out = lax.broadcasted_iota(jnp.int32, (ROWS, LANES), 1)
    for k in range(count):
        slabs[lax.bitwise_xor(me, k)] = got[k][:, per_device * width :]
    symmetric = jnp.concatenate([slabs[s] + flip_rows(slabs[count - 1 - s]) for s in range(half)], axis=0)
    per_tile = LANES // SPAN
    tiles = []
    for start in range(0, layers, per_tile):
        tile = jnp.zeros((rows, LANES), jnp.float32)
        for j in range(min(per_tile, layers - start)):
            at = PART * (start + j)
            source = symmetric[:, at // LANES * LANES : (at // LANES + 1) * LANES]
            low, high = SPAN * j + 1, SPAN * j + PART + STRIP - 1
            here = jnp.logical_and(lane >= low, lane < low + STRIP)
            tile = jnp.where(here, pltpu.roll(source, (low - at) % LANES, 1), tile)
            here = jnp.logical_and(lane >= high, lane < high + STRIP)
            tile = jnp.where(here, pltpu.roll(source, (high - at - STRIP) % LANES, 1), tile)
        tiles.append(tile)
    split_rows(jnp.concatenate(tiles, axis=1), parts)
    total = cone(taps_ref, parts, rows)
    for s in range(half):
        own = total[s * ROWS : (s + 1) * ROWS]
        mine[s] = own
        mine[count - 1 - s] = flip_rows(own)
    mine_now = mine[me]
    for layer in range(layers):
        tile = mine_now[:, layer // per_tile * LANES : (layer // per_tile + 1) * LANES]
        at = SPAN * (layer % per_tile)
        head = pltpu.roll(tile, (-at - STRIP) % LANES, 1)
        left[layer] = jnp.where(lane_out < STRIP - 1, head, 0.0)
        tail = pltpu.roll(tile, (LANES - STRIP - at - PART) % LANES, 1)
        right[layer] = jnp.where(lane_out > LANES - STRIP, tail, 0.0)

    copies = []
    for k in range(count):
        first = lax.bitwise_xor(me, k) * per_device
        for i in range(per_device):
            at = i * width
            done[k, i] = got[k][:, at : at + width]
            done[k, i, :, :LANES] += left[first + i]
            done[k, i, :, width - LANES :] += right[first + i]
        copies.append(pltpu.make_async_copy(done.at[k], out.at[pl.ds(first, per_device)], sems.at[k]))
        copies[-1].start()
    for copy in copies:
        copy.wait()


def finish(taps, parts, layers, width):
    count = len(parts)
    per_device = layers // count
    rows = count // 2 * ROWS
    edges = parts[0].shape[1] - per_device * width
    spread = math.ceil(layers * SPAN / LANES) * LANES
    return pl.pallas_call(
        functools.partial(finish_kernel, count, per_device, width),
        in_specs=[VMEM] * (1 + count),
        out_specs=ANY,
        out_shape=f32(layers, ROWS, width),
        scratch_shapes=[
            pltpu.VMEM((count, ROWS, edges), jnp.float32),
            pltpu.VMEM((3 * rows, spread), jnp.bfloat16),
            pltpu.VMEM((count, ROWS, spread), jnp.float32),
            pltpu.VMEM((layers, ROWS, LANES), jnp.float32),
            pltpu.VMEM((layers, ROWS, LANES), jnp.float32),
            pltpu.VMEM((count, per_device, ROWS, width), jnp.float32),
            pltpu.SemaphoreType.DMA((count,)),
        ],
        compiler_params=params(),
    )(taps, *parts[::-1])


def spread(parts):
    count = len(parts)
    got = list(parts)
    for k in range(count - 1, 0, -1):
        got[k] = lax.ppermute(parts[k], "gx", [(i, i ^ k) for i in range(count)])
    return got


def on_device(efield, hfield, forward, material, permit, design_mask, grad_sum):
    layers, _, width = grad_sum.shape
    efield, hfield = load(efield, hfield)
    zfaces, xfaces = halos(efield, hfield)
    forward, own_low, own_high, mask, inv = strips(
        permit, efield, hfield, forward, material, grad_sum, design_mask
    )
    arrays = (efield, hfield, forward, inv, grad_sum, mask)
    edges = own_edges(arrays)
    shares, own = own_gradient(arrays, zfaces, xfaces)
    got = spread(shares)
    yfaces = exchange(y_faces(own_low, own_high, zfaces, xfaces, own), "gy", "gz")
    message, edge = edge_gradient(own, edges, zfaces, xfaces, yfaces)
    taps = jnp.asarray(cone_matrix(len(got) // 2 * ROWS))
    parts = cone_filter(taps, message, got, layers // len(got), width)
    e_next, h_next, grad_total = step(efield, hfield, inv, own, edge, zfaces, xfaces, yfaces, parts[0])
    return e_next, h_next, grad_total, finish(taps, spread(parts), layers, width)


def solution(mesh):
    field = P(None, "gz", "gx", "gy")
    cells = P("gz", "gx", "gy")
    return jax.shard_map(
        on_device,
        mesh=mesh,
        in_specs=(field, field, field, cells, P(), P("gx", "gy"), cells),
        out_specs=(field, field, cells, cells),
        check_vma=False,
    )
```

```python
import functools
import math

import jax
import jax.numpy as jnp
import numpy as np
from jax import lax
from jax.experimental import pallas as pl
from jax.experimental.pallas import tpu as pltpu
from jax.sharding import PartitionSpec as P

RADIUS = 6
BLOCK = 8
HALF = 0.5

ROWS = 8
LANES = 128
STRIP = 8
SLOTS = LANES // STRIP
MIB = 1024 * 1024

VMEM = pl.BlockSpec(memory_space=pltpu.VMEM)
SMEM = pl.BlockSpec(memory_space=pltpu.SMEM)
ANY = pl.BlockSpec(memory_space=pl.ANY)


def params(mib=24):
    return pltpu.CompilerParams(vmem_limit_bytes=mib * MIB)


def f32(*shape):
    return jax.ShapeDtypeStruct(shape, jnp.float32)


def fast(*shape):
    return pltpu.VMEM(shape, jnp.float32)


def rounds(axis):
    return 2 if lax.axis_size(axis) > 2 else 1


def exchange(sends, axis, mate):
    count = lax.axis_size(axis)
    beside = lax.axis_size(mate)
    if count == 1:
        return sends
    got = []
    for start, value in enumerate(sends):
        partner = list(range(count))
        for low in range(start, count - 1, 2):
            partner[low], partner[low + 1] = low + 1, low
        axes = sorted((axis, mate))
        steps = (beside, 1) if axes[0] == axis else (1, count)
        pairs = []
        for i in range(count):
            for m in range(beside):
                if partner[i] != i:
                    to = (partner[i], m)
                elif beside % 2 == 0:
                    to = (i, m ^ 1)
                else:
                    continue
                pairs.append((i * steps[0] + m * steps[1], to[0] * steps[0] + to[1] * steps[1]))
        got.append(lax.ppermute(value, tuple(axes), pairs))
    return got


def exchange_diagonal(sends):
    along_x, along_y, along_z = (lax.axis_size(axis) for axis in AXES)

    def flat(x, y, z):
        return (x * along_y + y) * along_z + z

    got = []
    for start, value in enumerate(sends):
        partner = {}
        for low in range(start, along_z - 1, 2):
            for x in range(1, along_x):
                partner[x, low] = (x - 1, low + 1)
                partner[x - 1, low + 1] = (x, low)
        pairs = []
        for x in range(along_x):
            for z in range(along_z):
                for y in range(along_y):
                    if (x, z) in partner:
                        to = partner[x, z]
                        pairs.append((flat(x, y, z), flat(to[0], y, to[1])))
                    elif along_y % 2 == 0:
                        pairs.append((flat(x, y, z), flat(x, y ^ 1, z)))
        got.append(lax.ppermute(value, AXES, pairs))
    return got


AXES = ("gx", "gy", "gz")


class Side:
    def __init__(self, axis):
        index = lax.axis_index(axis)
        self.rounds = rounds(axis)
        self.odd = index % 2 == 1
        self.bottom = index == 0
        self.top = index == lax.axis_size(axis) - 1

    def sends(self, low, high):
        both = [jnp.where(self.odd, low, high)]
        if self.rounds > 1:
            both.append(jnp.where(self.odd, high, low))
        return both

    def lower(self, got):
        return jnp.where(self.bottom, 0.0, jnp.where(self.odd, got[0], got[-1]))

    def upper(self, got):
        return jnp.where(self.top, 0.0, jnp.where(self.odd, got[-1], got[0]))


def first_layer(cells_z, layers):
    return (cells_z - layers) * (1 - lax.axis_index("gz"))


def faces_kernel(x_rounds, e_ref, h_ref, *refs):
    x_sends, (low_ref, rows_ref) = refs[:x_rounds], refs[-2:]
    others = refs[x_rounds:-2]
    z_sends, d_sends = others[: len(others) // 2], others[len(others) // 2 :]
    cells_z = e_ref.shape[1]
    last, top = ROWS - 1, cells_z - 1

    low_ref[2 * cells_z :, :] = jnp.zeros_like(low_ref[2 * cells_z :, :])
    rows_ref[5, top : top + 1, :] = jnp.zeros_like(rows_ref[5, top : top + 1, :])
    for z in range(cells_z):
        low_ref[z : z + 1, :] = e_ref[1, z, 0:1, :]
        low_ref[cells_z + z : cells_z + z + 1, :] = e_ref[2, z, 0:1, :]
        for c in range(3):
            rows_ref[c, z : z + 1, :] = e_ref[c, z, last : last + 1, :]
        for c in range(2):
            rows_ref[3 + c, z : z + 1, :] = h_ref[1 + c, z, last : last + 1, :]
        if z > 0:
            rows_ref[5, z - 1 : z, :] = e_ref[0, z, last : last + 1, :]
    ex = rows_ref[0]
    high = (
        rows_ref[3] - HALF * (rows_ref[5] - ex + rows_ref[2]),
        rows_ref[4] + HALF * rows_ref[1] - HALF * ex,
        ex,
    )
    side = Side("gx")
    for c in range(3):
        here = slice(c * cells_z, (c + 1) * cells_z)
        for ref, value in zip(x_sends, side.sends(low_ref[here, :], high[c])):
            ref[here, :] = value

    side = Side("gz")
    ex, ey, ez = (e_ref[c, top] for c in range(3))
    low = (e_ref[0, 0], e_ref[1, 0], jnp.zeros_like(ez))
    high = (h_ref[0, top] + HALF * ez - HALF * ey, h_ref[1, top] + HALF * ex - HALF * ez, ez)
    for c in range(3):
        for ref, value in zip(z_sends, side.sends(low[c], high[c])):
            ref[c] = value

    down, up = (
        jnp.broadcast_to(line, (ROWS, line.shape[1]))
        for line in (e_ref[0, 0, last : last + 1, :], e_ref[2, top, 0:1, :])
    )
    for ref, value in zip(d_sends, side.sends(down, up)):
        ref[...] = value


def halos(efield, hfield):
    _, cells_z, cells_x, cells_y = efield.shape
    x_rounds, z_rounds = rounds("gx"), rounds("gz")
    x_face, z_face, line = fast(3 * cells_z, cells_y), fast(3, cells_x, cells_y), fast(ROWS, cells_y)
    sends = pl.pallas_call(
        functools.partial(faces_kernel, x_rounds),
        in_specs=[VMEM] * 2,
        out_specs=[VMEM] * (x_rounds + 2 * z_rounds),
        out_shape=[x_face] * x_rounds + [z_face] * z_rounds + [line] * z_rounds,
        scratch_shapes=[
            pltpu.VMEM(x_face.shape, jnp.float32),
            pltpu.VMEM((6, cells_z, cells_y), jnp.float32),
        ],
        compiler_params=params(),
    )(efield, hfield)
    xfaces = exchange(sends[:x_rounds], "gx", "gy")
    zfaces = exchange(sends[x_rounds : x_rounds + z_rounds], "gz", "gy")
    return zfaces, xfaces, exchange_diagonal(sends[x_rounds + z_rounds :])


def lane_group():
    return lax.broadcasted_iota(jnp.int32, (ROWS, LANES), 1) // STRIP


def pack_strips(tiles, low_ref, high_ref, first):
    group = lane_group()
    width = tiles[0][1]
    for start in range(0, len(tiles), SLOTS):
        low = jnp.zeros((ROWS, LANES), jnp.float32)
        high = jnp.zeros((ROWS, LANES), jnp.float32)
        for k, (load, _) in enumerate(tiles[start : start + SLOTS]):
            if load is None:
                continue
            here = group == k
            shift = (STRIP * k) % LANES
            left = load(slice(0, LANES))
            right = load(slice(width - LANES, width))
            low = jnp.where(here, pltpu.roll(left, shift, 1) if shift else left, low)
            shift = (STRIP * k + STRIP) % LANES
            high = jnp.where(here, pltpu.roll(right, shift, 1) if shift else right, high)
        low_ref[first + start // SLOTS] = low
        high_ref[first + start // SLOTS] = high


def load_kernel(e_in, h_in, e_ref, h_ref, sems):
    parts = [(source.at[c], target.at[c]) for source, target in ((e_in, e_ref), (h_in, h_ref)) for c in range(3)]
    copies = [pltpu.make_async_copy(*part, sems.at[n]) for n, part in enumerate(parts)]
    for copy in copies:
        copy.start()
    for copy in copies:
        copy.wait()


def load(*fields):
    return pl.pallas_call(
        load_kernel,
        in_specs=[ANY] * 2,
        out_specs=[VMEM] * 2,
        out_shape=[fast(*one.shape) for one in fields],
        scratch_shapes=[pltpu.SemaphoreType.DMA((6,))],
        compiler_params=params(56),
    )(*fields)


def strips_kernel(
    permit_ref, e_ref, h_ref, f_in, mat_ref, grad_ref, mask_ref, f_ref, low_ref, high_ref, wide_ref, inv_ref, sems
):
    cells_z, width = e_ref.shape[1], e_ref.shape[3]
    layers = grad_ref.shape[0]
    blocks = mask_ref.shape[1]
    copies = [pltpu.make_async_copy(f_in.at[c], f_ref.at[c], sems.at[c]) for c in range(3)]
    for copy in copies:
        copy.start()

    inverse = [
        jnp.broadcast_to(HALF * (1.0 / permit_ref[0:1, m : m + 1]), (ROWS, width))
        for m in range(permit_ref.shape[1])
    ]
    for z in range(cells_z):
        inv = inverse[0]
        for m in range(1, len(inverse)):
            inv = jnp.where(mat_ref[z] == m, inverse[m], inv)
        inv_ref[z] = inv
    spread = (
        lax.broadcasted_iota(jnp.int32, (blocks, width), 0)
        == lax.broadcasted_iota(jnp.int32, (blocks, width), 1) // BLOCK
    ).astype(jnp.float32)
    mask = jnp.broadcast_to(mask_ref[...].astype(jnp.float32), (ROWS, blocks))
    wide_ref[...] = jnp.dot(mask, spread, preferred_element_type=jnp.float32)
    first = first_layer(cells_z, layers)
    tiles = []
    for z in range(cells_z):
        for ref in (e_ref, h_ref):
            for c in range(3):
                tiles.append((lambda s, r=ref, c=c, z=z: r[c, z, :, s], width))
    pack_strips(tiles, low_ref, high_ref, 0)

    for copy in copies:
        copy.wait()
    done = len(tiles) // SLOTS
    tiles = []
    for layer in range(layers):
        for c in range(3):
            tiles.append((lambda s, c=c, l=layer: f_ref[c, first + l, :, s], width))
        tiles.append((lambda s, l=layer: inv_ref[first + l, :, s], width))
        tiles.append((lambda s, l=layer: grad_ref[l, :, s], width))
        tiles.append((lambda s: wide_ref[:, s], width) if layer % ROWS == 0 else (None, width))
    pack_strips(tiles, low_ref, high_ref, done)


def strips(permit, efield, hfield, forward, material, grad_sum, mask):
    cells_z, width = efield.shape[1], efield.shape[3]
    count = (cells_z * 6 + grad_sum.shape[0] * 6) // SLOTS
    packed = (count, ROWS, LANES)
    shapes = (forward.shape, packed, packed, (ROWS, width), material.shape)
    return pl.pallas_call(
        strips_kernel,
        in_specs=[VMEM] * 3 + [ANY] + [VMEM] * 3,
        out_specs=[VMEM] * 5,
        out_shape=[fast(*shape) for shape in shapes],
        scratch_shapes=[pltpu.SemaphoreType.DMA((3,))],
        compiler_params=params(40),
    )(permit.reshape(1, -1), efield, hfield, forward, material, grad_sum, mask)


def edge_tile(load, width):
    lane = lax.broadcasted_iota(jnp.int32, (ROWS, LANES), 1)
    head = pltpu.roll(load(slice(0, LANES)), STRIP, 1)
    tail = pltpu.roll(load(slice(width - LANES, width)), LANES - STRIP, 1)
    return jnp.where(lane < LANES // 2, head, tail)


def edges_kernel(e_ref, h_ref, f_ref, inv_ref, grad_ref, mask_ref, eh_out, grad_out, mask_out):
    cells_z, width = e_ref.shape[1], e_ref.shape[3]
    layers = grad_ref.shape[0]
    first = first_layer(cells_z, layers)
    for z in range(cells_z):
        for c in range(3):
            eh_out[z, c] = edge_tile(lambda s: e_ref[c, z, :, s], width)
            eh_out[z, 3 + c] = edge_tile(lambda s: h_ref[c, z, :, s], width)
    for layer in range(layers):
        for c in range(3):
            grad_out[layer, c] = edge_tile(lambda s: f_ref[c, first + layer, :, s], width)
        grad_out[layer, 3] = edge_tile(lambda s: inv_ref[first + layer, :, s], width)
        grad_out[layer, 4] = edge_tile(lambda s: grad_ref[layer, :, s], width)
    mask_out[...] = edge_tile(lambda s: mask_ref[:, s], width)


def own_edges(arrays):
    cells_z, layers = arrays[0].shape[1], arrays[4].shape[0]
    return pl.pallas_call(
        edges_kernel,
        in_specs=[VMEM] * 6,
        out_specs=[VMEM] * 3,
        out_shape=[fast(cells_z, 6, ROWS, LANES), fast(layers, 5, ROWS, LANES), fast(ROWS, LANES)],
        compiler_params=params(),
    )(*arrays)


def corner_lines(lines, s):
    z_side, x_side = Side("gz"), Side("gx")
    above = jnp.where(x_side.bottom, 0.0, z_side.upper([f[:, s] for f in lines]))
    beyond = jnp.where(x_side.top, 0.0, z_side.lower([f[:, s] for f in lines]))
    return above, beyond


def face_tiles(zfaces, xfaces, lines):
    width = xfaces[0].shape[1]
    rows = xfaces[0].shape[0]
    cells_z = rows // 3
    z_side, x_side = Side("gz"), Side("gx")

    def corner(s):
        row = lax.broadcasted_iota(jnp.int32, (ROWS, s.stop - s.start), 0)
        return jnp.where(row == ROWS - 1, -HALF * corner_lines(lines, s)[0], 0.0)

    def x_tile(pick, t, s):
        value = pick([f[t : t + ROWS, s] for f in xfaces])
        return value + corner(s) if lines and t == cells_z - ROWS and pick == x_side.lower else value

    tiles = []
    for c in range(3):
        tiles.append((lambda s, c=c: z_side.lower([f[c, :, s] for f in zfaces]), width))
    for c in range(2):
        tiles.append((lambda s, c=c: z_side.upper([f[c, :, s] for f in zfaces]), width))
    for t in range(0, rows, ROWS):
        tiles.append((lambda s, t=t: x_tile(x_side.lower, t, s), width))
    for t in range(0, rows, ROWS):
        if lines and t == 2 * cells_z:
            tiles.append((lambda s: corner_lines(lines, s)[1], width))
        else:
            tiles.append((lambda s, t=t: x_tile(x_side.upper, t, s), width))
    return tiles


def face_count(xface):
    return 5 + 2 * (xface.shape[0] // ROWS)


def y_faces_kernel(counts, *refs):
    own_low, own_high = refs[:2]
    ends = np.cumsum((2,) + counts)
    zfaces, xfaces, lines = (refs[i:j] for i, j in zip(ends[:-1], ends[1:]))
    sends, (low_ref, high_ref) = refs[3 + sum(counts) : -2], refs[-2:]
    own = own_low.shape[0]
    pack_strips(face_tiles(zfaces, xfaces, lines), low_ref, high_ref, 0)
    side = Side("gy")
    for ref, value in zip(sends, side.sends(own_low[...], own_high[...])):
        ref[0:own] = value
    for ref, value in zip(sends, side.sends(low_ref[...], high_ref[...])):
        ref[own:] = value


def y_faces(own_low, own_high, zfaces, xfaces, lines, after):
    extra = math.ceil(face_count(xfaces[0]) / SLOTS)
    packed = fast(own_low.shape[0] + extra, ROWS, LANES)
    return pl.pallas_call(
        functools.partial(y_faces_kernel, (len(zfaces), len(xfaces), len(lines))),
        in_specs=[VMEM] * (2 + len(zfaces) + len(xfaces) + len(lines)) + [ANY],
        out_specs=[VMEM] * rounds("gy"),
        out_shape=[packed] * rounds("gy"),
        scratch_shapes=[pltpu.VMEM((extra, ROWS, LANES), jnp.float32)] * 2,
        compiler_params=params(),
    )(own_low, own_high, *zfaces, *xfaces, *lines, after)


OWN, CIRCLE, EDGE = range(3)


def faces_wide(mode, width):
    return {OWN: width, CIRCLE: width + LANES, EDGE: LANES}[mode]


class Fields:
    def __init__(self, mode, layers, fields, zfaces, xfaces, lines, yfaces, scratch):
        self.mode = mode
        self.fields = fields
        if mode == EDGE:
            self.cells_z, self.width = fields.shape[0], xfaces[0].shape[1]
        else:
            self.cells_z, self.width = fields[0].shape[1], fields[0].shape[3]
        self.wide = faces_wide(mode, self.width)
        self.lane = lax.broadcasted_iota(jnp.int32, (ROWS, LANES), 1)
        self.row = lax.broadcasted_iota(jnp.int32, (ROWS, self.wide), 0)
        self.per_group = 6 * ROWS // SLOTS
        self.groups = self.cells_z // ROWS
        self.grad_base = self.per_group * self.groups
        halo_base = self.grad_base + self.per_group * (layers // ROWS)
        self.left_wide, self.right_wide = left_wide, right_wide = scratch[:2]
        if mode != OWN:
            self.ybuf = scratch[2]
            y_side = Side("gy")
            for t in range(yfaces[0].shape[0]):
                lower = y_side.lower([f[t] for f in yfaces])
                upper = y_side.upper([f[t] for f in yfaces])
                if mode == EDGE:
                    even = self.lane // STRIP % 2 == 0
                    lower, upper = (
                        jnp.where(even, upper, pltpu.roll(lower, STRIP, 1)),
                        jnp.where(even, pltpu.roll(upper, LANES - STRIP, 1), lower),
                    )
                self.ybuf[0, t] = lower
                self.ybuf[1, t] = upper

        def face(load, slot):
            if mode == EDGE:
                own = edge_tile(load, self.width)
                return self.edge(own, halo_base + slot // SLOTS, slot % SLOTS)
            return self.wider(load, halo_base + slot // SLOTS, slot % SLOTS)

        full = [face(load, slot) for slot, (load, _) in enumerate(face_tiles(zfaces, xfaces, lines))]
        self.below, self.above = full[:3], full[3:5]
        per_face = xfaces[0].shape[0] // ROWS
        for t in range(per_face):
            left_wide[t * ROWS : (t + 1) * ROWS, :] = full[5 + t]
            right_wide[t * ROWS : (t + 1) * ROWS, :] = full[5 + per_face + t]
        cells_z = self.cells_z
        left_wide[cells_z : 2 * cells_z, :] += HALF * self.y_up(left_wide[2 * cells_z : 3 * cells_z, :])

    def wider(self, load, tile, k):
        if self.mode == OWN:
            return load(slice(0, self.width))

        def moved(v, to):
            shift = (to - STRIP * k) % LANES
            return pltpu.roll(v, shift, 1) if shift else v

        lower, upper = self.ybuf[0, tile], self.ybuf[1, tile]
        halo = jnp.where(self.lane < STRIP, moved(upper, 0), moved(lower, LANES - STRIP))
        return jnp.concatenate([load(slice(0, self.width)), halo], axis=1)

    def edge(self, own, tile, k):
        shift = (LANES - STRIP - 2 * STRIP * (k // 2)) % LANES
        both = pltpu.roll(self.ybuf[k % 2, tile], shift, 1)
        inside = jnp.logical_and(self.lane >= STRIP, self.lane < LANES - STRIP)
        return jnp.where(inside, own, both)

    def y_up(self, v):
        return pltpu.roll(v, self.wide - 1, 1)

    def y_down(self, v):
        return pltpu.roll(v, 1, 1)

    def x_up(self, v, line):
        return jnp.where(self.row == ROWS - 1, line, pltpu.roll(v, ROWS - 1, 0))

    def x_down(self, v, line):
        return jnp.where(self.row == 0, line, pltpu.roll(v, 1, 0))

    def line(self, ref, at):
        return jnp.broadcast_to(ref[pl.ds(at, 1), :], (ROWS, self.wide))

    def field(self, which, c, a, b):
        slot = 6 * b + 3 * which + c
        tile = self.per_group * a + slot // SLOTS
        if self.mode == EDGE:
            return self.edge(self.fields[ROWS * a + b, 3 * which + c], tile, slot % SLOTS)
        ref = self.fields[which]
        return self.wider(lambda s: ref[c, ROWS * a + b, :, s], tile, slot % SLOTS)

    def hx(self, a, b, ey, ez, ey_next):
        return self.field(1, 0, a, b) - HALF * (self.y_up(ez) - ez - ey_next + ey)

    def hy(self, a, b, ex, ez, ex_next):
        up = self.x_up(ez, self.line(self.right_wide, self.cells_z + ROWS * a + b))
        return self.field(1, 1, a, b) - HALF * (ex_next - ex - up + ez)

    def hz(self, a, b, ex, ey):
        up = self.x_up(ey, self.line(self.right_wide, ROWS * a + b))
        return self.field(1, 2, a, b) - HALF * (up - ey - self.y_up(ex) + ex)

    def start(self, a):
        ex, ey = self.field(0, 0, a, 0), self.field(0, 1, a, 0)
        below = self.below
        at_bottom = (
            below[0] - HALF * self.y_up(below[2]) + HALF * ey,
            below[1] - HALF * ex + HALF * self.x_up(below[2], self.line(self.right_wide, 2 * self.cells_z)),
        )
        before, b = jnp.maximum(a - 1, 0), ROWS - 1
        ex_before, ey_before, ez_before = (self.field(0, c, before, b) for c in range(3))
        inside = (
            self.hx(before, b, ey_before, ez_before, ey),
            self.hy(before, b, ex_before, ez_before, ex),
        )
        bottom = a == 0
        return (ex, ey) + tuple(jnp.where(bottom, one, two) for one, two in zip(at_bottom, inside))

    def group(self, a, carry, emit):
        ex, ey, hx_z, hy_z = carry
        for b in range(ROWS):
            z = ROWS * a + b
            ez = self.field(0, 2, a, b)
            if b < ROWS - 1:
                ex_next, ey_next = (self.field(0, c, a, b + 1) for c in range(2))
            else:
                end = a == self.groups - 1
                after = jnp.minimum(a + 1, self.groups - 1)
                ex_next, ey_next = (
                    jnp.where(end, self.above[c], self.field(0, c, after, 0)) for c in range(2)
                )
            hx = self.hx(a, b, ey, ez, ey_next)
            hy = self.hy(a, b, ex, ez, ex_next)
            hz = self.hz(a, b, ex, ey)
            hy_x = self.x_down(hy, self.line(self.left_wide, z) + HALF * ez)
            hz_x = self.x_down(hz, self.line(self.left_wide, self.cells_z + z) - HALF * ey)
            curl = (
                (hz - self.y_down(hz)) - (hy - hy_z),
                (hx - hx_z) - (hz - hz_x),
                (hy - hy_x) - (hx - self.y_down(hx)),
            )
            emit(a, b, (ex, ey, ez), (hx, hy, hz), curl)
            ex, ey, hx_z, hy_z = ex_next, ey_next, hx, hy
        return ex, ey, hx_z, hy_z

    def gradient(self, layers, arrays, store):
        first = first_layer(self.cells_z, layers)
        first_group = first // ROWS
        if self.mode == EDGE:
            grad_edges, mask_ref = arrays
            mask = self.edge(mask_ref[...], self.grad_base, 5)
        else:
            f_ref, inv_ref, grad_ref, mask_ref = arrays
            mask = mask_ref[...]

        def emit(a, b, efield, hfield, curl):
            z = ROWS * a + b
            layer = z - first
            if self.mode == EDGE:
                tile = self.grad_base + self.per_group * (a - first_group)
                slots = [6 * b + n for n in range(5)]
                values = [
                    self.edge(grad_edges[layer, n], tile + slot // SLOTS, slot % SLOTS)
                    for n, slot in enumerate(slots)
                ]
            else:
                values = [f_ref[c, z] for c in range(3)] + [inv_ref[z], grad_ref[layer]]
            total = None
            for c in range(3):
                term = values[c] * (efield[c] + values[3] * curl[c])
                total = term if total is None else total + term
            store(layer, values[4] + mask * total)

        def body(i, carry):
            return self.group(first_group + i, carry, emit)

        lax.fori_loop(0, layers // ROWS, body, self.start(first_group))


def fields_scratch(mode, xface, yface, width):
    rows, wide = xface.shape[0], faces_wide(mode, width)
    out = [pltpu.VMEM((rows, wide), jnp.float32)] * 2
    if mode != OWN:
        out.append(pltpu.VMEM((2,) + yface.shape, jnp.float32))
    return out


def own_gradient_kernel(counts, per_device, *refs):
    e_ref, h_ref, f_ref, inv_ref, grad_ref, mask_ref = refs[:6]
    zfaces, xfaces = refs[6 : 6 + counts[0]], refs[6 + counts[0] : 6 + sum(counts)]
    shares, (own_ref, *scratch) = refs[6 + sum(counts) : -3][::-1], refs[-3:]
    layers, _, width = grad_ref.shape
    fields = Fields(OWN, layers, (e_ref, h_ref), zfaces, xfaces, (), None, scratch)

    def store(layer, value):
        own_ref[layer] = value

    fields.gradient(layers, (f_ref, inv_ref, grad_ref, mask_ref), store)

    me = lax.axis_index("gx")
    for k, share in enumerate(shares):
        chunk = lax.bitwise_xor(me, k)
        for i in range(per_device):
            share[:, i * width : (i + 1) * width] = own_ref[chunk * per_device + i]


def own_gradient(arrays, zfaces, xfaces):
    layers, _, width = arrays[4].shape
    count = lax.axis_size("gx")
    per_device = layers // count
    *shares, own = pl.pallas_call(
        functools.partial(own_gradient_kernel, (len(zfaces), len(xfaces)), per_device),
        in_specs=[VMEM] * (6 + len(zfaces) + len(xfaces)),
        out_specs=[VMEM] * (count + 1),
        out_shape=[fast(ROWS, per_device * width)] * count + [fast(layers, ROWS, width)],
        scratch_shapes=fields_scratch(OWN, xfaces[0], None, width),
        compiler_params=params(),
    )(*arrays, *zfaces, *xfaces)
    return shares[::-1], own


PART = 2 * STRIP


def edge_gradient_kernel(counts, *refs):
    own_ref, f_ref, inv_ref, wide_ref, eh_ref, grad_ref, mask_ref = refs[:7]
    ends = np.cumsum((7,) + counts)
    zfaces, xfaces, lines, yfaces = (refs[i:j] for i, j in zip(ends[:-1], ends[1:]))
    (message, edge_ref), scratch = refs[ends[-1] : -3], refs[-3:]
    layers, _, width = own_ref.shape
    lane = lax.broadcasted_iota(jnp.int32, (ROWS, LANES), 1)
    first, last = STRIP, LANES - STRIP - 1
    fields = Fields(EDGE, layers, eh_ref, zfaces, xfaces, lines, yfaces, scratch)

    def store(layer, value):
        edge_ref[layer] = value

    fields.gradient(layers, (grad_ref, mask_ref), store)

    per_tile = LANES // PART
    for start in range(0, layers, per_tile):
        packed = jnp.zeros((ROWS, LANES), jnp.float32)
        for j in range(min(per_tile, layers - start)):
            layer = start + j
            edge = edge_ref[layer]
            own = edge_tile(lambda s: own_ref[layer, :, s], width)
            more = jnp.where(jnp.logical_or(lane == first, lane == last), edge - own, edge)
            left = pltpu.roll(more, (PART * j - 1) % LANES, 1)
            right = pltpu.roll(more, (PART * j + STRIP - last) % LANES, 1)
            packed = jnp.where(lane // STRIP == 2 * j, left, packed)
            packed = jnp.where(lane // STRIP == 2 * j + 1, right, packed)
        message[:, start // per_tile * LANES : (start // per_tile + 1) * LANES] = packed

    tail = math.ceil(layers / per_tile) * LANES
    message[:, tail:] = jnp.zeros_like(message[:, tail:])
    top, last = fields.cells_z - 1, ROWS - 1
    above, beyond = (line[0:1] for line in corner_lines(lines, slice(0, width)))
    added = wide_ref[0:1, :] * f_ref[2, top, 0:1, :] * inv_ref[top, 0:1, :] * (HALF * above)
    added += wide_ref[last:, :] * f_ref[0, 0, last:, :] * inv_ref[0, last:, :] * (HALF * beyond)
    column = lax.broadcasted_iota(jnp.int32, (1, width), 1)
    added = jnp.where(jnp.logical_or(column == 0, column == width - 1), 0.0, added)
    for at, n in line_places(width):
        message[n : n + 1, tail + at : tail + at + LANES] = added[:, (at // LANES * ROWS + n) * LANES :][:, :LANES]


def line_places(width):
    return [(t // ROWS * LANES, t % ROWS) for t in range(width // LANES)]


def line_of(message, width):
    tail = message.shape[1] - math.ceil(width / LANES / ROWS) * LANES
    return jnp.concatenate([message[n : n + 1, tail + at : tail + at + LANES] for at, n in line_places(width)], axis=1)


def line_spot(layers):
    bottom = lax.axis_index("gz") == 0
    return jnp.where(bottom, layers - 1, 0), jnp.where(bottom, 0, ROWS - 1)


def edge_gradient(own, arrays, edges, zfaces, xfaces, lines, yfaces):
    layers, _, width = own.shape
    faces = (*zfaces, *xfaces, *lines, *yfaces)
    tiles = math.ceil(layers * PART / LANES) + math.ceil(width / LANES / ROWS)
    return pl.pallas_call(
        functools.partial(edge_gradient_kernel, (len(zfaces), len(xfaces), len(lines), len(yfaces))),
        in_specs=[VMEM] * (7 + len(faces)),
        out_specs=[VMEM] * 2,
        out_shape=[fast(ROWS, tiles * LANES), fast(layers, ROWS, LANES)],
        scratch_shapes=fields_scratch(EDGE, xfaces[0], yfaces[0], width),
        compiler_params=params(),
    )(own, arrays[2], arrays[3], arrays[5], *edges, *faces)


def step_kernel(counts, *refs):
    e_ref, h_ref, inv_ref, own_ref, edge_ref, message = refs[:6]
    ends = np.cumsum((6,) + counts)
    zfaces, xfaces, lines, yfaces = (refs[i:j] for i, j in zip(ends[:-1], ends[1:]))
    e_out, h_out, grad_out = refs[ends[-1] + 1 : ends[-1] + 4]
    left_wide, right_wide, ybuf, e_new, h_new, grad_new, sems = refs[ends[-1] + 4 :]
    layers, _, width = own_ref.shape
    lane = lax.broadcasted_iota(jnp.int32, (ROWS, LANES), 1)

    for layer in range(layers):
        edge = edge_ref[layer]
        head, tail = own_ref[layer, :, 0:LANES], own_ref[layer, :, width - LANES :]
        grad_new[layer] = own_ref[layer]
        grad_new[layer, :, 0:LANES] = jnp.where(lane == 0, pltpu.roll(edge, LANES - STRIP, 1), head)
        grad_new[layer, :, width - LANES :] = jnp.where(lane == LANES - 1, pltpu.roll(edge, STRIP, 1), tail)
    layer, spot = line_spot(layers)
    row = lax.broadcasted_iota(jnp.int32, (ROWS, width), 0)
    grad_new[layer] += jnp.where(row == spot, line_of(message, width), 0.0)
    grad_copy = pltpu.make_async_copy(grad_new, grad_out, sems.at[0, 0])
    grad_copy.start()

    fields = Fields(CIRCLE, layers, (e_ref, h_ref), zfaces, xfaces, lines, yfaces, (left_wide, right_wide, ybuf))

    def emit(a, b, efield, hfield, curl):
        z = ROWS * a + b
        half_inv = inv_ref[z]
        for c in range(3):
            e_new[c, z] = efield[c][:, :width] + half_inv * curl[c][:, :width]
            h_new[c, z] = hfield[c][:, :width]

    def copies(a):
        here = pl.ds(a * ROWS, ROWS)
        return [
            pltpu.make_async_copy(new.at[c, here], out.at[c, here], sems.at[1 + a, 3 * n + c])
            for n, (new, out) in enumerate(((e_new, e_out), (h_new, h_out)))
            for c in range(3)
        ]

    def body(a, carry):
        carry = fields.group(a, carry, emit)
        for copy in copies(a):
            copy.start()
        return carry

    lax.fori_loop(0, fields.groups, body, fields.start(0))
    for a in range(fields.groups):
        for copy in copies(a):
            copy.wait()
    grad_copy.wait()


def step(efield, hfield, inv, own, edge, message, zfaces, xfaces, lines, yfaces, after):
    _, cells_z, _, width = efield.shape
    groups = (zfaces, xfaces, lines, yfaces)
    counts = tuple(len(group) for group in groups)
    shapes = (efield.shape, hfield.shape, own.shape)
    return pl.pallas_call(
        functools.partial(step_kernel, counts),
        in_specs=[VMEM] * (6 + sum(counts)) + [ANY],
        out_specs=[ANY] * 3,
        out_shape=[f32(*shape) for shape in shapes],
        scratch_shapes=fields_scratch(CIRCLE, xfaces[0], yfaces[0], width)
        + [pltpu.VMEM(shape, jnp.float32) for shape in shapes]
        + [pltpu.SemaphoreType.DMA((1 + cells_z // ROWS, 6))],
        compiler_params=params(),
    )(efield, hfield, inv, own, edge, message, *(one for group in groups for one in group), after)


def cone_matrix(rows):
    span = np.arange(-RADIUS, RADIUS + 1, dtype=np.float64)
    cone = np.maximum(RADIUS - np.sqrt(span[:, None] ** 2 + span[None, :] ** 2), 0.0)
    weight = cone / cone.sum()
    x = np.arange(rows)
    out = np.zeros((RADIUS + 1, rows, rows))
    for b in range(RADIUS + 1):
        for apart in (x[:, None] - x[None, :], 2 * rows - 1 - x[:, None] - x[None, :]):
            near = np.abs(apart) <= RADIUS
            out[b] += np.where(near, weight[np.clip(apart, -RADIUS, RADIUS) + RADIUS, RADIUS + b], 0.0)
    out = out.reshape((RADIUS + 1) * rows, rows).astype(np.float32)
    high = out.astype(jnp.bfloat16)
    low = (out - high.astype(np.float32)).astype(jnp.bfloat16)
    return np.concatenate([high, low, high], axis=1)


def flip_rows(v):
    row = lax.broadcasted_iota(jnp.int32, v.shape, 0)
    v = pltpu.roll(v, 4, 0)
    v = jnp.where(row % 4 < 2, pltpu.roll(v, ROWS - 2, 0), pltpu.roll(v, 2, 0))
    return jnp.where(row % 2 < 1, pltpu.roll(v, ROWS - 1, 0), pltpu.roll(v, 1, 0))


def split_rows(symmetric, parts):
    rows = symmetric.shape[0]
    high = symmetric.astype(jnp.bfloat16)
    low = (symmetric - high.astype(jnp.float32)).astype(jnp.bfloat16)
    parts[0:rows, :] = high
    parts[rows : 2 * rows, :] = high
    parts[2 * rows : 3 * rows, :] = low


def cone(taps_ref, parts, rows):
    wide = parts.shape[1]
    mixed = jnp.dot(taps_ref[...], parts[...], preferred_element_type=jnp.float32)
    total = mixed[0:rows]
    for b in range(1, RADIUS + 1):
        part = mixed[b * rows : (b + 1) * rows]
        total = total + (pltpu.roll(part, b, 1) + pltpu.roll(part, wide - b, 1))
    return total


def filter_kernel(count, per_device, width, *refs):
    taps_ref, edges_ref = refs[:2]
    got = refs[count + 1 : 1 : -1]
    outs = refs[2 + count : 2 + 2 * count]
    slabs, parts, done = refs[2 + 2 * count :]
    me = lax.axis_index("gx")
    half = count // 2
    rows = half * ROWS
    for k in range(count):
        slabs[lax.bitwise_xor(me, k)] = got[k][...]

    side = jnp.zeros((rows, LANES), jnp.float32)
    for i in range(per_device):
        here = slice(i * width, (i + 1) * width)
        halves = [slabs[s, :, here] + flip_rows(slabs[count - 1 - s, :, here]) for s in range(half)]
        split_rows(jnp.concatenate([jnp.concatenate(halves, axis=0), side], axis=1), parts)
        total = cone(taps_ref, parts, rows)
        for s in range(half):
            own = total[s * ROWS : (s + 1) * ROWS, :width]
            done[s, :, here] = own
            done[count - 1 - s, :, here] = flip_rows(own)
    for k in range(count):
        outs[k][:, : per_device * width] = done[lax.bitwise_xor(me, k)]
        outs[k][:, per_device * width :] = edges_ref[...]


def cone_filter(taps, edges, got, per_device, width):
    count = len(got)
    rows = count // 2 * ROWS
    return pl.pallas_call(
        functools.partial(filter_kernel, count, per_device, width),
        in_specs=[VMEM] * (2 + count),
        out_specs=[VMEM] * count,
        out_shape=[fast(ROWS, per_device * width + edges.shape[1])] * count,
        scratch_shapes=[
            pltpu.VMEM((count, ROWS, per_device * width), jnp.float32),
            pltpu.VMEM((3 * rows, width + LANES), jnp.bfloat16),
            pltpu.VMEM((count, ROWS, per_device * width), jnp.float32),
        ],
        compiler_params=params(),
    )(taps, edges, *got[::-1])


SPAN = 2 * PART


def finish_kernel(count, per_device, width, *refs):
    taps_ref = refs[0]
    got = refs[count:0:-1]
    out, (slabs, parts, mine, line_parts, line_mine, left, right, done, sems) = refs[count + 1], refs[count + 2 :]
    me = lax.axis_index("gx")
    layers = count * per_device
    half = count // 2
    rows = half * ROWS
    lane = lax.broadcasted_iota(jnp.int32, (rows, LANES), 1)
    lane_out = lax.broadcasted_iota(jnp.int32, (ROWS, LANES), 1)
    for k in range(count):
        slabs[lax.bitwise_xor(me, k)] = got[k][:, per_device * width :]
    symmetric = jnp.concatenate([slabs[s] + flip_rows(slabs[count - 1 - s]) for s in range(half)], axis=0)
    per_tile = LANES // SPAN

    line_layer, spot = line_spot(layers)
    row = lax.broadcasted_iota(jnp.int32, (ROWS, width), 0)
    folded = [
        jnp.where(row == spot, line_of(slabs[s], width), 0.0)
        + jnp.where(row == ROWS - 1 - spot, line_of(slabs[count - 1 - s], width), 0.0)
        for s in range(half)
    ]
    side = jnp.zeros((rows, LANES), jnp.float32)
    split_rows(jnp.concatenate([jnp.concatenate(folded, axis=0), side], axis=1), line_parts)
    total = cone(taps_ref, line_parts, rows)
    for s in range(half):
        own = total[s * ROWS : (s + 1) * ROWS, :width]
        line_mine[s] = own
        line_mine[count - 1 - s] = flip_rows(own)
    tiles = []
    for start in range(0, layers, per_tile):
        tile = jnp.zeros((rows, LANES), jnp.float32)
        for j in range(min(per_tile, layers - start)):
            at = PART * (start + j)
            source = symmetric[:, at // LANES * LANES : (at // LANES + 1) * LANES]
            low, high = SPAN * j + 1, SPAN * j + PART + STRIP - 1
            here = jnp.logical_and(lane >= low, lane < low + STRIP)
            tile = jnp.where(here, pltpu.roll(source, (low - at) % LANES, 1), tile)
            here = jnp.logical_and(lane >= high, lane < high + STRIP)
            tile = jnp.where(here, pltpu.roll(source, (high - at - STRIP) % LANES, 1), tile)
        tiles.append(tile)
    split_rows(jnp.concatenate(tiles, axis=1), parts)
    total = cone(taps_ref, parts, rows)
    for s in range(half):
        own = total[s * ROWS : (s + 1) * ROWS]
        mine[s] = own
        mine[count - 1 - s] = flip_rows(own)
    mine_now = mine[me]
    for layer in range(layers):
        tile = mine_now[:, layer // per_tile * LANES : (layer // per_tile + 1) * LANES]
        at = SPAN * (layer % per_tile)
        head = pltpu.roll(tile, (-at - STRIP) % LANES, 1)
        left[layer] = jnp.where(lane_out < STRIP - 1, head, 0.0)
        tail = pltpu.roll(tile, (LANES - STRIP - at - PART) % LANES, 1)
        right[layer] = jnp.where(lane_out > LANES - STRIP, tail, 0.0)

    copies = []
    for k in range(count):
        first = lax.bitwise_xor(me, k) * per_device
        for i in range(per_device):
            at = i * width
            line = jnp.where(first + i == line_layer, line_mine[me], 0.0)
            done[k, i] = got[k][:, at : at + width] + line
            done[k, i, :, :LANES] += left[first + i]
            done[k, i, :, width - LANES :] += right[first + i]
        copies.append(pltpu.make_async_copy(done.at[k], out.at[pl.ds(first, per_device)], sems.at[k]))
        copies[-1].start()
    for copy in copies:
        copy.wait()


def finish(taps, parts, layers, width):
    count = len(parts)
    per_device = layers // count
    rows = count // 2 * ROWS
    edges = parts[0].shape[1] - per_device * width
    spread = math.ceil(layers * SPAN / LANES) * LANES
    return pl.pallas_call(
        functools.partial(finish_kernel, count, per_device, width),
        in_specs=[VMEM] * (1 + count),
        out_specs=ANY,
        out_shape=f32(layers, ROWS, width),
        scratch_shapes=[
            pltpu.VMEM((count, ROWS, edges), jnp.float32),
            pltpu.VMEM((3 * rows, spread), jnp.bfloat16),
            pltpu.VMEM((count, ROWS, spread), jnp.float32),
            pltpu.VMEM((3 * rows, width + LANES), jnp.bfloat16),
            pltpu.VMEM((count, ROWS, width), jnp.float32),
            pltpu.VMEM((layers, ROWS, LANES), jnp.float32),
            pltpu.VMEM((layers, ROWS, LANES), jnp.float32),
            pltpu.VMEM((count, per_device, ROWS, width), jnp.float32),
            pltpu.SemaphoreType.DMA((count,)),
        ],
        compiler_params=params(),
    )(taps, *parts[::-1])


def spread(parts):
    count = len(parts)
    got = list(parts)
    for k in range(count - 1, 0, -1):
        got[k] = lax.ppermute(parts[k], "gx", [(i, i ^ k) for i in range(count)])
    return got


def on_device(efield, hfield, forward, material, permit, design_mask, grad_sum):
    layers, _, width = grad_sum.shape
    efield, hfield = load(efield, hfield)
    zfaces, xfaces, lines = halos(efield, hfield)
    forward, own_low, own_high, mask, inv = strips(
        permit, efield, hfield, forward, material, grad_sum, design_mask
    )
    arrays = (efield, hfield, forward, inv, grad_sum, mask)
    edges = own_edges(arrays)
    shares, own = own_gradient(arrays, zfaces, xfaces)
    got = spread(shares)
    yfaces = exchange(y_faces(own_low, own_high, zfaces, xfaces, lines, own), "gy", "gz")
    message, edge = edge_gradient(own, arrays, edges, zfaces, xfaces, lines, yfaces)
    taps = jnp.asarray(cone_matrix(len(got) // 2 * ROWS))
    parts = cone_filter(taps, message, got, layers // len(got), width)
    e_next, h_next, grad_total = step(
        efield, hfield, inv, own, edge, message, zfaces, xfaces, lines, yfaces, parts[0]
    )
    return e_next, h_next, grad_total, finish(taps, spread(parts), layers, width)


def solution(mesh):
    field = P(None, "gz", "gx", "gy")
    cells = P("gz", "gx", "gy")
    return jax.shard_map(
        on_device,
        mesh=mesh,
        in_specs=(field, field, field, cells, P(), P("gx", "gy"), cells),
        out_specs=(field, field, cells, cells),
        check_vma=False,
    )
```

```python
import functools
import math

import jax
import jax.numpy as jnp
import numpy as np
from jax import lax
from jax.experimental import pallas as pl
from jax.experimental.pallas import tpu as pltpu
from jax.sharding import PartitionSpec as P

RADIUS = 6
BLOCK = 8
HALF = 0.5

ROWS = 8
LANES = 128
STRIP = 8
SLOTS = LANES // STRIP
MIB = 1024 * 1024

VMEM = pl.BlockSpec(memory_space=pltpu.VMEM)
SMEM = pl.BlockSpec(memory_space=pltpu.SMEM)
ANY = pl.BlockSpec(memory_space=pl.ANY)


def params(mib=24):
    return pltpu.CompilerParams(vmem_limit_bytes=mib * MIB)


def f32(*shape):
    return jax.ShapeDtypeStruct(shape, jnp.float32)


def fast(*shape):
    return pltpu.VMEM(shape, jnp.float32)


def rounds(axis):
    return 2 if lax.axis_size(axis) > 2 else 1


def exchange(sends, axis, mate):
    count = lax.axis_size(axis)
    beside = lax.axis_size(mate)
    if count == 1:
        return sends
    got = []
    for start, value in enumerate(sends):
        partner = list(range(count))
        for low in range(start, count - 1, 2):
            partner[low], partner[low + 1] = low + 1, low
        axes = sorted((axis, mate))
        steps = (beside, 1) if axes[0] == axis else (1, count)
        pairs = []
        for i in range(count):
            for m in range(beside):
                if partner[i] != i:
                    to = (partner[i], m)
                elif beside % 2 == 0:
                    to = (i, m ^ 1)
                else:
                    continue
                pairs.append((i * steps[0] + m * steps[1], to[0] * steps[0] + to[1] * steps[1]))
        got.append(lax.ppermute(value, tuple(axes), pairs))
    return got


def exchange_diagonal(sends):
    along_x, along_y, along_z = (lax.axis_size(axis) for axis in AXES)

    def flat(x, y, z):
        return (x * along_y + y) * along_z + z

    got = []
    for start, value in enumerate(sends):
        partner = {}
        for low in range(start, along_z - 1, 2):
            for x in range(1, along_x):
                partner[x, low] = (x - 1, low + 1)
                partner[x - 1, low + 1] = (x, low)
        pairs = []
        for x in range(along_x):
            for z in range(along_z):
                for y in range(along_y):
                    if (x, z) in partner:
                        to = partner[x, z]
                        pairs.append((flat(x, y, z), flat(to[0], y, to[1])))
                    elif along_y % 2 == 0:
                        pairs.append((flat(x, y, z), flat(x, y ^ 1, z)))
        got.append(lax.ppermute(value, AXES, pairs))
    return got


AXES = ("gx", "gy", "gz")


class Side:
    def __init__(self, axis):
        index = lax.axis_index(axis)
        self.rounds = rounds(axis)
        self.odd = index % 2 == 1
        self.bottom = index == 0
        self.top = index == lax.axis_size(axis) - 1

    def sends(self, low, high):
        both = [jnp.where(self.odd, low, high)]
        if self.rounds > 1:
            both.append(jnp.where(self.odd, high, low))
        return both

    def lower(self, got):
        return jnp.where(self.bottom, 0.0, jnp.where(self.odd, got[0], got[-1]))

    def upper(self, got):
        return jnp.where(self.top, 0.0, jnp.where(self.odd, got[-1], got[0]))


def first_layer(cells_z, layers):
    return (cells_z - layers) * (1 - lax.axis_index("gz"))


def faces_kernel(x_rounds, e_ref, h_ref, *refs):
    x_sends, (low_ref, rows_ref) = refs[:x_rounds], refs[-2:]
    others = refs[x_rounds:-2]
    z_sends, d_sends = others[: len(others) // 2], others[len(others) // 2 :]
    cells_z = e_ref.shape[1]
    last, top = ROWS - 1, cells_z - 1

    low_ref[2 * cells_z :, :] = jnp.zeros_like(low_ref[2 * cells_z :, :])
    rows_ref[5, top : top + 1, :] = jnp.zeros_like(rows_ref[5, top : top + 1, :])
    for z in range(cells_z):
        low_ref[z : z + 1, :] = e_ref[1, z, 0:1, :]
        low_ref[cells_z + z : cells_z + z + 1, :] = e_ref[2, z, 0:1, :]
        for c in range(3):
            rows_ref[c, z : z + 1, :] = e_ref[c, z, last : last + 1, :]
        for c in range(2):
            rows_ref[3 + c, z : z + 1, :] = h_ref[1 + c, z, last : last + 1, :]
        if z > 0:
            rows_ref[5, z - 1 : z, :] = e_ref[0, z, last : last + 1, :]
    width = e_ref.shape[3]
    ex, ey, ez = (rows_ref[c] for c in range(3))
    column = lax.broadcasted_iota(jnp.int32, ex.shape, 1)
    ex_next = jnp.where(column == width - 1, 0.0, pltpu.roll(ex, width - 1, 1))
    lane = lax.broadcasted_iota(jnp.int32, (ROWS, LANES), 1)
    strip = jnp.zeros((ROWS, LANES), jnp.float32)
    for j in range(cells_z // ROWS):
        head = rows_ref[0, j * ROWS : (j + 1) * ROWS, 0:LANES]
        strip = jnp.where(lane // STRIP == j, pltpu.roll(head, STRIP * j, 1) if j else head, strip)
    high = (
        rows_ref[3] - HALF * (rows_ref[5] - ex + ez),
        rows_ref[4] + HALF * ey - HALF * (ex - ex_next),
        jnp.concatenate([strip, jnp.zeros((ROWS, width - LANES), jnp.float32)], axis=1),
    )
    side = Side("gx")
    for c, value in enumerate(high):
        here = slice(c * cells_z, c * cells_z + value.shape[0])
        for ref, one in zip(x_sends, side.sends(low_ref[here, :], value)):
            ref[here, :] = one

    side = Side("gz")
    ex, ey, ez = (e_ref[c, top] for c in range(3))
    low = (e_ref[0, 0], e_ref[1, 0], jnp.zeros_like(ez))
    high = (h_ref[0, top] + HALF * ez - HALF * ey, h_ref[1, top] + HALF * ex - HALF * ez, ez)
    for c in range(3):
        for ref, value in zip(z_sends, side.sends(low[c], high[c])):
            ref[c] = value

    down, up = (
        jnp.broadcast_to(line, (ROWS, line.shape[1]))
        for line in (e_ref[0, 0, last : last + 1, :], e_ref[2, top, 0:1, :])
    )
    for ref, value in zip(d_sends, side.sends(down, up)):
        ref[...] = value


def halos(efield, hfield):
    _, cells_z, cells_x, cells_y = efield.shape
    x_rounds, z_rounds = rounds("gx"), rounds("gz")
    x_face, z_face, line = fast(2 * cells_z + ROWS, cells_y), fast(3, cells_x, cells_y), fast(ROWS, cells_y)
    sends = pl.pallas_call(
        functools.partial(faces_kernel, x_rounds),
        in_specs=[VMEM] * 2,
        out_specs=[VMEM] * (x_rounds + 2 * z_rounds),
        out_shape=[x_face] * x_rounds + [z_face] * z_rounds + [line] * z_rounds,
        scratch_shapes=[
            pltpu.VMEM(x_face.shape, jnp.float32),
            pltpu.VMEM((6, cells_z, cells_y), jnp.float32),
        ],
        compiler_params=params(),
    )(efield, hfield)
    xfaces = exchange(sends[:x_rounds], "gx", "gy")
    zfaces = exchange(sends[x_rounds : x_rounds + z_rounds], "gz", "gy")
    return zfaces, xfaces, exchange_diagonal(sends[x_rounds + z_rounds :])


def lane_group():
    return lax.broadcasted_iota(jnp.int32, (ROWS, LANES), 1) // STRIP


def pack_strips(tiles, low_ref, high_ref, first):
    group = lane_group()
    width = tiles[0][1]
    for start in range(0, len(tiles), SLOTS):
        low = jnp.zeros((ROWS, LANES), jnp.float32)
        high = jnp.zeros((ROWS, LANES), jnp.float32)
        for k, (load, _) in enumerate(tiles[start : start + SLOTS]):
            if load is None:
                continue
            here = group == k
            shift = (STRIP * k) % LANES
            left = load(slice(0, LANES))
            right = load(slice(width - LANES, width))
            low = jnp.where(here, pltpu.roll(left, shift, 1) if shift else left, low)
            shift = (STRIP * k + STRIP) % LANES
            high = jnp.where(here, pltpu.roll(right, shift, 1) if shift else right, high)
        low_ref[first + start // SLOTS] = low
        high_ref[first + start // SLOTS] = high


def load_kernel(e_in, h_in, e_ref, h_ref, sems):
    parts = [(source.at[c], target.at[c]) for source, target in ((e_in, e_ref), (h_in, h_ref)) for c in range(3)]
    copies = [pltpu.make_async_copy(*part, sems.at[n]) for n, part in enumerate(parts)]
    for copy in copies:
        copy.start()
    for copy in copies:
        copy.wait()


def load(*fields):
    return pl.pallas_call(
        load_kernel,
        in_specs=[ANY] * 2,
        out_specs=[VMEM] * 2,
        out_shape=[fast(*one.shape) for one in fields],
        scratch_shapes=[pltpu.SemaphoreType.DMA((6,))],
        compiler_params=params(56),
    )(*fields)


def strips_kernel(
    permit_ref, e_ref, h_ref, f_in, mat_ref, grad_ref, mask_ref, f_ref, low_ref, high_ref, wide_ref, inv_ref, sems
):
    cells_z, width = e_ref.shape[1], e_ref.shape[3]
    layers = grad_ref.shape[0]
    blocks = mask_ref.shape[1]
    copies = [pltpu.make_async_copy(f_in.at[c], f_ref.at[c], sems.at[c]) for c in range(3)]
    for copy in copies:
        copy.start()

    inverse = [
        jnp.broadcast_to(HALF * (1.0 / permit_ref[0:1, m : m + 1]), (ROWS, width))
        for m in range(permit_ref.shape[1])
    ]
    for z in range(cells_z):
        inv = inverse[0]
        for m in range(1, len(inverse)):
            inv = jnp.where(mat_ref[z] == m, inverse[m], inv)
        inv_ref[z] = inv
    spread = (
        lax.broadcasted_iota(jnp.int32, (blocks, width), 0)
        == lax.broadcasted_iota(jnp.int32, (blocks, width), 1) // BLOCK
    ).astype(jnp.float32)
    mask = jnp.broadcast_to(mask_ref[...].astype(jnp.float32), (ROWS, blocks))
    wide_ref[...] = jnp.dot(mask, spread, preferred_element_type=jnp.float32)
    first = first_layer(cells_z, layers)
    tiles = []
    for z in range(cells_z):
        for ref in (e_ref, h_ref):
            for c in range(3):
                tiles.append((lambda s, r=ref, c=c, z=z: r[c, z, :, s], width))
    pack_strips(tiles, low_ref, high_ref, 0)

    for copy in copies:
        copy.wait()
    done = len(tiles) // SLOTS
    tiles = []
    for layer in range(layers):
        for c in range(3):
            tiles.append((lambda s, c=c, l=layer: f_ref[c, first + l, :, s], width))
        tiles.append((lambda s, l=layer: inv_ref[first + l, :, s], width))
        tiles.append((lambda s, l=layer: grad_ref[l, :, s], width))
        tiles.append((lambda s: wide_ref[:, s], width) if layer % ROWS == 0 else (None, width))
    pack_strips(tiles, low_ref, high_ref, done)


def strips(permit, efield, hfield, forward, material, grad_sum, mask):
    cells_z, width = efield.shape[1], efield.shape[3]
    count = (cells_z * 6 + grad_sum.shape[0] * 6) // SLOTS
    packed = (count, ROWS, LANES)
    shapes = (forward.shape, packed, packed, (ROWS, width), material.shape)
    return pl.pallas_call(
        strips_kernel,
        in_specs=[VMEM] * 3 + [ANY] + [VMEM] * 3,
        out_specs=[VMEM] * 5,
        out_shape=[fast(*shape) for shape in shapes],
        scratch_shapes=[pltpu.SemaphoreType.DMA((3,))],
        compiler_params=params(40),
    )(permit.reshape(1, -1), efield, hfield, forward, material, grad_sum, mask)


def edge_tile(load, width):
    lane = lax.broadcasted_iota(jnp.int32, (ROWS, LANES), 1)
    head = pltpu.roll(load(slice(0, LANES)), STRIP, 1)
    tail = pltpu.roll(load(slice(width - LANES, width)), LANES - STRIP, 1)
    return jnp.where(lane < LANES // 2, head, tail)


def edges_kernel(e_ref, h_ref, f_ref, inv_ref, grad_ref, mask_ref, eh_out, grad_out, mask_out):
    cells_z, width = e_ref.shape[1], e_ref.shape[3]
    layers = grad_ref.shape[0]
    first = first_layer(cells_z, layers)
    for z in range(cells_z):
        for c in range(3):
            eh_out[z, c] = edge_tile(lambda s: e_ref[c, z, :, s], width)
            eh_out[z, 3 + c] = edge_tile(lambda s: h_ref[c, z, :, s], width)
    for layer in range(layers):
        for c in range(3):
            grad_out[layer, c] = edge_tile(lambda s: f_ref[c, first + layer, :, s], width)
        grad_out[layer, 3] = edge_tile(lambda s: inv_ref[first + layer, :, s], width)
        grad_out[layer, 4] = edge_tile(lambda s: grad_ref[layer, :, s], width)
    mask_out[...] = edge_tile(lambda s: mask_ref[:, s], width)


def own_edges(arrays):
    cells_z, layers = arrays[0].shape[1], arrays[4].shape[0]
    return pl.pallas_call(
        edges_kernel,
        in_specs=[VMEM] * 6,
        out_specs=[VMEM] * 3,
        out_shape=[fast(cells_z, 6, ROWS, LANES), fast(layers, 5, ROWS, LANES), fast(ROWS, LANES)],
        compiler_params=params(),
    )(*arrays)


def corner_lines(lines, s):
    z_side, x_side = Side("gz"), Side("gx")
    above = jnp.where(x_side.bottom, 0.0, z_side.upper([f[:, s] for f in lines]))
    beyond = jnp.where(x_side.top, 0.0, z_side.lower([f[:, s] for f in lines]))
    return above, beyond


def face_tiles(zfaces, xfaces, lines):
    width = xfaces[0].shape[1]
    rows = xfaces[0].shape[0]
    cells_z = (rows - ROWS) // 2
    z_side, x_side = Side("gz"), Side("gx")

    def corner(s):
        row = lax.broadcasted_iota(jnp.int32, (ROWS, s.stop - s.start), 0)
        return jnp.where(row == ROWS - 1, -HALF * corner_lines(lines, s)[0], 0.0)

    def x_tile(pick, t, s):
        value = pick([f[t : t + ROWS, s] for f in xfaces])
        return value + corner(s) if lines and t == cells_z - ROWS and pick == x_side.lower else value

    def strip(j, s):
        zeros = jnp.zeros((ROWS, s.stop - s.start), jnp.float32)
        if s.start:
            return zeros
        lane = lax.broadcasted_iota(jnp.int32, (ROWS, LANES), 1)
        packed = x_side.lower([f[2 * cells_z :, 0:LANES] for f in xfaces])
        head = jnp.where(lane < STRIP, pltpu.roll(packed, LANES - STRIP * j, 1) if j else packed, 0.0)
        return head if s.stop == LANES else jnp.concatenate([head, zeros[:, LANES:]], axis=1)

    tiles = []
    for c in range(3):
        tiles.append((lambda s, c=c: z_side.lower([f[c, :, s] for f in zfaces]), width))
    for c in range(2):
        tiles.append((lambda s, c=c: z_side.upper([f[c, :, s] for f in zfaces]), width))
    for t in range(0, 2 * cells_z, ROWS):
        tiles.append((lambda s, t=t: x_tile(x_side.lower, t, s), width))
    for j in range(cells_z // ROWS):
        tiles.append((lambda s, j=j: strip(j, s), width))
    for t in range(0, rows, ROWS):
        if lines and t == 2 * cells_z:
            tiles.append((lambda s: corner_lines(lines, s)[1], width))
        else:
            tiles.append((lambda s, t=t: x_tile(x_side.upper, t, s), width))
    return tiles


def face_count(xface):
    per_field = (xface.shape[0] - ROWS) // ROWS // 2
    return 5 + 3 * per_field + 2 * per_field + 1


def y_faces_kernel(counts, *refs):
    own_low, own_high = refs[:2]
    ends = np.cumsum((2,) + counts)
    zfaces, xfaces, lines = (refs[i:j] for i, j in zip(ends[:-1], ends[1:]))
    sends, (low_ref, high_ref) = refs[3 + sum(counts) : -2], refs[-2:]
    own = own_low.shape[0]
    pack_strips(face_tiles(zfaces, xfaces, lines), low_ref, high_ref, 0)
    side = Side("gy")
    for ref, value in zip(sends, side.sends(own_low[...], own_high[...])):
        ref[0:own] = value
    for ref, value in zip(sends, side.sends(low_ref[...], high_ref[...])):
        ref[own:] = value


def y_faces(own_low, own_high, zfaces, xfaces, lines, after):
    extra = math.ceil(face_count(xfaces[0]) / SLOTS)
    packed = fast(own_low.shape[0] + extra, ROWS, LANES)
    return pl.pallas_call(
        functools.partial(y_faces_kernel, (len(zfaces), len(xfaces), len(lines))),
        in_specs=[VMEM] * (2 + len(zfaces) + len(xfaces) + len(lines)) + [ANY],
        out_specs=[VMEM] * rounds("gy"),
        out_shape=[packed] * rounds("gy"),
        scratch_shapes=[pltpu.VMEM((extra, ROWS, LANES), jnp.float32)] * 2,
        compiler_params=params(),
    )(own_low, own_high, *zfaces, *xfaces, *lines, after)


OWN, CIRCLE, EDGE = range(3)


def faces_wide(mode, width):
    return {OWN: width, CIRCLE: width + LANES, EDGE: LANES}[mode]


class Fields:
    def __init__(self, mode, layers, fields, zfaces, xfaces, lines, yfaces, scratch):
        self.mode = mode
        self.fields = fields
        if mode == EDGE:
            self.cells_z, self.width = fields.shape[0], xfaces[0].shape[1]
        else:
            self.cells_z, self.width = fields[0].shape[1], fields[0].shape[3]
        self.wide = faces_wide(mode, self.width)
        self.lane = lax.broadcasted_iota(jnp.int32, (ROWS, LANES), 1)
        self.row = lax.broadcasted_iota(jnp.int32, (ROWS, self.wide), 0)
        self.per_group = 6 * ROWS // SLOTS
        self.groups = self.cells_z // ROWS
        self.grad_base = self.per_group * self.groups
        halo_base = self.grad_base + self.per_group * (layers // ROWS)
        self.left_wide, self.right_wide = left_wide, right_wide = scratch[:2]
        if mode != OWN:
            self.ybuf = scratch[2]
            y_side = Side("gy")
            for t in range(yfaces[0].shape[0]):
                lower = y_side.lower([f[t] for f in yfaces])
                upper = y_side.upper([f[t] for f in yfaces])
                if mode == EDGE:
                    even = self.lane // STRIP % 2 == 0
                    lower, upper = (
                        jnp.where(even, upper, pltpu.roll(lower, STRIP, 1)),
                        jnp.where(even, pltpu.roll(upper, LANES - STRIP, 1), lower),
                    )
                self.ybuf[0, t] = lower
                self.ybuf[1, t] = upper

        def face(load, slot):
            if mode == EDGE:
                own = edge_tile(load, self.width)
                return self.edge(own, halo_base + slot // SLOTS, slot % SLOTS)
            return self.wider(load, halo_base + slot // SLOTS, slot % SLOTS)

        full = [face(load, slot) for slot, (load, _) in enumerate(face_tiles(zfaces, xfaces, lines))]
        self.below, self.above = full[:3], full[3:5]
        groups = self.groups
        for t in range(2 * groups):
            left_wide[t * ROWS : (t + 1) * ROWS, :] = full[5 + t]
        for t in range(2 * groups + 1):
            right_wide[t * ROWS : (t + 1) * ROWS, :] = full[5 + 3 * groups + t]
        if mode != OWN:
            column = lax.broadcasted_iota(jnp.int32, (ROWS, self.wide), 1)
            ends = {CIRCLE: (self.width - 1, self.wide - 1), EDGE: (STRIP - 1, LANES - STRIP - 1)}[mode]
            here = jnp.logical_or(column == ends[0], column == ends[1])
            for j in range(groups):
                ex_next = self.y_up(full[5 + 2 * groups + j])
                at = (groups + j) * ROWS
                left_wide[at : at + ROWS, :] += jnp.where(here, HALF * ex_next, 0.0)

    def wider(self, load, tile, k):
        if self.mode == OWN:
            return load(slice(0, self.width))

        def moved(v, to):
            shift = (to - STRIP * k) % LANES
            return pltpu.roll(v, shift, 1) if shift else v

        lower, upper = self.ybuf[0, tile], self.ybuf[1, tile]
        halo = jnp.where(self.lane < STRIP, moved(upper, 0), moved(lower, LANES - STRIP))
        return jnp.concatenate([load(slice(0, self.width)), halo], axis=1)

    def edge(self, own, tile, k):
        shift = (LANES - STRIP - 2 * STRIP * (k // 2)) % LANES
        both = pltpu.roll(self.ybuf[k % 2, tile], shift, 1)
        inside = jnp.logical_and(self.lane >= STRIP, self.lane < LANES - STRIP)
        return jnp.where(inside, own, both)

    def y_up(self, v):
        return pltpu.roll(v, self.wide - 1, 1)

    def y_down(self, v):
        return pltpu.roll(v, 1, 1)

    def x_up(self, v, line):
        return jnp.where(self.row == ROWS - 1, line, pltpu.roll(v, ROWS - 1, 0))

    def x_down(self, v, line):
        return jnp.where(self.row == 0, line, pltpu.roll(v, 1, 0))

    def line(self, ref, at):
        return jnp.broadcast_to(ref[pl.ds(at, 1), :], (ROWS, self.wide))

    def field(self, which, c, a, b):
        slot = 6 * b + 3 * which + c
        tile = self.per_group * a + slot // SLOTS
        if self.mode == EDGE:
            return self.edge(self.fields[ROWS * a + b, 3 * which + c], tile, slot % SLOTS)
        ref = self.fields[which]
        return self.wider(lambda s: ref[c, ROWS * a + b, :, s], tile, slot % SLOTS)

    def hx(self, a, b, ey, ez, ey_next):
        return self.field(1, 0, a, b) - HALF * (self.y_up(ez) - ez - ey_next + ey)

    def hy(self, a, b, ex, ez, ex_next):
        up = self.x_up(ez, self.line(self.right_wide, self.cells_z + ROWS * a + b))
        return self.field(1, 1, a, b) - HALF * (ex_next - ex - up + ez)

    def hz(self, a, b, ex, ey):
        up = self.x_up(ey, self.line(self.right_wide, ROWS * a + b))
        return self.field(1, 2, a, b) - HALF * (up - ey - self.y_up(ex) + ex)

    def start(self, a):
        ex, ey = self.field(0, 0, a, 0), self.field(0, 1, a, 0)
        below = self.below
        at_bottom = (
            below[0] - HALF * self.y_up(below[2]) + HALF * ey,
            below[1] - HALF * ex + HALF * self.x_up(below[2], self.line(self.right_wide, 2 * self.cells_z)),
        )
        before, b = jnp.maximum(a - 1, 0), ROWS - 1
        ex_before, ey_before, ez_before = (self.field(0, c, before, b) for c in range(3))
        inside = (
            self.hx(before, b, ey_before, ez_before, ey),
            self.hy(before, b, ex_before, ez_before, ex),
        )
        bottom = a == 0
        return (ex, ey) + tuple(jnp.where(bottom, one, two) for one, two in zip(at_bottom, inside))

    def group(self, a, carry, emit):
        ex, ey, hx_z, hy_z = carry
        for b in range(ROWS):
            z = ROWS * a + b
            ez = self.field(0, 2, a, b)
            if b < ROWS - 1:
                ex_next, ey_next = (self.field(0, c, a, b + 1) for c in range(2))
            else:
                end = a == self.groups - 1
                after = jnp.minimum(a + 1, self.groups - 1)
                ex_next, ey_next = (
                    jnp.where(end, self.above[c], self.field(0, c, after, 0)) for c in range(2)
                )
            hx = self.hx(a, b, ey, ez, ey_next)
            hy = self.hy(a, b, ex, ez, ex_next)
            hz = self.hz(a, b, ex, ey)
            hy_x = self.x_down(hy, self.line(self.left_wide, z) + HALF * ez)
            hz_x = self.x_down(hz, self.line(self.left_wide, self.cells_z + z) - HALF * ey)
            curl = (
                (hz - self.y_down(hz)) - (hy - hy_z),
                (hx - hx_z) - (hz - hz_x),
                (hy - hy_x) - (hx - self.y_down(hx)),
            )
            emit(a, b, (ex, ey, ez), (hx, hy, hz), curl)
            ex, ey, hx_z, hy_z = ex_next, ey_next, hx, hy
        return ex, ey, hx_z, hy_z

    def gradient(self, layers, arrays, store):
        first = first_layer(self.cells_z, layers)
        first_group = first // ROWS
        if self.mode == EDGE:
            grad_edges, mask_ref = arrays
            mask = self.edge(mask_ref[...], self.grad_base, 5)
        else:
            f_ref, inv_ref, grad_ref, mask_ref = arrays
            mask = mask_ref[...]

        def emit(a, b, efield, hfield, curl):
            z = ROWS * a + b
            layer = z - first
            if self.mode == EDGE:
                tile = self.grad_base + self.per_group * (a - first_group)
                slots = [6 * b + n for n in range(5)]
                values = [
                    self.edge(grad_edges[layer, n], tile + slot // SLOTS, slot % SLOTS)
                    for n, slot in enumerate(slots)
                ]
            else:
                values = [f_ref[c, z] for c in range(3)] + [inv_ref[z], grad_ref[layer]]
            total = None
            for c in range(3):
                term = values[c] * (efield[c] + values[3] * curl[c])
                total = term if total is None else total + term
            store(layer, values[4] + mask * total)

        def body(i, carry):
            return self.group(first_group + i, carry, emit)

        lax.fori_loop(0, layers // ROWS, body, self.start(first_group))


def fields_scratch(mode, xface, yface, width):
    rows, wide = xface.shape[0], faces_wide(mode, width)
    out = [pltpu.VMEM((rows, wide), jnp.float32)] * 2
    if mode != OWN:
        out.append(pltpu.VMEM((2,) + yface.shape, jnp.float32))
    return out


def own_gradient_kernel(counts, per_device, *refs):
    e_ref, h_ref, f_ref, inv_ref, grad_ref, mask_ref = refs[:6]
    zfaces, xfaces = refs[6 : 6 + counts[0]], refs[6 + counts[0] : 6 + sum(counts)]
    shares, (own_ref, *scratch) = refs[6 + sum(counts) : -3][::-1], refs[-3:]
    layers, _, width = grad_ref.shape
    fields = Fields(OWN, layers, (e_ref, h_ref), zfaces, xfaces, (), None, scratch)

    def store(layer, value):
        own_ref[layer] = value

    fields.gradient(layers, (f_ref, inv_ref, grad_ref, mask_ref), store)

    me = lax.axis_index("gx")
    for k, share in enumerate(shares):
        chunk = lax.bitwise_xor(me, k)
        for i in range(per_device):
            share[:, i * width : (i + 1) * width] = own_ref[chunk * per_device + i]
        if share.shape[1] > per_device * width:
            share[:, per_device * width :] = jnp.zeros((ROWS, SPARE), jnp.float32)


SPARE = 2 * LANES


def own_gradient(arrays, zfaces, xfaces):
    layers, _, width = arrays[4].shape
    count = lax.axis_size("gx")
    per_device = layers // count
    *shares, own = pl.pallas_call(
        functools.partial(own_gradient_kernel, (len(zfaces), len(xfaces)), per_device),
        in_specs=[VMEM] * (6 + len(zfaces) + len(xfaces)),
        out_specs=[VMEM] * (count + 1),
        out_shape=[fast(ROWS, per_device * width + SPARE)]
        + [fast(ROWS, per_device * width)] * (count - 1)
        + [fast(layers, ROWS, width)],
        scratch_shapes=fields_scratch(OWN, xfaces[0], None, width),
        compiler_params=params(),
    )(*arrays, *zfaces, *xfaces)
    return shares[::-1], own


PART = 2 * STRIP


def edge_gradient_kernel(counts, *refs):
    own_ref, f_ref, inv_ref, wide_ref, eh_ref, grad_ref, mask_ref = refs[:7]
    ends = np.cumsum((7,) + counts)
    zfaces, xfaces, lines, yfaces = (refs[i:j] for i, j in zip(ends[:-1], ends[1:]))
    (message, edge_ref), scratch = refs[ends[-1] : -3], refs[-3:]
    layers, _, width = own_ref.shape
    lane = lax.broadcasted_iota(jnp.int32, (ROWS, LANES), 1)
    first, last = STRIP, LANES - STRIP - 1
    fields = Fields(EDGE, layers, eh_ref, zfaces, xfaces, lines, yfaces, scratch)

    def store(layer, value):
        edge_ref[layer] = value

    fields.gradient(layers, (grad_ref, mask_ref), store)

    per_tile = LANES // PART
    for start in range(0, layers, per_tile):
        packed = jnp.zeros((ROWS, LANES), jnp.float32)
        for j in range(min(per_tile, layers - start)):
            layer = start + j
            edge = edge_ref[layer]
            own = edge_tile(lambda s: own_ref[layer, :, s], width)
            more = jnp.where(jnp.logical_or(lane == first, lane == last), edge - own, edge)
            left = pltpu.roll(more, (PART * j - 1) % LANES, 1)
            right = pltpu.roll(more, (PART * j + STRIP - last) % LANES, 1)
            packed = jnp.where(lane // STRIP == 2 * j, left, packed)
            packed = jnp.where(lane // STRIP == 2 * j + 1, right, packed)
        message[:, start // per_tile * LANES : (start // per_tile + 1) * LANES] = packed

    tail = math.ceil(layers / per_tile) * LANES
    message[:, tail:] = jnp.zeros_like(message[:, tail:])
    top, last = fields.cells_z - 1, ROWS - 1
    above, beyond = (line[0:1] for line in corner_lines(lines, slice(0, width)))
    added = wide_ref[0:1, :] * f_ref[2, top, 0:1, :] * inv_ref[top, 0:1, :] * (HALF * above)
    added += wide_ref[last:, :] * f_ref[0, 0, last:, :] * inv_ref[0, last:, :] * (HALF * beyond)
    column = lax.broadcasted_iota(jnp.int32, (1, width), 1)
    added = jnp.where(jnp.logical_or(column == 0, column == width - 1), 0.0, added)
    for at, n in line_places(width):
        message[n : n + 1, tail + at : tail + at + LANES] = added[:, (at // LANES * ROWS + n) * LANES :][:, :LANES]


def line_places(width):
    return [(t // ROWS * LANES, t % ROWS) for t in range(width // LANES)]


def line_of(message, width):
    tail = message.shape[1] - math.ceil(width / LANES / ROWS) * LANES
    return jnp.concatenate([message[n : n + 1, tail + at : tail + at + LANES] for at, n in line_places(width)], axis=1)


def line_spot(layers):
    bottom = lax.axis_index("gz") == 0
    return jnp.where(bottom, layers - 1, 0), jnp.where(bottom, 0, ROWS - 1)


def edge_gradient(own, arrays, edges, zfaces, xfaces, lines, yfaces):
    layers, _, width = own.shape
    faces = (*zfaces, *xfaces, *lines, *yfaces)
    tiles = math.ceil(layers * PART / LANES) + math.ceil(width / LANES / ROWS)
    return pl.pallas_call(
        functools.partial(edge_gradient_kernel, (len(zfaces), len(xfaces), len(lines), len(yfaces))),
        in_specs=[VMEM] * (7 + len(faces)),
        out_specs=[VMEM] * 2,
        out_shape=[fast(ROWS, tiles * LANES), fast(layers, ROWS, LANES)],
        scratch_shapes=fields_scratch(EDGE, xfaces[0], yfaces[0], width),
        compiler_params=params(),
    )(own, arrays[2], arrays[3], arrays[5], *edges, *faces)


def step_kernel(counts, *refs):
    e_ref, h_ref, inv_ref, own_ref, edge_ref, message = refs[:6]
    ends = np.cumsum((6,) + counts)
    zfaces, xfaces, lines, yfaces = (refs[i:j] for i, j in zip(ends[:-1], ends[1:]))
    e_out, h_out, grad_out = refs[ends[-1] + 1 : ends[-1] + 4]
    left_wide, right_wide, ybuf, e_new, h_new, grad_new, sems = refs[ends[-1] + 4 :]
    layers, _, width = own_ref.shape
    lane = lax.broadcasted_iota(jnp.int32, (ROWS, LANES), 1)

    for layer in range(layers):
        edge = edge_ref[layer]
        head, tail = own_ref[layer, :, 0:LANES], own_ref[layer, :, width - LANES :]
        grad_new[layer] = own_ref[layer]
        grad_new[layer, :, 0:LANES] = jnp.where(lane == 0, pltpu.roll(edge, LANES - STRIP, 1), head)
        grad_new[layer, :, width - LANES :] = jnp.where(lane == LANES - 1, pltpu.roll(edge, STRIP, 1), tail)
    layer, spot = line_spot(layers)
    row = lax.broadcasted_iota(jnp.int32, (ROWS, width), 0)
    grad_new[layer] += jnp.where(row == spot, line_of(message, width), 0.0)
    grad_copy = pltpu.make_async_copy(grad_new, grad_out, sems.at[0, 0])
    grad_copy.start()

    fields = Fields(CIRCLE, layers, (e_ref, h_ref), zfaces, xfaces, lines, yfaces, (left_wide, right_wide, ybuf))

    def emit(a, b, efield, hfield, curl):
        z = ROWS * a + b
        half_inv = inv_ref[z]
        for c in range(3):
            e_new[c, z] = efield[c][:, :width] + half_inv * curl[c][:, :width]
            h_new[c, z] = hfield[c][:, :width]

    def copies(a):
        here = pl.ds(a * ROWS, ROWS)
        return [
            pltpu.make_async_copy(new.at[c, here], out.at[c, here], sems.at[1 + a, 3 * n + c])
            for n, (new, out) in enumerate(((e_new, e_out), (h_new, h_out)))
            for c in range(3)
        ]

    def body(a, carry):
        carry = fields.group(a, carry, emit)
        for copy in copies(a):
            copy.start()
        return carry

    lax.fori_loop(0, fields.groups, body, fields.start(0))
    for a in range(fields.groups):
        for copy in copies(a):
            copy.wait()
    grad_copy.wait()


def step(efield, hfield, inv, own, edge, message, zfaces, xfaces, lines, yfaces, after):
    _, cells_z, _, width = efield.shape
    groups = (zfaces, xfaces, lines, yfaces)
    counts = tuple(len(group) for group in groups)
    shapes = (efield.shape, hfield.shape, own.shape)
    return pl.pallas_call(
        functools.partial(step_kernel, counts),
        in_specs=[VMEM] * (6 + sum(counts)) + [ANY],
        out_specs=[ANY] * 3,
        out_shape=[f32(*shape) for shape in shapes],
        scratch_shapes=fields_scratch(CIRCLE, xfaces[0], yfaces[0], width)
        + [pltpu.VMEM(shape, jnp.float32) for shape in shapes]
        + [pltpu.SemaphoreType.DMA((1 + cells_z // ROWS, 6))],
        compiler_params=params(),
    )(efield, hfield, inv, own, edge, message, *(one for group in groups for one in group), after)


def cone_matrix(rows):
    span = np.arange(-RADIUS, RADIUS + 1, dtype=np.float64)
    cone = np.maximum(RADIUS - np.sqrt(span[:, None] ** 2 + span[None, :] ** 2), 0.0)
    weight = cone / cone.sum()
    x = np.arange(rows)
    out = np.zeros((RADIUS + 1, rows, rows))
    for b in range(RADIUS + 1):
        for apart in (x[:, None] - x[None, :], 2 * rows - 1 - x[:, None] - x[None, :]):
            near = np.abs(apart) <= RADIUS
            out[b] += np.where(near, weight[np.clip(apart, -RADIUS, RADIUS) + RADIUS, RADIUS + b], 0.0)
    out = out.reshape((RADIUS + 1) * rows, rows).astype(np.float32)
    high = out.astype(jnp.bfloat16)
    low = (out - high.astype(np.float32)).astype(jnp.bfloat16)
    return np.concatenate([high, low, high], axis=1)


def flip_rows(v):
    row = lax.broadcasted_iota(jnp.int32, v.shape, 0)
    v = pltpu.roll(v, 4, 0)
    v = jnp.where(row % 4 < 2, pltpu.roll(v, ROWS - 2, 0), pltpu.roll(v, 2, 0))
    return jnp.where(row % 2 < 1, pltpu.roll(v, ROWS - 1, 0), pltpu.roll(v, 1, 0))


def split_rows(symmetric, parts):
    rows = symmetric.shape[0]
    high = symmetric.astype(jnp.bfloat16)
    low = (symmetric - high.astype(jnp.float32)).astype(jnp.bfloat16)
    parts[0:rows, :] = high
    parts[rows : 2 * rows, :] = high
    parts[2 * rows : 3 * rows, :] = low


def cone(taps_ref, parts, rows):
    wide = parts.shape[1]
    mixed = jnp.dot(taps_ref[...], parts[...], preferred_element_type=jnp.float32)
    total = mixed[0:rows]
    for b in range(1, RADIUS + 1):
        part = mixed[b * rows : (b + 1) * rows]
        total = total + (pltpu.roll(part, b, 1) + pltpu.roll(part, wide - b, 1))
    return total


def filter_kernel(count, per_device, width, *refs):
    taps_ref, edges_ref = refs[:2]
    got = refs[count + 1 : 1 : -1]
    outs = refs[2 + count : 2 + 2 * count]
    slabs, parts, done = refs[2 + 2 * count :]
    me = lax.axis_index("gx")
    half = count // 2
    rows = half * ROWS
    for k in range(count):
        slabs[lax.bitwise_xor(me, k)] = got[k][:, : per_device * width]

    side = jnp.zeros((rows, LANES), jnp.float32)
    for i in range(per_device):
        here = slice(i * width, (i + 1) * width)
        halves = [slabs[s, :, here] + flip_rows(slabs[count - 1 - s, :, here]) for s in range(half)]
        split_rows(jnp.concatenate([jnp.concatenate(halves, axis=0), side], axis=1), parts)
        total = cone(taps_ref, parts, rows)
        for s in range(half):
            own = total[s * ROWS : (s + 1) * ROWS, :width]
            done[s, :, here] = own
            done[count - 1 - s, :, here] = flip_rows(own)
    for k in range(count):
        outs[k][:, : per_device * width] = done[lax.bitwise_xor(me, k)]
        outs[k][:, per_device * width :] = edges_ref[...]


def cone_filter(taps, edges, got, per_device, width):
    count = len(got)
    rows = count // 2 * ROWS
    return pl.pallas_call(
        functools.partial(filter_kernel, count, per_device, width),
        in_specs=[VMEM] * (2 + count),
        out_specs=[VMEM] * count,
        out_shape=[fast(ROWS, per_device * width + edges.shape[1])] * count,
        scratch_shapes=[
            pltpu.VMEM((count, ROWS, per_device * width), jnp.float32),
            pltpu.VMEM((3 * rows, width + LANES), jnp.bfloat16),
            pltpu.VMEM((count, ROWS, per_device * width), jnp.float32),
        ],
        compiler_params=params(),
    )(taps, edges, *got[::-1])


SPAN = 2 * PART


def finish_kernel(count, per_device, width, *refs):
    taps_ref = refs[0]
    got = refs[count:0:-1]
    out, (slabs, parts, mine, line_parts, line_mine, left, right, done, sems) = refs[count + 1], refs[count + 2 :]
    me = lax.axis_index("gx")
    layers = count * per_device
    half = count // 2
    rows = half * ROWS
    lane = lax.broadcasted_iota(jnp.int32, (rows, LANES), 1)
    lane_out = lax.broadcasted_iota(jnp.int32, (ROWS, LANES), 1)
    for k in range(count):
        slabs[lax.bitwise_xor(me, k)] = got[k][:, per_device * width :]
    symmetric = jnp.concatenate([slabs[s] + flip_rows(slabs[count - 1 - s]) for s in range(half)], axis=0)
    per_tile = LANES // SPAN

    line_layer, spot = line_spot(layers)
    row = lax.broadcasted_iota(jnp.int32, (ROWS, width), 0)
    folded = [
        jnp.where(row == spot, line_of(slabs[s], width), 0.0)
        + jnp.where(row == ROWS - 1 - spot, line_of(slabs[count - 1 - s], width), 0.0)
        for s in range(half)
    ]
    side = jnp.zeros((rows, LANES), jnp.float32)
    split_rows(jnp.concatenate([jnp.concatenate(folded, axis=0), side], axis=1), line_parts)
    total = cone(taps_ref, line_parts, rows)
    for s in range(half):
        own = total[s * ROWS : (s + 1) * ROWS, :width]
        line_mine[s] = own
        line_mine[count - 1 - s] = flip_rows(own)
    tiles = []
    for start in range(0, layers, per_tile):
        tile = jnp.zeros((rows, LANES), jnp.float32)
        for j in range(min(per_tile, layers - start)):
            at = PART * (start + j)
            source = symmetric[:, at // LANES * LANES : (at // LANES + 1) * LANES]
            low, high = SPAN * j + 1, SPAN * j + PART + STRIP - 1
            here = jnp.logical_and(lane >= low, lane < low + STRIP)
            tile = jnp.where(here, pltpu.roll(source, (low - at) % LANES, 1), tile)
            here = jnp.logical_and(lane >= high, lane < high + STRIP)
            tile = jnp.where(here, pltpu.roll(source, (high - at - STRIP) % LANES, 1), tile)
        tiles.append(tile)
    split_rows(jnp.concatenate(tiles, axis=1), parts)
    total = cone(taps_ref, parts, rows)
    for s in range(half):
        own = total[s * ROWS : (s + 1) * ROWS]
        mine[s] = own
        mine[count - 1 - s] = flip_rows(own)
    mine_now = mine[me]
    for layer in range(layers):
        tile = mine_now[:, layer // per_tile * LANES : (layer // per_tile + 1) * LANES]
        at = SPAN * (layer % per_tile)
        head = pltpu.roll(tile, (-at - STRIP) % LANES, 1)
        left[layer] = jnp.where(lane_out < STRIP - 1, head, 0.0)
        tail = pltpu.roll(tile, (LANES - STRIP - at - PART) % LANES, 1)
        right[layer] = jnp.where(lane_out > LANES - STRIP, tail, 0.0)

    copies = []
    for k in range(count):
        first = lax.bitwise_xor(me, k) * per_device
        for i in range(per_device):
            at = i * width
            line = jnp.where(first + i == line_layer, line_mine[me], 0.0)
            done[k, i] = got[k][:, at : at + width] + line
            done[k, i, :, :LANES] += left[first + i]
            done[k, i, :, width - LANES :] += right[first + i]
        copies.append(pltpu.make_async_copy(done.at[k], out.at[pl.ds(first, per_device)], sems.at[k]))
        copies[-1].start()
    for copy in copies:
        copy.wait()


def finish(taps, parts, layers, width):
    count = len(parts)
    per_device = layers // count
    rows = count // 2 * ROWS
    edges = parts[0].shape[1] - per_device * width
    spread = math.ceil(layers * SPAN / LANES) * LANES
    return pl.pallas_call(
        functools.partial(finish_kernel, count, per_device, width),
        in_specs=[VMEM] * (1 + count),
        out_specs=ANY,
        out_shape=f32(layers, ROWS, width),
        scratch_shapes=[
            pltpu.VMEM((count, ROWS, edges), jnp.float32),
            pltpu.VMEM((3 * rows, spread), jnp.bfloat16),
            pltpu.VMEM((count, ROWS, spread), jnp.float32),
            pltpu.VMEM((3 * rows, width + LANES), jnp.bfloat16),
            pltpu.VMEM((count, ROWS, width), jnp.float32),
            pltpu.VMEM((layers, ROWS, LANES), jnp.float32),
            pltpu.VMEM((layers, ROWS, LANES), jnp.float32),
            pltpu.VMEM((count, per_device, ROWS, width), jnp.float32),
            pltpu.SemaphoreType.DMA((count,)),
        ],
        compiler_params=params(),
    )(taps, *parts[::-1])


def spread(parts):
    count = len(parts)
    got = list(parts)
    for k in range(count - 1, 0, -1):
        got[k] = lax.ppermute(parts[k], "gx", [(i, i ^ k) for i in range(count)])
    return got


def on_device(efield, hfield, forward, material, permit, design_mask, grad_sum):
    layers, _, width = grad_sum.shape
    efield, hfield = load(efield, hfield)
    zfaces, xfaces, lines = halos(efield, hfield)
    forward, own_low, own_high, mask, inv = strips(
        permit, efield, hfield, forward, material, grad_sum, design_mask
    )
    arrays = (efield, hfield, forward, inv, grad_sum, mask)
    edges = own_edges(arrays)
    shares, own = own_gradient(arrays, zfaces, xfaces)
    got = spread(shares)
    yfaces = exchange(y_faces(own_low, own_high, zfaces, xfaces, lines, own), "gy", "gz")
    message, edge = edge_gradient(own, arrays, edges, zfaces, xfaces, lines, yfaces)
    taps = jnp.asarray(cone_matrix(len(got) // 2 * ROWS))
    parts = cone_filter(taps, message, got, layers // len(got), width)
    e_next, h_next, grad_total = step(
        efield, hfield, inv, own, edge, message, zfaces, xfaces, lines, yfaces, parts[0]
    )
    return e_next, h_next, grad_total, finish(taps, spread(parts), layers, width)


def solution(mesh):
    field = P(None, "gz", "gx", "gy")
    cells = P("gz", "gx", "gy")
    return jax.shard_map(
        on_device,
        mesh=mesh,
        in_specs=(field, field, field, cells, P(), P("gx", "gy"), cells),
        out_specs=(field, field, cells, cells),
        check_vma=False,
    )
```

```python
import functools
import math

import jax
import jax.numpy as jnp
import numpy as np
from jax import lax
from jax.experimental import pallas as pl
from jax.experimental.pallas import tpu as pltpu
from jax.sharding import PartitionSpec as P

RADIUS = 6
BLOCK = 8
HALF = 0.5

ROWS = 8
LANES = 128
STRIP = 8
SLOTS = LANES // STRIP
MIB = 1024 * 1024

VMEM = pl.BlockSpec(memory_space=pltpu.VMEM)
SMEM = pl.BlockSpec(memory_space=pltpu.SMEM)
ANY = pl.BlockSpec(memory_space=pl.ANY)


def params(mib=24):
    return pltpu.CompilerParams(vmem_limit_bytes=mib * MIB)


def f32(*shape):
    return jax.ShapeDtypeStruct(shape, jnp.float32)


def fast(*shape):
    return pltpu.VMEM(shape, jnp.float32)


def rounds(axis):
    return 2 if lax.axis_size(axis) > 2 else 1


def exchange(sends, axis, mate):
    count = lax.axis_size(axis)
    beside = lax.axis_size(mate)
    if count == 1:
        return sends
    got = []
    for start, value in enumerate(sends):
        partner = list(range(count))
        for low in range(start, count - 1, 2):
            partner[low], partner[low + 1] = low + 1, low
        axes = sorted((axis, mate))
        steps = (beside, 1) if axes[0] == axis else (1, count)
        pairs = []
        for i in range(count):
            for m in range(beside):
                if partner[i] != i:
                    to = (partner[i], m)
                elif beside % 2 == 0:
                    to = (i, m ^ 1)
                else:
                    continue
                pairs.append((i * steps[0] + m * steps[1], to[0] * steps[0] + to[1] * steps[1]))
        got.append(lax.ppermute(value, tuple(axes), pairs))
    return got


def exchange_diagonal(sends):
    along_x, along_y, along_z = (lax.axis_size(axis) for axis in AXES)

    def flat(x, y, z):
        return (x * along_y + y) * along_z + z

    got = []
    for start, value in enumerate(sends):
        partner = {}
        for low in range(start, along_z - 1, 2):
            for x in range(1, along_x):
                partner[x, low] = (x - 1, low + 1)
                partner[x - 1, low + 1] = (x, low)
        pairs = []
        for x in range(along_x):
            for z in range(along_z):
                for y in range(along_y):
                    if (x, z) in partner:
                        to = partner[x, z]
                        pairs.append((flat(x, y, z), flat(to[0], y, to[1])))
                    elif along_y % 2 == 0:
                        pairs.append((flat(x, y, z), flat(x, y ^ 1, z)))
        got.append(lax.ppermute(value, AXES, pairs))
    return got


AXES = ("gx", "gy", "gz")


class Side:
    def __init__(self, axis):
        index = lax.axis_index(axis)
        self.rounds = rounds(axis)
        self.odd = index % 2 == 1
        self.bottom = index == 0
        self.top = index == lax.axis_size(axis) - 1

    def sends(self, low, high):
        both = [jnp.where(self.odd, low, high)]
        if self.rounds > 1:
            both.append(jnp.where(self.odd, high, low))
        return both

    def lower(self, got):
        return jnp.where(self.bottom, 0.0, jnp.where(self.odd, got[0], got[-1]))

    def upper(self, got):
        return jnp.where(self.top, 0.0, jnp.where(self.odd, got[-1], got[0]))


def first_layer(cells_z, layers):
    return (cells_z - layers) * (1 - lax.axis_index("gz"))


def faces_kernel(x_rounds, e_in, h_in, e_ref, h_ref, *refs):
    x_sends, (low_ref, rows_ref, sems) = refs[:x_rounds], refs[-3:]
    others = refs[x_rounds:-3]
    z_sends, d_sends = others[: len(others) // 2], others[len(others) // 2 :]
    cells_z = e_ref.shape[1]
    last, top = ROWS - 1, cells_z - 1
    copies = [
        [pltpu.make_async_copy(source.at[c], target.at[c], sems.at[n, c]) for c in range(3)]
        for n, (source, target) in enumerate(((e_in, e_ref), (h_in, h_ref)))
    ]
    for copy in copies[0] + copies[1]:
        copy.start()

    low_ref[2 * cells_z :, :] = jnp.zeros_like(low_ref[2 * cells_z :, :])
    rows_ref[5, top : top + 1, :] = jnp.zeros_like(rows_ref[5, top : top + 1, :])
    for copy in copies[0]:
        copy.wait()
    for z in range(cells_z):
        low_ref[z : z + 1, :] = e_ref[1, z, 0:1, :]
        low_ref[cells_z + z : cells_z + z + 1, :] = e_ref[2, z, 0:1, :]
        for c in range(3):
            rows_ref[c, z : z + 1, :] = e_ref[c, z, last : last + 1, :]
        if z > 0:
            rows_ref[5, z - 1 : z, :] = e_ref[0, z, last : last + 1, :]
    for copy in copies[1]:
        copy.wait()
    for z in range(cells_z):
        for c in range(2):
            rows_ref[3 + c, z : z + 1, :] = h_ref[1 + c, z, last : last + 1, :]
    width = e_ref.shape[3]
    ex, ey, ez = (rows_ref[c] for c in range(3))
    column = lax.broadcasted_iota(jnp.int32, ex.shape, 1)
    ex_next = jnp.where(column == width - 1, 0.0, pltpu.roll(ex, width - 1, 1))
    lane = lax.broadcasted_iota(jnp.int32, (ROWS, LANES), 1)
    strip = jnp.zeros((ROWS, LANES), jnp.float32)
    for j in range(cells_z // ROWS):
        head = rows_ref[0, j * ROWS : (j + 1) * ROWS, 0:LANES]
        strip = jnp.where(lane // STRIP == j, pltpu.roll(head, STRIP * j, 1) if j else head, strip)
    high = (
        rows_ref[3] - HALF * (rows_ref[5] - ex + ez),
        rows_ref[4] + HALF * ey - HALF * (ex - ex_next),
        jnp.concatenate([strip, jnp.zeros((ROWS, width - LANES), jnp.float32)], axis=1),
    )
    side = Side("gx")
    for c, value in enumerate(high):
        here = slice(c * cells_z, c * cells_z + value.shape[0])
        for ref, one in zip(x_sends, side.sends(low_ref[here, :], value)):
            ref[here, :] = one

    side = Side("gz")
    ex, ey, ez = (e_ref[c, top] for c in range(3))
    low = (e_ref[0, 0], e_ref[1, 0], jnp.zeros_like(ez))
    high = (h_ref[0, top] + HALF * ez - HALF * ey, h_ref[1, top] + HALF * ex - HALF * ez, ez)
    for c in range(3):
        for ref, value in zip(z_sends, side.sends(low[c], high[c])):
            ref[c] = value

    down, up = (
        jnp.broadcast_to(line, (ROWS, line.shape[1]))
        for line in (e_ref[0, 0, last : last + 1, :], e_ref[2, top, 0:1, :])
    )
    for ref, value in zip(d_sends, side.sends(down, up)):
        ref[...] = value


def halos(efield, hfield):
    _, cells_z, cells_x, cells_y = efield.shape
    x_rounds, z_rounds = rounds("gx"), rounds("gz")
    x_face, z_face, line = fast(2 * cells_z + ROWS, cells_y), fast(3, cells_x, cells_y), fast(ROWS, cells_y)
    fields = [fast(*field.shape) for field in (efield, hfield)]
    efield, hfield, *sends = pl.pallas_call(
        functools.partial(faces_kernel, x_rounds),
        in_specs=[ANY] * 2,
        out_specs=[VMEM] * (2 + x_rounds + 2 * z_rounds),
        out_shape=fields + [x_face] * x_rounds + [z_face] * z_rounds + [line] * z_rounds,
        scratch_shapes=[
            pltpu.VMEM(x_face.shape, jnp.float32),
            pltpu.VMEM((6, cells_z, cells_y), jnp.float32),
            pltpu.SemaphoreType.DMA((2, 3)),
        ],
        compiler_params=params(54),
    )(efield, hfield)
    xfaces = exchange(sends[:x_rounds], "gx", "gy")
    zfaces = exchange(sends[x_rounds : x_rounds + z_rounds], "gz", "gy")
    return efield, hfield, zfaces, xfaces, exchange_diagonal(sends[x_rounds + z_rounds :])


def lane_group():
    return lax.broadcasted_iota(jnp.int32, (ROWS, LANES), 1) // STRIP


def pack_strips(tiles, low_ref, high_ref, first):
    group = lane_group()
    width = tiles[0][1]
    for start in range(0, len(tiles), SLOTS):
        low = jnp.zeros((ROWS, LANES), jnp.float32)
        high = jnp.zeros((ROWS, LANES), jnp.float32)
        for k, (load, _) in enumerate(tiles[start : start + SLOTS]):
            if load is None:
                continue
            here = group == k
            shift = (STRIP * k) % LANES
            left = load(slice(0, LANES))
            right = load(slice(width - LANES, width))
            low = jnp.where(here, pltpu.roll(left, shift, 1) if shift else left, low)
            shift = (STRIP * k + STRIP) % LANES
            high = jnp.where(here, pltpu.roll(right, shift, 1) if shift else right, high)
        low_ref[first + start // SLOTS] = low
        high_ref[first + start // SLOTS] = high


def strips_kernel(
    permit_ref, e_ref, h_ref, f_in, mat_ref, grad_ref, mask_ref, f_ref, low_ref, high_ref, wide_ref, inv_ref, sems
):
    cells_z, width = e_ref.shape[1], e_ref.shape[3]
    layers = grad_ref.shape[0]
    blocks = mask_ref.shape[1]
    copies = [pltpu.make_async_copy(f_in.at[c], f_ref.at[c], sems.at[c]) for c in range(3)]
    for copy in copies:
        copy.start()

    inverse = [
        jnp.broadcast_to(HALF * (1.0 / permit_ref[0:1, m : m + 1]), (ROWS, width))
        for m in range(permit_ref.shape[1])
    ]
    for z in range(cells_z):
        inv = inverse[0]
        for m in range(1, len(inverse)):
            inv = jnp.where(mat_ref[z] == m, inverse[m], inv)
        inv_ref[z] = inv
    spread = (
        lax.broadcasted_iota(jnp.int32, (blocks, width), 0)
        == lax.broadcasted_iota(jnp.int32, (blocks, width), 1) // BLOCK
    ).astype(jnp.float32)
    mask = jnp.broadcast_to(mask_ref[...].astype(jnp.float32), (ROWS, blocks))
    wide_ref[...] = jnp.dot(mask, spread, preferred_element_type=jnp.float32)
    first = first_layer(cells_z, layers)
    tiles = []
    for z in range(cells_z):
        for ref in (e_ref, h_ref):
            for c in range(3):
                tiles.append((lambda s, r=ref, c=c, z=z: r[c, z, :, s], width))
    pack_strips(tiles, low_ref, high_ref, 0)

    for copy in copies:
        copy.wait()
    done = len(tiles) // SLOTS
    tiles = []
    for layer in range(layers):
        for c in range(3):
            tiles.append((lambda s, c=c, l=layer: f_ref[c, first + l, :, s], width))
        tiles.append((lambda s, l=layer: inv_ref[first + l, :, s], width))
        tiles.append((lambda s, l=layer: grad_ref[l, :, s], width))
        tiles.append((lambda s: wide_ref[:, s], width) if layer % ROWS == 0 else (None, width))
    pack_strips(tiles, low_ref, high_ref, done)


def strips(permit, efield, hfield, forward, material, grad_sum, mask):
    cells_z, width = efield.shape[1], efield.shape[3]
    count = (cells_z * 6 + grad_sum.shape[0] * 6) // SLOTS
    packed = (count, ROWS, LANES)
    shapes = (forward.shape, packed, packed, (ROWS, width), material.shape)
    return pl.pallas_call(
        strips_kernel,
        in_specs=[VMEM] * 3 + [ANY] + [VMEM] * 3,
        out_specs=[VMEM] * 5,
        out_shape=[fast(*shape) for shape in shapes],
        scratch_shapes=[pltpu.SemaphoreType.DMA((3,))],
        compiler_params=params(40),
    )(permit.reshape(1, -1), efield, hfield, forward, material, grad_sum, mask)


def edge_tile(load, width):
    lane = lax.broadcasted_iota(jnp.int32, (ROWS, LANES), 1)
    head = pltpu.roll(load(slice(0, LANES)), STRIP, 1)
    tail = pltpu.roll(load(slice(width - LANES, width)), LANES - STRIP, 1)
    return jnp.where(lane < LANES // 2, head, tail)


def edges_kernel(e_ref, h_ref, f_ref, inv_ref, grad_ref, mask_ref, eh_out, grad_out, mask_out):
    cells_z, width = e_ref.shape[1], e_ref.shape[3]
    layers = grad_ref.shape[0]
    first = first_layer(cells_z, layers)
    for z in range(cells_z):
        for c in range(3):
            eh_out[z, c] = edge_tile(lambda s: e_ref[c, z, :, s], width)
            eh_out[z, 3 + c] = edge_tile(lambda s: h_ref[c, z, :, s], width)
    for layer in range(layers):
        for c in range(3):
            grad_out[layer, c] = edge_tile(lambda s: f_ref[c, first + layer, :, s], width)
        grad_out[layer, 3] = edge_tile(lambda s: inv_ref[first + layer, :, s], width)
        grad_out[layer, 4] = edge_tile(lambda s: grad_ref[layer, :, s], width)
    mask_out[...] = edge_tile(lambda s: mask_ref[:, s], width)


def own_edges(arrays):
    cells_z, layers = arrays[0].shape[1], arrays[4].shape[0]
    return pl.pallas_call(
        edges_kernel,
        in_specs=[VMEM] * 6,
        out_specs=[VMEM] * 3,
        out_shape=[fast(cells_z, 6, ROWS, LANES), fast(layers, 5, ROWS, LANES), fast(ROWS, LANES)],
        compiler_params=params(),
    )(*arrays)


def corner_lines(lines, s):
    z_side, x_side = Side("gz"), Side("gx")
    above = jnp.where(x_side.bottom, 0.0, z_side.upper([f[:, s] for f in lines]))
    beyond = jnp.where(x_side.top, 0.0, z_side.lower([f[:, s] for f in lines]))
    return above, beyond


def face_tiles(zfaces, xfaces, lines):
    width = xfaces[0].shape[1]
    rows = xfaces[0].shape[0]
    cells_z = (rows - ROWS) // 2
    z_side, x_side = Side("gz"), Side("gx")

    def corner(s):
        row = lax.broadcasted_iota(jnp.int32, (ROWS, s.stop - s.start), 0)
        return jnp.where(row == ROWS - 1, -HALF * corner_lines(lines, s)[0], 0.0)

    def x_tile(pick, t, s):
        value = pick([f[t : t + ROWS, s] for f in xfaces])
        return value + corner(s) if lines and t == cells_z - ROWS and pick == x_side.lower else value

    def strip(j, s):
        zeros = jnp.zeros((ROWS, s.stop - s.start), jnp.float32)
        if s.start:
            return zeros
        lane = lax.broadcasted_iota(jnp.int32, (ROWS, LANES), 1)
        packed = x_side.lower([f[2 * cells_z :, 0:LANES] for f in xfaces])
        head = jnp.where(lane < STRIP, pltpu.roll(packed, LANES - STRIP * j, 1) if j else packed, 0.0)
        return head if s.stop == LANES else jnp.concatenate([head, zeros[:, LANES:]], axis=1)

    tiles = []
    for c in range(3):
        tiles.append((lambda s, c=c: z_side.lower([f[c, :, s] for f in zfaces]), width))
    for c in range(2):
        tiles.append((lambda s, c=c: z_side.upper([f[c, :, s] for f in zfaces]), width))
    for t in range(0, 2 * cells_z, ROWS):
        tiles.append((lambda s, t=t: x_tile(x_side.lower, t, s), width))
    for j in range(cells_z // ROWS):
        tiles.append((lambda s, j=j: strip(j, s), width))
    for t in range(0, rows, ROWS):
        if lines and t == 2 * cells_z:
            tiles.append((lambda s: corner_lines(lines, s)[1], width))
        else:
            tiles.append((lambda s, t=t: x_tile(x_side.upper, t, s), width))
    return tiles


def face_count(xface):
    per_field = (xface.shape[0] - ROWS) // ROWS // 2
    return 5 + 3 * per_field + 2 * per_field + 1


def y_faces_kernel(counts, *refs):
    own_low, own_high = refs[:2]
    ends = np.cumsum((2,) + counts)
    zfaces, xfaces, lines = (refs[i:j] for i, j in zip(ends[:-1], ends[1:]))
    sends, (low_ref, high_ref) = refs[3 + sum(counts) : -2], refs[-2:]
    own = own_low.shape[0]
    pack_strips(face_tiles(zfaces, xfaces, lines), low_ref, high_ref, 0)
    side = Side("gy")
    for ref, value in zip(sends, side.sends(own_low[...], own_high[...])):
        ref[0:own] = value
    for ref, value in zip(sends, side.sends(low_ref[...], high_ref[...])):
        ref[own:] = value


def y_faces(own_low, own_high, zfaces, xfaces, lines, after):
    extra = math.ceil(face_count(xfaces[0]) / SLOTS)
    packed = fast(own_low.shape[0] + extra, ROWS, LANES)
    return pl.pallas_call(
        functools.partial(y_faces_kernel, (len(zfaces), len(xfaces), len(lines))),
        in_specs=[VMEM] * (2 + len(zfaces) + len(xfaces) + len(lines)) + [ANY],
        out_specs=[VMEM] * rounds("gy"),
        out_shape=[packed] * rounds("gy"),
        scratch_shapes=[pltpu.VMEM((extra, ROWS, LANES), jnp.float32)] * 2,
        compiler_params=params(),
    )(own_low, own_high, *zfaces, *xfaces, *lines, after)


OWN, CIRCLE, EDGE = range(3)


def faces_wide(mode, width):
    return {OWN: width, CIRCLE: width + LANES, EDGE: LANES}[mode]


class Fields:
    def __init__(self, mode, layers, fields, zfaces, xfaces, lines, yfaces, scratch):
        self.mode = mode
        self.fields = fields
        if mode == EDGE:
            self.cells_z, self.width = fields.shape[0], xfaces[0].shape[1]
        else:
            self.cells_z, self.width = fields[0].shape[1], fields[0].shape[3]
        self.wide = faces_wide(mode, self.width)
        self.lane = lax.broadcasted_iota(jnp.int32, (ROWS, LANES), 1)
        self.row = lax.broadcasted_iota(jnp.int32, (ROWS, self.wide), 0)
        self.per_group = 6 * ROWS // SLOTS
        self.groups = self.cells_z // ROWS
        self.grad_base = self.per_group * self.groups
        halo_base = self.grad_base + self.per_group * (layers // ROWS)
        self.left_wide, self.right_wide = left_wide, right_wide = scratch[:2]
        if mode != OWN:
            self.ybuf = scratch[2]
            y_side = Side("gy")
            for t in range(yfaces[0].shape[0]):
                lower = y_side.lower([f[t] for f in yfaces])
                upper = y_side.upper([f[t] for f in yfaces])
                if mode == EDGE:
                    even = self.lane // STRIP % 2 == 0
                    lower, upper = (
                        jnp.where(even, upper, pltpu.roll(lower, STRIP, 1)),
                        jnp.where(even, pltpu.roll(upper, LANES - STRIP, 1), lower),
                    )
                self.ybuf[0, t] = lower
                self.ybuf[1, t] = upper

        def face(load, slot):
            if mode == EDGE:
                own = edge_tile(load, self.width)
                return self.edge(own, halo_base + slot // SLOTS, slot % SLOTS)
            return self.wider(load, halo_base + slot // SLOTS, slot % SLOTS)

        full = [face(load, slot) for slot, (load, _) in enumerate(face_tiles(zfaces, xfaces, lines))]
        self.below, self.above = full[:3], full[3:5]
        groups = self.groups
        for t in range(2 * groups):
            left_wide[t * ROWS : (t + 1) * ROWS, :] = full[5 + t]
        for t in range(2 * groups + 1):
            right_wide[t * ROWS : (t + 1) * ROWS, :] = full[5 + 3 * groups + t]
        if mode != OWN:
            column = lax.broadcasted_iota(jnp.int32, (ROWS, self.wide), 1)
            ends = {CIRCLE: (self.width - 1, self.wide - 1), EDGE: (STRIP - 1, LANES - STRIP - 1)}[mode]
            here = jnp.logical_or(column == ends[0], column == ends[1])
            for j in range(groups):
                ex_next = self.y_up(full[5 + 2 * groups + j])
                at = (groups + j) * ROWS
                left_wide[at : at + ROWS, :] += jnp.where(here, HALF * ex_next, 0.0)

    def wider(self, load, tile, k):
        if self.mode == OWN:
            return load(slice(0, self.width))

        def moved(v, to):
            shift = (to - STRIP * k) % LANES
            return pltpu.roll(v, shift, 1) if shift else v

        lower, upper = self.ybuf[0, tile], self.ybuf[1, tile]
        halo = jnp.where(self.lane < STRIP, moved(upper, 0), moved(lower, LANES - STRIP))
        return jnp.concatenate([load(slice(0, self.width)), halo], axis=1)

    def edge(self, own, tile, k):
        shift = (LANES - STRIP - 2 * STRIP * (k // 2)) % LANES
        both = pltpu.roll(self.ybuf[k % 2, tile], shift, 1)
        inside = jnp.logical_and(self.lane >= STRIP, self.lane < LANES - STRIP)
        return jnp.where(inside, own, both)

    def y_up(self, v):
        return pltpu.roll(v, self.wide - 1, 1)

    def y_down(self, v):
        return pltpu.roll(v, 1, 1)

    def x_up(self, v, line):
        return jnp.where(self.row == ROWS - 1, line, pltpu.roll(v, ROWS - 1, 0))

    def x_down(self, v, line):
        return jnp.where(self.row == 0, line, pltpu.roll(v, 1, 0))

    def line(self, ref, at):
        return jnp.broadcast_to(ref[pl.ds(at, 1), :], (ROWS, self.wide))

    def field(self, which, c, a, b):
        slot = 6 * b + 3 * which + c
        tile = self.per_group * a + slot // SLOTS
        if self.mode == EDGE:
            return self.edge(self.fields[ROWS * a + b, 3 * which + c], tile, slot % SLOTS)
        ref = self.fields[which]
        return self.wider(lambda s: ref[c, ROWS * a + b, :, s], tile, slot % SLOTS)

    def hx(self, a, b, ey, ez, ey_next):
        return self.field(1, 0, a, b) - HALF * (self.y_up(ez) - ez - ey_next + ey)

    def hy(self, a, b, ex, ez, ex_next):
        up = self.x_up(ez, self.line(self.right_wide, self.cells_z + ROWS * a + b))
        return self.field(1, 1, a, b) - HALF * (ex_next - ex - up + ez)

    def hz(self, a, b, ex, ey):
        up = self.x_up(ey, self.line(self.right_wide, ROWS * a + b))
        return self.field(1, 2, a, b) - HALF * (up - ey - self.y_up(ex) + ex)

    def start(self, a):
        ex, ey = self.field(0, 0, a, 0), self.field(0, 1, a, 0)
        below = self.below
        at_bottom = (
            below[0] - HALF * self.y_up(below[2]) + HALF * ey,
            below[1] - HALF * ex + HALF * self.x_up(below[2], self.line(self.right_wide, 2 * self.cells_z)),
        )
        before, b = jnp.maximum(a - 1, 0), ROWS - 1
        ex_before, ey_before, ez_before = (self.field(0, c, before, b) for c in range(3))
        inside = (
            self.hx(before, b, ey_before, ez_before, ey),
            self.hy(before, b, ex_before, ez_before, ex),
        )
        bottom = a == 0
        return (ex, ey) + tuple(jnp.where(bottom, one, two) for one, two in zip(at_bottom, inside))

    def group(self, a, carry, emit):
        ex, ey, hx_z, hy_z = carry
        for b in range(ROWS):
            z = ROWS * a + b
            ez = self.field(0, 2, a, b)
            if b < ROWS - 1:
                ex_next, ey_next = (self.field(0, c, a, b + 1) for c in range(2))
            else:
                end = a == self.groups - 1
                after = jnp.minimum(a + 1, self.groups - 1)
                ex_next, ey_next = (
                    jnp.where(end, self.above[c], self.field(0, c, after, 0)) for c in range(2)
                )
            hx = self.hx(a, b, ey, ez, ey_next)
            hy = self.hy(a, b, ex, ez, ex_next)
            hz = self.hz(a, b, ex, ey)
            hy_x = self.x_down(hy, self.line(self.left_wide, z) + HALF * ez)
            hz_x = self.x_down(hz, self.line(self.left_wide, self.cells_z + z) - HALF * ey)
            curl = (
                (hz - self.y_down(hz)) - (hy - hy_z),
                (hx - hx_z) - (hz - hz_x),
                (hy - hy_x) - (hx - self.y_down(hx)),
            )
            emit(a, b, (ex, ey, ez), (hx, hy, hz), curl)
            ex, ey, hx_z, hy_z = ex_next, ey_next, hx, hy
        return ex, ey, hx_z, hy_z

    def gradient(self, layers, arrays, store):
        first = first_layer(self.cells_z, layers)
        first_group = first // ROWS
        if self.mode == EDGE:
            grad_edges, mask_ref = arrays
            mask = self.edge(mask_ref[...], self.grad_base, 5)
        else:
            f_ref, inv_ref, grad_ref, mask_ref = arrays
            mask = mask_ref[...]

        def emit(a, b, efield, hfield, curl):
            z = ROWS * a + b
            layer = z - first
            if self.mode == EDGE:
                tile = self.grad_base + self.per_group * (a - first_group)
                slots = [6 * b + n for n in range(5)]
                values = [
                    self.edge(grad_edges[layer, n], tile + slot // SLOTS, slot % SLOTS)
                    for n, slot in enumerate(slots)
                ]
            else:
                values = [f_ref[c, z] for c in range(3)] + [inv_ref[z], grad_ref[layer]]
            total = None
            for c in range(3):
                term = values[c] * (efield[c] + values[3] * curl[c])
                total = term if total is None else total + term
            store(layer, values[4] + mask * total)

        def body(i, carry):
            return self.group(first_group + i, carry, emit)

        lax.fori_loop(0, layers // ROWS, body, self.start(first_group))


def fields_scratch(mode, xface, yface, width):
    rows, wide = xface.shape[0], faces_wide(mode, width)
    out = [pltpu.VMEM((rows, wide), jnp.float32)] * 2
    if mode != OWN:
        out.append(pltpu.VMEM((2,) + yface.shape, jnp.float32))
    return out


def own_gradient_kernel(counts, per_device, *refs):
    e_ref, h_ref, f_ref, inv_ref, grad_ref, mask_ref = refs[:6]
    zfaces, xfaces = refs[6 : 6 + counts[0]], refs[6 + counts[0] : 6 + sum(counts)]
    shares, (own_ref, *scratch) = refs[6 + sum(counts) : -3][::-1], refs[-3:]
    layers, _, width = grad_ref.shape
    fields = Fields(OWN, layers, (e_ref, h_ref), zfaces, xfaces, (), None, scratch)

    def store(layer, value):
        own_ref[layer] = value

    fields.gradient(layers, (f_ref, inv_ref, grad_ref, mask_ref), store)

    me = lax.axis_index("gx")
    for k, share in enumerate(shares):
        chunk = lax.bitwise_xor(me, k)
        for i in range(per_device):
            share[:, i * width : (i + 1) * width] = own_ref[chunk * per_device + i]
        if share.shape[1] > per_device * width:
            share[:, per_device * width :] = jnp.zeros((ROWS, SPARE), jnp.float32)


SPARE = 2 * LANES


def own_gradient(arrays, zfaces, xfaces):
    layers, _, width = arrays[4].shape
    count = lax.axis_size("gx")
    per_device = layers // count
    *shares, own = pl.pallas_call(
        functools.partial(own_gradient_kernel, (len(zfaces), len(xfaces)), per_device),
        in_specs=[VMEM] * (6 + len(zfaces) + len(xfaces)),
        out_specs=[VMEM] * (count + 1),
        out_shape=[fast(ROWS, per_device * width + SPARE)]
        + [fast(ROWS, per_device * width)] * (count - 1)
        + [fast(layers, ROWS, width)],
        scratch_shapes=fields_scratch(OWN, xfaces[0], None, width),
        compiler_params=params(),
    )(*arrays, *zfaces, *xfaces)
    return shares[::-1], own


PART = 2 * STRIP
SPAN = 2 * PART


def edge_gradient_kernel(counts, *refs):
    own_ref, f_ref, inv_ref, wide_ref, eh_ref, grad_ref, mask_ref, taps_ref = refs[:8]
    ends = np.cumsum((8,) + counts)
    zfaces, xfaces, lines, yfaces = (refs[i:j] for i, j in zip(ends[:-1], ends[1:]))
    (shares, message, edge_ref), scratch = refs[ends[-1] : -6], refs[-6:-3]
    folded, parts, slabs = refs[-3:]
    layers, _, width = own_ref.shape
    lane = lax.broadcasted_iota(jnp.int32, (ROWS, LANES), 1)
    first, last = STRIP, LANES - STRIP - 1
    fields = Fields(EDGE, layers, eh_ref, zfaces, xfaces, lines, yfaces, scratch)

    def store(layer, value):
        edge_ref[layer] = value

    fields.gradient(layers, (grad_ref, mask_ref), store)

    count = shares.shape[0]
    half = count // 2
    rows = half * ROWS
    me = lax.axis_index("gx")
    folded[...] = jnp.zeros_like(folded)
    fold = jnp.minimum(me, count - 1 - me)
    per_tile = LANES // SPAN
    for start in range(0, layers, per_tile):
        tile = jnp.zeros((ROWS, LANES), jnp.float32)
        for j in range(min(per_tile, layers - start)):
            edge = edge_ref[start + j]
            own = edge_tile(lambda s: own_ref[start + j, :, s], width)
            more = jnp.where(jnp.logical_or(lane == first, lane == last), edge - own, edge)
            low, high = SPAN * j + 1, SPAN * j + PART + STRIP - 1
            here = jnp.logical_and(lane >= low, lane < low + STRIP)
            tile = jnp.where(here, pltpu.roll(more, (low - 1) % LANES, 1), tile)
            here = jnp.logical_and(lane >= high, lane < high + STRIP)
            tile = jnp.where(here, pltpu.roll(more, (high - last) % LANES, 1), tile)
        tile = jnp.where(me < half, tile, flip_rows(tile))
        folded[fold, :, start // per_tile * LANES : (start // per_tile + 1) * LANES] = tile
    split_rows(jnp.concatenate([folded[s] for s in range(half)], axis=0), parts)
    total = cone(taps_ref, parts, rows)
    lanes = lax.broadcasted_iota(jnp.int32, (rows, LANES), 1)
    per_share = LANES // PART
    for start in range(0, layers, per_share):
        packed = jnp.zeros((rows, LANES), jnp.float32)
        for j in range(min(per_share, layers - start)):
            at = SPAN * (start + j)
            tile = total[:, at // LANES * LANES : (at // LANES + 1) * LANES]
            left = pltpu.roll(tile, (PART * j - STRIP - at) % LANES, 1)
            right = pltpu.roll(tile, (PART * j + STRIP - PART - 1 - at) % LANES, 1)
            packed = jnp.where(lanes // STRIP == 2 * j, left, packed)
            packed = jnp.where(lanes // STRIP == 2 * j + 1, right, packed)
        here = slice(start // per_share * LANES, (start // per_share + 1) * LANES)
        for s in range(half):
            one = packed[s * ROWS : (s + 1) * ROWS]
            slabs[s, :, here] = one
            slabs[count - 1 - s, :, here] = flip_rows(one)
    for k in range(count):
        shares[k] = slabs[lax.bitwise_xor(me, k)]

    message[...] = jnp.zeros_like(message)
    top, last = fields.cells_z - 1, ROWS - 1
    above, beyond = (line[0:1] for line in corner_lines(lines, slice(0, width)))
    added = wide_ref[0:1, :] * f_ref[2, top, 0:1, :] * inv_ref[top, 0:1, :] * (HALF * above)
    added += wide_ref[last:, :] * f_ref[0, 0, last:, :] * inv_ref[0, last:, :] * (HALF * beyond)
    column = lax.broadcasted_iota(jnp.int32, (1, width), 1)
    added = jnp.where(jnp.logical_or(column == 0, column == width - 1), 0.0, added)
    for at, n in line_places(width):
        message[n : n + 1, at : at + LANES] = added[:, (at // LANES * ROWS + n) * LANES :][:, :LANES]


def line_places(width):
    return [(t // ROWS * LANES, t % ROWS) for t in range(width // LANES)]


def line_of(message, width):
    return jnp.concatenate([message[n : n + 1, at : at + LANES] for at, n in line_places(width)], axis=1)


def line_spot(layers):
    bottom = lax.axis_index("gz") == 0
    return jnp.where(bottom, layers - 1, 0), jnp.where(bottom, 0, ROWS - 1)


def edge_gradient(own, arrays, edges, taps, zfaces, xfaces, lines, yfaces):
    layers, _, width = own.shape
    faces = (*zfaces, *xfaces, *lines, *yfaces)
    count = lax.axis_size("gx")
    share = (count, ROWS, math.ceil(layers * PART / LANES) * LANES)
    spread = math.ceil(layers * SPAN / LANES) * LANES
    line = math.ceil(width / LANES / ROWS) * LANES
    return pl.pallas_call(
        functools.partial(edge_gradient_kernel, (len(zfaces), len(xfaces), len(lines), len(yfaces))),
        in_specs=[VMEM] * (8 + len(faces)),
        out_specs=[VMEM] * 3,
        out_shape=[fast(*share), fast(ROWS, line), fast(layers, ROWS, LANES)],
        scratch_shapes=fields_scratch(EDGE, xfaces[0], yfaces[0], width)
        + [
            pltpu.VMEM((count // 2, ROWS, spread), jnp.float32),
            pltpu.VMEM((3 * count // 2 * ROWS, spread), jnp.bfloat16),
            pltpu.VMEM(share, jnp.float32),
        ],
        compiler_params=params(),
    )(own, arrays[2], arrays[3], arrays[5], *edges, taps, *faces)


def step_kernel(counts, *refs):
    e_ref, h_ref, inv_ref, own_ref, edge_ref, message = refs[:6]
    ends = np.cumsum((6,) + counts)
    zfaces, xfaces, lines, yfaces = (refs[i:j] for i, j in zip(ends[:-1], ends[1:]))
    e_out, h_out, grad_out = refs[ends[-1] + 1 : ends[-1] + 4]
    left_wide, right_wide, ybuf, e_new, h_new, grad_new, sems = refs[ends[-1] + 4 :]
    layers, _, width = own_ref.shape
    lane = lax.broadcasted_iota(jnp.int32, (ROWS, LANES), 1)

    for layer in range(layers):
        edge = edge_ref[layer]
        head, tail = own_ref[layer, :, 0:LANES], own_ref[layer, :, width - LANES :]
        grad_new[layer] = own_ref[layer]
        grad_new[layer, :, 0:LANES] = jnp.where(lane == 0, pltpu.roll(edge, LANES - STRIP, 1), head)
        grad_new[layer, :, width - LANES :] = jnp.where(lane == LANES - 1, pltpu.roll(edge, STRIP, 1), tail)
    layer, spot = line_spot(layers)
    row = lax.broadcasted_iota(jnp.int32, (ROWS, width), 0)
    grad_new[layer] += jnp.where(row == spot, line_of(message, width), 0.0)
    grad_copy = pltpu.make_async_copy(grad_new, grad_out, sems.at[0, 0])
    grad_copy.start()

    fields = Fields(CIRCLE, layers, (e_ref, h_ref), zfaces, xfaces, lines, yfaces, (left_wide, right_wide, ybuf))

    def emit(a, b, efield, hfield, curl):
        z = ROWS * a + b
        half_inv = inv_ref[z]
        for c in range(3):
            e_new[c, z] = efield[c][:, :width] + half_inv * curl[c][:, :width]
            h_new[c, z] = hfield[c][:, :width]

    def copies(a):
        here = pl.ds(a * ROWS, ROWS)
        return [
            pltpu.make_async_copy(new.at[c, here], out.at[c, here], sems.at[1 + a, 3 * n + c])
            for n, (new, out) in enumerate(((e_new, e_out), (h_new, h_out)))
            for c in range(3)
        ]

    def body(a, carry):
        carry = fields.group(a, carry, emit)
        for copy in copies(a):
            copy.start()
        return carry

    lax.fori_loop(0, fields.groups, body, fields.start(0))
    for a in range(fields.groups):
        for copy in copies(a):
            copy.wait()
    grad_copy.wait()


def step(efield, hfield, inv, own, edge, message, zfaces, xfaces, lines, yfaces, after):
    _, cells_z, _, width = efield.shape
    groups = (zfaces, xfaces, lines, yfaces)
    counts = tuple(len(group) for group in groups)
    shapes = (efield.shape, hfield.shape, own.shape)
    return pl.pallas_call(
        functools.partial(step_kernel, counts),
        in_specs=[VMEM] * (6 + sum(counts)) + [ANY],
        out_specs=[ANY] * 3,
        out_shape=[f32(*shape) for shape in shapes],
        scratch_shapes=fields_scratch(CIRCLE, xfaces[0], yfaces[0], width)
        + [pltpu.VMEM(shape, jnp.float32) for shape in shapes]
        + [pltpu.SemaphoreType.DMA((1 + cells_z // ROWS, 6))],
        compiler_params=params(),
    )(efield, hfield, inv, own, edge, message, *(one for group in groups for one in group), after)


def cone_taps():
    span = np.arange(-RADIUS, RADIUS + 1, dtype=np.float64)
    return np.maximum(RADIUS - np.sqrt(span[:, None] ** 2 + span[None, :] ** 2), 0.0)


def cone_sum():
    return cone_taps().sum()


def cone_matrix(rows):
    weight = cone_taps() / cone_sum()
    x = np.arange(rows)
    out = np.zeros((RADIUS + 1, rows, rows))
    for b in range(RADIUS + 1):
        for apart in (x[:, None] - x[None, :], 2 * rows - 1 - x[:, None] - x[None, :]):
            near = np.abs(apart) <= RADIUS
            out[b] += np.where(near, weight[np.clip(apart, -RADIUS, RADIUS) + RADIUS, RADIUS + b], 0.0)
    out = out.reshape((RADIUS + 1) * rows, rows).astype(np.float32)
    high = out.astype(jnp.bfloat16)
    low = (out - high.astype(np.float32)).astype(jnp.bfloat16)
    return np.concatenate([high, low, high], axis=1)


def flip_rows(v):
    row = lax.broadcasted_iota(jnp.int32, v.shape, 0)
    v = pltpu.roll(v, 4, 0)
    v = jnp.where(row % 4 < 2, pltpu.roll(v, ROWS - 2, 0), pltpu.roll(v, 2, 0))
    return jnp.where(row % 2 < 1, pltpu.roll(v, ROWS - 1, 0), pltpu.roll(v, 1, 0))


def split_rows(symmetric, parts):
    rows = symmetric.shape[0]
    high = symmetric.astype(jnp.bfloat16)
    low = (symmetric - high.astype(jnp.float32)).astype(jnp.bfloat16)
    parts[0:rows, :] = high
    parts[rows : 2 * rows, :] = high
    parts[2 * rows : 3 * rows, :] = low


def cone(taps_ref, parts, rows):
    wide = parts.shape[1]
    mixed = jnp.dot(taps_ref[...], parts[...], preferred_element_type=jnp.float32)
    total = mixed[0:rows]
    for b in range(1, RADIUS + 1):
        part = mixed[b * rows : (b + 1) * rows]
        total = total + (pltpu.roll(part, b, 1) + pltpu.roll(part, wide - b, 1))
    return total


def filter_kernel(count, per_device, width, *refs):
    taps_ref, edges_ref, line_ref = refs[:3]
    got = refs[count + 2 : 2 : -1]
    outs = refs[3 + count : 3 + 2 * count]
    slabs, parts, done = refs[3 + 2 * count :]
    me = lax.axis_index("gx")
    half = count // 2
    rows = half * ROWS
    for k in range(count):
        slabs[lax.bitwise_xor(me, k)] = got[k][:, : per_device * width]

    side = jnp.zeros((rows, LANES), jnp.float32)
    for i in range(per_device):
        here = slice(i * width, (i + 1) * width)
        halves = [slabs[s, :, here] + flip_rows(slabs[count - 1 - s, :, here]) for s in range(half)]
        split_rows(jnp.concatenate([jnp.concatenate(halves, axis=0), side], axis=1), parts)
        total = cone(taps_ref, parts, rows)
        for s in range(half):
            own = total[s * ROWS : (s + 1) * ROWS, :width]
            done[s, :, here] = own
            done[count - 1 - s, :, here] = flip_rows(own)
    for k in range(count):
        outs[k][:, : per_device * width] = done[lax.bitwise_xor(me, k)]
        tail = per_device * width + edges_ref.shape[2]
        outs[k][:, per_device * width : tail] = edges_ref[k]
        outs[k][:, tail:] = line_ref[...]


def cone_filter(taps, edges, line, got, per_device, width):
    count = len(got)
    rows = count // 2 * ROWS
    return pl.pallas_call(
        functools.partial(filter_kernel, count, per_device, width),
        in_specs=[VMEM] * (3 + count),
        out_specs=[VMEM] * count,
        out_shape=[fast(ROWS, per_device * width + edges.shape[2] + line.shape[1])] * count,
        scratch_shapes=[
            pltpu.VMEM((count, ROWS, per_device * width), jnp.float32),
            pltpu.VMEM((3 * rows, width + LANES), jnp.bfloat16),
            pltpu.VMEM((count, ROWS, per_device * width), jnp.float32),
        ],
        compiler_params=params(),
    )(taps, edges, line, *got[::-1])


def cone_weight(along_x, along_y):
    near = jnp.maximum(RADIUS - jnp.sqrt(along_x * along_x + float(along_y * along_y)), 0.0)
    return near * float(1.0 / cone_sum())


def finish_kernel(count, per_device, width, *refs):
    got = refs[count - 1 :: -1]
    out, (left, right, done, sems) = refs[count], refs[count + 1 :]
    me = lax.axis_index("gx")
    layers = count * per_device
    lane = lax.broadcasted_iota(jnp.int32, (ROWS, LANES), 1)
    edges_at = per_device * width
    line_at = edges_at + math.ceil(layers * PART / LANES) * LANES

    per_tile = LANES // PART
    for start in range(0, layers, per_tile):
        at = edges_at + start * PART
        tile = got[0][:, at : at + LANES]
        for k in range(1, count):
            tile = tile + got[k][:, at : at + LANES]
        for j in range(min(per_tile, layers - start)):
            head = pltpu.roll(tile, (-PART * j) % LANES, 1)
            left[start + j] = jnp.where(lane < STRIP - 1, head, 0.0)
            tail = pltpu.roll(tile, (LANES + 1 - 2 * STRIP - PART * j) % LANES, 1)
            right[start + j] = jnp.where(lane > LANES - STRIP, tail, 0.0)

    line_layer, spot = line_spot(layers)
    end = count * ROWS - 1
    row = lax.broadcasted_iota(jnp.int32, (ROWS, LANES), 0) + me * ROWS
    lines, near, far = [], [], []
    for k in range(count):
        lines.append(line_of(got[k][:, line_at:], width))
        where = lax.bitwise_xor(me, k) * ROWS + spot
        near.append((row - where).astype(jnp.float32))
        far.append((row - (end - where)).astype(jnp.float32))
    total = None
    for b in range(RADIUS + 1):
        mixed = jnp.zeros((ROWS, width), jnp.float32)
        for k in range(count):
            weight = cone_weight(near[k], b) + cone_weight(far[k], b)
            mixed = mixed + jnp.concatenate([weight] * (width // LANES), axis=1) * lines[k]
        mixed = jnp.concatenate([mixed, jnp.zeros((ROWS, LANES), jnp.float32)], axis=1)
        if b:
            mixed = pltpu.roll(mixed, b, 1) + pltpu.roll(mixed, width + LANES - b, 1)
        total = mixed if total is None else total + mixed
    line = total[:, :width]

    copies = []
    for k in range(count):
        first = lax.bitwise_xor(me, k) * per_device
        for i in range(per_device):
            at = i * width
            done[k, i] = got[k][:, at : at + width] + jnp.where(first + i == line_layer, line, 0.0)
            done[k, i, :, :LANES] += left[first + i]
            done[k, i, :, width - LANES :] += right[first + i]
        copies.append(pltpu.make_async_copy(done.at[k], out.at[pl.ds(first, per_device)], sems.at[k]))
        copies[-1].start()
    for copy in copies:
        copy.wait()


def finish(parts, layers, width):
    count = len(parts)
    per_device = layers // count
    return pl.pallas_call(
        functools.partial(finish_kernel, count, per_device, width),
        in_specs=[VMEM] * count,
        out_specs=ANY,
        out_shape=f32(layers, ROWS, width),
        scratch_shapes=[
            pltpu.VMEM((layers, ROWS, LANES), jnp.float32),
            pltpu.VMEM((layers, ROWS, LANES), jnp.float32),
            pltpu.VMEM((count, per_device, ROWS, width), jnp.float32),
            pltpu.SemaphoreType.DMA((count,)),
        ],
        compiler_params=params(),
    )(*parts[::-1])


def spread(parts):
    count = len(parts)
    got = list(parts)
    for k in range(count - 1, 0, -1):
        got[k] = lax.ppermute(parts[k], "gx", [(i, i ^ k) for i in range(count)])
    return got


def on_device(efield, hfield, forward, material, permit, design_mask, grad_sum):
    layers, _, width = grad_sum.shape
    efield, hfield, zfaces, xfaces, lines = halos(efield, hfield)
    forward, own_low, own_high, mask, inv = strips(
        permit, efield, hfield, forward, material, grad_sum, design_mask
    )
    arrays = (efield, hfield, forward, inv, grad_sum, mask)
    edges = own_edges(arrays)
    shares, own = own_gradient(arrays, zfaces, xfaces)
    got = spread(shares)
    yfaces = exchange(y_faces(own_low, own_high, zfaces, xfaces, lines, own), "gy", "gz")
    taps = jnp.asarray(cone_matrix(len(got) // 2 * ROWS))
    added, line, edge = edge_gradient(own, arrays, edges, taps, zfaces, xfaces, lines, yfaces)
    parts = cone_filter(taps, added, line, got, layers // len(got), width)
    e_next, h_next, grad_total = step(
        efield, hfield, inv, own, edge, line, zfaces, xfaces, lines, yfaces, parts[0]
    )
    return e_next, h_next, grad_total, finish(spread(parts), layers, width)


def solution(mesh):
    field = P(None, "gz", "gx", "gy")
    cells = P("gz", "gx", "gy")
    return jax.shard_map(
        on_device,
        mesh=mesh,
        in_specs=(field, field, field, cells, P(), P("gx", "gy"), cells),
        out_specs=(field, field, cells, cells),
        check_vma=False,
    )
```

```python
import functools
import math

import jax
import jax.numpy as jnp
import numpy as np
from jax import lax
from jax.experimental import pallas as pl
from jax.experimental.pallas import tpu as pltpu
from jax.sharding import PartitionSpec as P

RADIUS = 6
BLOCK = 8
HALF = 0.5

ROWS = 8
LANES = 128
STRIP = 8
SLOTS = LANES // STRIP
MIB = 1024 * 1024

VMEM = pl.BlockSpec(memory_space=pltpu.VMEM)
SMEM = pl.BlockSpec(memory_space=pltpu.SMEM)
ANY = pl.BlockSpec(memory_space=pl.ANY)


def params(mib=24):
    return pltpu.CompilerParams(vmem_limit_bytes=mib * MIB)


def f32(*shape):
    return jax.ShapeDtypeStruct(shape, jnp.float32)


def fast(*shape):
    return pltpu.VMEM(shape, jnp.float32)


def rounds(axis):
    return 2 if lax.axis_size(axis) > 2 else 1


def exchange(sends, axis, mate):
    count = lax.axis_size(axis)
    beside = lax.axis_size(mate)
    if count == 1:
        return sends
    got = []
    for start, value in enumerate(sends):
        partner = list(range(count))
        for low in range(start, count - 1, 2):
            partner[low], partner[low + 1] = low + 1, low
        axes = sorted((axis, mate))
        steps = (beside, 1) if axes[0] == axis else (1, count)
        pairs = []
        for i in range(count):
            for m in range(beside):
                if partner[i] != i:
                    to = (partner[i], m)
                elif beside % 2 == 0:
                    to = (i, m ^ 1)
                else:
                    continue
                pairs.append((i * steps[0] + m * steps[1], to[0] * steps[0] + to[1] * steps[1]))
        got.append(lax.ppermute(value, tuple(axes), pairs))
    return got


def exchange_diagonal(sends):
    along_x, along_y, along_z = (lax.axis_size(axis) for axis in AXES)

    def flat(x, y, z):
        return (x * along_y + y) * along_z + z

    got = []
    for start, value in enumerate(sends):
        partner = {}
        for low in range(start, along_z - 1, 2):
            for x in range(1, along_x):
                partner[x, low] = (x - 1, low + 1)
                partner[x - 1, low + 1] = (x, low)
        pairs = []
        for x in range(along_x):
            for z in range(along_z):
                for y in range(along_y):
                    if (x, z) in partner:
                        to = partner[x, z]
                        pairs.append((flat(x, y, z), flat(to[0], y, to[1])))
                    elif along_y % 2 == 0:
                        pairs.append((flat(x, y, z), flat(x, y ^ 1, z)))
        got.append(lax.ppermute(value, AXES, pairs))
    return got


AXES = ("gx", "gy", "gz")


class Side:
    def __init__(self, axis):
        index = lax.axis_index(axis)
        self.rounds = rounds(axis)
        self.odd = index % 2 == 1
        self.bottom = index == 0
        self.top = index == lax.axis_size(axis) - 1

    def sends(self, low, high):
        both = [jnp.where(self.odd, low, high)]
        if self.rounds > 1:
            both.append(jnp.where(self.odd, high, low))
        return both

    def lower(self, got):
        return jnp.where(self.bottom, 0.0, jnp.where(self.odd, got[0], got[-1]))

    def upper(self, got):
        return jnp.where(self.top, 0.0, jnp.where(self.odd, got[-1], got[0]))


def first_layer(cells_z, layers):
    return (cells_z - layers) * (1 - lax.axis_index("gz"))


def faces_kernel(x_rounds, e_in, h_in, e_ref, h_ref, *refs):
    x_sends, (low_ref, rows_ref, sems) = refs[:x_rounds], refs[-3:]
    others = refs[x_rounds:-3]
    z_sends, d_sends = others[: len(others) // 2], others[len(others) // 2 :]
    cells_z = e_ref.shape[1]
    last, top = ROWS - 1, cells_z - 1
    copies = [
        [pltpu.make_async_copy(source.at[c], target.at[c], sems.at[n, c]) for c in range(3)]
        for n, (source, target) in enumerate(((e_in, e_ref), (h_in, h_ref)))
    ]
    for copy in copies[0] + copies[1]:
        copy.start()

    low_ref[2 * cells_z :, :] = jnp.zeros_like(low_ref[2 * cells_z :, :])
    rows_ref[5, top : top + 1, :] = jnp.zeros_like(rows_ref[5, top : top + 1, :])
    for copy in copies[0]:
        copy.wait()
    for z in range(cells_z):
        low_ref[z : z + 1, :] = e_ref[1, z, 0:1, :]
        low_ref[cells_z + z : cells_z + z + 1, :] = e_ref[2, z, 0:1, :]
        for c in range(3):
            rows_ref[c, z : z + 1, :] = e_ref[c, z, last : last + 1, :]
        if z > 0:
            rows_ref[5, z - 1 : z, :] = e_ref[0, z, last : last + 1, :]
    for copy in copies[1]:
        copy.wait()
    for z in range(cells_z):
        for c in range(2):
            rows_ref[3 + c, z : z + 1, :] = h_ref[1 + c, z, last : last + 1, :]
    width = e_ref.shape[3]
    ex, ey, ez = (rows_ref[c] for c in range(3))
    column = lax.broadcasted_iota(jnp.int32, ex.shape, 1)
    ex_next = jnp.where(column == width - 1, 0.0, pltpu.roll(ex, width - 1, 1))
    lane = lax.broadcasted_iota(jnp.int32, (ROWS, LANES), 1)
    strip = jnp.zeros((ROWS, LANES), jnp.float32)
    for j in range(cells_z // ROWS):
        head = rows_ref[0, j * ROWS : (j + 1) * ROWS, 0:LANES]
        strip = jnp.where(lane // STRIP == j, pltpu.roll(head, STRIP * j, 1) if j else head, strip)
    high = (
        rows_ref[3] - HALF * (rows_ref[5] - ex + ez),
        rows_ref[4] + HALF * ey - HALF * (ex - ex_next),
        jnp.concatenate([strip, jnp.zeros((ROWS, width - LANES), jnp.float32)], axis=1),
    )
    side = Side("gx")
    for c, value in enumerate(high):
        here = slice(c * cells_z, c * cells_z + value.shape[0])
        for ref, one in zip(x_sends, side.sends(low_ref[here, :], value)):
            ref[here, :] = one

    side = Side("gz")
    ex, ey, ez = (e_ref[c, top] for c in range(3))
    low = (e_ref[0, 0], e_ref[1, 0], jnp.zeros_like(ez))
    high = (h_ref[0, top] + HALF * ez - HALF * ey, h_ref[1, top] + HALF * ex - HALF * ez, ez)
    for c in range(3):
        for ref, value in zip(z_sends, side.sends(low[c], high[c])):
            ref[c] = value

    down, up = (
        jnp.broadcast_to(line, (ROWS, line.shape[1]))
        for line in (e_ref[0, 0, last : last + 1, :], e_ref[2, top, 0:1, :])
    )
    for ref, value in zip(d_sends, side.sends(down, up)):
        ref[...] = value


def halos(efield, hfield):
    _, cells_z, cells_x, cells_y = efield.shape
    x_rounds, z_rounds = rounds("gx"), rounds("gz")
    x_face, z_face, line = fast(2 * cells_z + ROWS, cells_y), fast(3, cells_x, cells_y), fast(ROWS, cells_y)
    fields = [fast(*field.shape) for field in (efield, hfield)]
    efield, hfield, *sends = pl.pallas_call(
        functools.partial(faces_kernel, x_rounds),
        in_specs=[ANY] * 2,
        out_specs=[VMEM] * (2 + x_rounds + 2 * z_rounds),
        out_shape=fields + [x_face] * x_rounds + [z_face] * z_rounds + [line] * z_rounds,
        scratch_shapes=[
            pltpu.VMEM(x_face.shape, jnp.float32),
            pltpu.VMEM((6, cells_z, cells_y), jnp.float32),
            pltpu.SemaphoreType.DMA((2, 3)),
        ],
        compiler_params=params(54),
    )(efield, hfield)
    xfaces = exchange(sends[:x_rounds], "gx", "gy")
    zfaces = exchange(sends[x_rounds : x_rounds + z_rounds], "gz", "gy")
    return efield, hfield, zfaces, xfaces, exchange_diagonal(sends[x_rounds + z_rounds :])


def lane_group():
    return lax.broadcasted_iota(jnp.int32, (ROWS, LANES), 1) // STRIP


def pack_strips(tiles, low_ref, high_ref, first):
    group = lane_group()
    width = tiles[0][1]
    for start in range(0, len(tiles), SLOTS):
        low = jnp.zeros((ROWS, LANES), jnp.float32)
        high = jnp.zeros((ROWS, LANES), jnp.float32)
        for k, (load, _) in enumerate(tiles[start : start + SLOTS]):
            if load is None:
                continue
            here = group == k
            shift = (STRIP * k) % LANES
            left = load(slice(0, LANES))
            right = load(slice(width - LANES, width))
            low = jnp.where(here, pltpu.roll(left, shift, 1) if shift else left, low)
            shift = (STRIP * k + STRIP) % LANES
            high = jnp.where(here, pltpu.roll(right, shift, 1) if shift else right, high)
        low_ref[first + start // SLOTS] = low
        high_ref[first + start // SLOTS] = high


def strips_kernel(
    permit_ref, e_ref, h_ref, f_ref, mat_ref, grad_ref, mask_ref, low_ref, high_ref, wide_ref, inv_ref
):
    cells_z, width = e_ref.shape[1], e_ref.shape[3]
    layers = grad_ref.shape[0]
    blocks = mask_ref.shape[1]
    inverse = [
        jnp.broadcast_to(HALF * (1.0 / permit_ref[0:1, m : m + 1]), (ROWS, width))
        for m in range(permit_ref.shape[1])
    ]
    for z in range(cells_z):
        inv = inverse[0]
        for m in range(1, len(inverse)):
            inv = jnp.where(mat_ref[z] == m, inverse[m], inv)
        inv_ref[z] = inv
    spread = (
        lax.broadcasted_iota(jnp.int32, (blocks, width), 0)
        == lax.broadcasted_iota(jnp.int32, (blocks, width), 1) // BLOCK
    ).astype(jnp.float32)
    mask = jnp.broadcast_to(mask_ref[...].astype(jnp.float32), (ROWS, blocks))
    wide_ref[...] = jnp.dot(mask, spread, preferred_element_type=jnp.float32)
    first = first_layer(cells_z, layers)
    tiles = []
    for z in range(cells_z):
        for ref in (e_ref, h_ref):
            for c in range(3):
                tiles.append((lambda s, r=ref, c=c, z=z: r[c, z, :, s], width))
    pack_strips(tiles, low_ref, high_ref, 0)

    done = len(tiles) // SLOTS
    tiles = []
    for layer in range(layers):
        for c in range(3):
            tiles.append((lambda s, c=c, l=layer: f_ref[c, first + l, :, s], width))
        tiles.append((lambda s, l=layer: inv_ref[first + l, :, s], width))
        tiles.append((lambda s, l=layer: grad_ref[l, :, s], width))
        tiles.append((lambda s: wide_ref[:, s], width) if layer % ROWS == 0 else (None, width))
    pack_strips(tiles, low_ref, high_ref, done)


def strips(permit, efield, hfield, forward, material, grad_sum, mask):
    cells_z, width = efield.shape[1], efield.shape[3]
    count = (cells_z * 6 + grad_sum.shape[0] * 6) // SLOTS
    packed = (count, ROWS, LANES)
    shapes = (packed, packed, (ROWS, width), material.shape)
    return pl.pallas_call(
        strips_kernel,
        in_specs=[VMEM] * 7,
        out_specs=[VMEM] * 4,
        out_shape=[fast(*shape) for shape in shapes],
        compiler_params=params(),
    )(permit.reshape(1, -1), efield, hfield, forward, material, grad_sum, mask)


def edge_tile(load, width):
    lane = lax.broadcasted_iota(jnp.int32, (ROWS, LANES), 1)
    head = pltpu.roll(load(slice(0, LANES)), STRIP, 1)
    tail = pltpu.roll(load(slice(width - LANES, width)), LANES - STRIP, 1)
    return jnp.where(lane < LANES // 2, head, tail)


def edges_kernel(e_ref, h_ref, f_ref, inv_ref, grad_ref, mask_ref, eh_out, grad_out, mask_out):
    cells_z, width = e_ref.shape[1], e_ref.shape[3]
    layers = grad_ref.shape[0]
    first = first_layer(cells_z, layers)
    for z in range(cells_z):
        for c in range(3):
            eh_out[z, c] = edge_tile(lambda s: e_ref[c, z, :, s], width)
            eh_out[z, 3 + c] = edge_tile(lambda s: h_ref[c, z, :, s], width)
    for layer in range(layers):
        for c in range(3):
            grad_out[layer, c] = edge_tile(lambda s: f_ref[c, first + layer, :, s], width)
        grad_out[layer, 3] = edge_tile(lambda s: inv_ref[first + layer, :, s], width)
        grad_out[layer, 4] = edge_tile(lambda s: grad_ref[layer, :, s], width)
    mask_out[...] = edge_tile(lambda s: mask_ref[:, s], width)


def own_edges(arrays):
    cells_z, layers = arrays[0].shape[1], arrays[4].shape[0]
    return pl.pallas_call(
        edges_kernel,
        in_specs=[VMEM] * 6,
        out_specs=[VMEM] * 3,
        out_shape=[fast(cells_z, 6, ROWS, LANES), fast(layers, 5, ROWS, LANES), fast(ROWS, LANES)],
        compiler_params=params(),
    )(*arrays)


def corner_lines(lines, s):
    z_side, x_side = Side("gz"), Side("gx")
    above = jnp.where(x_side.bottom, 0.0, z_side.upper([f[:, s] for f in lines]))
    beyond = jnp.where(x_side.top, 0.0, z_side.lower([f[:, s] for f in lines]))
    return above, beyond


def face_tiles(zfaces, xfaces, lines):
    width = xfaces[0].shape[1]
    rows = xfaces[0].shape[0]
    cells_z = (rows - ROWS) // 2
    z_side, x_side = Side("gz"), Side("gx")

    def corner(s):
        row = lax.broadcasted_iota(jnp.int32, (ROWS, s.stop - s.start), 0)
        return jnp.where(row == ROWS - 1, -HALF * corner_lines(lines, s)[0], 0.0)

    def x_tile(pick, t, s):
        value = pick([f[t : t + ROWS, s] for f in xfaces])
        return value + corner(s) if lines and t == cells_z - ROWS and pick == x_side.lower else value

    def strip(j, s):
        zeros = jnp.zeros((ROWS, s.stop - s.start), jnp.float32)
        if s.start:
            return zeros
        lane = lax.broadcasted_iota(jnp.int32, (ROWS, LANES), 1)
        packed = x_side.lower([f[2 * cells_z :, 0:LANES] for f in xfaces])
        head = jnp.where(lane < STRIP, pltpu.roll(packed, LANES - STRIP * j, 1) if j else packed, 0.0)
        return head if s.stop == LANES else jnp.concatenate([head, zeros[:, LANES:]], axis=1)

    tiles = []
    for c in range(3):
        tiles.append((lambda s, c=c: z_side.lower([f[c, :, s] for f in zfaces]), width))
    for c in range(2):
        tiles.append((lambda s, c=c: z_side.upper([f[c, :, s] for f in zfaces]), width))
    for t in range(0, 2 * cells_z, ROWS):
        tiles.append((lambda s, t=t: x_tile(x_side.lower, t, s), width))
    for j in range(cells_z // ROWS):
        tiles.append((lambda s, j=j: strip(j, s), width))
    for t in range(0, rows, ROWS):
        if lines and t == 2 * cells_z:
            tiles.append((lambda s: corner_lines(lines, s)[1], width))
        else:
            tiles.append((lambda s, t=t: x_tile(x_side.upper, t, s), width))
    return tiles


def face_count(xface):
    per_field = (xface.shape[0] - ROWS) // ROWS // 2
    return 5 + 3 * per_field + 2 * per_field + 1


def y_faces_kernel(counts, *refs):
    own_low, own_high = refs[:2]
    ends = np.cumsum((2,) + counts)
    zfaces, xfaces, lines = (refs[i:j] for i, j in zip(ends[:-1], ends[1:]))
    sends, (low_ref, high_ref) = refs[3 + sum(counts) : -2], refs[-2:]
    own = own_low.shape[0]
    pack_strips(face_tiles(zfaces, xfaces, lines), low_ref, high_ref, 0)
    side = Side("gy")
    for ref, value in zip(sends, side.sends(own_low[...], own_high[...])):
        ref[0:own] = value
    for ref, value in zip(sends, side.sends(low_ref[...], high_ref[...])):
        ref[own:] = value


def y_faces(own_low, own_high, zfaces, xfaces, lines, after):
    extra = math.ceil(face_count(xfaces[0]) / SLOTS)
    packed = fast(own_low.shape[0] + extra, ROWS, LANES)
    return pl.pallas_call(
        functools.partial(y_faces_kernel, (len(zfaces), len(xfaces), len(lines))),
        in_specs=[VMEM] * (2 + len(zfaces) + len(xfaces) + len(lines)) + [ANY],
        out_specs=[VMEM] * rounds("gy"),
        out_shape=[packed] * rounds("gy"),
        scratch_shapes=[pltpu.VMEM((extra, ROWS, LANES), jnp.float32)] * 2,
        compiler_params=params(),
    )(own_low, own_high, *zfaces, *xfaces, *lines, after)


OWN, CIRCLE, EDGE = range(3)


def faces_wide(mode, width):
    return {OWN: width, CIRCLE: width + LANES, EDGE: LANES}[mode]


class Fields:
    def __init__(self, mode, layers, fields, zfaces, xfaces, lines, yfaces, scratch):
        self.mode = mode
        self.fields = fields
        if mode == EDGE:
            self.cells_z, self.width = fields.shape[0], xfaces[0].shape[1]
        else:
            self.cells_z, self.width = fields[0].shape[1], fields[0].shape[3]
        self.wide = faces_wide(mode, self.width)
        self.lane = lax.broadcasted_iota(jnp.int32, (ROWS, LANES), 1)
        self.row = lax.broadcasted_iota(jnp.int32, (ROWS, self.wide), 0)
        self.per_group = 6 * ROWS // SLOTS
        self.groups = self.cells_z // ROWS
        self.grad_base = self.per_group * self.groups
        halo_base = self.grad_base + self.per_group * (layers // ROWS)
        self.left_wide, self.right_wide = left_wide, right_wide = scratch[:2]
        if mode != OWN:
            self.ybuf = scratch[2]
            y_side = Side("gy")
            for t in range(yfaces[0].shape[0]):
                lower = y_side.lower([f[t] for f in yfaces])
                upper = y_side.upper([f[t] for f in yfaces])
                if mode == EDGE:
                    even = self.lane // STRIP % 2 == 0
                    lower, upper = (
                        jnp.where(even, upper, pltpu.roll(lower, STRIP, 1)),
                        jnp.where(even, pltpu.roll(upper, LANES - STRIP, 1), lower),
                    )
                self.ybuf[0, t] = lower
                self.ybuf[1, t] = upper

        def face(load, slot):
            if mode == EDGE:
                own = edge_tile(load, self.width)
                return self.edge(own, halo_base + slot // SLOTS, slot % SLOTS)
            return self.wider(load, halo_base + slot // SLOTS, slot % SLOTS)

        full = [face(load, slot) for slot, (load, _) in enumerate(face_tiles(zfaces, xfaces, lines))]
        self.below, self.above = full[:3], full[3:5]
        groups = self.groups
        for t in range(2 * groups):
            left_wide[t * ROWS : (t + 1) * ROWS, :] = full[5 + t]
        for t in range(2 * groups + 1):
            right_wide[t * ROWS : (t + 1) * ROWS, :] = full[5 + 3 * groups + t]
        if mode != OWN:
            column = lax.broadcasted_iota(jnp.int32, (ROWS, self.wide), 1)
            ends = {CIRCLE: (self.width - 1, self.wide - 1), EDGE: (STRIP - 1, LANES - STRIP - 1)}[mode]
            here = jnp.logical_or(column == ends[0], column == ends[1])
            for j in range(groups):
                ex_next = self.y_up(full[5 + 2 * groups + j])
                at = (groups + j) * ROWS
                left_wide[at : at + ROWS, :] += jnp.where(here, HALF * ex_next, 0.0)

    def wider(self, load, tile, k):
        if self.mode == OWN:
            return load(slice(0, self.width))

        def moved(v, to):
            shift = (to - STRIP * k) % LANES
            return pltpu.roll(v, shift, 1) if shift else v

        lower, upper = self.ybuf[0, tile], self.ybuf[1, tile]
        halo = jnp.where(self.lane < STRIP, moved(upper, 0), moved(lower, LANES - STRIP))
        return jnp.concatenate([load(slice(0, self.width)), halo], axis=1)

    def edge(self, own, tile, k):
        shift = (LANES - STRIP - 2 * STRIP * (k // 2)) % LANES
        both = pltpu.roll(self.ybuf[k % 2, tile], shift, 1)
        inside = jnp.logical_and(self.lane >= STRIP, self.lane < LANES - STRIP)
        return jnp.where(inside, own, both)

    def y_up(self, v):
        return pltpu.roll(v, self.wide - 1, 1)

    def y_down(self, v):
        return pltpu.roll(v, 1, 1)

    def x_up(self, v, line):
        return jnp.where(self.row == ROWS - 1, line, pltpu.roll(v, ROWS - 1, 0))

    def x_down(self, v, line):
        return jnp.where(self.row == 0, line, pltpu.roll(v, 1, 0))

    def line(self, ref, at):
        return jnp.broadcast_to(ref[pl.ds(at, 1), :], (ROWS, self.wide))

    def field(self, which, c, a, b):
        slot = 6 * b + 3 * which + c
        tile = self.per_group * a + slot // SLOTS
        if self.mode == EDGE:
            return self.edge(self.fields[ROWS * a + b, 3 * which + c], tile, slot % SLOTS)
        ref = self.fields[which]
        return self.wider(lambda s: ref[c, ROWS * a + b, :, s], tile, slot % SLOTS)

    def hx(self, a, b, ey, ez, ey_next):
        return self.field(1, 0, a, b) - HALF * (self.y_up(ez) - ez - ey_next + ey)

    def hy(self, a, b, ex, ez, ex_next):
        up = self.x_up(ez, self.line(self.right_wide, self.cells_z + ROWS * a + b))
        return self.field(1, 1, a, b) - HALF * (ex_next - ex - up + ez)

    def hz(self, a, b, ex, ey):
        up = self.x_up(ey, self.line(self.right_wide, ROWS * a + b))
        return self.field(1, 2, a, b) - HALF * (up - ey - self.y_up(ex) + ex)

    def start(self, a):
        ex, ey = self.field(0, 0, a, 0), self.field(0, 1, a, 0)
        below = self.below
        at_bottom = (
            below[0] - HALF * self.y_up(below[2]) + HALF * ey,
            below[1] - HALF * ex + HALF * self.x_up(below[2], self.line(self.right_wide, 2 * self.cells_z)),
        )
        before, b = jnp.maximum(a - 1, 0), ROWS - 1
        ex_before, ey_before, ez_before = (self.field(0, c, before, b) for c in range(3))
        inside = (
            self.hx(before, b, ey_before, ez_before, ey),
            self.hy(before, b, ex_before, ez_before, ex),
        )
        bottom = a == 0
        return (ex, ey) + tuple(jnp.where(bottom, one, two) for one, two in zip(at_bottom, inside))

    def group(self, a, carry, emit):
        ex, ey, hx_z, hy_z = carry
        for b in range(ROWS):
            z = ROWS * a + b
            ez = self.field(0, 2, a, b)
            if b < ROWS - 1:
                ex_next, ey_next = (self.field(0, c, a, b + 1) for c in range(2))
            else:
                end = a == self.groups - 1
                after = jnp.minimum(a + 1, self.groups - 1)
                ex_next, ey_next = (
                    jnp.where(end, self.above[c], self.field(0, c, after, 0)) for c in range(2)
                )
            hx = self.hx(a, b, ey, ez, ey_next)
            hy = self.hy(a, b, ex, ez, ex_next)
            hz = self.hz(a, b, ex, ey)
            hy_x = self.x_down(hy, self.line(self.left_wide, z) + HALF * ez)
            hz_x = self.x_down(hz, self.line(self.left_wide, self.cells_z + z) - HALF * ey)
            curl = (
                (hz - self.y_down(hz)) - (hy - hy_z),
                (hx - hx_z) - (hz - hz_x),
                (hy - hy_x) - (hx - self.y_down(hx)),
            )
            emit(a, b, (ex, ey, ez), (hx, hy, hz), curl)
            ex, ey, hx_z, hy_z = ex_next, ey_next, hx, hy
        return ex, ey, hx_z, hy_z

    def gradient(self, layers, arrays, store):
        first = first_layer(self.cells_z, layers)
        first_group = first // ROWS
        if self.mode == EDGE:
            grad_edges, mask_ref = arrays
            mask = self.edge(mask_ref[...], self.grad_base, 5)
        else:
            f_ref, inv_ref, grad_ref, mask_ref = arrays
            mask = mask_ref[...]

        def emit(a, b, efield, hfield, curl):
            z = ROWS * a + b
            layer = z - first
            if self.mode == EDGE:
                tile = self.grad_base + self.per_group * (a - first_group)
                slots = [6 * b + n for n in range(5)]
                values = [
                    self.edge(grad_edges[layer, n], tile + slot // SLOTS, slot % SLOTS)
                    for n, slot in enumerate(slots)
                ]
            else:
                values = [f_ref[c, z] for c in range(3)] + [inv_ref[z], grad_ref[layer]]
            total = None
            for c in range(3):
                term = values[c] * (efield[c] + values[3] * curl[c])
                total = term if total is None else total + term
            store(layer, values[4] + mask * total)

        def body(i, carry):
            return self.group(first_group + i, carry, emit)

        lax.fori_loop(0, layers // ROWS, body, self.start(first_group))


def fields_scratch(mode, xface, yface, width):
    rows, wide = xface.shape[0], faces_wide(mode, width)
    out = [pltpu.VMEM((rows, wide), jnp.float32)] * 2
    if mode != OWN:
        out.append(pltpu.VMEM((2,) + yface.shape, jnp.float32))
    return out


def own_gradient_kernel(counts, per_device, *refs):
    e_ref, h_ref, f_ref, inv_ref, grad_ref, mask_ref = refs[:6]
    zfaces, xfaces = refs[6 : 6 + counts[0]], refs[6 + counts[0] : 6 + sum(counts)]
    shares, (own_ref, *scratch) = refs[6 + sum(counts) : -3][::-1], refs[-3:]
    layers, _, width = grad_ref.shape
    fields = Fields(OWN, layers, (e_ref, h_ref), zfaces, xfaces, (), None, scratch)

    def store(layer, value):
        own_ref[layer] = value

    fields.gradient(layers, (f_ref, inv_ref, grad_ref, mask_ref), store)

    me = lax.axis_index("gx")
    for k, share in enumerate(shares):
        chunk = lax.bitwise_xor(me, way_there(len(shares))[k])
        for i in range(per_device):
            share[:, i * width : (i + 1) * width] = own_ref[chunk * per_device + i]
        if share.shape[1] > per_device * width:
            share[:, per_device * width :] = jnp.zeros((ROWS, SPARE), jnp.float32)


SPARE = 2 * LANES


def own_gradient(arrays, zfaces, xfaces):
    layers, _, width = arrays[4].shape
    count = lax.axis_size("gx")
    per_device = layers // count
    *shares, own = pl.pallas_call(
        functools.partial(own_gradient_kernel, (len(zfaces), len(xfaces)), per_device),
        in_specs=[VMEM] * (6 + len(zfaces) + len(xfaces)),
        out_specs=[VMEM] * (count + 1),
        out_shape=[fast(ROWS, per_device * width + SPARE)]
        + [fast(ROWS, per_device * width)] * (count - 1)
        + [fast(layers, ROWS, width)],
        scratch_shapes=fields_scratch(OWN, xfaces[0], None, width),
        compiler_params=params(),
    )(*arrays, *zfaces, *xfaces)
    return shares[::-1], own


PART = 2 * STRIP
SPAN = 2 * PART


def edge_gradient_kernel(counts, *refs):
    own_ref, f_ref, inv_ref, wide_ref, eh_ref, grad_ref, mask_ref, taps_ref = refs[:8]
    ends = np.cumsum((8,) + counts)
    zfaces, xfaces, lines, yfaces = (refs[i:j] for i, j in zip(ends[:-1], ends[1:]))
    (shares, message, edge_ref), scratch = refs[ends[-1] : -6], refs[-6:-3]
    folded, parts, slabs = refs[-3:]
    layers, _, width = own_ref.shape
    lane = lax.broadcasted_iota(jnp.int32, (ROWS, LANES), 1)
    first, last = STRIP, LANES - STRIP - 1
    fields = Fields(EDGE, layers, eh_ref, zfaces, xfaces, lines, yfaces, scratch)

    def store(layer, value):
        edge_ref[layer] = value

    fields.gradient(layers, (grad_ref, mask_ref), store)

    count = shares.shape[0]
    half = count // 2
    rows = half * ROWS
    me = lax.axis_index("gx")
    folded[...] = jnp.zeros_like(folded)
    fold = jnp.minimum(me, count - 1 - me)
    per_tile = LANES // SPAN
    for start in range(0, layers, per_tile):
        tile = jnp.zeros((ROWS, LANES), jnp.float32)
        for j in range(min(per_tile, layers - start)):
            edge = edge_ref[start + j]
            own = edge_tile(lambda s: own_ref[start + j, :, s], width)
            more = jnp.where(jnp.logical_or(lane == first, lane == last), edge - own, edge)
            low, high = SPAN * j + 1, SPAN * j + PART + STRIP - 1
            here = jnp.logical_and(lane >= low, lane < low + STRIP)
            tile = jnp.where(here, pltpu.roll(more, (low - 1) % LANES, 1), tile)
            here = jnp.logical_and(lane >= high, lane < high + STRIP)
            tile = jnp.where(here, pltpu.roll(more, (high - last) % LANES, 1), tile)
        tile = jnp.where(me < half, tile, flip_rows(tile))
        folded[fold, :, start // per_tile * LANES : (start // per_tile + 1) * LANES] = tile
    split_rows(jnp.concatenate([folded[s] for s in range(half)], axis=0), parts)
    total = cone(taps_ref, parts, rows)
    lanes = lax.broadcasted_iota(jnp.int32, (rows, LANES), 1)
    per_share = LANES // PART
    for start in range(0, layers, per_share):
        packed = jnp.zeros((rows, LANES), jnp.float32)
        for j in range(min(per_share, layers - start)):
            at = SPAN * (start + j)
            tile = total[:, at // LANES * LANES : (at // LANES + 1) * LANES]
            left = pltpu.roll(tile, (PART * j - STRIP - at) % LANES, 1)
            right = pltpu.roll(tile, (PART * j + STRIP - PART - 1 - at) % LANES, 1)
            packed = jnp.where(lanes // STRIP == 2 * j, left, packed)
            packed = jnp.where(lanes // STRIP == 2 * j + 1, right, packed)
        here = slice(start // per_share * LANES, (start // per_share + 1) * LANES)
        for s in range(half):
            one = packed[s * ROWS : (s + 1) * ROWS]
            slabs[s, :, here] = one
            slabs[count - 1 - s, :, here] = flip_rows(one)
    for k in range(count):
        shares[k] = slabs[lax.bitwise_xor(me, k)]

    message[...] = jnp.zeros_like(message)
    top, last = fields.cells_z - 1, ROWS - 1
    above, beyond = (line[0:1] for line in corner_lines(lines, slice(0, width)))
    added = wide_ref[0:1, :] * f_ref[2, top, 0:1, :] * inv_ref[top, 0:1, :] * (HALF * above)
    added += wide_ref[last:, :] * f_ref[0, 0, last:, :] * inv_ref[0, last:, :] * (HALF * beyond)
    column = lax.broadcasted_iota(jnp.int32, (1, width), 1)
    added = jnp.where(jnp.logical_or(column == 0, column == width - 1), 0.0, added)
    for at, n in line_places(width):
        message[n : n + 1, at : at + LANES] = added[:, (at // LANES * ROWS + n) * LANES :][:, :LANES]


def line_places(width):
    return [(t // ROWS * LANES, t % ROWS) for t in range(width // LANES)]


def line_of(message, width):
    return jnp.concatenate([message[n : n + 1, at : at + LANES] for at, n in line_places(width)], axis=1)


def line_spot(layers):
    bottom = lax.axis_index("gz") == 0
    return jnp.where(bottom, layers - 1, 0), jnp.where(bottom, 0, ROWS - 1)


def edge_gradient(own, arrays, edges, taps, zfaces, xfaces, lines, yfaces):
    layers, _, width = own.shape
    faces = (*zfaces, *xfaces, *lines, *yfaces)
    count = lax.axis_size("gx")
    share = (count, ROWS, math.ceil(layers * PART / LANES) * LANES)
    spread = math.ceil(layers * SPAN / LANES) * LANES
    line = math.ceil(width / LANES / ROWS) * LANES
    return pl.pallas_call(
        functools.partial(edge_gradient_kernel, (len(zfaces), len(xfaces), len(lines), len(yfaces))),
        in_specs=[VMEM] * (8 + len(faces)),
        out_specs=[VMEM] * 3,
        out_shape=[fast(*share), fast(ROWS, line), fast(layers, ROWS, LANES)],
        scratch_shapes=fields_scratch(EDGE, xfaces[0], yfaces[0], width)
        + [
            pltpu.VMEM((count // 2, ROWS, spread), jnp.float32),
            pltpu.VMEM((3 * count // 2 * ROWS, spread), jnp.bfloat16),
            pltpu.VMEM(share, jnp.float32),
        ],
        compiler_params=params(),
    )(own, arrays[2], arrays[3], arrays[5], *edges, taps, *faces)


def step_kernel(counts, *refs):
    e_ref, h_ref, inv_ref, own_ref, edge_ref, message = refs[:6]
    ends = np.cumsum((6,) + counts)
    zfaces, xfaces, lines, yfaces = (refs[i:j] for i, j in zip(ends[:-1], ends[1:]))
    e_out, h_out, grad_out = refs[ends[-1] + 1 : ends[-1] + 4]
    left_wide, right_wide, ybuf, e_new, h_new, grad_new, sems = refs[ends[-1] + 4 :]
    layers, _, width = own_ref.shape
    lane = lax.broadcasted_iota(jnp.int32, (ROWS, LANES), 1)

    for layer in range(layers):
        edge = edge_ref[layer]
        head, tail = own_ref[layer, :, 0:LANES], own_ref[layer, :, width - LANES :]
        grad_new[layer] = own_ref[layer]
        grad_new[layer, :, 0:LANES] = jnp.where(lane == 0, pltpu.roll(edge, LANES - STRIP, 1), head)
        grad_new[layer, :, width - LANES :] = jnp.where(lane == LANES - 1, pltpu.roll(edge, STRIP, 1), tail)
    layer, spot = line_spot(layers)
    row = lax.broadcasted_iota(jnp.int32, (ROWS, width), 0)
    grad_new[layer] += jnp.where(row == spot, line_of(message, width), 0.0)
    grad_copy = pltpu.make_async_copy(grad_new, grad_out, sems.at[0, 0])
    grad_copy.start()

    fields = Fields(CIRCLE, layers, (e_ref, h_ref), zfaces, xfaces, lines, yfaces, (left_wide, right_wide, ybuf))

    def emit(a, b, efield, hfield, curl):
        z = ROWS * a + b
        half_inv = inv_ref[z]
        for c in range(3):
            e_new[c, z] = efield[c][:, :width] + half_inv * curl[c][:, :width]
            h_new[c, z] = hfield[c][:, :width]

    def copies(a):
        here = pl.ds(a * ROWS, ROWS)
        return [
            pltpu.make_async_copy(new.at[c, here], out.at[c, here], sems.at[1 + a, 3 * n + c])
            for n, (new, out) in enumerate(((e_new, e_out), (h_new, h_out)))
            for c in range(3)
        ]

    def body(a, carry):
        carry = fields.group(a, carry, emit)
        for copy in copies(a):
            copy.start()
        return carry

    lax.fori_loop(0, fields.groups, body, fields.start(0))
    for a in range(fields.groups):
        for copy in copies(a):
            copy.wait()
    grad_copy.wait()


def step(efield, hfield, inv, own, edge, message, zfaces, xfaces, lines, yfaces, after):
    _, cells_z, _, width = efield.shape
    groups = (zfaces, xfaces, lines, yfaces)
    counts = tuple(len(group) for group in groups)
    shapes = (efield.shape, hfield.shape, own.shape)
    return pl.pallas_call(
        functools.partial(step_kernel, counts),
        in_specs=[VMEM] * (6 + sum(counts)) + [ANY],
        out_specs=[ANY] * 3,
        out_shape=[f32(*shape) for shape in shapes],
        scratch_shapes=fields_scratch(CIRCLE, xfaces[0], yfaces[0], width)
        + [pltpu.VMEM(shape, jnp.float32) for shape in shapes]
        + [pltpu.SemaphoreType.DMA((1 + cells_z // ROWS, 6))],
        compiler_params=params(),
    )(efield, hfield, inv, own, edge, message, *(one for group in groups for one in group), after)


def cone_taps():
    span = np.arange(-RADIUS, RADIUS + 1, dtype=np.float64)
    return np.maximum(RADIUS - np.sqrt(span[:, None] ** 2 + span[None, :] ** 2), 0.0)


def cone_sum():
    return cone_taps().sum()


def cone_matrix(rows):
    weight = cone_taps() / cone_sum()
    x = np.arange(rows)
    out = np.zeros((RADIUS + 1, rows, rows))
    for b in range(RADIUS + 1):
        for apart in (x[:, None] - x[None, :], 2 * rows - 1 - x[:, None] - x[None, :]):
            near = np.abs(apart) <= RADIUS
            out[b] += np.where(near, weight[np.clip(apart, -RADIUS, RADIUS) + RADIUS, RADIUS + b], 0.0)
    out = out.reshape((RADIUS + 1) * rows, rows).astype(np.float32)
    high = out.astype(jnp.bfloat16)
    low = (out - high.astype(np.float32)).astype(jnp.bfloat16)
    return np.concatenate([high, low, high], axis=1)


def flip_rows(v):
    row = lax.broadcasted_iota(jnp.int32, v.shape, 0)
    v = pltpu.roll(v, 4, 0)
    v = jnp.where(row % 4 < 2, pltpu.roll(v, ROWS - 2, 0), pltpu.roll(v, 2, 0))
    return jnp.where(row % 2 < 1, pltpu.roll(v, ROWS - 1, 0), pltpu.roll(v, 1, 0))


def split_rows(symmetric, parts):
    rows = symmetric.shape[0]
    high = symmetric.astype(jnp.bfloat16)
    low = (symmetric - high.astype(jnp.float32)).astype(jnp.bfloat16)
    parts[0:rows, :] = high
    parts[rows : 2 * rows, :] = high
    parts[2 * rows : 3 * rows, :] = low


def cone(taps_ref, parts, rows):
    wide = parts.shape[1]
    mixed = jnp.dot(taps_ref[...], parts[...], preferred_element_type=jnp.float32)
    total = mixed[0:rows]
    for b in range(1, RADIUS + 1):
        part = mixed[b * rows : (b + 1) * rows]
        total = total + (pltpu.roll(part, b, 1) + pltpu.roll(part, wide - b, 1))
    return total


def filter_kernel(count, per_device, width, *refs):
    taps_ref, edges_ref, line_ref = refs[:3]
    got = refs[count + 2 : 2 : -1]
    outs = refs[3 + count : 3 + 2 * count]
    slabs, parts, done = refs[3 + 2 * count :]
    me = lax.axis_index("gx")
    half = count // 2
    rows = half * ROWS
    for k in range(count):
        slabs[lax.bitwise_xor(me, way_there(count)[k])] = got[k][:, : per_device * width]

    side = jnp.zeros((rows, LANES), jnp.float32)
    for i in range(per_device):
        here = slice(i * width, (i + 1) * width)
        halves = [slabs[s, :, here] + flip_rows(slabs[count - 1 - s, :, here]) for s in range(half)]
        split_rows(jnp.concatenate([jnp.concatenate(halves, axis=0), side], axis=1), parts)
        total = cone(taps_ref, parts, rows)
        for s in range(half):
            own = total[s * ROWS : (s + 1) * ROWS, :width]
            done[s, :, here] = own
            done[count - 1 - s, :, here] = flip_rows(own)
    for k, apart in enumerate(way_back(count)):
        outs[k][:, : per_device * width] = done[lax.bitwise_xor(me, apart)]
        tail = per_device * width + edges_ref.shape[2]
        outs[k][:, per_device * width : tail] = edges_ref[apart]
        outs[k][:, tail:] = line_ref[...]


def cone_filter(taps, edges, line, got, per_device, width):
    count = len(got)
    rows = count // 2 * ROWS
    return pl.pallas_call(
        functools.partial(filter_kernel, count, per_device, width),
        in_specs=[VMEM] * (3 + count),
        out_specs=[VMEM] * count,
        out_shape=[fast(ROWS, per_device * width + edges.shape[2] + line.shape[1])] * count,
        scratch_shapes=[
            pltpu.VMEM((count, ROWS, per_device * width), jnp.float32),
            pltpu.VMEM((3 * rows, width + LANES), jnp.bfloat16),
            pltpu.VMEM((count, ROWS, per_device * width), jnp.float32),
        ],
        compiler_params=params(),
    )(taps, edges, line, *got[::-1])


def cone_weight(along_x, along_y):
    near = jnp.maximum(RADIUS - jnp.sqrt(along_x * along_x + float(along_y * along_y)), 0.0)
    return near * float(1.0 / cone_sum())


def finish_kernel(count, per_device, width, *refs):
    got = refs[count - 1 :: -1]
    out, (left, right, done, sems) = refs[count], refs[count + 1 :]
    me = lax.axis_index("gx")
    layers = count * per_device
    lane = lax.broadcasted_iota(jnp.int32, (ROWS, LANES), 1)
    edges_at = per_device * width
    line_at = edges_at + math.ceil(layers * PART / LANES) * LANES

    per_tile = LANES // PART
    for start in range(0, layers, per_tile):
        at = edges_at + start * PART
        tile = got[0][:, at : at + LANES]
        for k in range(1, count):
            tile = tile + got[k][:, at : at + LANES]
        for j in range(min(per_tile, layers - start)):
            head = pltpu.roll(tile, (-PART * j) % LANES, 1)
            left[start + j] = jnp.where(lane < STRIP - 1, head, 0.0)
            tail = pltpu.roll(tile, (LANES + 1 - 2 * STRIP - PART * j) % LANES, 1)
            right[start + j] = jnp.where(lane > LANES - STRIP, tail, 0.0)

    line_layer, spot = line_spot(layers)
    end = count * ROWS - 1
    row = lax.broadcasted_iota(jnp.int32, (ROWS, LANES), 0) + me * ROWS
    lines, near, far = [], [], []
    for k, apart in enumerate(way_back(count)):
        lines.append(line_of(got[k][:, line_at:], width))
        where = lax.bitwise_xor(me, apart) * ROWS + spot
        near.append((row - where).astype(jnp.float32))
        far.append((row - (end - where)).astype(jnp.float32))
    total = None
    for b in range(RADIUS + 1):
        mixed = jnp.zeros((ROWS, width), jnp.float32)
        for k in range(count):
            weight = cone_weight(near[k], b) + cone_weight(far[k], b)
            mixed = mixed + jnp.concatenate([weight] * (width // LANES), axis=1) * lines[k]
        mixed = jnp.concatenate([mixed, jnp.zeros((ROWS, LANES), jnp.float32)], axis=1)
        if b:
            mixed = pltpu.roll(mixed, b, 1) + pltpu.roll(mixed, width + LANES - b, 1)
        total = mixed if total is None else total + mixed
    line = total[:, :width]

    copies = []
    for k, apart in enumerate(way_back(count)):
        first = lax.bitwise_xor(me, apart) * per_device
        for i in range(per_device):
            at = i * width
            done[k, i] = got[k][:, at : at + width] + jnp.where(first + i == line_layer, line, 0.0)
            done[k, i, :, :LANES] += left[first + i]
            done[k, i, :, width - LANES :] += right[first + i]
        copies.append(pltpu.make_async_copy(done.at[k], out.at[pl.ds(first, per_device)], sems.at[k]))
        copies[-1].start()
    for copy in copies:
        copy.wait()


def finish(parts, layers, width):
    count = len(parts)
    per_device = layers // count
    return pl.pallas_call(
        functools.partial(finish_kernel, count, per_device, width),
        in_specs=[VMEM] * count,
        out_specs=ANY,
        out_shape=f32(layers, ROWS, width),
        scratch_shapes=[
            pltpu.VMEM((layers, ROWS, LANES), jnp.float32),
            pltpu.VMEM((layers, ROWS, LANES), jnp.float32),
            pltpu.VMEM((count, per_device, ROWS, width), jnp.float32),
            pltpu.SemaphoreType.DMA((count,)),
        ],
        compiler_params=params(),
    )(*parts[::-1])


def spread(parts, order):
    count = len(parts)
    got = list(parts)
    for j in range(count - 1, 0, -1):
        got[j] = lax.ppermute(parts[j], "gx", [(i, i ^ order[j]) for i in range(count)])
    return got


def way_there(count):
    return list(range(count))


def way_back(count):
    if count < 4:
        return list(range(count))
    return [0] + list(range(2, count - 1)) + [1, count - 1]


def on_device(efield, hfield, forward, material, permit, design_mask, grad_sum):
    layers, _, width = grad_sum.shape
    efield, hfield, zfaces, xfaces, lines = halos(efield, hfield)
    own_low, own_high, mask, inv = strips(
        permit, efield, hfield, forward, material, grad_sum, design_mask
    )
    arrays = (efield, hfield, forward, inv, grad_sum, mask)
    edges = own_edges(arrays)
    shares, own = own_gradient(arrays, zfaces, xfaces)
    got = spread(shares, way_there(len(shares)))
    yfaces = exchange(y_faces(own_low, own_high, zfaces, xfaces, lines, own), "gy", "gz")
    taps = jnp.asarray(cone_matrix(len(got) // 2 * ROWS))
    added, line, edge = edge_gradient(own, arrays, edges, taps, zfaces, xfaces, lines, yfaces)
    parts = cone_filter(taps, added, line, got, layers // len(got), width)
    e_next, h_next, grad_total = step(
        efield, hfield, inv, own, edge, line, zfaces, xfaces, lines, yfaces, parts[0]
    )
    return e_next, h_next, grad_total, finish(spread(parts, way_back(len(parts))), layers, width)


def solution(mesh):
    field = P(None, "gz", "gx", "gy")
    cells = P("gz", "gx", "gy")
    return jax.shard_map(
        on_device,
        mesh=mesh,
        in_specs=(field, field, field, cells, P(), P("gx", "gy"), cells),
        out_specs=(field, field, cells, cells),
        check_vma=False,
    )
```

```python
import functools
import math

import jax
import jax.numpy as jnp
import numpy as np
from jax import lax
from jax.experimental import pallas as pl
from jax.experimental.pallas import tpu as pltpu
from jax.sharding import PartitionSpec as P

RADIUS = 6
BLOCK = 8
HALF = 0.5

ROWS = 8
LANES = 128
STRIP = 8
SLOTS = LANES // STRIP
MIB = 1024 * 1024

VMEM = pl.BlockSpec(memory_space=pltpu.VMEM)
SMEM = pl.BlockSpec(memory_space=pltpu.SMEM)
ANY = pl.BlockSpec(memory_space=pl.ANY)


def params(mib=24):
    return pltpu.CompilerParams(vmem_limit_bytes=mib * MIB)


def f32(*shape):
    return jax.ShapeDtypeStruct(shape, jnp.float32)


def fast(*shape):
    return pltpu.VMEM(shape, jnp.float32)


def rounds(axis):
    return 2 if lax.axis_size(axis) > 2 else 1


def exchange(sends, axis, mate):
    count = lax.axis_size(axis)
    beside = lax.axis_size(mate)
    if count == 1:
        return sends
    got = []
    for start, value in enumerate(sends):
        partner = list(range(count))
        for low in range(start, count - 1, 2):
            partner[low], partner[low + 1] = low + 1, low
        axes = sorted((axis, mate))
        steps = (beside, 1) if axes[0] == axis else (1, count)
        pairs = []
        for i in range(count):
            for m in range(beside):
                if partner[i] != i:
                    to = (partner[i], m)
                elif beside % 2 == 0:
                    to = (i, m ^ 1)
                else:
                    continue
                pairs.append((i * steps[0] + m * steps[1], to[0] * steps[0] + to[1] * steps[1]))
        got.append(lax.ppermute(value, tuple(axes), pairs))
    return got


def exchange_diagonal(sends):
    along_x, along_y, along_z = (lax.axis_size(axis) for axis in AXES)

    def flat(x, y, z):
        return (x * along_y + y) * along_z + z

    got = []
    for start, value in enumerate(sends):
        partner = {}
        for low in range(start, along_z - 1, 2):
            for x in range(1, along_x):
                partner[x, low] = (x - 1, low + 1)
                partner[x - 1, low + 1] = (x, low)
        pairs = []
        for x in range(along_x):
            for z in range(along_z):
                for y in range(along_y):
                    if (x, z) in partner:
                        to = partner[x, z]
                        pairs.append((flat(x, y, z), flat(to[0], y, to[1])))
                    elif along_y % 2 == 0:
                        pairs.append((flat(x, y, z), flat(x, y ^ 1, z)))
        got.append(lax.ppermute(value, AXES, pairs))
    return got


AXES = ("gx", "gy", "gz")


class Side:
    def __init__(self, axis):
        index = lax.axis_index(axis)
        self.rounds = rounds(axis)
        self.odd = index % 2 == 1
        self.bottom = index == 0
        self.top = index == lax.axis_size(axis) - 1

    def sends(self, low, high):
        both = [jnp.where(self.odd, low, high)]
        if self.rounds > 1:
            both.append(jnp.where(self.odd, high, low))
        return both

    def lower(self, got):
        return jnp.where(self.bottom, 0.0, jnp.where(self.odd, got[0], got[-1]))

    def upper(self, got):
        return jnp.where(self.top, 0.0, jnp.where(self.odd, got[-1], got[0]))


def first_layer(cells_z, layers):
    return (cells_z - layers) * (1 - lax.axis_index("gz"))


def faces_kernel(x_rounds, e_in, h_in, e_ref, h_ref, *refs):
    x_sends, (low_ref, rows_ref, sems) = refs[:x_rounds], refs[-3:]
    others = refs[x_rounds:-3]
    z_sends, d_sends = others[: len(others) // 2], others[len(others) // 2 :]
    cells_z = e_ref.shape[1]
    last, top = ROWS - 1, cells_z - 1
    copies = [
        [pltpu.make_async_copy(source.at[c], target.at[c], sems.at[n, c]) for c in range(3)]
        for n, (source, target) in enumerate(((e_in, e_ref), (h_in, h_ref)))
    ]
    for copy in copies[0] + copies[1]:
        copy.start()

    low_ref[2 * cells_z :, :] = jnp.zeros_like(low_ref[2 * cells_z :, :])
    rows_ref[5, top : top + 1, :] = jnp.zeros_like(rows_ref[5, top : top + 1, :])
    for copy in copies[0]:
        copy.wait()
    for z in range(cells_z):
        low_ref[z : z + 1, :] = e_ref[1, z, 0:1, :]
        low_ref[cells_z + z : cells_z + z + 1, :] = e_ref[2, z, 0:1, :]
        for c in range(3):
            rows_ref[c, z : z + 1, :] = e_ref[c, z, last : last + 1, :]
        if z > 0:
            rows_ref[5, z - 1 : z, :] = e_ref[0, z, last : last + 1, :]
    for copy in copies[1]:
        copy.wait()
    for z in range(cells_z):
        for c in range(2):
            rows_ref[3 + c, z : z + 1, :] = h_ref[1 + c, z, last : last + 1, :]
    width = e_ref.shape[3]
    ex, ey, ez = (rows_ref[c] for c in range(3))
    column = lax.broadcasted_iota(jnp.int32, ex.shape, 1)
    ex_next = jnp.where(column == width - 1, 0.0, pltpu.roll(ex, width - 1, 1))
    lane = lax.broadcasted_iota(jnp.int32, (ROWS, LANES), 1)
    strip = jnp.zeros((ROWS, LANES), jnp.float32)
    for j in range(cells_z // ROWS):
        head = rows_ref[0, j * ROWS : (j + 1) * ROWS, 0:LANES]
        strip = jnp.where(lane // STRIP == j, pltpu.roll(head, STRIP * j, 1) if j else head, strip)
    high = (
        rows_ref[3] - HALF * (rows_ref[5] - ex + ez),
        rows_ref[4] + HALF * ey - HALF * (ex - ex_next),
        jnp.concatenate([strip, jnp.zeros((ROWS, width - LANES), jnp.float32)], axis=1),
    )
    side = Side("gx")
    for c, value in enumerate(high):
        here = slice(c * cells_z, c * cells_z + value.shape[0])
        for ref, one in zip(x_sends, side.sends(low_ref[here, :], value)):
            ref[here, :] = one

    side = Side("gz")
    ex, ey, ez = (e_ref[c, top] for c in range(3))
    low = (e_ref[0, 0], e_ref[1, 0], jnp.zeros_like(ez))
    high = (h_ref[0, top] + HALF * ez - HALF * ey, h_ref[1, top] + HALF * ex - HALF * ez, ez)
    for c in range(3):
        for ref, value in zip(z_sends, side.sends(low[c], high[c])):
            ref[c] = value

    down, up = (
        jnp.broadcast_to(line, (ROWS, line.shape[1]))
        for line in (e_ref[0, 0, last : last + 1, :], e_ref[2, top, 0:1, :])
    )
    for ref, value in zip(d_sends, side.sends(down, up)):
        ref[...] = value


def halos(efield, hfield):
    _, cells_z, cells_x, cells_y = efield.shape
    x_rounds, z_rounds = rounds("gx"), rounds("gz")
    x_face, z_face, line = fast(2 * cells_z + ROWS, cells_y), fast(3, cells_x, cells_y), fast(ROWS, cells_y)
    fields = [fast(*field.shape) for field in (efield, hfield)]
    efield, hfield, *sends = pl.pallas_call(
        functools.partial(faces_kernel, x_rounds),
        in_specs=[ANY] * 2,
        out_specs=[VMEM] * (2 + x_rounds + 2 * z_rounds),
        out_shape=fields + [x_face] * x_rounds + [z_face] * z_rounds + [line] * z_rounds,
        scratch_shapes=[
            pltpu.VMEM(x_face.shape, jnp.float32),
            pltpu.VMEM((6, cells_z, cells_y), jnp.float32),
            pltpu.SemaphoreType.DMA((2, 3)),
        ],
        compiler_params=params(54),
    )(efield, hfield)
    xfaces = exchange(sends[:x_rounds], "gx", "gy")
    zfaces = exchange(sends[x_rounds : x_rounds + z_rounds], "gz", "gy")
    return efield, hfield, zfaces, xfaces, exchange_diagonal(sends[x_rounds + z_rounds :])


def lane_group():
    return lax.broadcasted_iota(jnp.int32, (ROWS, LANES), 1) // STRIP


def pack_strips(tiles, low_ref, high_ref, first):
    group = lane_group()
    width = tiles[0][1]
    for start in range(0, len(tiles), SLOTS):
        low = jnp.zeros((ROWS, LANES), jnp.float32)
        high = jnp.zeros((ROWS, LANES), jnp.float32)
        for k, (load, _) in enumerate(tiles[start : start + SLOTS]):
            if load is None:
                continue
            here = group == k
            shift = (STRIP * k) % LANES
            left = load(slice(0, LANES))
            right = load(slice(width - LANES, width))
            low = jnp.where(here, pltpu.roll(left, shift, 1) if shift else left, low)
            shift = (STRIP * k + STRIP) % LANES
            high = jnp.where(here, pltpu.roll(right, shift, 1) if shift else right, high)
        low_ref[first + start // SLOTS] = low
        high_ref[first + start // SLOTS] = high


def strips_kernel(
    permit_ref, e_ref, h_ref, f_ref, mat_ref, grad_ref, mask_ref, low_ref, high_ref, wide_ref, inv_ref
):
    cells_z, width = e_ref.shape[1], e_ref.shape[3]
    layers = grad_ref.shape[0]
    blocks = mask_ref.shape[1]
    inverse = [
        jnp.broadcast_to(HALF * (1.0 / permit_ref[0:1, m : m + 1]), (ROWS, width))
        for m in range(permit_ref.shape[1])
    ]
    for z in range(cells_z):
        inv = inverse[0]
        for m in range(1, len(inverse)):
            inv = jnp.where(mat_ref[z] == m, inverse[m], inv)
        inv_ref[z] = inv
    spread = (
        lax.broadcasted_iota(jnp.int32, (blocks, width), 0)
        == lax.broadcasted_iota(jnp.int32, (blocks, width), 1) // BLOCK
    ).astype(jnp.float32)
    mask = jnp.broadcast_to(mask_ref[...].astype(jnp.float32), (ROWS, blocks))
    wide_ref[...] = jnp.dot(mask, spread, preferred_element_type=jnp.float32)
    first = first_layer(cells_z, layers)
    tiles = []
    for z in range(cells_z):
        for ref in (e_ref, h_ref):
            for c in range(3):
                tiles.append((lambda s, r=ref, c=c, z=z: r[c, z, :, s], width))
    pack_strips(tiles, low_ref, high_ref, 0)

    done = len(tiles) // SLOTS
    tiles = []
    for layer in range(layers):
        for c in range(3):
            tiles.append((lambda s, c=c, l=layer: f_ref[c, first + l, :, s], width))
        tiles.append((lambda s, l=layer: inv_ref[first + l, :, s], width))
        tiles.append((lambda s, l=layer: grad_ref[l, :, s], width))
        tiles.append((lambda s: wide_ref[:, s], width) if layer % ROWS == 0 else (None, width))
    pack_strips(tiles, low_ref, high_ref, done)


def strips(permit, efield, hfield, forward, material, grad_sum, mask):
    cells_z, width = efield.shape[1], efield.shape[3]
    count = (cells_z * 6 + grad_sum.shape[0] * 6) // SLOTS
    packed = (count, ROWS, LANES)
    shapes = (packed, packed, (ROWS, width), material.shape)
    return pl.pallas_call(
        strips_kernel,
        in_specs=[VMEM] * 7,
        out_specs=[VMEM] * 4,
        out_shape=[fast(*shape) for shape in shapes],
        compiler_params=params(),
    )(permit.reshape(1, -1), efield, hfield, forward, material, grad_sum, mask)


def edge_tile(load, width):
    lane = lax.broadcasted_iota(jnp.int32, (ROWS, LANES), 1)
    head = pltpu.roll(load(slice(0, LANES)), STRIP, 1)
    tail = pltpu.roll(load(slice(width - LANES, width)), LANES - STRIP, 1)
    return jnp.where(lane < LANES // 2, head, tail)


def edges_kernel(e_ref, h_ref, f_ref, inv_ref, grad_ref, mask_ref, eh_out, grad_out, mask_out):
    cells_z, width = e_ref.shape[1], e_ref.shape[3]
    layers = grad_ref.shape[0]
    first = first_layer(cells_z, layers)
    for z in range(cells_z):
        for c in range(3):
            eh_out[z, c] = edge_tile(lambda s: e_ref[c, z, :, s], width)
            eh_out[z, 3 + c] = edge_tile(lambda s: h_ref[c, z, :, s], width)
    for layer in range(layers):
        for c in range(3):
            grad_out[layer, c] = edge_tile(lambda s: f_ref[c, first + layer, :, s], width)
        grad_out[layer, 3] = edge_tile(lambda s: inv_ref[first + layer, :, s], width)
        grad_out[layer, 4] = edge_tile(lambda s: grad_ref[layer, :, s], width)
    mask_out[...] = edge_tile(lambda s: mask_ref[:, s], width)


def own_edges(arrays):
    cells_z, layers = arrays[0].shape[1], arrays[4].shape[0]
    return pl.pallas_call(
        edges_kernel,
        in_specs=[VMEM] * 6,
        out_specs=[VMEM] * 3,
        out_shape=[fast(cells_z, 6, ROWS, LANES), fast(layers, 5, ROWS, LANES), fast(ROWS, LANES)],
        compiler_params=params(),
    )(*arrays)


def corner_lines(lines, s):
    z_side, x_side = Side("gz"), Side("gx")
    above = jnp.where(x_side.bottom, 0.0, z_side.upper([f[:, s] for f in lines]))
    beyond = jnp.where(x_side.top, 0.0, z_side.lower([f[:, s] for f in lines]))
    return above, beyond


def face_tiles(zfaces, xfaces, lines):
    width = xfaces[0].shape[1]
    rows = xfaces[0].shape[0]
    cells_z = (rows - ROWS) // 2
    z_side, x_side = Side("gz"), Side("gx")

    def corner(s):
        row = lax.broadcasted_iota(jnp.int32, (ROWS, s.stop - s.start), 0)
        return jnp.where(row == ROWS - 1, -HALF * corner_lines(lines, s)[0], 0.0)

    def x_tile(pick, t, s):
        value = pick([f[t : t + ROWS, s] for f in xfaces])
        return value + corner(s) if lines and t == cells_z - ROWS and pick == x_side.lower else value

    def strip(j, s):
        zeros = jnp.zeros((ROWS, s.stop - s.start), jnp.float32)
        if s.start:
            return zeros
        lane = lax.broadcasted_iota(jnp.int32, (ROWS, LANES), 1)
        packed = x_side.lower([f[2 * cells_z :, 0:LANES] for f in xfaces])
        head = jnp.where(lane < STRIP, pltpu.roll(packed, LANES - STRIP * j, 1) if j else packed, 0.0)
        return head if s.stop == LANES else jnp.concatenate([head, zeros[:, LANES:]], axis=1)

    tiles = []
    for c in range(3):
        tiles.append((lambda s, c=c: z_side.lower([f[c, :, s] for f in zfaces]), width))
    for c in range(2):
        tiles.append((lambda s, c=c: z_side.upper([f[c, :, s] for f in zfaces]), width))
    for t in range(0, 2 * cells_z, ROWS):
        tiles.append((lambda s, t=t: x_tile(x_side.lower, t, s), width))
    for j in range(cells_z // ROWS):
        tiles.append((lambda s, j=j: strip(j, s), width))
    for t in range(0, rows, ROWS):
        if lines and t == 2 * cells_z:
            tiles.append((lambda s: corner_lines(lines, s)[1], width))
        else:
            tiles.append((lambda s, t=t: x_tile(x_side.upper, t, s), width))
    return tiles


FREE = 5


def face_slot(index, layers, cells_z):
    grad_base = 6 * cells_z // SLOTS
    if index < FREE:
        slot = 6 * (index + 1) + 5
        return grad_base + slot // SLOTS, slot % SLOTS
    return grad_base + 6 * layers // SLOTS + (index - FREE) // SLOTS, (index - FREE) % SLOTS


def face_count(xface):
    per_field = (xface.shape[0] - ROWS) // ROWS // 2
    return 5 + 3 * per_field + 2 * per_field + 1


def y_faces_kernel(counts, *refs):
    own_low, own_high = refs[:2]
    ends = np.cumsum((2,) + counts)
    zfaces, xfaces, lines = (refs[i:j] for i, j in zip(ends[:-1], ends[1:]))
    sends, (low_ref, high_ref) = refs[3 + sum(counts) : -2], refs[-2:]
    own = own_low.shape[0]
    tiles = face_tiles(zfaces, xfaces, lines)
    pack_strips(tiles[FREE:], low_ref, high_ref, 0)
    side = Side("gy")
    for ref, value in zip(sends, side.sends(own_low[...], own_high[...])):
        ref[0:own] = value
    group = lane_group()
    cells_z = (xfaces[0].shape[0] - ROWS) // 2
    layers = own * SLOTS // 6 - cells_z
    for index, (load, width) in enumerate(tiles[:FREE]):
        tile, k = face_slot(index, layers, cells_z)
        low = pltpu.roll(load(slice(0, LANES)), STRIP * k, 1)
        high = pltpu.roll(load(slice(width - LANES, width)), (STRIP * k + STRIP) % LANES, 1)
        for ref, value in zip(sends, side.sends(low, high)):
            ref[tile] = jnp.where(group == k, value, ref[tile])
    for ref, value in zip(sends, side.sends(low_ref[...], high_ref[...])):
        ref[own:] = value


def y_faces(own_low, own_high, zfaces, xfaces, lines, after):
    extra = math.ceil((face_count(xfaces[0]) - FREE) / SLOTS)
    packed = fast(own_low.shape[0] + extra, ROWS, LANES)
    return pl.pallas_call(
        functools.partial(y_faces_kernel, (len(zfaces), len(xfaces), len(lines))),
        in_specs=[VMEM] * (2 + len(zfaces) + len(xfaces) + len(lines)) + [ANY],
        out_specs=[VMEM] * rounds("gy"),
        out_shape=[packed] * rounds("gy"),
        scratch_shapes=[pltpu.VMEM((extra, ROWS, LANES), jnp.float32)] * 2,
        compiler_params=params(),
    )(own_low, own_high, *zfaces, *xfaces, *lines, after)


OWN, CIRCLE, EDGE = range(3)


def faces_wide(mode, width):
    return {OWN: width, CIRCLE: width + LANES, EDGE: LANES}[mode]


class Fields:
    def __init__(self, mode, layers, fields, zfaces, xfaces, lines, yfaces, scratch):
        self.mode = mode
        self.fields = fields
        if mode == EDGE:
            self.cells_z, self.width = fields.shape[0], xfaces[0].shape[1]
        else:
            self.cells_z, self.width = fields[0].shape[1], fields[0].shape[3]
        self.wide = faces_wide(mode, self.width)
        self.lane = lax.broadcasted_iota(jnp.int32, (ROWS, LANES), 1)
        self.row = lax.broadcasted_iota(jnp.int32, (ROWS, self.wide), 0)
        self.per_group = 6 * ROWS // SLOTS
        self.groups = self.cells_z // ROWS
        self.grad_base = self.per_group * self.groups
        self.left_wide, self.right_wide = left_wide, right_wide = scratch[:2]
        if mode != OWN:
            self.ybuf = scratch[2]
            y_side = Side("gy")
            for t in range(yfaces[0].shape[0]):
                lower = y_side.lower([f[t] for f in yfaces])
                upper = y_side.upper([f[t] for f in yfaces])
                if mode == EDGE:
                    even = self.lane // STRIP % 2 == 0
                    lower, upper = (
                        jnp.where(even, upper, pltpu.roll(lower, STRIP, 1)),
                        jnp.where(even, pltpu.roll(upper, LANES - STRIP, 1), lower),
                    )
                self.ybuf[0, t] = lower
                self.ybuf[1, t] = upper

        def face(load, slot):
            if mode == EDGE:
                own = edge_tile(load, self.width)
                return self.edge(own, *face_slot(slot, layers, self.cells_z))
            return self.wider(load, *face_slot(slot, layers, self.cells_z))

        full = [face(load, slot) for slot, (load, _) in enumerate(face_tiles(zfaces, xfaces, lines))]
        self.below, self.above = full[:3], full[3:5]
        groups = self.groups
        for t in range(2 * groups):
            left_wide[t * ROWS : (t + 1) * ROWS, :] = full[5 + t]
        for t in range(2 * groups + 1):
            right_wide[t * ROWS : (t + 1) * ROWS, :] = full[5 + 3 * groups + t]
        if mode != OWN:
            column = lax.broadcasted_iota(jnp.int32, (ROWS, self.wide), 1)
            ends = {CIRCLE: (self.width - 1, self.wide - 1), EDGE: (STRIP - 1, LANES - STRIP - 1)}[mode]
            here = jnp.logical_or(column == ends[0], column == ends[1])
            for j in range(groups):
                ex_next = self.y_up(full[5 + 2 * groups + j])
                at = (groups + j) * ROWS
                left_wide[at : at + ROWS, :] += jnp.where(here, HALF * ex_next, 0.0)

    def wider(self, load, tile, k):
        if self.mode == OWN:
            return load(slice(0, self.width))

        def moved(v, to):
            shift = (to - STRIP * k) % LANES
            return pltpu.roll(v, shift, 1) if shift else v

        lower, upper = self.ybuf[0, tile], self.ybuf[1, tile]
        halo = jnp.where(self.lane < STRIP, moved(upper, 0), moved(lower, LANES - STRIP))
        return jnp.concatenate([load(slice(0, self.width)), halo], axis=1)

    def edge(self, own, tile, k):
        shift = (LANES - STRIP - 2 * STRIP * (k // 2)) % LANES
        both = pltpu.roll(self.ybuf[k % 2, tile], shift, 1)
        inside = jnp.logical_and(self.lane >= STRIP, self.lane < LANES - STRIP)
        return jnp.where(inside, own, both)

    def y_up(self, v):
        return pltpu.roll(v, self.wide - 1, 1)

    def y_down(self, v):
        return pltpu.roll(v, 1, 1)

    def x_up(self, v, line):
        return jnp.where(self.row == ROWS - 1, line, pltpu.roll(v, ROWS - 1, 0))

    def x_down(self, v, line):
        return jnp.where(self.row == 0, line, pltpu.roll(v, 1, 0))

    def line(self, ref, at):
        return jnp.broadcast_to(ref[pl.ds(at, 1), :], (ROWS, self.wide))

    def field(self, which, c, a, b):
        slot = 6 * b + 3 * which + c
        tile = self.per_group * a + slot // SLOTS
        if self.mode == EDGE:
            return self.edge(self.fields[ROWS * a + b, 3 * which + c], tile, slot % SLOTS)
        ref = self.fields[which]
        return self.wider(lambda s: ref[c, ROWS * a + b, :, s], tile, slot % SLOTS)

    def hx(self, a, b, ey, ez, ey_next):
        return self.field(1, 0, a, b) - HALF * (self.y_up(ez) - ez - ey_next + ey)

    def hy(self, a, b, ex, ez, ex_next):
        up = self.x_up(ez, self.line(self.right_wide, self.cells_z + ROWS * a + b))
        return self.field(1, 1, a, b) - HALF * (ex_next - ex - up + ez)

    def hz(self, a, b, ex, ey):
        up = self.x_up(ey, self.line(self.right_wide, ROWS * a + b))
        return self.field(1, 2, a, b) - HALF * (up - ey - self.y_up(ex) + ex)

    def start(self, a):
        ex, ey = self.field(0, 0, a, 0), self.field(0, 1, a, 0)
        below = self.below
        at_bottom = (
            below[0] - HALF * self.y_up(below[2]) + HALF * ey,
            below[1] - HALF * ex + HALF * self.x_up(below[2], self.line(self.right_wide, 2 * self.cells_z)),
        )
        before, b = jnp.maximum(a - 1, 0), ROWS - 1
        ex_before, ey_before, ez_before = (self.field(0, c, before, b) for c in range(3))
        inside = (
            self.hx(before, b, ey_before, ez_before, ey),
            self.hy(before, b, ex_before, ez_before, ex),
        )
        bottom = a == 0
        return (ex, ey) + tuple(jnp.where(bottom, one, two) for one, two in zip(at_bottom, inside))

    def group(self, a, carry, emit):
        ex, ey, hx_z, hy_z = carry
        for b in range(ROWS):
            z = ROWS * a + b
            ez = self.field(0, 2, a, b)
            if b < ROWS - 1:
                ex_next, ey_next = (self.field(0, c, a, b + 1) for c in range(2))
            else:
                end = a == self.groups - 1
                after = jnp.minimum(a + 1, self.groups - 1)
                ex_next, ey_next = (
                    jnp.where(end, self.above[c], self.field(0, c, after, 0)) for c in range(2)
                )
            hx = self.hx(a, b, ey, ez, ey_next)
            hy = self.hy(a, b, ex, ez, ex_next)
            hz = self.hz(a, b, ex, ey)
            hy_x = self.x_down(hy, self.line(self.left_wide, z) + HALF * ez)
            hz_x = self.x_down(hz, self.line(self.left_wide, self.cells_z + z) - HALF * ey)
            curl = (
                (hz - self.y_down(hz)) - (hy - hy_z),
                (hx - hx_z) - (hz - hz_x),
                (hy - hy_x) - (hx - self.y_down(hx)),
            )
            emit(a, b, (ex, ey, ez), (hx, hy, hz), curl)
            ex, ey, hx_z, hy_z = ex_next, ey_next, hx, hy
        return ex, ey, hx_z, hy_z

    def gradient(self, layers, arrays, store):
        first = first_layer(self.cells_z, layers)
        first_group = first // ROWS
        if self.mode == EDGE:
            grad_edges, mask_ref = arrays
            mask = self.edge(mask_ref[...], self.grad_base, 5)
        else:
            f_ref, inv_ref, grad_ref, mask_ref = arrays
            mask = mask_ref[...]

        def emit(a, b, efield, hfield, curl):
            z = ROWS * a + b
            layer = z - first
            if self.mode == EDGE:
                tile = self.grad_base + self.per_group * (a - first_group)
                slots = [6 * b + n for n in range(5)]
                values = [
                    self.edge(grad_edges[layer, n], tile + slot // SLOTS, slot % SLOTS)
                    for n, slot in enumerate(slots)
                ]
            else:
                values = [f_ref[c, z] for c in range(3)] + [inv_ref[z], grad_ref[layer]]
            total = None
            for c in range(3):
                term = values[c] * (efield[c] + values[3] * curl[c])
                total = term if total is None else total + term
            store(layer, values[4] + mask * total)

        def body(i, carry):
            return self.group(first_group + i, carry, emit)

        lax.fori_loop(0, layers // ROWS, body, self.start(first_group))


def fields_scratch(mode, xface, yface, width):
    rows, wide = xface.shape[0], faces_wide(mode, width)
    out = [pltpu.VMEM((rows, wide), jnp.float32)] * 2
    if mode != OWN:
        out.append(pltpu.VMEM((2,) + yface.shape, jnp.float32))
    return out


def own_gradient_kernel(counts, per_device, *refs):
    e_ref, h_ref, f_ref, inv_ref, grad_ref, mask_ref = refs[:6]
    zfaces, xfaces = refs[6 : 6 + counts[0]], refs[6 + counts[0] : 6 + sum(counts)]
    shares, (own_ref, *scratch) = refs[6 + sum(counts) : -3][::-1], refs[-3:]
    layers, _, width = grad_ref.shape
    fields = Fields(OWN, layers, (e_ref, h_ref), zfaces, xfaces, (), None, scratch)

    def store(layer, value):
        own_ref[layer] = value

    fields.gradient(layers, (f_ref, inv_ref, grad_ref, mask_ref), store)

    me = lax.axis_index("gx")
    for k, share in enumerate(shares):
        chunk = lax.bitwise_xor(me, way_there(len(shares))[k])
        for i in range(per_device):
            share[:, i * width : (i + 1) * width] = own_ref[chunk * per_device + i]
        if share.shape[1] > per_device * width:
            share[:, per_device * width :] = jnp.zeros((ROWS, SPARE), jnp.float32)


SPARE = LANES


def own_gradient(arrays, zfaces, xfaces):
    layers, _, width = arrays[4].shape
    count = lax.axis_size("gx")
    per_device = layers // count
    *shares, own = pl.pallas_call(
        functools.partial(own_gradient_kernel, (len(zfaces), len(xfaces)), per_device),
        in_specs=[VMEM] * (6 + len(zfaces) + len(xfaces)),
        out_specs=[VMEM] * (count + 1),
        out_shape=[fast(ROWS, per_device * width + SPARE)]
        + [fast(ROWS, per_device * width)] * (count - 1)
        + [fast(layers, ROWS, width)],
        scratch_shapes=fields_scratch(OWN, xfaces[0], None, width),
        compiler_params=params(),
    )(*arrays, *zfaces, *xfaces)
    return shares[::-1], own


PART = 2 * STRIP
SPAN = 2 * PART


def edge_gradient_kernel(counts, *refs):
    own_ref, f_ref, inv_ref, wide_ref, eh_ref, grad_ref, mask_ref, taps_ref = refs[:8]
    ends = np.cumsum((8,) + counts)
    zfaces, xfaces, lines, yfaces = (refs[i:j] for i, j in zip(ends[:-1], ends[1:]))
    (shares, message, edge_ref), scratch = refs[ends[-1] : -6], refs[-6:-3]
    folded, parts, slabs = refs[-3:]
    layers, _, width = own_ref.shape
    lane = lax.broadcasted_iota(jnp.int32, (ROWS, LANES), 1)
    first, last = STRIP, LANES - STRIP - 1
    fields = Fields(EDGE, layers, eh_ref, zfaces, xfaces, lines, yfaces, scratch)

    def store(layer, value):
        edge_ref[layer] = value

    fields.gradient(layers, (grad_ref, mask_ref), store)

    count = shares.shape[0]
    half = count // 2
    rows = half * ROWS
    me = lax.axis_index("gx")
    folded[...] = jnp.zeros_like(folded)
    fold = jnp.minimum(me, count - 1 - me)
    per_tile = LANES // SPAN
    for start in range(0, layers, per_tile):
        tile = jnp.zeros((ROWS, LANES), jnp.float32)
        for j in range(min(per_tile, layers - start)):
            edge = edge_ref[start + j]
            own = edge_tile(lambda s: own_ref[start + j, :, s], width)
            more = jnp.where(jnp.logical_or(lane == first, lane == last), edge - own, edge)
            low, high = SPAN * j + 1, SPAN * j + PART + STRIP - 1
            here = jnp.logical_and(lane >= low, lane < low + STRIP)
            tile = jnp.where(here, pltpu.roll(more, (low - 1) % LANES, 1), tile)
            here = jnp.logical_and(lane >= high, lane < high + STRIP)
            tile = jnp.where(here, pltpu.roll(more, (high - last) % LANES, 1), tile)
        tile = jnp.where(me < half, tile, flip_rows(tile))
        folded[fold, :, start // per_tile * LANES : (start // per_tile + 1) * LANES] = tile
    split_rows(jnp.concatenate([folded[s] for s in range(half)], axis=0), parts)
    total = cone(taps_ref, parts, rows)
    lanes = lax.broadcasted_iota(jnp.int32, (rows, LANES), 1)
    per_share = LANES // PART
    for start in range(0, layers, per_share):
        packed = jnp.zeros((rows, LANES), jnp.float32)
        for j in range(min(per_share, layers - start)):
            at = SPAN * (start + j)
            tile = total[:, at // LANES * LANES : (at // LANES + 1) * LANES]
            left = pltpu.roll(tile, (PART * j - STRIP - at) % LANES, 1)
            right = pltpu.roll(tile, (PART * j + STRIP - PART - 1 - at) % LANES, 1)
            packed = jnp.where(lanes // STRIP == 2 * j, left, packed)
            packed = jnp.where(lanes // STRIP == 2 * j + 1, right, packed)
        here = slice(start // per_share * LANES, (start // per_share + 1) * LANES)
        for s in range(half):
            one = packed[s * ROWS : (s + 1) * ROWS]
            slabs[s, :, here] = one
            slabs[count - 1 - s, :, here] = flip_rows(one)
    for k in range(count):
        shares[k] = slabs[lax.bitwise_xor(me, k)]

    message[...] = jnp.zeros_like(message)
    top, last = fields.cells_z - 1, ROWS - 1
    above, beyond = (line[0:1] for line in corner_lines(lines, slice(0, width)))
    added = wide_ref[0:1, :] * f_ref[2, top, 0:1, :] * inv_ref[top, 0:1, :] * (HALF * above)
    added += wide_ref[last:, :] * f_ref[0, 0, last:, :] * inv_ref[0, last:, :] * (HALF * beyond)
    column = lax.broadcasted_iota(jnp.int32, (1, width), 1)
    added = jnp.where(jnp.logical_or(column == 0, column == width - 1), 0.0, added)
    for at, n in line_places(width):
        message[n : n + 1, at : at + LANES] = added[:, (at // LANES * ROWS + n) * LANES :][:, :LANES]


def line_places(width):
    return [(t // ROWS * LANES, t % ROWS) for t in range(width // LANES)]


def line_of(message, width):
    return jnp.concatenate([message[n : n + 1, at : at + LANES] for at, n in line_places(width)], axis=1)


def line_spot(layers):
    bottom = lax.axis_index("gz") == 0
    return jnp.where(bottom, layers - 1, 0), jnp.where(bottom, 0, ROWS - 1)


def edge_gradient(own, arrays, edges, taps, zfaces, xfaces, lines, yfaces):
    layers, _, width = own.shape
    faces = (*zfaces, *xfaces, *lines, *yfaces)
    count = lax.axis_size("gx")
    share = (count, ROWS, math.ceil(layers * PART / LANES) * LANES)
    spread = math.ceil(layers * SPAN / LANES) * LANES
    line = math.ceil(width / LANES / ROWS) * LANES
    return pl.pallas_call(
        functools.partial(edge_gradient_kernel, (len(zfaces), len(xfaces), len(lines), len(yfaces))),
        in_specs=[VMEM] * (8 + len(faces)),
        out_specs=[VMEM] * 3,
        out_shape=[fast(*share), fast(ROWS, line), fast(layers, ROWS, LANES)],
        scratch_shapes=fields_scratch(EDGE, xfaces[0], yfaces[0], width)
        + [
            pltpu.VMEM((count // 2, ROWS, spread), jnp.float32),
            pltpu.VMEM((3 * count // 2 * ROWS, spread), jnp.bfloat16),
            pltpu.VMEM(share, jnp.float32),
        ],
        compiler_params=params(),
    )(own, arrays[2], arrays[3], arrays[5], *edges, taps, *faces)


def step_kernel(counts, *refs):
    e_ref, h_ref, inv_ref, own_ref, edge_ref, message = refs[:6]
    ends = np.cumsum((6,) + counts)
    zfaces, xfaces, lines, yfaces = (refs[i:j] for i, j in zip(ends[:-1], ends[1:]))
    e_out, h_out, grad_out = refs[ends[-1] + 1 : ends[-1] + 4]
    left_wide, right_wide, ybuf, e_new, h_new, grad_new, sems = refs[ends[-1] + 4 :]
    layers, _, width = own_ref.shape
    lane = lax.broadcasted_iota(jnp.int32, (ROWS, LANES), 1)

    for layer in range(layers):
        edge = edge_ref[layer]
        head, tail = own_ref[layer, :, 0:LANES], own_ref[layer, :, width - LANES :]
        grad_new[layer] = own_ref[layer]
        grad_new[layer, :, 0:LANES] = jnp.where(lane == 0, pltpu.roll(edge, LANES - STRIP, 1), head)
        grad_new[layer, :, width - LANES :] = jnp.where(lane == LANES - 1, pltpu.roll(edge, STRIP, 1), tail)
    layer, spot = line_spot(layers)
    row = lax.broadcasted_iota(jnp.int32, (ROWS, width), 0)
    grad_new[layer] += jnp.where(row == spot, line_of(message, width), 0.0)
    grad_copy = pltpu.make_async_copy(grad_new, grad_out, sems.at[0, 0])
    grad_copy.start()

    fields = Fields(CIRCLE, layers, (e_ref, h_ref), zfaces, xfaces, lines, yfaces, (left_wide, right_wide, ybuf))

    def emit(a, b, efield, hfield, curl):
        z = ROWS * a + b
        half_inv = inv_ref[z]
        for c in range(3):
            e_new[c, z] = efield[c][:, :width] + half_inv * curl[c][:, :width]
            h_new[c, z] = hfield[c][:, :width]

    def copies(a):
        here = pl.ds(a * ROWS, ROWS)
        return [
            pltpu.make_async_copy(new.at[c, here], out.at[c, here], sems.at[1 + a, 3 * n + c])
            for n, (new, out) in enumerate(((e_new, e_out), (h_new, h_out)))
            for c in range(3)
        ]

    def body(a, carry):
        carry = fields.group(a, carry, emit)
        for copy in copies(a):
            copy.start()
        return carry

    lax.fori_loop(0, fields.groups, body, fields.start(0))
    for a in range(fields.groups):
        for copy in copies(a):
            copy.wait()
    grad_copy.wait()


def step(efield, hfield, inv, own, edge, message, zfaces, xfaces, lines, yfaces, after):
    _, cells_z, _, width = efield.shape
    groups = (zfaces, xfaces, lines, yfaces)
    counts = tuple(len(group) for group in groups)
    shapes = (efield.shape, hfield.shape, own.shape)
    return pl.pallas_call(
        functools.partial(step_kernel, counts),
        in_specs=[VMEM] * (6 + sum(counts)) + [ANY],
        out_specs=[ANY] * 3,
        out_shape=[f32(*shape) for shape in shapes],
        scratch_shapes=fields_scratch(CIRCLE, xfaces[0], yfaces[0], width)
        + [pltpu.VMEM(shape, jnp.float32) for shape in shapes]
        + [pltpu.SemaphoreType.DMA((1 + cells_z // ROWS, 6))],
        compiler_params=params(),
    )(efield, hfield, inv, own, edge, message, *(one for group in groups for one in group), after)


def cone_taps():
    span = np.arange(-RADIUS, RADIUS + 1, dtype=np.float64)
    return np.maximum(RADIUS - np.sqrt(span[:, None] ** 2 + span[None, :] ** 2), 0.0)


def cone_sum():
    return cone_taps().sum()


def cone_matrix(rows):
    weight = cone_taps() / cone_sum()
    x = np.arange(rows)
    out = np.zeros((RADIUS + 1, rows, rows))
    for b in range(RADIUS + 1):
        for apart in (x[:, None] - x[None, :], 2 * rows - 1 - x[:, None] - x[None, :]):
            near = np.abs(apart) <= RADIUS
            out[b] += np.where(near, weight[np.clip(apart, -RADIUS, RADIUS) + RADIUS, RADIUS + b], 0.0)
    out = out.reshape((RADIUS + 1) * rows, rows).astype(np.float32)
    high = out.astype(jnp.bfloat16)
    low = (out - high.astype(np.float32)).astype(jnp.bfloat16)
    return np.concatenate([high, low, high], axis=1)


def flip_rows(v):
    row = lax.broadcasted_iota(jnp.int32, v.shape, 0)
    v = pltpu.roll(v, 4, 0)
    v = jnp.where(row % 4 < 2, pltpu.roll(v, ROWS - 2, 0), pltpu.roll(v, 2, 0))
    return jnp.where(row % 2 < 1, pltpu.roll(v, ROWS - 1, 0), pltpu.roll(v, 1, 0))


def split_rows(symmetric, parts):
    rows = symmetric.shape[0]
    high = symmetric.astype(jnp.bfloat16)
    low = (symmetric - high.astype(jnp.float32)).astype(jnp.bfloat16)
    parts[0:rows, :] = high
    parts[rows : 2 * rows, :] = high
    parts[2 * rows : 3 * rows, :] = low


def cone(taps_ref, parts, rows):
    wide = parts.shape[1]
    mixed = jnp.dot(taps_ref[...], parts[...], preferred_element_type=jnp.float32)
    total = mixed[0:rows]
    for b in range(1, RADIUS + 1):
        part = mixed[b * rows : (b + 1) * rows]
        total = total + (pltpu.roll(part, b, 1) + pltpu.roll(part, wide - b, 1))
    return total


def filter_kernel(count, per_device, width, *refs):
    taps_ref, edges_ref, line_ref = refs[:3]
    got = refs[count + 2 : 2 : -1]
    outs = refs[3 + count : 3 + 2 * count]
    slabs, parts, done = refs[3 + 2 * count :]
    me = lax.axis_index("gx")
    half = count // 2
    rows = half * ROWS
    for k in range(count):
        slabs[lax.bitwise_xor(me, way_there(count)[k])] = got[k][:, : per_device * width]

    side = jnp.zeros((rows, LANES), jnp.float32)
    for i in range(per_device):
        here = slice(i * width, (i + 1) * width)
        halves = [slabs[s, :, here] + flip_rows(slabs[count - 1 - s, :, here]) for s in range(half)]
        split_rows(jnp.concatenate([jnp.concatenate(halves, axis=0), side], axis=1), parts)
        total = cone(taps_ref, parts, rows)
        for s in range(half):
            own = total[s * ROWS : (s + 1) * ROWS, :width]
            done[s, :, here] = own
            done[count - 1 - s, :, here] = flip_rows(own)
    for k, apart in enumerate(way_back(count)):
        outs[k][:, : per_device * width] = done[lax.bitwise_xor(me, apart)]
        tail = per_device * width + edges_ref.shape[2]
        outs[k][:, per_device * width : tail] = edges_ref[apart]
        outs[k][:, tail:] = line_ref[...]


def cone_filter(taps, edges, line, got, per_device, width):
    count = len(got)
    rows = count // 2 * ROWS
    return pl.pallas_call(
        functools.partial(filter_kernel, count, per_device, width),
        in_specs=[VMEM] * (3 + count),
        out_specs=[VMEM] * count,
        out_shape=[fast(ROWS, per_device * width + edges.shape[2] + line.shape[1])] * count,
        scratch_shapes=[
            pltpu.VMEM((count, ROWS, per_device * width), jnp.float32),
            pltpu.VMEM((3 * rows, width + LANES), jnp.bfloat16),
            pltpu.VMEM((count, ROWS, per_device * width), jnp.float32),
        ],
        compiler_params=params(),
    )(taps, edges, line, *got[::-1])


def cone_weight(along_x, along_y):
    near = jnp.maximum(RADIUS - jnp.sqrt(along_x * along_x + float(along_y * along_y)), 0.0)
    return near * float(1.0 / cone_sum())


def finish_kernel(count, per_device, width, *refs):
    got = refs[count - 1 :: -1]
    out, (left, right, done, sems) = refs[count], refs[count + 1 :]
    me = lax.axis_index("gx")
    layers = count * per_device
    lane = lax.broadcasted_iota(jnp.int32, (ROWS, LANES), 1)
    edges_at = per_device * width
    line_at = edges_at + math.ceil(layers * PART / LANES) * LANES

    per_tile = LANES // PART
    for start in range(0, layers, per_tile):
        at = edges_at + start * PART
        tile = got[0][:, at : at + LANES]
        for k in range(1, count):
            tile = tile + got[k][:, at : at + LANES]
        for j in range(min(per_tile, layers - start)):
            head = pltpu.roll(tile, (-PART * j) % LANES, 1)
            left[start + j] = jnp.where(lane < STRIP - 1, head, 0.0)
            tail = pltpu.roll(tile, (LANES + 1 - 2 * STRIP - PART * j) % LANES, 1)
            right[start + j] = jnp.where(lane > LANES - STRIP, tail, 0.0)

    line_layer, spot = line_spot(layers)
    end = count * ROWS - 1
    row = lax.broadcasted_iota(jnp.int32, (ROWS, LANES), 0) + me * ROWS
    lines, near, far = [], [], []
    for k, apart in enumerate(way_back(count)):
        lines.append(line_of(got[k][:, line_at:], width))
        where = lax.bitwise_xor(me, apart) * ROWS + spot
        near.append((row - where).astype(jnp.float32))
        far.append((row - (end - where)).astype(jnp.float32))
    total = None
    for b in range(RADIUS + 1):
        mixed = jnp.zeros((ROWS, width), jnp.float32)
        for k in range(count):
            weight = cone_weight(near[k], b) + cone_weight(far[k], b)
            mixed = mixed + jnp.concatenate([weight] * (width // LANES), axis=1) * lines[k]
        mixed = jnp.concatenate([mixed, jnp.zeros((ROWS, LANES), jnp.float32)], axis=1)
        if b:
            mixed = pltpu.roll(mixed, b, 1) + pltpu.roll(mixed, width + LANES - b, 1)
        total = mixed if total is None else total + mixed
    line = total[:, :width]

    copies = []
    for k, apart in enumerate(way_back(count)):
        first = lax.bitwise_xor(me, apart) * per_device
        for i in range(per_device):
            at = i * width
            done[k, i] = got[k][:, at : at + width] + jnp.where(first + i == line_layer, line, 0.0)
            done[k, i, :, :LANES] += left[first + i]
            done[k, i, :, width - LANES :] += right[first + i]
        copies.append(pltpu.make_async_copy(done.at[k], out.at[pl.ds(first, per_device)], sems.at[k]))
        copies[-1].start()
    for copy in copies:
        copy.wait()


def finish(parts, layers, width):
    count = len(parts)
    per_device = layers // count
    return pl.pallas_call(
        functools.partial(finish_kernel, count, per_device, width),
        in_specs=[VMEM] * count,
        out_specs=ANY,
        out_shape=f32(layers, ROWS, width),
        scratch_shapes=[
            pltpu.VMEM((layers, ROWS, LANES), jnp.float32),
            pltpu.VMEM((layers, ROWS, LANES), jnp.float32),
            pltpu.VMEM((count, per_device, ROWS, width), jnp.float32),
            pltpu.SemaphoreType.DMA((count,)),
        ],
        compiler_params=params(),
    )(*parts[::-1])


def spread(parts, order):
    count = len(parts)
    got = list(parts)
    for j in range(count - 1, 0, -1):
        got[j] = lax.ppermute(parts[j], "gx", [(i, i ^ order[j]) for i in range(count)])
    return got


def way_there(count):
    return list(range(count))


def way_back(count):
    if count < 4:
        return list(range(count))
    return [0] + list(range(2, count - 1)) + [1, count - 1]


def on_device(efield, hfield, forward, material, permit, design_mask, grad_sum):
    layers, _, width = grad_sum.shape
    efield, hfield, zfaces, xfaces, lines = halos(efield, hfield)
    own_low, own_high, mask, inv = strips(
        permit, efield, hfield, forward, material, grad_sum, design_mask
    )
    arrays = (efield, hfield, forward, inv, grad_sum, mask)
    edges = own_edges(arrays)
    shares, own = own_gradient(arrays, zfaces, xfaces)
    got = spread(shares, way_there(len(shares)))
    yfaces = exchange(y_faces(own_low, own_high, zfaces, xfaces, lines, own), "gy", "gz")
    taps = jnp.asarray(cone_matrix(len(got) // 2 * ROWS))
    added, line, edge = edge_gradient(own, arrays, edges, taps, zfaces, xfaces, lines, yfaces)
    parts = cone_filter(taps, added, line, got, layers // len(got), width)
    e_next, h_next, grad_total = step(
        efield, hfield, inv, own, edge, line, zfaces, xfaces, lines, yfaces, parts[0]
    )
    return e_next, h_next, grad_total, finish(spread(parts, way_back(len(parts))), layers, width)


def solution(mesh):
    field = P(None, "gz", "gx", "gy")
    cells = P("gz", "gx", "gy")
    return jax.shard_map(
        on_device,
        mesh=mesh,
        in_specs=(field, field, field, cells, P(), P("gx", "gy"), cells),
        out_specs=(field, field, cells, cells),
        check_vma=False,
    )
```

```python
import functools
import math

import jax
import jax.numpy as jnp
import numpy as np
from jax import lax
from jax.experimental import pallas as pl
from jax.experimental.pallas import tpu as pltpu
from jax.sharding import PartitionSpec as P

RADIUS = 6
BLOCK = 8
HALF = 0.5

ROWS = 8
LANES = 128
STRIP = 8
SLOTS = LANES // STRIP
MIB = 1024 * 1024

VMEM = pl.BlockSpec(memory_space=pltpu.VMEM)
SMEM = pl.BlockSpec(memory_space=pltpu.SMEM)
ANY = pl.BlockSpec(memory_space=pl.ANY)


def params(mib=24):
    return pltpu.CompilerParams(vmem_limit_bytes=mib * MIB)


def f32(*shape):
    return jax.ShapeDtypeStruct(shape, jnp.float32)


def fast(*shape):
    return pltpu.VMEM(shape, jnp.float32)


def rounds(axis):
    return 2 if lax.axis_size(axis) > 2 else 1


def exchange(sends, axis, mate):
    count = lax.axis_size(axis)
    beside = lax.axis_size(mate)
    if count == 1:
        return sends
    got = []
    for start, value in enumerate(sends):
        partner = list(range(count))
        for low in range(start, count - 1, 2):
            partner[low], partner[low + 1] = low + 1, low
        axes = sorted((axis, mate))
        steps = (beside, 1) if axes[0] == axis else (1, count)
        pairs = []
        for i in range(count):
            for m in range(beside):
                if partner[i] != i:
                    to = (partner[i], m)
                elif beside % 2 == 0:
                    to = (i, m ^ 1)
                else:
                    continue
                pairs.append((i * steps[0] + m * steps[1], to[0] * steps[0] + to[1] * steps[1]))
        got.append(lax.ppermute(value, tuple(axes), pairs))
    return got


def exchange_diagonal(sends):
    along_x, along_y, along_z = (lax.axis_size(axis) for axis in AXES)

    def flat(x, y, z):
        return (x * along_y + y) * along_z + z

    got = []
    for start, value in enumerate(sends):
        partner = {}
        for low in range(start, along_z - 1, 2):
            for x in range(1, along_x):
                partner[x, low] = (x - 1, low + 1)
                partner[x - 1, low + 1] = (x, low)
        pairs = []
        for x in range(along_x):
            for z in range(along_z):
                for y in range(along_y):
                    if (x, z) in partner:
                        to = partner[x, z]
                        pairs.append((flat(x, y, z), flat(to[0], y, to[1])))
                    elif along_y % 2 == 0:
                        pairs.append((flat(x, y, z), flat(x, y ^ 1, z)))
        got.append(lax.ppermute(value, AXES, pairs))
    return got


AXES = ("gx", "gy", "gz")


class Side:
    def __init__(self, axis):
        index = lax.axis_index(axis)
        self.rounds = rounds(axis)
        self.odd = index % 2 == 1
        self.bottom = index == 0
        self.top = index == lax.axis_size(axis) - 1

    def sends(self, low, high):
        both = [jnp.where(self.odd, low, high)]
        if self.rounds > 1:
            both.append(jnp.where(self.odd, high, low))
        return both

    def lower(self, got):
        return jnp.where(self.bottom, 0.0, jnp.where(self.odd, got[0], got[-1]))

    def upper(self, got):
        return jnp.where(self.top, 0.0, jnp.where(self.odd, got[-1], got[0]))


def first_layer(cells_z, layers):
    return (cells_z - layers) * (1 - lax.axis_index("gz"))


def faces_kernel(x_rounds, e_in, h_in, e_ref, h_ref, *refs):
    x_sends, (low_ref, rows_ref, sems) = refs[:x_rounds], refs[-3:]
    others = refs[x_rounds:-3]
    z_sends, d_sends = others[: len(others) // 2], others[len(others) // 2 :]
    cells_z = e_ref.shape[1]
    last, top = ROWS - 1, cells_z - 1
    copies = [
        [pltpu.make_async_copy(source.at[c], target.at[c], sems.at[n, c]) for c in range(3)]
        for n, (source, target) in enumerate(((e_in, e_ref), (h_in, h_ref)))
    ]
    for copy in copies[0] + copies[1][1:] + copies[1][:1]:
        copy.start()

    low_ref[2 * cells_z :, :] = jnp.zeros_like(low_ref[2 * cells_z :, :])
    rows_ref[5, top : top + 1, :] = jnp.zeros_like(rows_ref[5, top : top + 1, :])
    for copy in copies[0]:
        copy.wait()
    for z in range(cells_z):
        low_ref[z : z + 1, :] = e_ref[1, z, 0:1, :]
        low_ref[cells_z + z : cells_z + z + 1, :] = e_ref[2, z, 0:1, :]
        for c in range(3):
            rows_ref[c, z : z + 1, :] = e_ref[c, z, last : last + 1, :]
        if z > 0:
            rows_ref[5, z - 1 : z, :] = e_ref[0, z, last : last + 1, :]
    for copy in copies[1][1:]:
        copy.wait()
    for z in range(cells_z):
        for c in range(2):
            rows_ref[3 + c, z : z + 1, :] = h_ref[1 + c, z, last : last + 1, :]
    width = e_ref.shape[3]
    ex, ey, ez = (rows_ref[c] for c in range(3))
    column = lax.broadcasted_iota(jnp.int32, ex.shape, 1)
    ex_next = jnp.where(column == width - 1, 0.0, pltpu.roll(ex, width - 1, 1))
    lane = lax.broadcasted_iota(jnp.int32, (ROWS, LANES), 1)
    strip = jnp.zeros((ROWS, LANES), jnp.float32)
    for j in range(cells_z // ROWS):
        head = rows_ref[0, j * ROWS : (j + 1) * ROWS, 0:LANES]
        strip = jnp.where(lane // STRIP == j, pltpu.roll(head, STRIP * j, 1) if j else head, strip)
    high = (
        rows_ref[3] - HALF * (rows_ref[5] - ex + ez),
        rows_ref[4] + HALF * ey - HALF * (ex - ex_next),
        jnp.concatenate([strip, jnp.zeros((ROWS, width - LANES), jnp.float32)], axis=1),
    )
    side = Side("gx")
    for c, value in enumerate(high):
        here = slice(c * cells_z, c * cells_z + value.shape[0])
        for ref, one in zip(x_sends, side.sends(low_ref[here, :], value)):
            ref[here, :] = one

    copies[1][0].wait()
    side = Side("gz")
    ex, ey, ez = (e_ref[c, top] for c in range(3))
    low = (e_ref[0, 0], e_ref[1, 0], jnp.zeros_like(ez))
    high = (h_ref[0, top] + HALF * ez - HALF * ey, h_ref[1, top] + HALF * ex - HALF * ez, ez)
    for c in range(3):
        for ref, value in zip(z_sends, side.sends(low[c], high[c])):
            ref[c] = value

    down, up = (
        jnp.broadcast_to(line, (ROWS, line.shape[1]))
        for line in (e_ref[0, 0, last : last + 1, :], e_ref[2, top, 0:1, :])
    )
    for ref, value in zip(d_sends, side.sends(down, up)):
        ref[...] = value


def halos(efield, hfield):
    _, cells_z, cells_x, cells_y = efield.shape
    x_rounds, z_rounds = rounds("gx"), rounds("gz")
    x_face, z_face, line = fast(2 * cells_z + ROWS, cells_y), fast(3, cells_x, cells_y), fast(ROWS, cells_y)
    fields = [fast(*field.shape) for field in (efield, hfield)]
    efield, hfield, *sends = pl.pallas_call(
        functools.partial(faces_kernel, x_rounds),
        in_specs=[ANY] * 2,
        out_specs=[VMEM] * (2 + x_rounds + 2 * z_rounds),
        out_shape=fields + [x_face] * x_rounds + [z_face] * z_rounds + [line] * z_rounds,
        scratch_shapes=[
            pltpu.VMEM(x_face.shape, jnp.float32),
            pltpu.VMEM((6, cells_z, cells_y), jnp.float32),
            pltpu.SemaphoreType.DMA((2, 3)),
        ],
        compiler_params=params(54),
    )(efield, hfield)
    xfaces = exchange(sends[:x_rounds], "gx", "gy")
    zfaces = exchange(sends[x_rounds : x_rounds + z_rounds], "gz", "gy")
    return efield, hfield, zfaces, xfaces, exchange_diagonal(sends[x_rounds + z_rounds :])


def lane_group():
    return lax.broadcasted_iota(jnp.int32, (ROWS, LANES), 1) // STRIP


def pack_strips(tiles, low_ref, high_ref, first):
    group = lane_group()
    width = tiles[0][1]
    for start in range(0, len(tiles), SLOTS):
        low = jnp.zeros((ROWS, LANES), jnp.float32)
        high = jnp.zeros((ROWS, LANES), jnp.float32)
        for k, (load, _) in enumerate(tiles[start : start + SLOTS]):
            if load is None:
                continue
            here = group == k
            shift = (STRIP * k) % LANES
            left = load(slice(0, LANES))
            right = load(slice(width - LANES, width))
            low = jnp.where(here, pltpu.roll(left, shift, 1) if shift else left, low)
            shift = (STRIP * k + STRIP) % LANES
            high = jnp.where(here, pltpu.roll(right, shift, 1) if shift else right, high)
        low_ref[first + start // SLOTS] = low
        high_ref[first + start // SLOTS] = high


def strips_kernel(
    permit_ref, e_ref, h_ref, f_ref, mat_ref, grad_ref, mask_ref, low_ref, high_ref, wide_ref, inv_ref
):
    cells_z, width = e_ref.shape[1], e_ref.shape[3]
    layers = grad_ref.shape[0]
    blocks = mask_ref.shape[1]
    inverse = [
        jnp.broadcast_to(HALF * (1.0 / permit_ref[0:1, m : m + 1]), (ROWS, width))
        for m in range(permit_ref.shape[1])
    ]
    for z in range(cells_z):
        inv = inverse[0]
        for m in range(1, len(inverse)):
            inv = jnp.where(mat_ref[z] == m, inverse[m], inv)
        inv_ref[z] = inv
    spread = (
        lax.broadcasted_iota(jnp.int32, (blocks, width), 0)
        == lax.broadcasted_iota(jnp.int32, (blocks, width), 1) // BLOCK
    ).astype(jnp.float32)
    mask = jnp.broadcast_to(mask_ref[...].astype(jnp.float32), (ROWS, blocks))
    wide_ref[...] = jnp.dot(mask, spread, preferred_element_type=jnp.float32)
    first = first_layer(cells_z, layers)
    tiles = []
    for z in range(cells_z):
        for ref in (e_ref, h_ref):
            for c in range(3):
                tiles.append((lambda s, r=ref, c=c, z=z: r[c, z, :, s], width))
    pack_strips(tiles, low_ref, high_ref, 0)

    done = len(tiles) // SLOTS
    tiles = []
    for layer in range(layers):
        for c in range(3):
            tiles.append((lambda s, c=c, l=layer: f_ref[c, first + l, :, s], width))
        tiles.append((lambda s, l=layer: inv_ref[first + l, :, s], width))
        tiles.append((lambda s, l=layer: grad_ref[l, :, s], width))
        tiles.append((lambda s: wide_ref[:, s], width) if layer % ROWS == 0 else (None, width))
    pack_strips(tiles, low_ref, high_ref, done)


def strips(permit, efield, hfield, forward, material, grad_sum, mask):
    cells_z, width = efield.shape[1], efield.shape[3]
    count = (cells_z * 6 + grad_sum.shape[0] * 6) // SLOTS
    packed = (count, ROWS, LANES)
    shapes = (packed, packed, (ROWS, width), material.shape)
    return pl.pallas_call(
        strips_kernel,
        in_specs=[VMEM] * 7,
        out_specs=[VMEM] * 4,
        out_shape=[fast(*shape) for shape in shapes],
        compiler_params=params(),
    )(permit.reshape(1, -1), efield, hfield, forward, material, grad_sum, mask)


def edge_tile(load, width):
    lane = lax.broadcasted_iota(jnp.int32, (ROWS, LANES), 1)
    head = pltpu.roll(load(slice(0, LANES)), STRIP, 1)
    tail = pltpu.roll(load(slice(width - LANES, width)), LANES - STRIP, 1)
    return jnp.where(lane < LANES // 2, head, tail)


def edges_kernel(e_ref, h_ref, f_ref, inv_ref, grad_ref, mask_ref, eh_out, grad_out, mask_out):
    cells_z, width = e_ref.shape[1], e_ref.shape[3]
    layers = grad_ref.shape[0]
    first = first_layer(cells_z, layers)
    for z in range(cells_z):
        for c in range(3):
            eh_out[z, c] = edge_tile(lambda s: e_ref[c, z, :, s], width)
            eh_out[z, 3 + c] = edge_tile(lambda s: h_ref[c, z, :, s], width)
    for layer in range(layers):
        for c in range(3):
            grad_out[layer, c] = edge_tile(lambda s: f_ref[c, first + layer, :, s], width)
        grad_out[layer, 3] = edge_tile(lambda s: inv_ref[first + layer, :, s], width)
        grad_out[layer, 4] = edge_tile(lambda s: grad_ref[layer, :, s], width)
    mask_out[...] = edge_tile(lambda s: mask_ref[:, s], width)


def own_edges(arrays):
    cells_z, layers = arrays[0].shape[1], arrays[4].shape[0]
    return pl.pallas_call(
        edges_kernel,
        in_specs=[VMEM] * 6,
        out_specs=[VMEM] * 3,
        out_shape=[fast(cells_z, 6, ROWS, LANES), fast(layers, 5, ROWS, LANES), fast(ROWS, LANES)],
        compiler_params=params(),
    )(*arrays)


def corner_lines(lines, s):
    z_side, x_side = Side("gz"), Side("gx")
    above = jnp.where(x_side.bottom, 0.0, z_side.upper([f[:, s] for f in lines]))
    beyond = jnp.where(x_side.top, 0.0, z_side.lower([f[:, s] for f in lines]))
    return above, beyond


def face_tiles(zfaces, xfaces, lines):
    width = xfaces[0].shape[1]
    rows = xfaces[0].shape[0]
    cells_z = (rows - ROWS) // 2
    z_side, x_side = Side("gz"), Side("gx")

    def corner(s):
        row = lax.broadcasted_iota(jnp.int32, (ROWS, s.stop - s.start), 0)
        return jnp.where(row == ROWS - 1, -HALF * corner_lines(lines, s)[0], 0.0)

    def x_tile(pick, t, s):
        value = pick([f[t : t + ROWS, s] for f in xfaces])
        return value + corner(s) if lines and t == cells_z - ROWS and pick == x_side.lower else value

    def strip(j, s):
        zeros = jnp.zeros((ROWS, s.stop - s.start), jnp.float32)
        if s.start:
            return zeros
        lane = lax.broadcasted_iota(jnp.int32, (ROWS, LANES), 1)
        packed = x_side.lower([f[2 * cells_z :, 0:LANES] for f in xfaces])
        head = jnp.where(lane < STRIP, pltpu.roll(packed, LANES - STRIP * j, 1) if j else packed, 0.0)
        return head if s.stop == LANES else jnp.concatenate([head, zeros[:, LANES:]], axis=1)

    tiles = []
    for c in range(3):
        tiles.append((lambda s, c=c: z_side.lower([f[c, :, s] for f in zfaces]), width))
    for c in range(2):
        tiles.append((lambda s, c=c: z_side.upper([f[c, :, s] for f in zfaces]), width))
    for t in range(0, 2 * cells_z, ROWS):
        tiles.append((lambda s, t=t: x_tile(x_side.lower, t, s), width))
    for j in range(cells_z // ROWS):
        tiles.append((lambda s, j=j: strip(j, s), width))
    for t in range(0, rows, ROWS):
        if lines and t == 2 * cells_z:
            tiles.append((lambda s: corner_lines(lines, s)[1], width))
        else:
            tiles.append((lambda s, t=t: x_tile(x_side.upper, t, s), width))
    return tiles


FREE = 5


def face_slot(index, layers, cells_z):
    grad_base = 6 * cells_z // SLOTS
    if index < FREE:
        slot = 6 * (index + 1) + 5
        return grad_base + slot // SLOTS, slot % SLOTS
    return grad_base + 6 * layers // SLOTS + (index - FREE) // SLOTS, (index - FREE) % SLOTS


def face_count(xface):
    per_field = (xface.shape[0] - ROWS) // ROWS // 2
    return 5 + 3 * per_field + 2 * per_field + 1


def y_faces_kernel(counts, *refs):
    own_low, own_high = refs[:2]
    ends = np.cumsum((2,) + counts)
    zfaces, xfaces, lines = (refs[i:j] for i, j in zip(ends[:-1], ends[1:]))
    sends, (low_ref, high_ref) = refs[3 + sum(counts) : -2], refs[-2:]
    own = own_low.shape[0]
    tiles = face_tiles(zfaces, xfaces, lines)
    pack_strips(tiles[FREE:], low_ref, high_ref, 0)
    side = Side("gy")
    for ref, value in zip(sends, side.sends(own_low[...], own_high[...])):
        ref[0:own] = value
    group = lane_group()
    cells_z = (xfaces[0].shape[0] - ROWS) // 2
    layers = own * SLOTS // 6 - cells_z
    for index, (load, width) in enumerate(tiles[:FREE]):
        tile, k = face_slot(index, layers, cells_z)
        low = pltpu.roll(load(slice(0, LANES)), STRIP * k, 1)
        high = pltpu.roll(load(slice(width - LANES, width)), (STRIP * k + STRIP) % LANES, 1)
        for ref, value in zip(sends, side.sends(low, high)):
            ref[tile] = jnp.where(group == k, value, ref[tile])
    for ref, value in zip(sends, side.sends(low_ref[...], high_ref[...])):
        ref[own:] = value


def y_faces(own_low, own_high, zfaces, xfaces, lines, after):
    extra = math.ceil((face_count(xfaces[0]) - FREE) / SLOTS)
    packed = fast(own_low.shape[0] + extra, ROWS, LANES)
    return pl.pallas_call(
        functools.partial(y_faces_kernel, (len(zfaces), len(xfaces), len(lines))),
        in_specs=[VMEM] * (2 + len(zfaces) + len(xfaces) + len(lines)) + [ANY],
        out_specs=[VMEM] * rounds("gy"),
        out_shape=[packed] * rounds("gy"),
        scratch_shapes=[pltpu.VMEM((extra, ROWS, LANES), jnp.float32)] * 2,
        compiler_params=params(),
    )(own_low, own_high, *zfaces, *xfaces, *lines, after)


OWN, CIRCLE, EDGE = range(3)


def faces_wide(mode, width):
    return {OWN: width, CIRCLE: width + LANES, EDGE: LANES}[mode]


class Fields:
    def __init__(self, mode, layers, fields, zfaces, xfaces, lines, yfaces, scratch):
        self.mode = mode
        self.fields = fields
        if mode == EDGE:
            self.cells_z, self.width = fields.shape[0], xfaces[0].shape[1]
        else:
            self.cells_z, self.width = fields[0].shape[1], fields[0].shape[3]
        self.wide = faces_wide(mode, self.width)
        self.lane = lax.broadcasted_iota(jnp.int32, (ROWS, LANES), 1)
        self.row = lax.broadcasted_iota(jnp.int32, (ROWS, self.wide), 0)
        self.per_group = 6 * ROWS // SLOTS
        self.groups = self.cells_z // ROWS
        self.grad_base = self.per_group * self.groups
        self.left_wide, self.right_wide = left_wide, right_wide = scratch[:2]
        if mode != OWN:
            self.ybuf = scratch[2]
            y_side = Side("gy")
            for t in range(yfaces[0].shape[0]):
                lower = y_side.lower([f[t] for f in yfaces])
                upper = y_side.upper([f[t] for f in yfaces])
                if mode == EDGE:
                    even = self.lane // STRIP % 2 == 0
                    lower, upper = (
                        jnp.where(even, upper, pltpu.roll(lower, STRIP, 1)),
                        jnp.where(even, pltpu.roll(upper, LANES - STRIP, 1), lower),
                    )
                self.ybuf[0, t] = lower
                self.ybuf[1, t] = upper

        def face(load, slot):
            if mode == EDGE:
                own = edge_tile(load, self.width)
                return self.edge(own, *face_slot(slot, layers, self.cells_z))
            return self.wider(load, *face_slot(slot, layers, self.cells_z))

        full = [face(load, slot) for slot, (load, _) in enumerate(face_tiles(zfaces, xfaces, lines))]
        self.below, self.above = full[:3], full[3:5]
        groups = self.groups
        for t in range(2 * groups):
            left_wide[t * ROWS : (t + 1) * ROWS, :] = full[5 + t]
        for t in range(2 * groups + 1):
            right_wide[t * ROWS : (t + 1) * ROWS, :] = full[5 + 3 * groups + t]
        if mode != OWN:
            column = lax.broadcasted_iota(jnp.int32, (ROWS, self.wide), 1)
            ends = {CIRCLE: (self.width - 1, self.wide - 1), EDGE: (STRIP - 1, LANES - STRIP - 1)}[mode]
            here = jnp.logical_or(column == ends[0], column == ends[1])
            for j in range(groups):
                ex_next = self.y_up(full[5 + 2 * groups + j])
                at = (groups + j) * ROWS
                left_wide[at : at + ROWS, :] += jnp.where(here, HALF * ex_next, 0.0)

    def wider(self, load, tile, k):
        if self.mode == OWN:
            return load(slice(0, self.width))

        def moved(v, to):
            shift = (to - STRIP * k) % LANES
            return pltpu.roll(v, shift, 1) if shift else v

        lower, upper = self.ybuf[0, tile], self.ybuf[1, tile]
        halo = jnp.where(self.lane < STRIP, moved(upper, 0), moved(lower, LANES - STRIP))
        return jnp.concatenate([load(slice(0, self.width)), halo], axis=1)

    def edge(self, own, tile, k):
        shift = (LANES - STRIP - 2 * STRIP * (k // 2)) % LANES
        both = pltpu.roll(self.ybuf[k % 2, tile], shift, 1)
        inside = jnp.logical_and(self.lane >= STRIP, self.lane < LANES - STRIP)
        return jnp.where(inside, own, both)

    def y_up(self, v):
        return pltpu.roll(v, self.wide - 1, 1)

    def y_down(self, v):
        return pltpu.roll(v, 1, 1)

    def x_up(self, v, line):
        return jnp.where(self.row == ROWS - 1, line, pltpu.roll(v, ROWS - 1, 0))

    def x_down(self, v, line):
        return jnp.where(self.row == 0, line, pltpu.roll(v, 1, 0))

    def line(self, ref, at):
        return jnp.broadcast_to(ref[pl.ds(at, 1), :], (ROWS, self.wide))

    def field(self, which, c, a, b):
        slot = 6 * b + 3 * which + c
        tile = self.per_group * a + slot // SLOTS
        if self.mode == EDGE:
            return self.edge(self.fields[ROWS * a + b, 3 * which + c], tile, slot % SLOTS)
        ref = self.fields[which]
        return self.wider(lambda s: ref[c, ROWS * a + b, :, s], tile, slot % SLOTS)

    def hx(self, a, b, ey, ez, ey_next):
        return self.field(1, 0, a, b) - HALF * (self.y_up(ez) - ez - ey_next + ey)

    def hy(self, a, b, ex, ez, ex_next):
        up = self.x_up(ez, self.line(self.right_wide, self.cells_z + ROWS * a + b))
        return self.field(1, 1, a, b) - HALF * (ex_next - ex - up + ez)

    def hz(self, a, b, ex, ey):
        up = self.x_up(ey, self.line(self.right_wide, ROWS * a + b))
        return self.field(1, 2, a, b) - HALF * (up - ey - self.y_up(ex) + ex)

    def start(self, a):
        ex, ey = self.field(0, 0, a, 0), self.field(0, 1, a, 0)
        below = self.below
        at_bottom = (
            below[0] - HALF * self.y_up(below[2]) + HALF * ey,
            below[1] - HALF * ex + HALF * self.x_up(below[2], self.line(self.right_wide, 2 * self.cells_z)),
        )
        before, b = jnp.maximum(a - 1, 0), ROWS - 1
        ex_before, ey_before, ez_before = (self.field(0, c, before, b) for c in range(3))
        inside = (
            self.hx(before, b, ey_before, ez_before, ey),
            self.hy(before, b, ex_before, ez_before, ex),
        )
        bottom = a == 0
        return (ex, ey) + tuple(jnp.where(bottom, one, two) for one, two in zip(at_bottom, inside))

    def group(self, a, carry, emit):
        ex, ey, hx_z, hy_z = carry
        for b in range(ROWS):
            z = ROWS * a + b
            ez = self.field(0, 2, a, b)
            if b < ROWS - 1:
                ex_next, ey_next = (self.field(0, c, a, b + 1) for c in range(2))
            else:
                end = a == self.groups - 1
                after = jnp.minimum(a + 1, self.groups - 1)
                ex_next, ey_next = (
                    jnp.where(end, self.above[c], self.field(0, c, after, 0)) for c in range(2)
                )
            hx = self.hx(a, b, ey, ez, ey_next)
            hy = self.hy(a, b, ex, ez, ex_next)
            hz = self.hz(a, b, ex, ey)
            hy_x = self.x_down(hy, self.line(self.left_wide, z) + HALF * ez)
            hz_x = self.x_down(hz, self.line(self.left_wide, self.cells_z + z) - HALF * ey)
            curl = (
                (hz - self.y_down(hz)) - (hy - hy_z),
                (hx - hx_z) - (hz - hz_x),
                (hy - hy_x) - (hx - self.y_down(hx)),
            )
            emit(a, b, (ex, ey, ez), (hx, hy, hz), curl)
            ex, ey, hx_z, hy_z = ex_next, ey_next, hx, hy
        return ex, ey, hx_z, hy_z

    def gradient(self, layers, arrays, store):
        first = first_layer(self.cells_z, layers)
        first_group = first // ROWS
        if self.mode == EDGE:
            grad_edges, mask_ref = arrays
            mask = self.edge(mask_ref[...], self.grad_base, 5)
        else:
            f_ref, inv_ref, grad_ref, mask_ref = arrays
            mask = mask_ref[...]

        def emit(a, b, efield, hfield, curl):
            z = ROWS * a + b
            layer = z - first
            if self.mode == EDGE:
                tile = self.grad_base + self.per_group * (a - first_group)
                slots = [6 * b + n for n in range(5)]
                values = [
                    self.edge(grad_edges[layer, n], tile + slot // SLOTS, slot % SLOTS)
                    for n, slot in enumerate(slots)
                ]
            else:
                values = [f_ref[c, z] for c in range(3)] + [inv_ref[z], grad_ref[layer]]
            total = None
            for c in range(3):
                term = values[c] * (efield[c] + values[3] * curl[c])
                total = term if total is None else total + term
            store(layer, values[4] + mask * total)

        def body(i, carry):
            return self.group(first_group + i, carry, emit)

        lax.fori_loop(0, layers // ROWS, body, self.start(first_group))


def fields_scratch(mode, xface, yface, width):
    rows, wide = xface.shape[0], faces_wide(mode, width)
    out = [pltpu.VMEM((rows, wide), jnp.float32)] * 2
    if mode != OWN:
        out.append(pltpu.VMEM((2,) + yface.shape, jnp.float32))
    return out


def own_gradient_kernel(counts, per_device, *refs):
    e_ref, h_ref, f_ref, inv_ref, grad_ref, mask_ref = refs[:6]
    zfaces, xfaces = refs[6 : 6 + counts[0]], refs[6 + counts[0] : 6 + sum(counts)]
    shares, (own_ref, *scratch) = refs[6 + sum(counts) : -3][::-1], refs[-3:]
    layers, _, width = grad_ref.shape
    fields = Fields(OWN, layers, (e_ref, h_ref), zfaces, xfaces, (), None, scratch)

    def store(layer, value):
        own_ref[layer] = value

    fields.gradient(layers, (f_ref, inv_ref, grad_ref, mask_ref), store)

    me = lax.axis_index("gx")
    for k, share in enumerate(shares):
        chunk = lax.bitwise_xor(me, way_there(len(shares))[k])
        for i in range(per_device):
            share[:, i * width : (i + 1) * width] = own_ref[chunk * per_device + i]
        if share.shape[1] > per_device * width:
            share[:, per_device * width :] = jnp.zeros((ROWS, SPARE), jnp.float32)


SPARE = LANES


def own_gradient(arrays, zfaces, xfaces):
    layers, _, width = arrays[4].shape
    count = lax.axis_size("gx")
    per_device = layers // count
    *shares, own = pl.pallas_call(
        functools.partial(own_gradient_kernel, (len(zfaces), len(xfaces)), per_device),
        in_specs=[VMEM] * (6 + len(zfaces) + len(xfaces)),
        out_specs=[VMEM] * (count + 1),
        out_shape=[fast(ROWS, per_device * width + SPARE)]
        + [fast(ROWS, per_device * width)] * (count - 1)
        + [fast(layers, ROWS, width)],
        scratch_shapes=fields_scratch(OWN, xfaces[0], None, width),
        compiler_params=params(),
    )(*arrays, *zfaces, *xfaces)
    return shares[::-1], own


PART = 2 * STRIP
SPAN = 2 * PART


def edge_gradient_kernel(counts, *refs):
    own_ref, f_ref, inv_ref, wide_ref, eh_ref, grad_ref, mask_ref, taps_ref = refs[:8]
    ends = np.cumsum((8,) + counts)
    zfaces, xfaces, lines, yfaces = (refs[i:j] for i, j in zip(ends[:-1], ends[1:]))
    (shares, message, edge_ref), scratch = refs[ends[-1] : -6], refs[-6:-3]
    folded, parts, slabs = refs[-3:]
    layers, _, width = own_ref.shape
    lane = lax.broadcasted_iota(jnp.int32, (ROWS, LANES), 1)
    first, last = STRIP, LANES - STRIP - 1
    fields = Fields(EDGE, layers, eh_ref, zfaces, xfaces, lines, yfaces, scratch)

    def store(layer, value):
        edge_ref[layer] = value

    fields.gradient(layers, (grad_ref, mask_ref), store)

    count = shares.shape[0]
    half = count // 2
    rows = half * ROWS
    me = lax.axis_index("gx")
    folded[...] = jnp.zeros_like(folded)
    fold = jnp.minimum(me, count - 1 - me)
    per_tile = LANES // SPAN
    for start in range(0, layers, per_tile):
        tile = jnp.zeros((ROWS, LANES), jnp.float32)
        for j in range(min(per_tile, layers - start)):
            edge = edge_ref[start + j]
            own = edge_tile(lambda s: own_ref[start + j, :, s], width)
            more = jnp.where(jnp.logical_or(lane == first, lane == last), edge - own, edge)
            low, high = SPAN * j + 1, SPAN * j + PART + STRIP - 1
            here = jnp.logical_and(lane >= low, lane < low + STRIP)
            tile = jnp.where(here, pltpu.roll(more, (low - 1) % LANES, 1), tile)
            here = jnp.logical_and(lane >= high, lane < high + STRIP)
            tile = jnp.where(here, pltpu.roll(more, (high - last) % LANES, 1), tile)
        tile = jnp.where(me < half, tile, flip_rows(tile))
        folded[fold, :, start // per_tile * LANES : (start // per_tile + 1) * LANES] = tile
    split_rows(jnp.concatenate([folded[s] for s in range(half)], axis=0), parts)
    total = cone(taps_ref, parts, rows)
    lanes = lax.broadcasted_iota(jnp.int32, (rows, LANES), 1)
    per_share = LANES // PART
    for start in range(0, layers, per_share):
        packed = jnp.zeros((rows, LANES), jnp.float32)
        for j in range(min(per_share, layers - start)):
            at = SPAN * (start + j)
            tile = total[:, at // LANES * LANES : (at // LANES + 1) * LANES]
            left = pltpu.roll(tile, (PART * j - STRIP - at) % LANES, 1)
            right = pltpu.roll(tile, (PART * j + STRIP - PART - 1 - at) % LANES, 1)
            packed = jnp.where(lanes // STRIP == 2 * j, left, packed)
            packed = jnp.where(lanes // STRIP == 2 * j + 1, right, packed)
        here = slice(start // per_share * LANES, (start // per_share + 1) * LANES)
        for s in range(half):
            one = packed[s * ROWS : (s + 1) * ROWS]
            slabs[s, :, here] = one
            slabs[count - 1 - s, :, here] = flip_rows(one)
    for k in range(count):
        shares[k] = slabs[lax.bitwise_xor(me, k)]

    message[...] = jnp.zeros_like(message)
    top, last = fields.cells_z - 1, ROWS - 1
    above, beyond = (line[0:1] for line in corner_lines(lines, slice(0, width)))
    added = wide_ref[0:1, :] * f_ref[2, top, 0:1, :] * inv_ref[top, 0:1, :] * (HALF * above)
    added += wide_ref[last:, :] * f_ref[0, 0, last:, :] * inv_ref[0, last:, :] * (HALF * beyond)
    column = lax.broadcasted_iota(jnp.int32, (1, width), 1)
    added = jnp.where(jnp.logical_or(column == 0, column == width - 1), 0.0, added)
    for at, n in line_places(width):
        message[n : n + 1, at : at + LANES] = added[:, (at // LANES * ROWS + n) * LANES :][:, :LANES]


def line_places(width):
    return [(t // ROWS * LANES, t % ROWS) for t in range(width // LANES)]


def line_of(message, width):
    return jnp.concatenate([message[n : n + 1, at : at + LANES] for at, n in line_places(width)], axis=1)


def line_spot(layers):
    bottom = lax.axis_index("gz") == 0
    return jnp.where(bottom, layers - 1, 0), jnp.where(bottom, 0, ROWS - 1)


def edge_gradient(own, arrays, edges, taps, zfaces, xfaces, lines, yfaces):
    layers, _, width = own.shape
    faces = (*zfaces, *xfaces, *lines, *yfaces)
    count = lax.axis_size("gx")
    share = (count, ROWS, math.ceil(layers * PART / LANES) * LANES)
    spread = math.ceil(layers * SPAN / LANES) * LANES
    line = math.ceil(width / LANES / ROWS) * LANES
    return pl.pallas_call(
        functools.partial(edge_gradient_kernel, (len(zfaces), len(xfaces), len(lines), len(yfaces))),
        in_specs=[VMEM] * (8 + len(faces)),
        out_specs=[VMEM] * 3,
        out_shape=[fast(*share), fast(ROWS, line), fast(layers, ROWS, LANES)],
        scratch_shapes=fields_scratch(EDGE, xfaces[0], yfaces[0], width)
        + [
            pltpu.VMEM((count // 2, ROWS, spread), jnp.float32),
            pltpu.VMEM((3 * count // 2 * ROWS, spread), jnp.bfloat16),
            pltpu.VMEM(share, jnp.float32),
        ],
        compiler_params=params(),
    )(own, arrays[2], arrays[3], arrays[5], *edges, taps, *faces)


def step_kernel(counts, *refs):
    e_ref, h_ref, inv_ref, own_ref, edge_ref, message = refs[:6]
    ends = np.cumsum((6,) + counts)
    zfaces, xfaces, lines, yfaces = (refs[i:j] for i, j in zip(ends[:-1], ends[1:]))
    e_out, h_out, grad_out = refs[ends[-1] + 1 : ends[-1] + 4]
    left_wide, right_wide, ybuf, e_new, h_new, grad_new, sems = refs[ends[-1] + 4 :]
    layers, _, width = own_ref.shape
    lane = lax.broadcasted_iota(jnp.int32, (ROWS, LANES), 1)

    for layer in range(layers):
        edge = edge_ref[layer]
        head, tail = own_ref[layer, :, 0:LANES], own_ref[layer, :, width - LANES :]
        grad_new[layer] = own_ref[layer]
        grad_new[layer, :, 0:LANES] = jnp.where(lane == 0, pltpu.roll(edge, LANES - STRIP, 1), head)
        grad_new[layer, :, width - LANES :] = jnp.where(lane == LANES - 1, pltpu.roll(edge, STRIP, 1), tail)
    layer, spot = line_spot(layers)
    row = lax.broadcasted_iota(jnp.int32, (ROWS, width), 0)
    grad_new[layer] += jnp.where(row == spot, line_of(message, width), 0.0)
    grad_copy = pltpu.make_async_copy(grad_new, grad_out, sems.at[0, 0])
    grad_copy.start()

    fields = Fields(CIRCLE, layers, (e_ref, h_ref), zfaces, xfaces, lines, yfaces, (left_wide, right_wide, ybuf))

    def emit(a, b, efield, hfield, curl):
        z = ROWS * a + b
        half_inv = inv_ref[z]
        for c in range(3):
            e_new[c, z] = efield[c][:, :width] + half_inv * curl[c][:, :width]
            h_new[c, z] = hfield[c][:, :width]

    def copies(a):
        here = pl.ds(a * ROWS, ROWS)
        return [
            pltpu.make_async_copy(new.at[c, here], out.at[c, here], sems.at[1 + a, 3 * n + c])
            for n, (new, out) in enumerate(((e_new, e_out), (h_new, h_out)))
            for c in range(3)
        ]

    def body(a, carry):
        carry = fields.group(a, carry, emit)
        for copy in copies(a):
            copy.start()
        return carry

    lax.fori_loop(0, fields.groups, body, fields.start(0))
    for a in range(fields.groups):
        for copy in copies(a):
            copy.wait()
    grad_copy.wait()


def step(efield, hfield, inv, own, edge, message, zfaces, xfaces, lines, yfaces, after):
    _, cells_z, _, width = efield.shape
    groups = (zfaces, xfaces, lines, yfaces)
    counts = tuple(len(group) for group in groups)
    shapes = (efield.shape, hfield.shape, own.shape)
    return pl.pallas_call(
        functools.partial(step_kernel, counts),
        in_specs=[VMEM] * (6 + sum(counts)) + [ANY],
        out_specs=[ANY] * 3,
        out_shape=[f32(*shape) for shape in shapes],
        scratch_shapes=fields_scratch(CIRCLE, xfaces[0], yfaces[0], width)
        + [pltpu.VMEM(shape, jnp.float32) for shape in shapes]
        + [pltpu.SemaphoreType.DMA((1 + cells_z // ROWS, 6))],
        compiler_params=params(),
    )(efield, hfield, inv, own, edge, message, *(one for group in groups for one in group), after)


def cone_taps():
    span = np.arange(-RADIUS, RADIUS + 1, dtype=np.float64)
    return np.maximum(RADIUS - np.sqrt(span[:, None] ** 2 + span[None, :] ** 2), 0.0)


def cone_sum():
    return cone_taps().sum()


def cone_matrix(rows):
    weight = cone_taps() / cone_sum()
    x = np.arange(rows)
    out = np.zeros((RADIUS + 1, rows, rows))
    for b in range(RADIUS + 1):
        for apart in (x[:, None] - x[None, :], 2 * rows - 1 - x[:, None] - x[None, :]):
            near = np.abs(apart) <= RADIUS
            out[b] += np.where(near, weight[np.clip(apart, -RADIUS, RADIUS) + RADIUS, RADIUS + b], 0.0)
    out = out.reshape((RADIUS + 1) * rows, rows).astype(np.float32)
    high = out.astype(jnp.bfloat16)
    low = (out - high.astype(np.float32)).astype(jnp.bfloat16)
    return np.concatenate([high, low, high], axis=1)


def flip_rows(v):
    row = lax.broadcasted_iota(jnp.int32, v.shape, 0)
    v = pltpu.roll(v, 4, 0)
    v = jnp.where(row % 4 < 2, pltpu.roll(v, ROWS - 2, 0), pltpu.roll(v, 2, 0))
    return jnp.where(row % 2 < 1, pltpu.roll(v, ROWS - 1, 0), pltpu.roll(v, 1, 0))


def split_rows(symmetric, parts):
    rows = symmetric.shape[0]
    high = symmetric.astype(jnp.bfloat16)
    low = (symmetric - high.astype(jnp.float32)).astype(jnp.bfloat16)
    parts[0:rows, :] = high
    parts[rows : 2 * rows, :] = high
    parts[2 * rows : 3 * rows, :] = low


def cone(taps_ref, parts, rows):
    wide = parts.shape[1]
    mixed = jnp.dot(taps_ref[...], parts[...], preferred_element_type=jnp.float32)
    total = mixed[0:rows]
    for b in range(1, RADIUS + 1):
        part = mixed[b * rows : (b + 1) * rows]
        total = total + (pltpu.roll(part, b, 1) + pltpu.roll(part, wide - b, 1))
    return total


def filter_kernel(count, per_device, width, *refs):
    taps_ref, edges_ref, line_ref = refs[:3]
    got = refs[count + 2 : 2 : -1]
    outs = refs[3 + count : 3 + 2 * count]
    slabs, parts, done = refs[3 + 2 * count :]
    me = lax.axis_index("gx")
    half = count // 2
    rows = half * ROWS
    for k in range(count):
        slabs[lax.bitwise_xor(me, way_there(count)[k])] = got[k][:, : per_device * width]

    side = jnp.zeros((rows, LANES), jnp.float32)
    for i in range(per_device):
        here = slice(i * width, (i + 1) * width)
        halves = [slabs[s, :, here] + flip_rows(slabs[count - 1 - s, :, here]) for s in range(half)]
        split_rows(jnp.concatenate([jnp.concatenate(halves, axis=0), side], axis=1), parts)
        total = cone(taps_ref, parts, rows)
        for s in range(half):
            own = total[s * ROWS : (s + 1) * ROWS, :width]
            done[s, :, here] = own
            done[count - 1 - s, :, here] = flip_rows(own)
    for k, apart in enumerate(way_back(count)):
        outs[k][:, : per_device * width] = done[lax.bitwise_xor(me, apart)]
        tail = per_device * width + edges_ref.shape[2]
        outs[k][:, per_device * width : tail] = edges_ref[apart]
        outs[k][:, tail:] = line_ref[...]


def cone_filter(taps, edges, line, got, per_device, width):
    count = len(got)
    rows = count // 2 * ROWS
    return pl.pallas_call(
        functools.partial(filter_kernel, count, per_device, width),
        in_specs=[VMEM] * (3 + count),
        out_specs=[VMEM] * count,
        out_shape=[fast(ROWS, per_device * width + edges.shape[2] + line.shape[1])] * count,
        scratch_shapes=[
            pltpu.VMEM((count, ROWS, per_device * width), jnp.float32),
            pltpu.VMEM((3 * rows, width + LANES), jnp.bfloat16),
            pltpu.VMEM((count, ROWS, per_device * width), jnp.float32),
        ],
        compiler_params=params(),
    )(taps, edges, line, *got[::-1])


def cone_weight(along_x, along_y):
    near = jnp.maximum(RADIUS - jnp.sqrt(along_x * along_x + float(along_y * along_y)), 0.0)
    return near * float(1.0 / cone_sum())


def finish_kernel(count, per_device, width, *refs):
    got = refs[count - 1 :: -1]
    out, (left, right, done, sems) = refs[count], refs[count + 1 :]
    me = lax.axis_index("gx")
    layers = count * per_device
    lane = lax.broadcasted_iota(jnp.int32, (ROWS, LANES), 1)
    edges_at = per_device * width
    line_at = edges_at + math.ceil(layers * PART / LANES) * LANES

    per_tile = LANES // PART
    for start in range(0, layers, per_tile):
        at = edges_at + start * PART
        tile = got[0][:, at : at + LANES]
        for k in range(1, count):
            tile = tile + got[k][:, at : at + LANES]
        for j in range(min(per_tile, layers - start)):
            head = pltpu.roll(tile, (-PART * j) % LANES, 1)
            left[start + j] = jnp.where(lane < STRIP - 1, head, 0.0)
            tail = pltpu.roll(tile, (LANES + 1 - 2 * STRIP - PART * j) % LANES, 1)
            right[start + j] = jnp.where(lane > LANES - STRIP, tail, 0.0)

    line_layer, spot = line_spot(layers)
    end = count * ROWS - 1
    row = lax.broadcasted_iota(jnp.int32, (ROWS, LANES), 0) + me * ROWS
    lines, near, far = [], [], []
    for k, apart in enumerate(way_back(count)):
        lines.append(line_of(got[k][:, line_at:], width))
        where = lax.bitwise_xor(me, apart) * ROWS + spot
        near.append((row - where).astype(jnp.float32))
        far.append((row - (end - where)).astype(jnp.float32))
    total = None
    for b in range(RADIUS + 1):
        mixed = jnp.zeros((ROWS, width), jnp.float32)
        for k in range(count):
            weight = cone_weight(near[k], b) + cone_weight(far[k], b)
            mixed = mixed + jnp.concatenate([weight] * (width // LANES), axis=1) * lines[k]
        mixed = jnp.concatenate([mixed, jnp.zeros((ROWS, LANES), jnp.float32)], axis=1)
        if b:
            mixed = pltpu.roll(mixed, b, 1) + pltpu.roll(mixed, width + LANES - b, 1)
        total = mixed if total is None else total + mixed
    line = total[:, :width]

    copies = []
    for k, apart in enumerate(way_back(count)):
        first = lax.bitwise_xor(me, apart) * per_device
        for i in range(per_device):
            at = i * width
            done[k, i] = got[k][:, at : at + width] + jnp.where(first + i == line_layer, line, 0.0)
            done[k, i, :, :LANES] += left[first + i]
            done[k, i, :, width - LANES :] += right[first + i]
        copies.append(pltpu.make_async_copy(done.at[k], out.at[pl.ds(first, per_device)], sems.at[k]))
        copies[-1].start()
    for copy in copies:
        copy.wait()


def finish(parts, layers, width):
    count = len(parts)
    per_device = layers // count
    return pl.pallas_call(
        functools.partial(finish_kernel, count, per_device, width),
        in_specs=[VMEM] * count,
        out_specs=ANY,
        out_shape=f32(layers, ROWS, width),
        scratch_shapes=[
            pltpu.VMEM((layers, ROWS, LANES), jnp.float32),
            pltpu.VMEM((layers, ROWS, LANES), jnp.float32),
            pltpu.VMEM((count, per_device, ROWS, width), jnp.float32),
            pltpu.SemaphoreType.DMA((count,)),
        ],
        compiler_params=params(),
    )(*parts[::-1])


def spread(parts, order):
    count = len(parts)
    got = list(parts)
    for j in range(count - 1, 0, -1):
        got[j] = lax.ppermute(parts[j], "gx", [(i, i ^ order[j]) for i in range(count)])
    return got


def way_there(count):
    return list(range(count))


def way_back(count):
    if count < 4:
        return list(range(count))
    return [0] + list(range(2, count - 1)) + [1, count - 1]


def on_device(efield, hfield, forward, material, permit, design_mask, grad_sum):
    layers, _, width = grad_sum.shape
    efield, hfield, zfaces, xfaces, lines = halos(efield, hfield)
    own_low, own_high, mask, inv = strips(
        permit, efield, hfield, forward, material, grad_sum, design_mask
    )
    arrays = (efield, hfield, forward, inv, grad_sum, mask)
    edges = own_edges(arrays)
    shares, own = own_gradient(arrays, zfaces, xfaces)
    got = spread(shares, way_there(len(shares)))
    yfaces = exchange(y_faces(own_low, own_high, zfaces, xfaces, lines, own), "gy", "gz")
    taps = jnp.asarray(cone_matrix(len(got) // 2 * ROWS))
    added, line, edge = edge_gradient(own, arrays, edges, taps, zfaces, xfaces, lines, yfaces)
    parts = cone_filter(taps, added, line, got, layers // len(got), width)
    e_next, h_next, grad_total = step(
        efield, hfield, inv, own, edge, line, zfaces, xfaces, lines, yfaces, parts[0]
    )
    return e_next, h_next, grad_total, finish(spread(parts, way_back(len(parts))), layers, width)


def solution(mesh):
    field = P(None, "gz", "gx", "gy")
    cells = P("gz", "gx", "gy")
    return jax.shard_map(
        on_device,
        mesh=mesh,
        in_specs=(field, field, field, cells, P(), P("gx", "gy"), cells),
        out_specs=(field, field, cells, cells),
        check_vma=False,
    )
```

```python
import functools
import math

import jax
import jax.numpy as jnp
import numpy as np
from jax import lax
from jax.experimental import pallas as pl
from jax.experimental.pallas import tpu as pltpu
from jax.sharding import PartitionSpec as P

RADIUS = 6
BLOCK = 8
HALF = 0.5

ROWS = 8
LANES = 128
STRIP = 8
SLOTS = LANES // STRIP
MIB = 1024 * 1024

VMEM = pl.BlockSpec(memory_space=pltpu.VMEM)
SMEM = pl.BlockSpec(memory_space=pltpu.SMEM)
ANY = pl.BlockSpec(memory_space=pl.ANY)


def params(mib=24):
    return pltpu.CompilerParams(vmem_limit_bytes=mib * MIB)


def f32(*shape):
    return jax.ShapeDtypeStruct(shape, jnp.float32)


def fast(*shape):
    return pltpu.VMEM(shape, jnp.float32)


def rounds(axis):
    return 2 if lax.axis_size(axis) > 2 else 1


def exchange(sends, axis, mate):
    count = lax.axis_size(axis)
    beside = lax.axis_size(mate)
    if count == 1:
        return sends
    got = []
    for start, value in enumerate(sends):
        partner = list(range(count))
        for low in range(start, count - 1, 2):
            partner[low], partner[low + 1] = low + 1, low
        axes = sorted((axis, mate))
        steps = (beside, 1) if axes[0] == axis else (1, count)
        pairs = []
        for i in range(count):
            for m in range(beside):
                if partner[i] != i:
                    to = (partner[i], m)
                elif beside % 2 == 0:
                    to = (i, m ^ 1)
                else:
                    continue
                pairs.append((i * steps[0] + m * steps[1], to[0] * steps[0] + to[1] * steps[1]))
        got.append(lax.ppermute(value, tuple(axes), pairs))
    return got


def exchange_diagonal(sends):
    along_x, along_y, along_z = (lax.axis_size(axis) for axis in AXES)

    def flat(x, y, z):
        return (x * along_y + y) * along_z + z

    got = []
    for start, value in enumerate(sends):
        partner = {}
        for low in range(start, along_z - 1, 2):
            for x in range(1, along_x):
                partner[x, low] = (x - 1, low + 1)
                partner[x - 1, low + 1] = (x, low)
        pairs = []
        for x in range(along_x):
            for z in range(along_z):
                for y in range(along_y):
                    if (x, z) in partner:
                        to = partner[x, z]
                        pairs.append((flat(x, y, z), flat(to[0], y, to[1])))
                    elif along_y % 2 == 0:
                        pairs.append((flat(x, y, z), flat(x, y ^ 1, z)))
        got.append(lax.ppermute(value, AXES, pairs))
    return got


AXES = ("gx", "gy", "gz")


class Side:
    def __init__(self, axis):
        index = lax.axis_index(axis)
        self.rounds = rounds(axis)
        self.odd = index % 2 == 1
        self.bottom = index == 0
        self.top = index == lax.axis_size(axis) - 1

    def sends(self, low, high):
        both = [jnp.where(self.odd, low, high)]
        if self.rounds > 1:
            both.append(jnp.where(self.odd, high, low))
        return both

    def lower(self, got):
        return jnp.where(self.bottom, 0.0, jnp.where(self.odd, got[0], got[-1]))

    def upper(self, got):
        return jnp.where(self.top, 0.0, jnp.where(self.odd, got[-1], got[0]))


def first_layer(cells_z, layers):
    return (cells_z - layers) * (1 - lax.axis_index("gz"))


def faces_kernel(x_rounds, e_in, h_in, e_ref, h_ref, *refs):
    x_sends, (low_ref, rows_ref, sems) = refs[:x_rounds], refs[-3:]
    others = refs[x_rounds:-3]
    z_sends, d_sends = others[: len(others) // 2], others[len(others) // 2 :]
    cells_z = e_ref.shape[1]
    last, top = ROWS - 1, cells_z - 1
    copies = [
        [pltpu.make_async_copy(source.at[c], target.at[c], sems.at[n, c]) for c in range(3)]
        for n, (source, target) in enumerate(((e_in, e_ref), (h_in, h_ref)))
    ]
    for copy in copies[0][1:] + copies[0][:1] + copies[1][1:] + copies[1][:1]:
        copy.start()

    low_ref[2 * cells_z :, :] = jnp.zeros_like(low_ref[2 * cells_z :, :])
    rows_ref[5, top : top + 1, :] = jnp.zeros_like(rows_ref[5, top : top + 1, :])
    for copy in copies[0][1:]:
        copy.wait()
    for z in range(cells_z):
        low_ref[z : z + 1, :] = e_ref[1, z, 0:1, :]
        low_ref[cells_z + z : cells_z + z + 1, :] = e_ref[2, z, 0:1, :]
        for c in range(1, 3):
            rows_ref[c, z : z + 1, :] = e_ref[c, z, last : last + 1, :]
    copies[0][0].wait()
    for z in range(cells_z):
        rows_ref[0, z : z + 1, :] = e_ref[0, z, last : last + 1, :]
        if z > 0:
            rows_ref[5, z - 1 : z, :] = e_ref[0, z, last : last + 1, :]
    for copy in copies[1][1:]:
        copy.wait()
    for z in range(cells_z):
        for c in range(2):
            rows_ref[3 + c, z : z + 1, :] = h_ref[1 + c, z, last : last + 1, :]
    width = e_ref.shape[3]
    ex, ey, ez = (rows_ref[c] for c in range(3))
    column = lax.broadcasted_iota(jnp.int32, ex.shape, 1)
    ex_next = jnp.where(column == width - 1, 0.0, pltpu.roll(ex, width - 1, 1))
    lane = lax.broadcasted_iota(jnp.int32, (ROWS, LANES), 1)
    strip = jnp.zeros((ROWS, LANES), jnp.float32)
    for j in range(cells_z // ROWS):
        head = rows_ref[0, j * ROWS : (j + 1) * ROWS, 0:LANES]
        strip = jnp.where(lane // STRIP == j, pltpu.roll(head, STRIP * j, 1) if j else head, strip)
    high = (
        rows_ref[3] - HALF * (rows_ref[5] - ex + ez),
        rows_ref[4] + HALF * ey - HALF * (ex - ex_next),
        jnp.concatenate([strip, jnp.zeros((ROWS, width - LANES), jnp.float32)], axis=1),
    )
    side = Side("gx")
    for c, value in enumerate(high):
        here = slice(c * cells_z, c * cells_z + value.shape[0])
        for ref, one in zip(x_sends, side.sends(low_ref[here, :], value)):
            ref[here, :] = one

    copies[1][0].wait()
    side = Side("gz")
    ex, ey, ez = (e_ref[c, top] for c in range(3))
    low = (e_ref[0, 0], e_ref[1, 0], jnp.zeros_like(ez))
    high = (h_ref[0, top] + HALF * ez - HALF * ey, h_ref[1, top] + HALF * ex - HALF * ez, ez)
    for c in range(3):
        for ref, value in zip(z_sends, side.sends(low[c], high[c])):
            ref[c] = value

    down, up = (
        jnp.broadcast_to(line, (ROWS, line.shape[1]))
        for line in (e_ref[0, 0, last : last + 1, :], e_ref[2, top, 0:1, :])
    )
    for ref, value in zip(d_sends, side.sends(down, up)):
        ref[...] = value


def halos(efield, hfield):
    _, cells_z, cells_x, cells_y = efield.shape
    x_rounds, z_rounds = rounds("gx"), rounds("gz")
    x_face, z_face, line = fast(2 * cells_z + ROWS, cells_y), fast(3, cells_x, cells_y), fast(ROWS, cells_y)
    fields = [fast(*field.shape) for field in (efield, hfield)]
    efield, hfield, *sends = pl.pallas_call(
        functools.partial(faces_kernel, x_rounds),
        in_specs=[ANY] * 2,
        out_specs=[VMEM] * (2 + x_rounds + 2 * z_rounds),
        out_shape=fields + [x_face] * x_rounds + [z_face] * z_rounds + [line] * z_rounds,
        scratch_shapes=[
            pltpu.VMEM(x_face.shape, jnp.float32),
            pltpu.VMEM((6, cells_z, cells_y), jnp.float32),
            pltpu.SemaphoreType.DMA((2, 3)),
        ],
        compiler_params=params(54),
    )(efield, hfield)
    xfaces = exchange(sends[:x_rounds], "gx", "gy")
    zfaces = exchange(sends[x_rounds : x_rounds + z_rounds], "gz", "gy")
    return efield, hfield, zfaces, xfaces, exchange_diagonal(sends[x_rounds + z_rounds :])


def lane_group():
    return lax.broadcasted_iota(jnp.int32, (ROWS, LANES), 1) // STRIP


def pack_strips(tiles, low_ref, high_ref, first):
    group = lane_group()
    width = tiles[0][1]
    for start in range(0, len(tiles), SLOTS):
        low = jnp.zeros((ROWS, LANES), jnp.float32)
        high = jnp.zeros((ROWS, LANES), jnp.float32)
        for k, (load, _) in enumerate(tiles[start : start + SLOTS]):
            if load is None:
                continue
            here = group == k
            shift = (STRIP * k) % LANES
            left = load(slice(0, LANES))
            right = load(slice(width - LANES, width))
            low = jnp.where(here, pltpu.roll(left, shift, 1) if shift else left, low)
            shift = (STRIP * k + STRIP) % LANES
            high = jnp.where(here, pltpu.roll(right, shift, 1) if shift else right, high)
        low_ref[first + start // SLOTS] = low
        high_ref[first + start // SLOTS] = high


def strips_kernel(
    permit_ref, e_ref, h_ref, f_ref, mat_ref, grad_ref, mask_ref, low_ref, high_ref, wide_ref, inv_ref
):
    cells_z, width = e_ref.shape[1], e_ref.shape[3]
    layers = grad_ref.shape[0]
    blocks = mask_ref.shape[1]
    inverse = [
        jnp.broadcast_to(HALF * (1.0 / permit_ref[0:1, m : m + 1]), (ROWS, width))
        for m in range(permit_ref.shape[1])
    ]
    for z in range(cells_z):
        inv = inverse[0]
        for m in range(1, len(inverse)):
            inv = jnp.where(mat_ref[z] == m, inverse[m], inv)
        inv_ref[z] = inv
    spread = (
        lax.broadcasted_iota(jnp.int32, (blocks, width), 0)
        == lax.broadcasted_iota(jnp.int32, (blocks, width), 1) // BLOCK
    ).astype(jnp.float32)
    mask = jnp.broadcast_to(mask_ref[...].astype(jnp.float32), (ROWS, blocks))
    wide_ref[...] = jnp.dot(mask, spread, preferred_element_type=jnp.float32)
    first = first_layer(cells_z, layers)
    tiles = []
    for z in range(cells_z):
        for ref in (e_ref, h_ref):
            for c in range(3):
                tiles.append((lambda s, r=ref, c=c, z=z: r[c, z, :, s], width))
    pack_strips(tiles, low_ref, high_ref, 0)

    done = len(tiles) // SLOTS
    tiles = []
    for layer in range(layers):
        for c in range(3):
            tiles.append((lambda s, c=c, l=layer: f_ref[c, first + l, :, s], width))
        tiles.append((lambda s, l=layer: inv_ref[first + l, :, s], width))
        tiles.append((lambda s, l=layer: grad_ref[l, :, s], width))
        tiles.append((lambda s: wide_ref[:, s], width) if layer % ROWS == 0 else (None, width))
    pack_strips(tiles, low_ref, high_ref, done)


def strips(permit, efield, hfield, forward, material, grad_sum, mask):
    cells_z, width = efield.shape[1], efield.shape[3]
    count = (cells_z * 6 + grad_sum.shape[0] * 6) // SLOTS
    packed = (count, ROWS, LANES)
    shapes = (packed, packed, (ROWS, width), material.shape)
    return pl.pallas_call(
        strips_kernel,
        in_specs=[VMEM] * 7,
        out_specs=[VMEM] * 4,
        out_shape=[fast(*shape) for shape in shapes],
        compiler_params=params(),
    )(permit.reshape(1, -1), efield, hfield, forward, material, grad_sum, mask)


def edge_tile(load, width):
    lane = lax.broadcasted_iota(jnp.int32, (ROWS, LANES), 1)
    head = pltpu.roll(load(slice(0, LANES)), STRIP, 1)
    tail = pltpu.roll(load(slice(width - LANES, width)), LANES - STRIP, 1)
    return jnp.where(lane < LANES // 2, head, tail)


def edges_kernel(e_ref, h_ref, f_ref, inv_ref, grad_ref, mask_ref, eh_out, grad_out, mask_out):
    cells_z, width = e_ref.shape[1], e_ref.shape[3]
    layers = grad_ref.shape[0]
    first = first_layer(cells_z, layers)
    for z in range(cells_z):
        for c in range(3):
            eh_out[z, c] = edge_tile(lambda s: e_ref[c, z, :, s], width)
            eh_out[z, 3 + c] = edge_tile(lambda s: h_ref[c, z, :, s], width)
    for layer in range(layers):
        for c in range(3):
            grad_out[layer, c] = edge_tile(lambda s: f_ref[c, first + layer, :, s], width)
        grad_out[layer, 3] = edge_tile(lambda s: inv_ref[first + layer, :, s], width)
        grad_out[layer, 4] = edge_tile(lambda s: grad_ref[layer, :, s], width)
    mask_out[...] = edge_tile(lambda s: mask_ref[:, s], width)


def own_edges(arrays):
    cells_z, layers = arrays[0].shape[1], arrays[4].shape[0]
    return pl.pallas_call(
        edges_kernel,
        in_specs=[VMEM] * 6,
        out_specs=[VMEM] * 3,
        out_shape=[fast(cells_z, 6, ROWS, LANES), fast(layers, 5, ROWS, LANES), fast(ROWS, LANES)],
        compiler_params=params(),
    )(*arrays)


def corner_lines(lines, s):
    z_side, x_side = Side("gz"), Side("gx")
    above = jnp.where(x_side.bottom, 0.0, z_side.upper([f[:, s] for f in lines]))
    beyond = jnp.where(x_side.top, 0.0, z_side.lower([f[:, s] for f in lines]))
    return above, beyond


def face_tiles(zfaces, xfaces, lines):
    width = xfaces[0].shape[1]
    rows = xfaces[0].shape[0]
    cells_z = (rows - ROWS) // 2
    z_side, x_side = Side("gz"), Side("gx")

    def corner(s):
        row = lax.broadcasted_iota(jnp.int32, (ROWS, s.stop - s.start), 0)
        return jnp.where(row == ROWS - 1, -HALF * corner_lines(lines, s)[0], 0.0)

    def x_tile(pick, t, s):
        value = pick([f[t : t + ROWS, s] for f in xfaces])
        return value + corner(s) if lines and t == cells_z - ROWS and pick == x_side.lower else value

    def strip(j, s):
        zeros = jnp.zeros((ROWS, s.stop - s.start), jnp.float32)
        if s.start:
            return zeros
        lane = lax.broadcasted_iota(jnp.int32, (ROWS, LANES), 1)
        packed = x_side.lower([f[2 * cells_z :, 0:LANES] for f in xfaces])
        head = jnp.where(lane < STRIP, pltpu.roll(packed, LANES - STRIP * j, 1) if j else packed, 0.0)
        return head if s.stop == LANES else jnp.concatenate([head, zeros[:, LANES:]], axis=1)

    tiles = []
    for c in range(3):
        tiles.append((lambda s, c=c: z_side.lower([f[c, :, s] for f in zfaces]), width))
    for c in range(2):
        tiles.append((lambda s, c=c: z_side.upper([f[c, :, s] for f in zfaces]), width))
    for t in range(0, 2 * cells_z, ROWS):
        tiles.append((lambda s, t=t: x_tile(x_side.lower, t, s), width))
    for j in range(cells_z // ROWS):
        tiles.append((lambda s, j=j: strip(j, s), width))
    for t in range(0, rows, ROWS):
        if lines and t == 2 * cells_z:
            tiles.append((lambda s: corner_lines(lines, s)[1], width))
        else:
            tiles.append((lambda s, t=t: x_tile(x_side.upper, t, s), width))
    return tiles


FREE = 5


def face_slot(index, layers, cells_z):
    grad_base = 6 * cells_z // SLOTS
    if index < FREE:
        slot = 6 * (index + 1) + 5
        return grad_base + slot // SLOTS, slot % SLOTS
    return grad_base + 6 * layers // SLOTS + (index - FREE) // SLOTS, (index - FREE) % SLOTS


def face_count(xface):
    per_field = (xface.shape[0] - ROWS) // ROWS // 2
    return 5 + 3 * per_field + 2 * per_field + 1


def y_faces_kernel(counts, *refs):
    own_low, own_high = refs[:2]
    ends = np.cumsum((2,) + counts)
    zfaces, xfaces, lines = (refs[i:j] for i, j in zip(ends[:-1], ends[1:]))
    sends, (low_ref, high_ref) = refs[3 + sum(counts) : -2], refs[-2:]
    own = own_low.shape[0]
    tiles = face_tiles(zfaces, xfaces, lines)
    pack_strips(tiles[FREE:], low_ref, high_ref, 0)
    side = Side("gy")
    for ref, value in zip(sends, side.sends(own_low[...], own_high[...])):
        ref[0:own] = value
    group = lane_group()
    cells_z = (xfaces[0].shape[0] - ROWS) // 2
    layers = own * SLOTS // 6 - cells_z
    for index, (load, width) in enumerate(tiles[:FREE]):
        tile, k = face_slot(index, layers, cells_z)
        low = pltpu.roll(load(slice(0, LANES)), STRIP * k, 1)
        high = pltpu.roll(load(slice(width - LANES, width)), (STRIP * k + STRIP) % LANES, 1)
        for ref, value in zip(sends, side.sends(low, high)):
            ref[tile] = jnp.where(group == k, value, ref[tile])
    for ref, value in zip(sends, side.sends(low_ref[...], high_ref[...])):
        ref[own:] = value


def y_faces(own_low, own_high, zfaces, xfaces, lines, after):
    extra = math.ceil((face_count(xfaces[0]) - FREE) / SLOTS)
    packed = fast(own_low.shape[0] + extra, ROWS, LANES)
    return pl.pallas_call(
        functools.partial(y_faces_kernel, (len(zfaces), len(xfaces), len(lines))),
        in_specs=[VMEM] * (2 + len(zfaces) + len(xfaces) + len(lines)) + [ANY],
        out_specs=[VMEM] * rounds("gy"),
        out_shape=[packed] * rounds("gy"),
        scratch_shapes=[pltpu.VMEM((extra, ROWS, LANES), jnp.float32)] * 2,
        compiler_params=params(),
    )(own_low, own_high, *zfaces, *xfaces, *lines, after)


OWN, CIRCLE, EDGE = range(3)


def faces_wide(mode, width):
    return {OWN: width, CIRCLE: width + LANES, EDGE: LANES}[mode]


class Fields:
    def __init__(self, mode, layers, fields, zfaces, xfaces, lines, yfaces, scratch):
        self.mode = mode
        self.fields = fields
        if mode == EDGE:
            self.cells_z, self.width = fields.shape[0], xfaces[0].shape[1]
        else:
            self.cells_z, self.width = fields[0].shape[1], fields[0].shape[3]
        self.wide = faces_wide(mode, self.width)
        self.lane = lax.broadcasted_iota(jnp.int32, (ROWS, LANES), 1)
        self.row = lax.broadcasted_iota(jnp.int32, (ROWS, self.wide), 0)
        self.per_group = 6 * ROWS // SLOTS
        self.groups = self.cells_z // ROWS
        self.grad_base = self.per_group * self.groups
        self.left_wide, self.right_wide = left_wide, right_wide = scratch[:2]
        if mode != OWN:
            self.ybuf = scratch[2]
            y_side = Side("gy")
            for t in range(yfaces[0].shape[0]):
                lower = y_side.lower([f[t] for f in yfaces])
                upper = y_side.upper([f[t] for f in yfaces])
                if mode == EDGE:
                    even = self.lane // STRIP % 2 == 0
                    lower, upper = (
                        jnp.where(even, upper, pltpu.roll(lower, STRIP, 1)),
                        jnp.where(even, pltpu.roll(upper, LANES - STRIP, 1), lower),
                    )
                self.ybuf[0, t] = lower
                self.ybuf[1, t] = upper

        def face(load, slot):
            if mode == EDGE:
                own = edge_tile(load, self.width)
                return self.edge(own, *face_slot(slot, layers, self.cells_z))
            return self.wider(load, *face_slot(slot, layers, self.cells_z))

        full = [face(load, slot) for slot, (load, _) in enumerate(face_tiles(zfaces, xfaces, lines))]
        self.below, self.above = full[:3], full[3:5]
        groups = self.groups
        for t in range(2 * groups):
            left_wide[t * ROWS : (t + 1) * ROWS, :] = full[5 + t]
        for t in range(2 * groups + 1):
            right_wide[t * ROWS : (t + 1) * ROWS, :] = full[5 + 3 * groups + t]
        if mode != OWN:
            column = lax.broadcasted_iota(jnp.int32, (ROWS, self.wide), 1)
            ends = {CIRCLE: (self.width - 1, self.wide - 1), EDGE: (STRIP - 1, LANES - STRIP - 1)}[mode]
            here = jnp.logical_or(column == ends[0], column == ends[1])
            for j in range(groups):
                ex_next = self.y_up(full[5 + 2 * groups + j])
                at = (groups + j) * ROWS
                left_wide[at : at + ROWS, :] += jnp.where(here, HALF * ex_next, 0.0)

    def wider(self, load, tile, k):
        if self.mode == OWN:
            return load(slice(0, self.width))

        def moved(v, to):
            shift = (to - STRIP * k) % LANES
            return pltpu.roll(v, shift, 1) if shift else v

        lower, upper = self.ybuf[0, tile], self.ybuf[1, tile]
        halo = jnp.where(self.lane < STRIP, moved(upper, 0), moved(lower, LANES - STRIP))
        return jnp.concatenate([load(slice(0, self.width)), halo], axis=1)

    def edge(self, own, tile, k):
        shift = (LANES - STRIP - 2 * STRIP * (k // 2)) % LANES
        both = pltpu.roll(self.ybuf[k % 2, tile], shift, 1)
        inside = jnp.logical_and(self.lane >= STRIP, self.lane < LANES - STRIP)
        return jnp.where(inside, own, both)

    def y_up(self, v):
        return pltpu.roll(v, self.wide - 1, 1)

    def y_down(self, v):
        return pltpu.roll(v, 1, 1)

    def x_up(self, v, line):
        return jnp.where(self.row == ROWS - 1, line, pltpu.roll(v, ROWS - 1, 0))

    def x_down(self, v, line):
        return jnp.where(self.row == 0, line, pltpu.roll(v, 1, 0))

    def line(self, ref, at):
        return jnp.broadcast_to(ref[pl.ds(at, 1), :], (ROWS, self.wide))

    def field(self, which, c, a, b):
        slot = 6 * b + 3 * which + c
        tile = self.per_group * a + slot // SLOTS
        if self.mode == EDGE:
            return self.edge(self.fields[ROWS * a + b, 3 * which + c], tile, slot % SLOTS)
        ref = self.fields[which]
        return self.wider(lambda s: ref[c, ROWS * a + b, :, s], tile, slot % SLOTS)

    def hx(self, a, b, ey, ez, ey_next):
        return self.field(1, 0, a, b) - HALF * (self.y_up(ez) - ez - ey_next + ey)

    def hy(self, a, b, ex, ez, ex_next):
        up = self.x_up(ez, self.line(self.right_wide, self.cells_z + ROWS * a + b))
        return self.field(1, 1, a, b) - HALF * (ex_next - ex - up + ez)

    def hz(self, a, b, ex, ey):
        up = self.x_up(ey, self.line(self.right_wide, ROWS * a + b))
        return self.field(1, 2, a, b) - HALF * (up - ey - self.y_up(ex) + ex)

    def start(self, a):
        ex, ey = self.field(0, 0, a, 0), self.field(0, 1, a, 0)
        below = self.below
        at_bottom = (
            below[0] - HALF * self.y_up(below[2]) + HALF * ey,
            below[1] - HALF * ex + HALF * self.x_up(below[2], self.line(self.right_wide, 2 * self.cells_z)),
        )
        before, b = jnp.maximum(a - 1, 0), ROWS - 1
        ex_before, ey_before, ez_before = (self.field(0, c, before, b) for c in range(3))
        inside = (
            self.hx(before, b, ey_before, ez_before, ey),
            self.hy(before, b, ex_before, ez_before, ex),
        )
        bottom = a == 0
        return (ex, ey) + tuple(jnp.where(bottom, one, two) for one, two in zip(at_bottom, inside))

    def group(self, a, carry, emit):
        ex, ey, hx_z, hy_z = carry
        for b in range(ROWS):
            z = ROWS * a + b
            ez = self.field(0, 2, a, b)
            if b < ROWS - 1:
                ex_next, ey_next = (self.field(0, c, a, b + 1) for c in range(2))
            else:
                end = a == self.groups - 1
                after = jnp.minimum(a + 1, self.groups - 1)
                ex_next, ey_next = (
                    jnp.where(end, self.above[c], self.field(0, c, after, 0)) for c in range(2)
                )
            hx = self.hx(a, b, ey, ez, ey_next)
            hy = self.hy(a, b, ex, ez, ex_next)
            hz = self.hz(a, b, ex, ey)
            hy_x = self.x_down(hy, self.line(self.left_wide, z) + HALF * ez)
            hz_x = self.x_down(hz, self.line(self.left_wide, self.cells_z + z) - HALF * ey)
            curl = (
                (hz - self.y_down(hz)) - (hy - hy_z),
                (hx - hx_z) - (hz - hz_x),
                (hy - hy_x) - (hx - self.y_down(hx)),
            )
            emit(a, b, (ex, ey, ez), (hx, hy, hz), curl)
            ex, ey, hx_z, hy_z = ex_next, ey_next, hx, hy
        return ex, ey, hx_z, hy_z

    def gradient(self, layers, arrays, store):
        first = first_layer(self.cells_z, layers)
        first_group = first // ROWS
        if self.mode == EDGE:
            grad_edges, mask_ref = arrays
            mask = self.edge(mask_ref[...], self.grad_base, 5)
        else:
            f_ref, inv_ref, grad_ref, mask_ref = arrays
            mask = mask_ref[...]

        def emit(a, b, efield, hfield, curl):
            z = ROWS * a + b
            layer = z - first
            if self.mode == EDGE:
                tile = self.grad_base + self.per_group * (a - first_group)
                slots = [6 * b + n for n in range(5)]
                values = [
                    self.edge(grad_edges[layer, n], tile + slot // SLOTS, slot % SLOTS)
                    for n, slot in enumerate(slots)
                ]
            else:
                values = [f_ref[c, z] for c in range(3)] + [inv_ref[z], grad_ref[layer]]
            total = None
            for c in range(3):
                term = values[c] * (efield[c] + values[3] * curl[c])
                total = term if total is None else total + term
            store(layer, values[4] + mask * total)

        def body(i, carry):
            return self.group(first_group + i, carry, emit)

        lax.fori_loop(0, layers // ROWS, body, self.start(first_group))


def fields_scratch(mode, xface, yface, width):
    rows, wide = xface.shape[0], faces_wide(mode, width)
    out = [pltpu.VMEM((rows, wide), jnp.float32)] * 2
    if mode != OWN:
        out.append(pltpu.VMEM((2,) + yface.shape, jnp.float32))
    return out


def own_gradient_kernel(counts, per_device, *refs):
    e_ref, h_ref, f_ref, inv_ref, grad_ref, mask_ref = refs[:6]
    zfaces, xfaces = refs[6 : 6 + counts[0]], refs[6 + counts[0] : 6 + sum(counts)]
    shares, (own_ref, *scratch) = refs[6 + sum(counts) : -3][::-1], refs[-3:]
    layers, _, width = grad_ref.shape
    fields = Fields(OWN, layers, (e_ref, h_ref), zfaces, xfaces, (), None, scratch)

    def store(layer, value):
        own_ref[layer] = value

    fields.gradient(layers, (f_ref, inv_ref, grad_ref, mask_ref), store)

    me = lax.axis_index("gx")
    for k, share in enumerate(shares):
        chunk = lax.bitwise_xor(me, way_there(len(shares))[k])
        for i in range(per_device):
            share[:, i * width : (i + 1) * width] = own_ref[chunk * per_device + i]
        if share.shape[1] > per_device * width:
            share[:, per_device * width :] = jnp.zeros((ROWS, SPARE), jnp.float32)


SPARE = LANES


def own_gradient(arrays, zfaces, xfaces):
    layers, _, width = arrays[4].shape
    count = lax.axis_size("gx")
    per_device = layers // count
    *shares, own = pl.pallas_call(
        functools.partial(own_gradient_kernel, (len(zfaces), len(xfaces)), per_device),
        in_specs=[VMEM] * (6 + len(zfaces) + len(xfaces)),
        out_specs=[VMEM] * (count + 1),
        out_shape=[fast(ROWS, per_device * width + SPARE)]
        + [fast(ROWS, per_device * width)] * (count - 1)
        + [fast(layers, ROWS, width)],
        scratch_shapes=fields_scratch(OWN, xfaces[0], None, width),
        compiler_params=params(),
    )(*arrays, *zfaces, *xfaces)
    return shares[::-1], own


PART = 2 * STRIP
SPAN = 2 * PART


def edge_gradient_kernel(counts, *refs):
    own_ref, f_ref, inv_ref, wide_ref, eh_ref, grad_ref, mask_ref, taps_ref = refs[:8]
    ends = np.cumsum((8,) + counts)
    zfaces, xfaces, lines, yfaces = (refs[i:j] for i, j in zip(ends[:-1], ends[1:]))
    (shares, message, edge_ref), scratch = refs[ends[-1] : -6], refs[-6:-3]
    folded, parts, slabs = refs[-3:]
    layers, _, width = own_ref.shape
    lane = lax.broadcasted_iota(jnp.int32, (ROWS, LANES), 1)
    first, last = STRIP, LANES - STRIP - 1
    fields = Fields(EDGE, layers, eh_ref, zfaces, xfaces, lines, yfaces, scratch)

    def store(layer, value):
        edge_ref[layer] = value

    fields.gradient(layers, (grad_ref, mask_ref), store)

    count = shares.shape[0]
    half = count // 2
    rows = half * ROWS
    me = lax.axis_index("gx")
    folded[...] = jnp.zeros_like(folded)
    fold = jnp.minimum(me, count - 1 - me)
    per_tile = LANES // SPAN
    for start in range(0, layers, per_tile):
        tile = jnp.zeros((ROWS, LANES), jnp.float32)
        for j in range(min(per_tile, layers - start)):
            edge = edge_ref[start + j]
            own = edge_tile(lambda s: own_ref[start + j, :, s], width)
            more = jnp.where(jnp.logical_or(lane == first, lane == last), edge - own, edge)
            low, high = SPAN * j + 1, SPAN * j + PART + STRIP - 1
            here = jnp.logical_and(lane >= low, lane < low + STRIP)
            tile = jnp.where(here, pltpu.roll(more, (low - 1) % LANES, 1), tile)
            here = jnp.logical_and(lane >= high, lane < high + STRIP)
            tile = jnp.where(here, pltpu.roll(more, (high - last) % LANES, 1), tile)
        tile = jnp.where(me < half, tile, flip_rows(tile))
        folded[fold, :, start // per_tile * LANES : (start // per_tile + 1) * LANES] = tile
    split_rows(jnp.concatenate([folded[s] for s in range(half)], axis=0), parts)
    total = cone(taps_ref, parts, rows)
    lanes = lax.broadcasted_iota(jnp.int32, (rows, LANES), 1)
    per_share = LANES // PART
    for start in range(0, layers, per_share):
        packed = jnp.zeros((rows, LANES), jnp.float32)
        for j in range(min(per_share, layers - start)):
            at = SPAN * (start + j)
            tile = total[:, at // LANES * LANES : (at // LANES + 1) * LANES]
            left = pltpu.roll(tile, (PART * j - STRIP - at) % LANES, 1)
            right = pltpu.roll(tile, (PART * j + STRIP - PART - 1 - at) % LANES, 1)
            packed = jnp.where(lanes // STRIP == 2 * j, left, packed)
            packed = jnp.where(lanes // STRIP == 2 * j + 1, right, packed)
        here = slice(start // per_share * LANES, (start // per_share + 1) * LANES)
        for s in range(half):
            one = packed[s * ROWS : (s + 1) * ROWS]
            slabs[s, :, here] = one
            slabs[count - 1 - s, :, here] = flip_rows(one)
    for k in range(count):
        shares[k] = slabs[lax.bitwise_xor(me, k)]

    message[...] = jnp.zeros_like(message)
    top, last = fields.cells_z - 1, ROWS - 1
    above, beyond = (line[0:1] for line in corner_lines(lines, slice(0, width)))
    added = wide_ref[0:1, :] * f_ref[2, top, 0:1, :] * inv_ref[top, 0:1, :] * (HALF * above)
    added += wide_ref[last:, :] * f_ref[0, 0, last:, :] * inv_ref[0, last:, :] * (HALF * beyond)
    column = lax.broadcasted_iota(jnp.int32, (1, width), 1)
    added = jnp.where(jnp.logical_or(column == 0, column == width - 1), 0.0, added)
    for at, n in line_places(width):
        message[n : n + 1, at : at + LANES] = added[:, (at // LANES * ROWS + n) * LANES :][:, :LANES]


def line_places(width):
    return [(t // ROWS * LANES, t % ROWS) for t in range(width // LANES)]


def line_of(message, width):
    return jnp.concatenate([message[n : n + 1, at : at + LANES] for at, n in line_places(width)], axis=1)


def line_spot(layers):
    bottom = lax.axis_index("gz") == 0
    return jnp.where(bottom, layers - 1, 0), jnp.where(bottom, 0, ROWS - 1)


def edge_gradient(own, arrays, edges, taps, zfaces, xfaces, lines, yfaces):
    layers, _, width = own.shape
    faces = (*zfaces, *xfaces, *lines, *yfaces)
    count = lax.axis_size("gx")
    share = (count, ROWS, math.ceil(layers * PART / LANES) * LANES)
    spread = math.ceil(layers * SPAN / LANES) * LANES
    line = math.ceil(width / LANES / ROWS) * LANES
    return pl.pallas_call(
        functools.partial(edge_gradient_kernel, (len(zfaces), len(xfaces), len(lines), len(yfaces))),
        in_specs=[VMEM] * (8 + len(faces)),
        out_specs=[VMEM] * 3,
        out_shape=[fast(*share), fast(ROWS, line), fast(layers, ROWS, LANES)],
        scratch_shapes=fields_scratch(EDGE, xfaces[0], yfaces[0], width)
        + [
            pltpu.VMEM((count // 2, ROWS, spread), jnp.float32),
            pltpu.VMEM((3 * count // 2 * ROWS, spread), jnp.bfloat16),
            pltpu.VMEM(share, jnp.float32),
        ],
        compiler_params=params(),
    )(own, arrays[2], arrays[3], arrays[5], *edges, taps, *faces)


def step_kernel(counts, *refs):
    e_ref, h_ref, inv_ref, own_ref, edge_ref, message = refs[:6]
    ends = np.cumsum((6,) + counts)
    zfaces, xfaces, lines, yfaces = (refs[i:j] for i, j in zip(ends[:-1], ends[1:]))
    e_out, h_out, grad_out = refs[ends[-1] + 1 : ends[-1] + 4]
    left_wide, right_wide, ybuf, e_new, h_new, grad_new, sems = refs[ends[-1] + 4 :]
    layers, _, width = own_ref.shape
    lane = lax.broadcasted_iota(jnp.int32, (ROWS, LANES), 1)

    for layer in range(layers):
        edge = edge_ref[layer]
        head, tail = own_ref[layer, :, 0:LANES], own_ref[layer, :, width - LANES :]
        grad_new[layer] = own_ref[layer]
        grad_new[layer, :, 0:LANES] = jnp.where(lane == 0, pltpu.roll(edge, LANES - STRIP, 1), head)
        grad_new[layer, :, width - LANES :] = jnp.where(lane == LANES - 1, pltpu.roll(edge, STRIP, 1), tail)
    layer, spot = line_spot(layers)
    row = lax.broadcasted_iota(jnp.int32, (ROWS, width), 0)
    grad_new[layer] += jnp.where(row == spot, line_of(message, width), 0.0)
    grad_copy = pltpu.make_async_copy(grad_new, grad_out, sems.at[0, 0])
    grad_copy.start()

    fields = Fields(CIRCLE, layers, (e_ref, h_ref), zfaces, xfaces, lines, yfaces, (left_wide, right_wide, ybuf))

    def emit(a, b, efield, hfield, curl):
        z = ROWS * a + b
        half_inv = inv_ref[z]
        for c in range(3):
            e_new[c, z] = efield[c][:, :width] + half_inv * curl[c][:, :width]
            h_new[c, z] = hfield[c][:, :width]

    def copies(a):
        here = pl.ds(a * ROWS, ROWS)
        return [
            pltpu.make_async_copy(new.at[c, here], out.at[c, here], sems.at[1 + a, 3 * n + c])
            for n, (new, out) in enumerate(((e_new, e_out), (h_new, h_out)))
            for c in range(3)
        ]

    def body(a, carry):
        carry = fields.group(a, carry, emit)
        for copy in copies(a):
            copy.start()
        return carry

    lax.fori_loop(0, fields.groups, body, fields.start(0))
    for a in range(fields.groups):
        for copy in copies(a):
            copy.wait()
    grad_copy.wait()


def step(efield, hfield, inv, own, edge, message, zfaces, xfaces, lines, yfaces, after):
    _, cells_z, _, width = efield.shape
    groups = (zfaces, xfaces, lines, yfaces)
    counts = tuple(len(group) for group in groups)
    shapes = (efield.shape, hfield.shape, own.shape)
    return pl.pallas_call(
        functools.partial(step_kernel, counts),
        in_specs=[VMEM] * (6 + sum(counts)) + [ANY],
        out_specs=[ANY] * 3,
        out_shape=[f32(*shape) for shape in shapes],
        scratch_shapes=fields_scratch(CIRCLE, xfaces[0], yfaces[0], width)
        + [pltpu.VMEM(shape, jnp.float32) for shape in shapes]
        + [pltpu.SemaphoreType.DMA((1 + cells_z // ROWS, 6))],
        compiler_params=params(),
    )(efield, hfield, inv, own, edge, message, *(one for group in groups for one in group), after)


def cone_taps():
    span = np.arange(-RADIUS, RADIUS + 1, dtype=np.float64)
    return np.maximum(RADIUS - np.sqrt(span[:, None] ** 2 + span[None, :] ** 2), 0.0)


def cone_sum():
    return cone_taps().sum()


def cone_matrix(rows):
    weight = cone_taps() / cone_sum()
    x = np.arange(rows)
    out = np.zeros((RADIUS + 1, rows, rows))
    for b in range(RADIUS + 1):
        for apart in (x[:, None] - x[None, :], 2 * rows - 1 - x[:, None] - x[None, :]):
            near = np.abs(apart) <= RADIUS
            out[b] += np.where(near, weight[np.clip(apart, -RADIUS, RADIUS) + RADIUS, RADIUS + b], 0.0)
    out = out.reshape((RADIUS + 1) * rows, rows).astype(np.float32)
    high = out.astype(jnp.bfloat16)
    low = (out - high.astype(np.float32)).astype(jnp.bfloat16)
    return np.concatenate([high, low, high], axis=1)


def flip_rows(v):
    row = lax.broadcasted_iota(jnp.int32, v.shape, 0)
    v = pltpu.roll(v, 4, 0)
    v = jnp.where(row % 4 < 2, pltpu.roll(v, ROWS - 2, 0), pltpu.roll(v, 2, 0))
    return jnp.where(row % 2 < 1, pltpu.roll(v, ROWS - 1, 0), pltpu.roll(v, 1, 0))


def split_rows(symmetric, parts):
    rows = symmetric.shape[0]
    high = symmetric.astype(jnp.bfloat16)
    low = (symmetric - high.astype(jnp.float32)).astype(jnp.bfloat16)
    parts[0:rows, :] = high
    parts[rows : 2 * rows, :] = high
    parts[2 * rows : 3 * rows, :] = low


def cone(taps_ref, parts, rows):
    wide = parts.shape[1]
    mixed = jnp.dot(taps_ref[...], parts[...], preferred_element_type=jnp.float32)
    total = mixed[0:rows]
    for b in range(1, RADIUS + 1):
        part = mixed[b * rows : (b + 1) * rows]
        total = total + (pltpu.roll(part, b, 1) + pltpu.roll(part, wide - b, 1))
    return total


def filter_kernel(count, per_device, width, *refs):
    taps_ref, edges_ref, line_ref = refs[:3]
    got = refs[count + 2 : 2 : -1]
    outs = refs[3 + count : 3 + 2 * count]
    slabs, parts, done = refs[3 + 2 * count :]
    me = lax.axis_index("gx")
    half = count // 2
    rows = half * ROWS
    for k in range(count):
        slabs[lax.bitwise_xor(me, way_there(count)[k])] = got[k][:, : per_device * width]

    side = jnp.zeros((rows, LANES), jnp.float32)
    for i in range(per_device):
        here = slice(i * width, (i + 1) * width)
        halves = [slabs[s, :, here] + flip_rows(slabs[count - 1 - s, :, here]) for s in range(half)]
        split_rows(jnp.concatenate([jnp.concatenate(halves, axis=0), side], axis=1), parts)
        total = cone(taps_ref, parts, rows)
        for s in range(half):
            own = total[s * ROWS : (s + 1) * ROWS, :width]
            done[s, :, here] = own
            done[count - 1 - s, :, here] = flip_rows(own)
    for k, apart in enumerate(way_back(count)):
        outs[k][:, : per_device * width] = done[lax.bitwise_xor(me, apart)]
        tail = per_device * width + edges_ref.shape[2]
        outs[k][:, per_device * width : tail] = edges_ref[apart]
        outs[k][:, tail:] = line_ref[...]


def cone_filter(taps, edges, line, got, per_device, width):
    count = len(got)
    rows = count // 2 * ROWS
    return pl.pallas_call(
        functools.partial(filter_kernel, count, per_device, width),
        in_specs=[VMEM] * (3 + count),
        out_specs=[VMEM] * count,
        out_shape=[fast(ROWS, per_device * width + edges.shape[2] + line.shape[1])] * count,
        scratch_shapes=[
            pltpu.VMEM((count, ROWS, per_device * width), jnp.float32),
            pltpu.VMEM((3 * rows, width + LANES), jnp.bfloat16),
            pltpu.VMEM((count, ROWS, per_device * width), jnp.float32),
        ],
        compiler_params=params(),
    )(taps, edges, line, *got[::-1])


def cone_weight(along_x, along_y):
    near = jnp.maximum(RADIUS - jnp.sqrt(along_x * along_x + float(along_y * along_y)), 0.0)
    return near * float(1.0 / cone_sum())


def finish_kernel(count, per_device, width, *refs):
    got = refs[count - 1 :: -1]
    out, (left, right, done, sems) = refs[count], refs[count + 1 :]
    me = lax.axis_index("gx")
    layers = count * per_device
    lane = lax.broadcasted_iota(jnp.int32, (ROWS, LANES), 1)
    edges_at = per_device * width
    line_at = edges_at + math.ceil(layers * PART / LANES) * LANES

    per_tile = LANES // PART
    for start in range(0, layers, per_tile):
        at = edges_at + start * PART
        tile = got[0][:, at : at + LANES]
        for k in range(1, count):
            tile = tile + got[k][:, at : at + LANES]
        for j in range(min(per_tile, layers - start)):
            head = pltpu.roll(tile, (-PART * j) % LANES, 1)
            left[start + j] = jnp.where(lane < STRIP - 1, head, 0.0)
            tail = pltpu.roll(tile, (LANES + 1 - 2 * STRIP - PART * j) % LANES, 1)
            right[start + j] = jnp.where(lane > LANES - STRIP, tail, 0.0)

    line_layer, spot = line_spot(layers)
    end = count * ROWS - 1
    row = lax.broadcasted_iota(jnp.int32, (ROWS, LANES), 0) + me * ROWS
    lines, near, far = [], [], []
    for k, apart in enumerate(way_back(count)):
        lines.append(line_of(got[k][:, line_at:], width))
        where = lax.bitwise_xor(me, apart) * ROWS + spot
        near.append((row - where).astype(jnp.float32))
        far.append((row - (end - where)).astype(jnp.float32))
    total = None
    for b in range(RADIUS + 1):
        mixed = jnp.zeros((ROWS, width), jnp.float32)
        for k in range(count):
            weight = cone_weight(near[k], b) + cone_weight(far[k], b)
            mixed = mixed + jnp.concatenate([weight] * (width // LANES), axis=1) * lines[k]
        mixed = jnp.concatenate([mixed, jnp.zeros((ROWS, LANES), jnp.float32)], axis=1)
        if b:
            mixed = pltpu.roll(mixed, b, 1) + pltpu.roll(mixed, width + LANES - b, 1)
        total = mixed if total is None else total + mixed
    line = total[:, :width]

    copies = []
    for k, apart in enumerate(way_back(count)):
        first = lax.bitwise_xor(me, apart) * per_device
        for i in range(per_device):
            at = i * width
            done[k, i] = got[k][:, at : at + width] + jnp.where(first + i == line_layer, line, 0.0)
            done[k, i, :, :LANES] += left[first + i]
            done[k, i, :, width - LANES :] += right[first + i]
        copies.append(pltpu.make_async_copy(done.at[k], out.at[pl.ds(first, per_device)], sems.at[k]))
        copies[-1].start()
    for copy in copies:
        copy.wait()


def finish(parts, layers, width):
    count = len(parts)
    per_device = layers // count
    return pl.pallas_call(
        functools.partial(finish_kernel, count, per_device, width),
        in_specs=[VMEM] * count,
        out_specs=ANY,
        out_shape=f32(layers, ROWS, width),
        scratch_shapes=[
            pltpu.VMEM((layers, ROWS, LANES), jnp.float32),
            pltpu.VMEM((layers, ROWS, LANES), jnp.float32),
            pltpu.VMEM((count, per_device, ROWS, width), jnp.float32),
            pltpu.SemaphoreType.DMA((count,)),
        ],
        compiler_params=params(),
    )(*parts[::-1])


def spread(parts, order):
    count = len(parts)
    got = list(parts)
    for j in range(count - 1, 0, -1):
        got[j] = lax.ppermute(parts[j], "gx", [(i, i ^ order[j]) for i in range(count)])
    return got


def way_there(count):
    return list(range(count))


def way_back(count):
    if count < 4:
        return list(range(count))
    return [0] + list(range(2, count - 1)) + [1, count - 1]


def on_device(efield, hfield, forward, material, permit, design_mask, grad_sum):
    layers, _, width = grad_sum.shape
    efield, hfield, zfaces, xfaces, lines = halos(efield, hfield)
    own_low, own_high, mask, inv = strips(
        permit, efield, hfield, forward, material, grad_sum, design_mask
    )
    arrays = (efield, hfield, forward, inv, grad_sum, mask)
    edges = own_edges(arrays)
    shares, own = own_gradient(arrays, zfaces, xfaces)
    got = spread(shares, way_there(len(shares)))
    yfaces = exchange(y_faces(own_low, own_high, zfaces, xfaces, lines, own), "gy", "gz")
    taps = jnp.asarray(cone_matrix(len(got) // 2 * ROWS))
    added, line, edge = edge_gradient(own, arrays, edges, taps, zfaces, xfaces, lines, yfaces)
    parts = cone_filter(taps, added, line, got, layers // len(got), width)
    e_next, h_next, grad_total = step(
        efield, hfield, inv, own, edge, line, zfaces, xfaces, lines, yfaces, parts[0]
    )
    return e_next, h_next, grad_total, finish(spread(parts, way_back(len(parts))), layers, width)


def solution(mesh):
    field = P(None, "gz", "gx", "gy")
    cells = P("gz", "gx", "gy")
    return jax.shard_map(
        on_device,
        mesh=mesh,
        in_specs=(field, field, field, cells, P(), P("gx", "gy"), cells),
        out_specs=(field, field, cells, cells),
        check_vma=False,
    )
```
